32 devices in a mesh: dp: 16 (over z, y, core), seq: 2 (over x).
Axes of the slice: x: 2, y: 2, z: 4, core: 2. Of those that a mesh axis runs over, the one named last changes fastest.
Arguments:
- short_tokens: bfloat16 [128, 128, 768], P(('dp', 'seq')), may hold values from -6 to 6
- long_tokens: bfloat16 [32, 512, 768], P('dp', 'seq'), may hold values from -6 to 6
- short_len: int32 [128], P(('dp', 'seq')), may hold values from 1 to 128, as said below
- long_len: int32 [32], P('dp'), may hold values from 129 to 512, as said below
- short_pool: int32 [128, 128], P(('dp', 'seq')), may hold values 0 or 1
- long_pool: int32 [32, 512], P('dp', 'seq'), may hold values 0 or 1
- short_cot: bfloat16 [128, 128, 768], P(('dp', 'seq')), may hold values from -6 to 6
- long_cot: bfloat16 [32, 512, 768], P('dp', 'seq'), may hold values from -6 to 6
- short_pool_cot: float32 [128, 768], P(('dp', 'seq')), may hold values from -6 to 6
- long_pool_cot: float32 [32, 768], P('dp'), may hold values from -6 to 6
- w_qkv: bfloat16 [768, 2304], P(('dp', 'seq')), may hold values from -0.21875 to 0.21875
- w_out: bfloat16 [768, 768], P(('dp', 'seq')), may hold values from -0.625 to 0.625
- w_up: bfloat16 [768, 3072], P(('dp', 'seq')), may hold values from -0.21875 to 0.21875
- w_down: bfloat16 [3072, 768], P(('dp', 'seq')), may hold values from -0.109375 to 0.109375
- qv_bias: bfloat16 [768, 2], P(('dp', 'seq')), may hold values from -3 to 3
- out_bias: bfloat16 [768, 2], P(('dp', 'seq')), may hold values from -3 to 3
- up_bias: bfloat16 [3072], P(('dp', 'seq')), may hold values from -3 to 3
- norm_gain: bfloat16 [768, 2], P(('dp', 'seq')), may hold values from 0.25 to 1.75
- norm_shift: bfloat16 [768, 2], P(('dp', 'seq')), may hold values from -3 to 3
Outputs:
- short_out: bfloat16 [128, 128, 768], P(('dp', 'seq'))
- long_out: bfloat16 [32, 512, 768], P('dp', 'seq')
- short_pooled: float32 [128, 768], P(('dp', 'seq'))
- long_pooled: float32 [32, 768], P('dp')
- short_grad_in: float32 [128, 128, 768], P(('dp', 'seq'))
- long_grad_in: float32 [32, 512, 768], P('dp', 'seq')
- grad_w_qkv: float32 [768, 2304], P(('dp', 'seq'))
- grad_w_out: float32 [768, 768], P(('dp', 'seq'))
- grad_w_up: float32 [768, 3072], P(('dp', 'seq'))
- grad_w_down: float32 [3072, 768], P(('dp', 'seq'))
- grad_qv_bias: float32 [768, 2], P(('dp', 'seq'))
- grad_out_bias: float32 [768, 2], P(('dp', 'seq'))
- grad_up_bias: float32 [3072], P(('dp', 'seq'))
- grad_norm_gain: float32 [768, 2], P(('dp', 'seq'))
- grad_norm_shift: float32 [768, 2], P(('dp', 'seq'))
The draws below stay inside these ranges and needn't reach their ends.
Inputs may be any that keep to these rules, and one draw needn't show every extreme that they name: `short_len`: among the 4 short sequences of each device, one has length exactly 128. `long_len`: among the 2 passages of each dp index, one has length exactly 512.
All inputs are finite; a program needn't handle non-finite values. No bound on the sum of `short_pool` or of `long_pool` on one device may be relied on, other than what follows from the above.
Results may differ from the reference program's by a relative error of at most 0.013.
Values may be sent and summed in bfloat16 or wider, within the bound.
A program may use at most 256 MiB of HBM per device.

```python
import math
import jax
import jax.numpy as jnp
from jax import lax

D = 768
HEADS = 12
FF = 3072
PASS = 512
QCAP = 128
PASS_DEV = 2
SHORT_DEV = 4
NPASS = 32
NSHORT = 128


def pinned_lengths(key, amount, per_group, lowest, highest):
    first_key, second_key = jax.random.split(key)
    drawn_len = jax.random.randint(first_key, (amount,), lowest, highest + 1)
    chosen_slot = jax.random.randint(second_key, (amount // per_group,), 0, per_group)
    marked_slot = (jnp.arange(per_group)[None, :] == chosen_slot[:, None]).reshape(amount)
    return jnp.where(marked_slot, highest, drawn_len).astype(jnp.int32)


def draw_short_len(key, part):
    key = jax.random.fold_in(key, 11)
    return pinned_lengths(key, NSHORT, SHORT_DEV, 1, QCAP)


def draw_long_len(key, part):
    key = jax.random.fold_in(key, 23)
    return pinned_lengths(key, NPASS, PASS_DEV, PASS // 4 + 1, PASS)


def place_ends(array, key, smallest, high):
    shape = array.shape
    index_at = [jax.random.randint(jax.random.fold_in(key, axis), (), 0, shape[axis]) for axis in range(len(shape))]
    array = array.at[tuple(index_at)].set(smallest)
    longest = shape.index(max(shape))
    index_at[longest] = (index_at[longest] + 1) % shape[longest]
    return array.at[tuple(index_at)].set(high)


def steps_of(key, extent, shards, smallest, top_value):
    level, own = 1.0, jax.random.fold_in(key, 6)
    for dim, parts in shards:
        draws = jnp.exp(jax.random.uniform(jax.random.fold_in(own, dim), (parts,), jnp.float32, smallest / len(shards), top_value / len(shards)))
        level = level * jnp.repeat(draws, extent[dim] // parts).reshape([-1 if axis == dim else 1 for axis in range(len(extent))])
    return level


def gaussian(rng, dims, width, reach, cuts=(), kind=jnp.bfloat16):
    array = jax.random.normal(rng, dims, jnp.float32) * width
    if len(cuts) > 0:
        array = steps_of(rng, dims, cuts, -0.22, 0.18) * array
    return jnp.clip(array, min=-reach, max=reach).astype(kind)


def setup_inputs(seed: int = 0) -> dict:
    arg_keys = jax.random.split(jax.random.key(seed), 20)
    return {
        "short_tokens": gaussian(arg_keys[0], (NSHORT, QCAP, D), 1.0, 6.0, ((0, 32),)),
        "long_tokens": gaussian(arg_keys[1], (NPASS, PASS, D), 1.0, 6.0, ((0, 16), (1, 2))),
        "short_len": draw_short_len(jax.random.fold_in(arg_keys[19], 71), 0),
        "long_len": draw_long_len(jax.random.fold_in(arg_keys[19], 71), 0),
        "short_pool": place_ends((jax.random.randint(arg_keys[4], (NSHORT, QCAP), 0, 4) < 3).astype(jnp.int32), jax.random.fold_in(arg_keys[4], 1), 0, 1),
        "long_pool": place_ends((jax.random.randint(arg_keys[5], (NPASS, PASS), 0, 4) < 3).astype(jnp.int32), jax.random.fold_in(arg_keys[5], 1), 0, 1),
        "short_cot": gaussian(arg_keys[6], (NSHORT, QCAP, D), 1.0, 6.0, ((0, 32),)),
        "long_cot": gaussian(arg_keys[7], (NPASS, PASS, D), 1.0, 6.0, ((0, 16), (1, 2))),
        "short_pool_cot": gaussian(arg_keys[8], (NSHORT, D), 1.0, 6.0, ((0, 32),), jnp.float32),
        "long_pool_cot": gaussian(arg_keys[9], (NPASS, D), 1.0, 6.0, ((0, 16),), jnp.float32),
        "w_qkv": gaussian(arg_keys[10], (D, 3 * D), D ** -0.5, 0.21875, ((0, 32),)),
        "w_out": gaussian(arg_keys[11], (D, D), (D // 8) ** -0.5, 0.625, ((0, 32),)),
        "w_up": gaussian(arg_keys[12], (D, FF), D ** -0.5, 0.21875, ((0, 32),)),
        "w_down": gaussian(arg_keys[13], (FF, D), FF ** -0.5, 0.109375, ((0, 32),)),
        "qv_bias": gaussian(arg_keys[14], (D, 2), 0.5, 3.0, ((0, 32),)),
        "out_bias": gaussian(arg_keys[15], (D, 2), 0.5, 3.0, ((0, 32),)),
        "up_bias": gaussian(arg_keys[16], (FF,), 0.5, 3.0, ((0, 32),)),
        "norm_gain": jnp.clip(1.0 + 0.15 * jax.random.normal(arg_keys[17], (D, 2), jnp.float32), 0.25, 1.75).astype(jnp.bfloat16),
        "norm_shift": gaussian(arg_keys[18], (D, 2), 0.5, 3.0, ((0, 32),)),
    }


EPS = 1e-12
HIGH = lax.Precision.HIGHEST

@jax.custom_vjp
def low(v):
    return lax.optimization_barrier(v.astype(jnp.bfloat16)).astype(jnp.float32)

@jax.custom_vjp
def low_back(v):
    return v

def low_keep(v):
    return (low(v), None)

def low_pass(kept, grad):
    return (grad,)

def back_keep(v):
    return (v, None)

def back_low(kept, grad):
    return (low(grad),)
low.defvjp(low_keep, low_pass)
low_back.defvjp(back_keep, back_low)

def layer_norm(row_data, gain_vec, shift_vec):
    center = row_data - lax.optimization_barrier(jnp.mean(row_data, axis=-1, keepdims=True))
    spread = lax.optimization_barrier(jnp.mean(center * center, axis=-1, keepdims=True))
    return center * lax.rsqrt(spread + EPS) * gain_vec + shift_vec

def project(row_data, matrix):
    return jnp.einsum('bld,de->ble', row_data, matrix, precision=HIGH)

def layer_block(params, tokens, lengths, pool_mask):
    qkv_matrix, out_matrix, up_matrix, down_matrix, qv_vec, out_vec, up_vec, gains, shifts = params
    seq_count, seqlen, model_width = tokens.shape
    head_dim = model_width // HEADS
    score_scale = 1.0 / math.sqrt(head_dim)
    positions = jnp.arange(seqlen, dtype=jnp.int32)
    is_live = positions[None, :] < lengths[:, None]
    joined = project(tokens, qkv_matrix)
    queries = low_back(low(joined[..., :model_width] + qv_vec[:, 0]))
    keys_all = low_back(low(joined[..., model_width:2 * model_width]))
    values = low_back(low(joined[..., 2 * model_width:] + qv_vec[:, 1]))
    shape_heads = (seq_count, seqlen, HEADS, head_dim)
    scores = jnp.einsum('bqhe,bkhe->bhqk', queries.reshape(shape_heads), keys_all.reshape(shape_heads), precision=HIGH)
    scores = low_back(scores * score_scale)
    scores = jnp.where(is_live[:, None, None, :], scores, -1e+30)
    highest = lax.optimization_barrier(jnp.max(scores, axis=-1, keepdims=True))
    exponent = jnp.exp(scores - highest)
    soft_probs = low(exponent / lax.optimization_barrier(jnp.sum(exponent, axis=-1, keepdims=True)))
    mixed_heads = jnp.einsum('bhqk,bkhe->bqhe', soft_probs, values.reshape(shape_heads), precision=HIGH)
    mixed_heads = low_back(low(mixed_heads.reshape(seq_count, seqlen, model_width)))
    attn_out = low_back(project(mixed_heads, out_matrix) + out_vec[:, 0])
    first_norm = layer_norm(tokens + attn_out, gains[:, 0], shifts[:, 0])
    inner_act = low_back(project(low(first_norm), up_matrix) + up_vec)
    activated = low(jax.nn.gelu(inner_act, approximate=False))
    branch = low_back(project(activated, down_matrix) + out_vec[:, 1])
    final_norm = layer_norm(first_norm + branch, gains[:, 1], shifts[:, 1]) * is_live[..., None]
    pool_weight = (is_live & ((pool_mask > 0) | (positions[None, :] == 0))).astype(tokens.dtype)
    pooled = lax.optimization_barrier(jnp.sum(final_norm * pool_weight[..., None], axis=1)) / lax.optimization_barrier(jnp.sum(pool_weight, axis=1))[:, None]
    return (final_norm, pooled)

def run_blocks(params, tokens, lengths, pool_mask, per_block):
    blocks = tokens.shape[0] // per_block

    def block_step(unused_carry, pieces):
        final_norm, pooled = jax.checkpoint(layer_block)(params, pieces[0], pieces[1], pieces[2])
        return (unused_carry, (final_norm, pooled))
    stacked = (tokens.reshape((blocks, per_block) + tokens.shape[1:]), lengths.reshape(blocks, per_block), pool_mask.reshape(blocks, per_block, tokens.shape[1]))
    _, (final_norm, pooled) = lax.scan(block_step, jnp.zeros((), jnp.float32), stacked)
    return (final_norm.reshape(tokens.shape), pooled.reshape(tokens.shape[0], tokens.shape[2]))

def reference(short_tokens, long_tokens, short_len, long_len, short_pool, long_pool, short_cot, long_cot, short_pool_cot, long_pool_cot, w_qkv, w_out, w_up, w_down, qv_bias, out_bias, up_bias, norm_gain, norm_shift):
    params = tuple((member.astype(jnp.float32) for member in (w_qkv, w_out, w_up, w_down, qv_bias, out_bias, up_bias, norm_gain, norm_shift)))
    short_block = math.gcd(NSHORT, max(1, 4096 // QCAP))
    long_block = math.gcd(NPASS, max(1, 4096 // PASS))

    def forward(weights, short_rows, long_rows):
        short_final, short_pooled = run_blocks(weights, short_rows, short_len, short_pool, short_block)
        long_final, long_pooled = run_blocks(weights, long_rows, long_len, long_pool, long_block)
        return (short_final, long_final, short_pooled, long_pooled)
    results, pullback = jax.vjp(forward, params, short_tokens.astype(jnp.float32), long_tokens.astype(jnp.float32))
    weight_grads, short_grad, long_grad = pullback((short_cot.astype(jnp.float32), long_cot.astype(jnp.float32), short_pool_cot.astype(jnp.float32), long_pool_cot.astype(jnp.float32)))
    return (results[0].astype(jnp.bfloat16), results[1].astype(jnp.bfloat16), results[2], results[3], short_grad, long_grad, weight_grads[0], weight_grads[1], weight_grads[2], weight_grads[3], weight_grads[4], weight_grads[5], weight_grads[6], weight_grads[7], weight_grads[8])
```

```python
import functools
import math

import jax
import jax.numpy as jnp
from jax import lax
from jax.experimental import pallas as pl
from jax.experimental.pallas import tpu as pltpu
from jax.sharding import PartitionSpec as P

HEADS = 12
EPS = 1e-12
MESH = pl.DeviceIdType.MESH

CHUNKS = ((0, 48, 32), (80, 64, 64), (208, 48, 48))
SLAB = 304


class Place:
    def __init__(self):
        dp = lax.axis_index("dp")
        self.x = lax.axis_index("seq")
        self.groups = lax.axis_size("dp") // 4
        self.z = lax.div(dp, 4)
        self.y = lax.rem(lax.div(dp, 2), 2)
        self.c = lax.rem(dp, 2)
        self.dp = dp

    def at_z(self, step):
        z = lax.rem(self.z + step, self.groups)
        return (z * 4 + self.y * 2 + self.c, self.x)

    def at_x(self):
        return (self.dp, 1 - self.x)

    def at_y(self):
        return (self.z * 4 + (1 - self.y) * 2 + self.c, self.x)

    def at_core(self):
        return (self.z * 4 + self.y * 2 + 1 - self.c, self.x)

    def slot(self, flip_y=0, flip_c=0, flip_x=0):
        y = 1 - self.y if flip_y else self.y
        c = 1 - self.c if flip_c else self.c
        x = 1 - self.x if flip_x else self.x
        return y * 4 + c * 2 + x

    def z_back(self, step):
        return lax.rem(self.z + self.groups - step, self.groups)

    def partners(self):
        return [self.at_z(step) for step in range(1, self.groups)] + [
            self.at_x(),
            self.at_y(),
            self.at_core(),
        ]

    def greet(self):
        barrier = pltpu.get_barrier_semaphore()
        partners = self.partners()
        for partner in partners:
            pl.semaphore_signal(barrier, inc=1, device_id=partner, device_id_type=MESH)
        pl.semaphore_wait(barrier, len(partners))


class Wires:
    def __init__(self, send, recv):
        self.send, self.recv, self.sent = send, recv, []

    def put(self, src, dst, to):
        number = len(self.sent)
        copy = pltpu.make_async_remote_copy(
            src_ref=src,
            dst_ref=dst,
            send_sem=self.send.at[number],
            recv_sem=self.recv.at[number],
            device_id=to,
            device_id_type=MESH,
        )
        copy.start()
        self.sent.append(copy)
        return (number, to)

    def landed(self, ticket, ref):
        number, to = ticket
        pltpu.make_async_remote_copy(
            src_ref=ref,
            dst_ref=ref,
            send_sem=self.send.at[number],
            recv_sem=self.recv.at[number],
            device_id=to,
            device_id_type=MESH,
        ).wait_recv()

    def close(self):
        for copy in self.sent:
            copy.wait_send()


class Gather:
    def __init__(self, wires, place, slab, whole):
        self.wires, self.place, self.slab, self.whole = wires, place, slab, whole
        self.steps = place.groups
        self.own, self.along_z, self.along_x, self.along_y = {}, {}, {}, {}
        self.by_x, self.by_y, self.core = {}, {}, {}

    def start(self, k):
        first, some, more = CHUNKS[k]
        rows = pl.ds(first, some + more)
        place, wires = self.place, self.wires
        src = self.slab.at[rows]
        dst = self.whole.at[place.z, place.slot(), rows]
        for step in range(1, self.steps):
            self.along_z[k, step] = wires.put(src, dst, place.at_z(step))
        self.along_x[k, 0] = wires.put(src, dst, place.at_x())
        self.along_y[k, 0] = wires.put(src, dst, place.at_y())
        self.core[k, 0, 0] = wires.put(src, dst, place.at_core())

    def relay_z(self, k):
        first, some, more = CHUNKS[k]
        rows = pl.ds(first, some + more)
        place, wires = self.place, self.wires
        for step in range(1, self.steps):
            ref = self.whole.at[place.z_back(step), place.slot(), rows]
            wires.landed(self.along_z[k, step], ref)
            self.along_x[k, step] = wires.put(ref, ref, place.at_x())
            self.along_y[k, step] = wires.put(ref, ref, place.at_y())
            self.core[k, 0, step] = wires.put(ref, ref, place.at_core())

    def relay_plane(self, k):
        first, some, more = CHUNKS[k]
        rows, upper, lower = pl.ds(first, some + more), pl.ds(first, some), pl.ds(first + some, more)
        place, wires = self.place, self.wires
        for step in range(self.steps):
            z = place.z_back(step)
            slot = place.slot(flip_x=1)
            ref = self.whole.at[z, slot, rows]
            wires.landed(self.along_x[k, step], ref)
            half = self.whole.at[z, slot, upper]
            self.by_y[k, step] = wires.put(half, half, place.at_y())
            self.core[k, 1, step] = wires.put(ref, ref, place.at_core())
            slot = place.slot(flip_y=1)
            ref = self.whole.at[z, slot, rows]
            wires.landed(self.along_y[k, step], ref)
            half = self.whole.at[z, slot, lower]
            self.by_x[k, step] = wires.put(half, half, place.at_x())
            self.core[k, 2, step] = wires.put(ref, ref, place.at_core())

    def relay_corner(self, k):
        first, some, more = CHUNKS[k]
        rows, upper, lower = pl.ds(first, some + more), pl.ds(first, some), pl.ds(first + some, more)
        place, wires = self.place, self.wires
        for step in range(self.steps):
            z = place.z_back(step)
            slot = place.slot(flip_x=1, flip_y=1)
            wires.landed(self.by_y[k, step], self.whole.at[z, slot, upper])
            wires.landed(self.by_x[k, step], self.whole.at[z, slot, lower])
            ref = self.whole.at[z, slot, rows]
            self.core[k, 3, step] = wires.put(ref, ref, place.at_core())

    def finish(self, k):
        first, some, more = CHUNKS[k]
        rows = pl.ds(first, some + more)
        place = self.place
        flips = ((0, 0), (0, 1), (1, 0), (1, 1))
        for part, (flip_y, flip_x) in enumerate(flips):
            slot = place.slot(flip_y=flip_y, flip_c=1, flip_x=flip_x)
            for step in range(self.steps):
                self.wires.landed(
                    self.core[k, part, step], self.whole.at[place.z_back(step), slot, rows]
                )


def gather_kernel(
    slab, short_tok, long_tok, short_cot, long_cot, pool,
    whole, rows_in, rows_cot, pool_out,
    send, recv, here,
):
    place = Place()
    short_rows, half = short_tok.shape[0], long_tok.shape[1]
    x, other = place.x, 1 - place.x
    mine = pl.ds(pl.multiple_of(short_rows + x * half, half), half)
    local = [
        (short_tok, rows_in.at[pl.ds(0, short_rows)]),
        (long_tok.at[x], rows_in.at[mine]),
        (short_cot, rows_cot.at[pl.ds(0, short_rows)]),
        (long_cot.at[x], rows_cot.at[mine]),
        (pool.at[x], pool_out.at[x]),
        (slab, whole.at[place.z, place.slot()]),
    ]
    copies = [pltpu.make_async_copy(src, dst, here.at[i]) for i, (src, dst) in enumerate(local)]
    for copy in copies:
        copy.start()
    place.greet()
    wires = Wires(send, recv)
    net = Gather(wires, place, slab, whole)
    net.start(0)
    theirs = pl.ds(pl.multiple_of(short_rows + other * half, half), half)
    tok = wires.put(long_tok.at[other], rows_in.at[mine], place.at_x())
    pooled = wires.put(pool.at[other], pool_out.at[x], place.at_x())
    last = len(CHUNKS) - 1
    for k in range(last + 1):
        if k < last:
            net.start(k + 1)
        net.relay_z(k)
        net.relay_plane(k)
        net.relay_corner(k)
        if k == 0:
            cot = wires.put(long_cot.at[other], rows_cot.at[mine], place.at_x())
    for k in range(last + 1):
        net.finish(k)
    wires.landed(tok, rows_in.at[theirs])
    wires.landed(cot, rows_cot.at[theirs])
    wires.landed(pooled, pool_out.at[other])
    wires.close()
    for copy in copies:
        copy.wait()


def gather_all(slab, short_tok, long_tok, short_cot, long_cot, pool, groups):
    short_rows, width = short_tok.shape
    rows = short_rows + 2 * long_tok.shape[1]
    copies = len(CHUNKS) * ((groups - 1) + 4 * groups + 4 * groups) + 3
    anywhere = pl.BlockSpec(memory_space=pl.ANY)
    return pl.pallas_call(
        gather_kernel,
        name="gather_parameters",
        out_shape=(
            jax.ShapeDtypeStruct((groups, 8) + slab.shape, slab.dtype),
            jax.ShapeDtypeStruct((rows, width), short_tok.dtype),
            jax.ShapeDtypeStruct((rows, width), short_cot.dtype),
            jax.ShapeDtypeStruct(pool.shape, pool.dtype),
        ),
        in_specs=[anywhere] * 6,
        out_specs=[anywhere] * 4,
        scratch_shapes=[
            pltpu.SemaphoreType.DMA((copies,)),
            pltpu.SemaphoreType.DMA((copies,)),
            pltpu.SemaphoreType.DMA((6,)),
        ],
        compiler_params=pltpu.CompilerParams(collective_id=0, has_side_effects=True),
    )(slab, short_tok, long_tok, short_cot, long_cot, pool)


class Scatter:
    def __init__(self, wires, place, sums, from_core, from_x, from_y, last_x, last_y, from_z, out):
        self.wires, self.place = wires, place
        self.sums, self.from_core, self.from_x, self.from_y = sums, from_core, from_x, from_y
        self.last_x, self.last_y, self.from_z, self.out = last_x, last_y, from_z, out
        self.steps = place.groups
        self.core, self.first, self.second, self.third = {}, {}, {}, {}

    def send_core(self, k, grads):
        first, some, more = CHUNKS[k]
        rows = pl.ds(first, some + more)
        place = self.place
        for part, (flip_y, flip_x) in enumerate(((0, 0), (0, 1), (1, 0), (1, 1))):
            slot = place.slot(flip_y=flip_y, flip_c=1, flip_x=flip_x)
            self.core[k, part] = self.wires.put(
                grads.at[:, slot, rows], self.from_core.at[part, :, rows], place.at_core()
            )

    def add(self, into, other):
        for z in range(self.steps):
            total = into[z].astype(jnp.float32) + other[z].astype(jnp.float32)
            into[z] = total.astype(into.dtype)

    def after_core(self, k):
        first, some, more = CHUNKS[k]
        rows, upper, lower = pl.ds(first, some + more), pl.ds(first, some), pl.ds(first + some, more)
        wires, place = self.wires, self.place
        for part in (3, 1, 2, 0):
            wires.landed(self.core[k, part], self.from_core.at[part, :, rows])
            self.add(self.sums.at[part, :, rows], self.from_core.at[part, :, rows])
            if part == 3:
                self.first[k, "x", 1] = wires.put(
                    self.sums.at[3, :, upper], self.from_x.at[1, :, upper], place.at_x()
                )
                self.first[k, "y", 1] = wires.put(
                    self.sums.at[3, :, lower], self.from_y.at[1, :, lower], place.at_y()
                )
            elif part == 1:
                self.first[k, "x", 0] = wires.put(
                    self.sums.at[1, :, upper], self.from_x.at[0, :, upper], place.at_x()
                )
            elif part == 2:
                self.first[k, "y", 0] = wires.put(
                    self.sums.at[2, :, lower], self.from_y.at[0, :, lower], place.at_y()
                )

    def after_first(self, k):
        first, some, more = CHUNKS[k]
        upper, lower = pl.ds(first, some), pl.ds(first + some, more)
        wires, place = self.wires, self.place
        wires.landed(self.first[k, "x", 1], self.from_x.at[1, :, upper])
        self.add(self.sums.at[2, :, upper], self.from_x.at[1, :, upper])
        self.second[k, "y"] = wires.put(
            self.sums.at[2, :, upper], self.last_y.at[:, upper], place.at_y()
        )
        wires.landed(self.first[k, "y", 1], self.from_y.at[1, :, lower])
        self.add(self.sums.at[1, :, lower], self.from_y.at[1, :, lower])
        self.second[k, "x"] = wires.put(
            self.sums.at[1, :, lower], self.last_x.at[:, lower], place.at_x()
        )
        wires.landed(self.first[k, "x", 0], self.from_x.at[0, :, upper])
        self.add(self.sums.at[0, :, upper], self.from_x.at[0, :, upper])
        wires.landed(self.first[k, "y", 0], self.from_y.at[0, :, lower])
        self.add(self.sums.at[0, :, lower], self.from_y.at[0, :, lower])

    def after_second(self, k):
        first, some, more = CHUNKS[k]
        rows, upper, lower = pl.ds(first, some + more), pl.ds(first, some), pl.ds(first + some, more)
        wires, place = self.wires, self.place
        wires.landed(self.second[k, "y"], self.last_y.at[:, upper])
        self.add(self.sums.at[0, :, upper], self.last_y.at[:, upper])
        wires.landed(self.second[k, "x"], self.last_x.at[:, lower])
        self.add(self.sums.at[0, :, lower], self.last_x.at[:, lower])
        for step in range(1, self.steps):
            z = lax.rem(place.z + step, self.steps)
            self.third[k, step] = wires.put(
                self.sums.at[0, z, rows], self.from_z.at[step - 1, rows], place.at_z(step)
            )

    def finish(self, k):
        first, some, more = CHUNKS[k]
        rows = pl.ds(first, some + more)
        total = self.sums[0, self.place.z, rows].astype(jnp.float32)
        for step in range(1, self.steps):
            self.wires.landed(self.third[k, step], self.from_z.at[step - 1, rows])
            total = total + self.from_z[step - 1, rows].astype(jnp.float32)
        self.out[rows] = total


def scatter_kernel(
    grads, long_out, long_grad, pooled,
    out, both_out, both_grad, both_pooled,
    sums, from_core, from_x, from_y, last_x, last_y, from_z,
    send, recv, load, here,
):
    place = Place()
    x, other = place.x, 1 - place.x
    half = both_out.shape[1]
    own_rows = pl.ds(pl.multiple_of(x * half, half), half)
    their_rows = pl.ds(pl.multiple_of(other * half, half), half)
    loads = {}
    order = (2, 1, 0)
    for k in order:
        first, some, more = CHUNKS[k]
        rows = pl.ds(first, some + more)
        for part, (flip_y, flip_x) in enumerate(((0, 0), (0, 1), (1, 0), (1, 1))):
            slot = place.slot(flip_y=flip_y, flip_x=flip_x)
            loads[k, part] = pltpu.make_async_copy(
                grads.at[:, slot, rows], sums.at[part, :, rows], load.at[k * 4 + part]
            )
            loads[k, part].start()
    copies = [
        pltpu.make_async_copy(long_out.at[own_rows], both_out.at[x], here.at[0]),
        pltpu.make_async_copy(long_grad.at[own_rows], both_grad.at[x], here.at[1]),
        pltpu.make_async_copy(pooled, both_pooled.at[x], here.at[2]),
    ]
    for copy in copies:
        copy.start()
    place.greet()
    wires = Wires(send, recv)
    net = Scatter(wires, place, sums, from_core, from_x, from_y, last_x, last_y, from_z, out)
    for k in order:
        net.send_core(k, grads)
    swaps = [
        (wires.put(long_out.at[their_rows], both_out.at[x], place.at_x()), both_out),
        (wires.put(long_grad.at[their_rows], both_grad.at[x], place.at_x()), both_grad),
        (wires.put(pooled, both_pooled.at[x], place.at_x()), both_pooled),
    ]
    todo = []
    for k in order:
        for part in range(4):
            loads[k, part].wait()
        net.after_core(k)
        if len(todo) >= 1:
            net.after_first(todo[-1])
        if len(todo) >= 2:
            net.after_second(todo[-2])
        todo.append(k)
    net.after_first(todo[-1])
    net.after_second(todo[-2])
    net.after_second(todo[-1])
    for k in order:
        net.finish(k)
    for ticket, ref in swaps:
        wires.landed(ticket, ref.at[other])
    wires.close()
    for copy in copies:
        copy.wait()


def scatter_all(grads, long_out, long_grad, pooled, groups):
    width = grads.shape[-1]
    half = long_out.shape[0] // 2
    copies = len(CHUNKS) * (4 + 6 + (groups - 1)) + 3
    anywhere = pl.BlockSpec(memory_space=pl.ANY)
    low = jnp.bfloat16
    return pl.pallas_call(
        scatter_kernel,
        name="scatter_gradients",
        out_shape=(
            jax.ShapeDtypeStruct((SLAB, width), jnp.float32),
            jax.ShapeDtypeStruct((2, half, width), long_out.dtype),
            jax.ShapeDtypeStruct((2, half, width), long_grad.dtype),
            jax.ShapeDtypeStruct((2,) + pooled.shape, pooled.dtype),
        ),
        in_specs=[anywhere] * 4,
        out_specs=[pl.BlockSpec(memory_space=pltpu.VMEM)] + [anywhere] * 3,
        scratch_shapes=[
            pltpu.VMEM((4, groups, SLAB, width), low),
            pltpu.VMEM((4, groups, SLAB, width), low),
            pltpu.VMEM((2, groups, SLAB, width), low),
            pltpu.VMEM((2, groups, SLAB, width), low),
            pltpu.VMEM((groups, SLAB, width), low),
            pltpu.VMEM((groups, SLAB, width), low),
            pltpu.VMEM((groups - 1, SLAB, width), low),
            pltpu.SemaphoreType.DMA((copies,)),
            pltpu.SemaphoreType.DMA((copies,)),
            pltpu.SemaphoreType.DMA((4 * len(CHUNKS),)),
            pltpu.SemaphoreType.DMA((3,)),
        ],
        compiler_params=pltpu.CompilerParams(
            collective_id=1, has_side_effects=True, vmem_limit_bytes=48 * 1024 * 1024
        ),
    )(grads, long_out, long_grad, pooled)


def layer_norm(row_data, gain_vec, shift_vec):
    center = row_data - jnp.mean(row_data, axis=-1, keepdims=True)
    spread = jnp.mean(center * center, axis=-1, keepdims=True)
    return center * lax.rsqrt(spread + EPS) * gain_vec + shift_vec


def exact_gelu(inner_act):
    return jax.nn.gelu(inner_act, approximate=False)


def outer_sum(left_rows, right_rows):
    return lax.dot_general(
        left_rows, right_rows, (((0,), (0,)), ((), ())), preferred_element_type=jnp.float32
    )


def times_transposed(left_rows, matrix):
    return lax.dot_general(
        left_rows, matrix, (((1,), (1,)), ((), ())), preferred_element_type=jnp.float32
    )


def masked_scores(queries, keys_all, key_live, score_scale):
    scores = (
        jnp.einsum("bqhe,bkhe->bhqk", queries, keys_all, preferred_element_type=jnp.float32)
        * score_scale
    )
    return jnp.where(key_live[:, None, None, :], scores, -1e30)


def attend_forward(pieces, score_scale):
    queries, keys_all, values, key_live = pieces
    scores = masked_scores(queries, keys_all, key_live, score_scale)
    highest = jnp.max(scores, axis=-1, keepdims=True)
    exponent = jnp.exp(scores - highest)
    totals = jnp.sum(exponent, axis=-1, keepdims=True)
    soft_probs = (exponent / totals).astype(jnp.bfloat16)
    mixed_heads = jnp.einsum(
        "bhqk,bkhe->bqhe", soft_probs, values, preferred_element_type=jnp.float32
    )
    return (mixed_heads.astype(jnp.bfloat16), (highest + jnp.log(totals))[..., 0])


def attend_backward(pieces, score_scale):
    queries, keys_all, values, key_live, grad_mixed, log_total = pieces
    scores = masked_scores(queries, keys_all, key_live, score_scale)
    soft_probs = jnp.exp(scores - log_total[..., None])
    grad_probs = jnp.einsum(
        "bqhe,bkhe->bhqk", grad_mixed, values, preferred_element_type=jnp.float32
    )
    grad_values = jnp.einsum(
        "bhqk,bqhe->bkhe",
        soft_probs.astype(jnp.bfloat16),
        grad_mixed,
        preferred_element_type=jnp.float32,
    )
    center = jnp.sum(soft_probs * grad_probs, axis=-1, keepdims=True)
    grad_scores = (soft_probs * (grad_probs - center)).astype(jnp.bfloat16)
    grad_queries = (
        jnp.einsum("bhqk,bkhe->bqhe", grad_scores, keys_all, preferred_element_type=jnp.float32)
        * score_scale
    )
    grad_keys = (
        jnp.einsum("bhqk,bqhe->bkhe", grad_scores, queries, preferred_element_type=jnp.float32)
        * score_scale
    )
    return (grad_queries, grad_keys, grad_values)


def by_blocks(function, per_block, arrays):
    blocks = arrays[0].shape[0] // per_block
    stacked = tuple((member.reshape((blocks, per_block) + member.shape[1:]) for member in arrays))
    results = lax.map(function, stacked)
    return jax.tree.map(
        lambda member: member.reshape((blocks * per_block,) + member.shape[2:]), results
    )


def general_shards(
    short_tokens,
    long_tokens,
    short_len,
    long_len,
    short_pool,
    long_pool,
    short_cot,
    long_cot,
    short_pool_cot,
    long_pool_cot,
    w_qkv,
    w_out,
    w_up,
    w_down,
    qv_bias,
    out_bias,
    up_bias,
    norm_gain,
    norm_shift,
):
    gathered = (
        lax.all_gather(w_qkv, ("dp", "seq"), axis=0, tiled=True),
        lax.all_gather(w_out, ("dp", "seq"), axis=0, tiled=True),
        lax.all_gather(w_up, ("dp", "seq"), axis=0, tiled=True),
        lax.all_gather(w_down, ("dp", "seq"), axis=0, tiled=True),
        lax.all_gather(qv_bias, ("dp", "seq"), axis=0, tiled=True),
        lax.all_gather(out_bias, ("dp", "seq"), axis=0, tiled=True),
        lax.all_gather(up_bias, ("dp", "seq"), axis=0, tiled=True),
        lax.all_gather(norm_gain, ("dp", "seq"), axis=0, tiled=True),
        lax.all_gather(norm_shift, ("dp", "seq"), axis=0, tiled=True),
    )
    qkv_matrix, out_matrix, up_matrix, down_matrix, qv_vec, out_vec, up_vec, gains, shifts = (
        gathered
    )
    gains = gains.astype(jnp.float32)
    shifts = shifts.astype(jnp.float32)
    short_count, short_cap, model_width = short_tokens.shape
    long_count, long_half = (long_tokens.shape[0], long_tokens.shape[1])
    head_count = HEADS
    head_dim = model_width // head_count
    score_scale = 1.0 / math.sqrt(head_dim)
    short_rows = short_count * short_cap
    long_rows = long_count * long_half
    short_place = jnp.arange(short_cap, dtype=jnp.int32)
    short_live = short_place[None, :] < short_len[:, None]
    long_place = lax.axis_index("seq") * long_half + jnp.arange(long_half, dtype=jnp.int32)
    long_live = long_place[None, :] < long_len[:, None]
    short_weight = (short_live & ((short_pool > 0) | (short_place[None, :] == 0))).astype(
        jnp.float32
    )
    long_weight = (long_live & ((long_pool > 0) | (long_place[None, :] == 0))).astype(jnp.float32)
    row_live = jnp.concatenate([short_live.reshape(-1), long_live.reshape(-1)]).astype(jnp.float32)
    inputs = jnp.concatenate(
        [
            short_tokens.reshape(short_rows, model_width),
            long_tokens.reshape(long_rows, model_width),
        ],
        axis=0,
    )
    joined = jnp.dot(inputs, qkv_matrix, preferred_element_type=jnp.float32)
    queries = (joined[:, :model_width] + qv_vec[:, 0]).astype(jnp.bfloat16)
    keys_all = joined[:, model_width : 2 * model_width].astype(jnp.bfloat16)
    values = (joined[:, 2 * model_width :] + qv_vec[:, 1]).astype(jnp.bfloat16)
    short_shape = (short_count, short_cap, head_count, head_dim)
    long_shape = (long_count, long_half, head_count, head_dim)
    short_q = queries[:short_rows].reshape(short_shape)
    short_k = keys_all[:short_rows].reshape(short_shape)
    short_v = values[:short_rows].reshape(short_shape)
    long_q = queries[short_rows:].reshape(long_shape)
    long_k = keys_all[short_rows:].reshape(long_count, long_half, model_width)
    long_v = values[short_rows:].reshape(long_count, long_half, model_width)
    short_block = math.gcd(short_count, max(1, 512 // short_cap))
    long_block = math.gcd(long_count, max(1, 512 // long_half))

    def forward_blocks(pieces):
        return attend_forward(pieces, score_scale)

    def backward_blocks(pieces):
        return attend_backward(pieces, score_scale)

    short_mixed, short_logsum = by_blocks(
        forward_blocks, short_block, (short_q, short_k, short_v, short_live)
    )
    gathered_k, gathered_v = (
        lax.all_gather(long_k, "seq", axis=1, tiled=True),
        lax.all_gather(long_v, "seq", axis=1, tiled=True),
    )
    full_len = gathered_k.shape[1]
    full_shape = (long_count, full_len, head_count, head_dim)
    long_key_live = jnp.arange(full_len, dtype=jnp.int32)[None, :] < long_len[:, None]
    long_mixed, long_logsum = by_blocks(
        forward_blocks,
        long_block,
        (long_q, gathered_k.reshape(full_shape), gathered_v.reshape(full_shape), long_key_live),
    )
    mixed_heads = jnp.concatenate(
        [short_mixed.reshape(short_rows, model_width), long_mixed.reshape(long_rows, model_width)],
        axis=0,
    )
    attn_out = jnp.dot(mixed_heads, out_matrix, preferred_element_type=jnp.float32) + out_vec[:, 0]
    first_in = inputs.astype(jnp.float32) + attn_out
    first_norm = layer_norm(first_in, gains[:, 0], shifts[:, 0])
    first_low = first_norm.astype(jnp.bfloat16)
    inner_act = jnp.dot(first_low, up_matrix, preferred_element_type=jnp.float32) + up_vec
    activated = exact_gelu(inner_act).astype(jnp.bfloat16)
    branch = jnp.dot(activated, down_matrix, preferred_element_type=jnp.float32) + out_vec[:, 1]
    second_in = first_norm + branch
    final_norm = layer_norm(second_in, gains[:, 1], shifts[:, 1]) * row_live[:, None]
    short_final = final_norm[:short_rows].reshape(short_count, short_cap, model_width)
    long_final = final_norm[short_rows:].reshape(long_count, long_half, model_width)
    short_total = jnp.sum(short_weight, axis=1)
    short_pooled = jnp.sum(short_final * short_weight[..., None], axis=1) / short_total[:, None]
    long_partial = jnp.sum(long_final * long_weight[..., None], axis=1)
    long_sum, long_total = lax.psum((long_partial, jnp.sum(long_weight, axis=1)), "seq")
    long_pooled = long_sum / long_total[:, None]
    grad_short = (
        short_cot.astype(jnp.float32) * short_live[..., None]
        + short_weight[..., None] * short_pool_cot[:, None, :] / short_total[:, None, None]
    )
    grad_long = (
        long_cot.astype(jnp.float32) * long_live[..., None]
        + long_weight[..., None] * long_pool_cot[:, None, :] / long_total[:, None, None]
    )
    grad_top = jnp.concatenate(
        [grad_short.reshape(short_rows, model_width), grad_long.reshape(long_rows, model_width)],
        axis=0,
    )
    _, second_back = jax.vjp(layer_norm, second_in, gains[:, 1], shifts[:, 1])
    grad_second, grad_gain_two, grad_shift_two = second_back(grad_top)
    grad_branch = grad_second.astype(jnp.bfloat16)
    grad_down = outer_sum(activated, grad_branch)
    grad_bias_two = jnp.sum(grad_branch.astype(jnp.float32), axis=0)
    grad_acted = times_transposed(grad_branch, down_matrix)
    _, gelu_back = jax.vjp(exact_gelu, inner_act)
    grad_inner = gelu_back(grad_acted)[0].astype(jnp.bfloat16)
    grad_up = outer_sum(first_low, grad_inner)
    grad_up_bias = jnp.sum(grad_inner.astype(jnp.float32), axis=0)
    grad_first = grad_second + times_transposed(grad_inner, up_matrix)
    _, first_back = jax.vjp(layer_norm, first_in, gains[:, 0], shifts[:, 0])
    grad_first_in, grad_gain_one, grad_shift_one = first_back(grad_first)
    grad_attn = grad_first_in.astype(jnp.bfloat16)
    grad_out = outer_sum(mixed_heads, grad_attn)
    grad_bias_one = jnp.sum(grad_attn.astype(jnp.float32), axis=0)
    grad_mixed = times_transposed(grad_attn, out_matrix).astype(jnp.bfloat16)
    short_dq, short_dk, short_dv = by_blocks(
        backward_blocks,
        short_block,
        (
            short_q,
            short_k,
            short_v,
            short_live,
            grad_mixed[:short_rows].reshape(short_shape),
            short_logsum,
        ),
    )
    again_k, again_v = (gathered_k, gathered_v)
    long_dq, long_dk, long_dv = by_blocks(
        backward_blocks,
        long_block,
        (
            long_q,
            again_k.reshape(full_shape),
            again_v.reshape(full_shape),
            long_key_live,
            grad_mixed[short_rows:].reshape(long_shape),
            long_logsum,
        ),
    )
    own_dk, own_dv = (
        lax.psum_scatter(
            long_dk.reshape(long_count, full_len, model_width).astype(jnp.bfloat16),
            "seq",
            scatter_dimension=1,
            tiled=True,
        ).astype(jnp.float32),
        lax.psum_scatter(
            long_dv.reshape(long_count, full_len, model_width).astype(jnp.bfloat16),
            "seq",
            scatter_dimension=1,
            tiled=True,
        ).astype(jnp.float32),
    )
    grad_queries = jnp.concatenate(
        [short_dq.reshape(short_rows, model_width), long_dq.reshape(long_rows, model_width)], axis=0
    ).astype(jnp.bfloat16)
    grad_keys = jnp.concatenate(
        [short_dk.reshape(short_rows, model_width), own_dk.reshape(long_rows, model_width)], axis=0
    ).astype(jnp.bfloat16)
    grad_values = jnp.concatenate(
        [short_dv.reshape(short_rows, model_width), own_dv.reshape(long_rows, model_width)], axis=0
    ).astype(jnp.bfloat16)
    grad_joined = jnp.concatenate([grad_queries, grad_keys, grad_values], axis=1)
    grad_qkv = outer_sum(inputs, grad_joined)
    grad_qv = jnp.stack(
        [
            jnp.sum(grad_queries.astype(jnp.float32), axis=0),
            jnp.sum(grad_values.astype(jnp.float32), axis=0),
        ],
        axis=1,
    )
    grad_inputs = grad_first_in + times_transposed(grad_joined, qkv_matrix)
    grad_out_vec = jnp.stack([grad_bias_one, grad_bias_two], axis=1)
    grad_gains = jnp.stack([grad_gain_one, grad_gain_two], axis=1)
    grad_shifts = jnp.stack([grad_shift_one, grad_shift_two], axis=1)
    shard_grads = (
        lax.psum_scatter(grad_qkv, ("dp", "seq"), scatter_dimension=0, tiled=True),
        lax.psum_scatter(grad_out, ("dp", "seq"), scatter_dimension=0, tiled=True),
        lax.psum_scatter(grad_up, ("dp", "seq"), scatter_dimension=0, tiled=True),
        lax.psum_scatter(grad_down, ("dp", "seq"), scatter_dimension=0, tiled=True),
        lax.psum_scatter(grad_qv, ("dp", "seq"), scatter_dimension=0, tiled=True),
        lax.psum_scatter(grad_out_vec, ("dp", "seq"), scatter_dimension=0, tiled=True),
        lax.psum_scatter(grad_up_bias, ("dp", "seq"), scatter_dimension=0, tiled=True),
        lax.psum_scatter(grad_gains, ("dp", "seq"), scatter_dimension=0, tiled=True),
        lax.psum_scatter(grad_shifts, ("dp", "seq"), scatter_dimension=0, tiled=True),
    )
    short_out = short_final.astype(jnp.bfloat16)
    long_out = long_final.astype(jnp.bfloat16)
    short_grad_in = grad_inputs[:short_rows].reshape(short_count, short_cap, model_width)
    long_grad_in = grad_inputs[short_rows:].reshape(long_count, long_half, model_width)
    return (
        short_out,
        long_out,
        short_pooled,
        long_pooled,
        short_grad_in,
        long_grad_in,
        shard_grads[0],
        shard_grads[1],
        shard_grads[2],
        shard_grads[3],
        shard_grads[4],
        shard_grads[5],
        shard_grads[6],
        shard_grads[7],
        shard_grads[8],
    )


def pack_slab(w_qkv, w_out, w_up, w_down, qv_bias, out_bias, up_bias, norm_gain, norm_shift):
    rows, width = w_out.shape
    pairs = [member.T for member in (qv_bias, out_bias, norm_gain, norm_shift)]
    vectors = jnp.concatenate([jnp.concatenate(pairs, axis=0).reshape(-1), up_bias])
    vectors = jnp.pad(vectors, (0, 8 * width - vectors.shape[0])).reshape(8, width)
    blocks = [w_qkv[:, i * width : (i + 1) * width] for i in range(3)]
    blocks += [vectors, w_out, jnp.zeros((8, width), w_out.dtype)]
    blocks += [w_up[:, i * width : (i + 1) * width] for i in range(4)]
    return jnp.concatenate(blocks + [w_down], axis=0)


def by_columns(slabs, first, rows, blocks):
    part = slabs[:, first : first + blocks * rows]
    width = part.shape[-1]
    part = part.reshape(slabs.shape[0], blocks, rows, width).transpose(0, 2, 1, 3)
    return part.reshape(slabs.shape[0] * rows, blocks * width)


def to_columns(grad, devices, blocks):
    rows, width = grad.shape[0] // devices, grad.shape[1] // blocks
    grad = grad.reshape(devices, rows, blocks, width).transpose(0, 2, 1, 3)
    return grad.reshape(devices, blocks * rows, width)


def fast_shards(
    short_tokens, long_tokens, short_len, long_len, short_pool, long_pool, short_cot, long_cot,
    short_pool_cot, long_pool_cot, w_qkv, w_out, w_up, w_down, qv_bias, out_bias, up_bias,
    norm_gain, norm_shift,
):
    groups = lax.axis_size("dp") // 4
    devices = groups * 8
    rows, width = w_out.shape
    x = lax.axis_index("seq")
    short_count, short_cap, _ = short_tokens.shape
    half = long_tokens.shape[1]
    short_rows, long_rows = short_count * short_cap, 2 * half
    slab = pack_slab(w_qkv, w_out, w_up, w_down, qv_bias, out_bias, up_bias, norm_gain, norm_shift)
    pool = jnp.broadcast_to(long_pool[:, None, :], (2, 8, half))
    whole, inputs, cot, pool = gather_all(
        slab,
        short_tokens.reshape(short_rows, width),
        long_tokens,
        short_cot.reshape(short_rows, width),
        long_cot,
        pool,
        groups,
    )
    slabs = whole.reshape(devices, SLAB, width)
    qkv_matrix = by_columns(slabs, 0, rows, 3)
    out_matrix = slabs[:, 80 : 80 + rows].reshape(width, width)
    up_matrix = by_columns(slabs, 112, rows, 4)
    down_matrix = slabs[:, 208:304].reshape(4 * width, width)
    vectors = slabs[:, 72].astype(jnp.float32)
    pairs = vectors[:, : 8 * rows].reshape(devices, 8, rows).transpose(1, 0, 2).reshape(8, width)
    up_vec = vectors[:, 8 * rows : 12 * rows].reshape(4 * width)
    long_pool = pool[:, 0].reshape(1, long_rows)
    long_len = lax.dynamic_slice_in_dim(long_len, x, 1)
    long_pool_cot = lax.dynamic_slice_in_dim(long_pool_cot, x, 1)

    score_scale = 1.0 / math.sqrt(width // HEADS)
    short_place = jnp.arange(short_cap, dtype=jnp.int32)
    short_live = short_place[None, :] < short_len[:, None]
    long_place = jnp.arange(long_rows, dtype=jnp.int32)
    long_live = long_place[None, :] < long_len[:, None]
    short_weight = (short_live & ((short_pool > 0) | (short_place[None, :] == 0))).astype(jnp.float32)
    long_weight = (long_live & ((long_pool > 0) | (long_place[None, :] == 0))).astype(jnp.float32)
    row_live = jnp.concatenate([short_live.reshape(-1), long_live.reshape(-1)]).astype(jnp.float32)
    joined = jnp.dot(inputs, qkv_matrix, preferred_element_type=jnp.float32)
    queries = (joined[:, :width] + pairs[0]).astype(jnp.bfloat16)
    keys_all = joined[:, width : 2 * width].astype(jnp.bfloat16)
    values = (joined[:, 2 * width :] + pairs[1]).astype(jnp.bfloat16)
    short_shape = (short_count, short_cap, HEADS, width // HEADS)
    long_shape = (1, long_rows, HEADS, width // HEADS)
    short_qkv = [m[:short_rows].reshape(short_shape) for m in (queries, keys_all, values)]
    long_qkv = [m[short_rows:].reshape(long_shape) for m in (queries, keys_all, values)]
    short_mixed, short_logsum = attend_forward((*short_qkv, short_live), score_scale)
    long_mixed, long_logsum = attend_forward((*long_qkv, long_live), score_scale)
    mixed_heads = jnp.concatenate(
        [short_mixed.reshape(short_rows, width), long_mixed.reshape(long_rows, width)], axis=0
    )
    attn_out = jnp.dot(mixed_heads, out_matrix, preferred_element_type=jnp.float32) + pairs[2]
    first_in = inputs.astype(jnp.float32) + attn_out
    first_norm = layer_norm(first_in, pairs[4], pairs[6])
    first_low = first_norm.astype(jnp.bfloat16)
    inner_act = jnp.dot(first_low, up_matrix, preferred_element_type=jnp.float32) + up_vec
    activated = exact_gelu(inner_act).astype(jnp.bfloat16)
    branch = jnp.dot(activated, down_matrix, preferred_element_type=jnp.float32) + pairs[3]
    second_in = first_norm + branch
    final_norm = layer_norm(second_in, pairs[5], pairs[7]) * row_live[:, None]
    short_final = final_norm[:short_rows].reshape(short_count, short_cap, width)
    long_final = final_norm[short_rows:].reshape(1, long_rows, width)
    short_total = jnp.sum(short_weight, axis=1)
    long_total = jnp.sum(long_weight, axis=1)
    short_pooled = jnp.sum(short_final * short_weight[..., None], axis=1) / short_total[:, None]
    long_pooled = jnp.sum(long_final * long_weight[..., None], axis=1) / long_total[:, None]
    weight = jnp.concatenate([short_weight.reshape(-1), long_weight.reshape(-1)])
    spread_cot = jnp.concatenate(
        [
            jnp.repeat(short_pool_cot / short_total[:, None], short_cap, axis=0),
            jnp.repeat(long_pool_cot / long_total[:, None], long_rows, axis=0),
        ],
        axis=0,
    )
    grad_top = cot.astype(jnp.float32) * row_live[:, None] + weight[:, None] * spread_cot
    _, second_back = jax.vjp(layer_norm, second_in, pairs[5], pairs[7])
    grad_second, grad_gain_two, grad_shift_two = second_back(grad_top)
    grad_branch = grad_second.astype(jnp.bfloat16)
    grad_down = outer_sum(activated, grad_branch)
    grad_bias_two = jnp.sum(grad_branch.astype(jnp.float32), axis=0)
    grad_acted = times_transposed(grad_branch, down_matrix)
    _, gelu_back = jax.vjp(exact_gelu, inner_act)
    grad_inner = gelu_back(grad_acted)[0].astype(jnp.bfloat16)
    grad_up = outer_sum(first_low, grad_inner)
    grad_up_bias = jnp.sum(grad_inner.astype(jnp.float32), axis=0)
    grad_first = grad_second + times_transposed(grad_inner, up_matrix)
    _, first_back = jax.vjp(layer_norm, first_in, pairs[4], pairs[6])
    grad_first_in, grad_gain_one, grad_shift_one = first_back(grad_first)
    grad_attn = grad_first_in.astype(jnp.bfloat16)
    grad_out = outer_sum(mixed_heads, grad_attn)
    grad_bias_one = jnp.sum(grad_attn.astype(jnp.float32), axis=0)
    grad_mixed = times_transposed(grad_attn, out_matrix).astype(jnp.bfloat16)
    short_back = attend_backward(
        (*short_qkv, short_live, grad_mixed[:short_rows].reshape(short_shape), short_logsum), score_scale
    )
    long_back = attend_backward(
        (*long_qkv, long_live, grad_mixed[short_rows:].reshape(long_shape), long_logsum), score_scale
    )
    grad_joined = jnp.concatenate(
        [
            jnp.concatenate([a.reshape(short_rows, width), b.reshape(long_rows, width)], axis=0)
            for a, b in zip(short_back, long_back)
        ],
        axis=1,
    ).astype(jnp.bfloat16)
    grad_qkv = outer_sum(inputs, grad_joined)
    grad_bias = jnp.sum(grad_joined.astype(jnp.float32), axis=0)
    grad_inputs = grad_first_in + times_transposed(grad_joined, qkv_matrix)

    grad_pairs = jnp.stack(
        [
            grad_bias[:width], grad_bias[2 * width :], grad_bias_one, grad_bias_two,
            grad_gain_one, grad_gain_two, grad_shift_one, grad_shift_two,
        ]
    )
    grad_vectors = jnp.concatenate(
        [
            grad_pairs.reshape(8, devices, rows).transpose(1, 0, 2).reshape(devices, 8 * rows),
            grad_up_bias.reshape(devices, 4 * rows),
        ],
        axis=1,
    )
    grad_vectors = jnp.pad(grad_vectors, ((0, 0), (0, 8 * width - 12 * rows)))
    grads = jnp.concatenate(
        [
            to_columns(grad_qkv, devices, 3),
            grad_vectors.reshape(devices, 8, width),
            grad_out.reshape(devices, rows, width),
            jnp.zeros((devices, 8, width), jnp.float32),
            to_columns(grad_up, devices, 4),
            grad_down.reshape(devices, 4 * rows, width),
        ],
        axis=1,
    ).astype(jnp.bfloat16)
    pooled = jnp.broadcast_to(long_pooled, (8, width))
    out, long_out, long_grad, both_pooled = scatter_all(
        grads.reshape(groups, 8, SLAB, width),
        final_norm[short_rows:].astype(jnp.bfloat16),
        grad_inputs[short_rows:].astype(jnp.bfloat16),
        pooled,
        groups,
    )

    def widen(first, blocks):
        part = out[first : first + blocks * rows].reshape(blocks, rows, width)
        return part.transpose(1, 0, 2).reshape(rows, blocks * width)

    small = out[72, : 8 * rows].reshape(8, rows)
    return (
        short_final.astype(jnp.bfloat16),
        long_out,
        short_pooled,
        both_pooled[:, 0],
        grad_inputs[:short_rows].reshape(short_count, short_cap, width),
        long_grad.astype(jnp.float32),
        widen(0, 3),
        out[80 : 80 + rows],
        widen(112, 4),
        out[208:304],
        small[0:2].T,
        small[2:4].T,
        out[72, 8 * rows : 12 * rows],
        small[4:6].T,
        small[6:8].T,
    )


def solution(mesh):
    short_spec, long_spec, spread = P(("dp", "seq"), None, None), P("dp", "seq", None), P(("dp", "seq"), None)
    vector, parameters = P(("dp", "seq")), [P(("dp", "seq"), None)] * 6
    in_specs = (
        short_spec, long_spec, vector, P("dp"), spread, P("dp", "seq"), short_spec, long_spec,
        spread, P("dp", None), *parameters, vector, spread, spread,
    )
    out_specs = (
        short_spec, long_spec, spread, P("dp", None), short_spec, long_spec, *parameters, vector,
        spread, spread,
    )
    dp, seq = mesh.shape["dp"], mesh.shape["seq"]

    def run(*arrays):
        width = arrays[11].shape[1]
        passages = arrays[1].shape[0] // dp
        regular = dp % 4 == 0 and seq == 2 and passages == 2 and width == 24 * dp * seq
        body = fast_shards if regular else general_shards
        return jax.shard_map(body, mesh=mesh, in_specs=in_specs, out_specs=out_specs, check_vma=False)(*arrays)

    return run
```

```python
import functools
import math

import jax
import jax.numpy as jnp
from jax import lax
from jax.experimental import pallas as pl
from jax.experimental.pallas import tpu as pltpu
from jax.sharding import PartitionSpec as P

HEADS = 12
EPS = 1e-12
MESH = pl.DeviceIdType.MESH

SIZES = (80, 32, 96, 96)
GATHER_X = (48, 16, 64, 64)
SCATTER_X = (32, 16, 32, 32)


FLIPS = ((0, 0), (0, 1), (1, 0), (1, 1))


class Place:
    def __init__(self):
        dp = lax.axis_index("dp")
        self.x = lax.axis_index("seq")
        self.groups = lax.axis_size("dp") // 4
        self.z = lax.div(dp, 4)
        self.y = lax.rem(lax.div(dp, 2), 2)
        self.c = lax.rem(dp, 2)
        self.dp = dp

    def at_z(self, step):
        z = lax.rem(self.z + step, self.groups)
        return (z * 4 + self.y * 2 + self.c, self.x)

    def at_x(self):
        return (self.dp, 1 - self.x)

    def at_y(self):
        return (self.z * 4 + (1 - self.y) * 2 + self.c, self.x)

    def at_core(self):
        return (self.z * 4 + self.y * 2 + 1 - self.c, self.x)

    def slot(self, flip_y=0, flip_c=0, flip_x=0):
        y = 1 - self.y if flip_y else self.y
        c = 1 - self.c if flip_c else self.c
        x = 1 - self.x if flip_x else self.x
        return y * 4 + c * 2 + x

    def z_back(self, step):
        return lax.rem(self.z + self.groups - step, self.groups)

    def partners(self):
        return [self.at_z(step) for step in range(1, self.groups)] + [
            self.at_x(),
            self.at_y(),
            self.at_core(),
        ]

    def greet(self):
        barrier = pltpu.get_barrier_semaphore()
        partners = self.partners()
        for partner in partners:
            pl.semaphore_signal(barrier, inc=1, device_id=partner, device_id_type=MESH)
        pl.semaphore_wait(barrier, len(partners))


class Wires:
    def __init__(self, send, recv):
        self.send, self.recv, self.sent, self.left = send, recv, [], set()

    def put(self, src, dst, to):
        number = len(self.sent)
        copy = pltpu.make_async_remote_copy(
            src_ref=src,
            dst_ref=dst,
            send_sem=self.send.at[number],
            recv_sem=self.recv.at[number],
            device_id=to,
            device_id_type=MESH,
        )
        copy.start()
        self.sent.append(copy)
        return (number, to)

    def landed(self, ticket, ref):
        number, to = ticket
        pltpu.make_async_remote_copy(
            src_ref=ref,
            dst_ref=ref,
            send_sem=self.send.at[number],
            recv_sem=self.recv.at[number],
            device_id=to,
            device_id_type=MESH,
        ).wait_recv()

    def has_left(self, ticket):
        self.sent[ticket[0]].wait_send()
        self.left.add(ticket[0])

    def close(self):
        for number, copy in enumerate(self.sent):
            if number not in self.left:
                copy.wait_send()


class Gather:
    def __init__(self, wires, place, slabs, wholes):
        self.wires, self.place, self.slabs, self.wholes = wires, place, slabs, wholes
        self.steps = place.groups
        self.along_z, self.along_x, self.along_y = {}, {}, {}
        self.by_x, self.by_y, self.core = {}, {}, {}

    def halves(self, k):
        some = GATHER_X[k]
        return pl.ds(0, some), pl.ds(some, SIZES[k] - some)

    def start(self, k):
        place, wires = self.place, self.wires
        src = self.slabs[k]
        dst = self.wholes[k].at[place.z, place.slot()]
        for step in range(1, self.steps):
            self.along_z[k, step] = wires.put(src, dst, place.at_z(step))
        self.along_x[k, 0] = wires.put(src, dst, place.at_x())
        self.along_y[k, 0] = wires.put(src, dst, place.at_y())
        self.core[k, 0, 0] = wires.put(src, dst, place.at_core())

    def relay_z(self, k):
        place, wires = self.place, self.wires
        for step in range(1, self.steps):
            ref = self.wholes[k].at[place.z_back(step), place.slot()]
            wires.landed(self.along_z[k, step], ref)
            self.along_x[k, step] = wires.put(ref, ref, place.at_x())
            self.along_y[k, step] = wires.put(ref, ref, place.at_y())
            self.core[k, 0, step] = wires.put(ref, ref, place.at_core())

    def relay_plane(self, k):
        upper, lower = self.halves(k)
        place, wires, whole = self.place, self.wires, self.wholes[k]
        for step in range(self.steps):
            z = place.z_back(step)
            slot = place.slot(flip_x=1)
            ref = whole.at[z, slot]
            wires.landed(self.along_x[k, step], ref)
            half = whole.at[z, slot, upper]
            self.by_y[k, step] = wires.put(half, half, place.at_y())
            self.core[k, 1, step] = wires.put(ref, ref, place.at_core())
            slot = place.slot(flip_y=1)
            ref = whole.at[z, slot]
            wires.landed(self.along_y[k, step], ref)
            half = whole.at[z, slot, lower]
            self.by_x[k, step] = wires.put(half, half, place.at_x())
            self.core[k, 2, step] = wires.put(ref, ref, place.at_core())

    def relay_corner(self, k):
        upper, lower = self.halves(k)
        place, wires, whole = self.place, self.wires, self.wholes[k]
        slot = place.slot(flip_x=1, flip_y=1)
        for step in range(self.steps):
            z = place.z_back(step)
            wires.landed(self.by_y[k, step], whole.at[z, slot, upper])
            wires.landed(self.by_x[k, step], whole.at[z, slot, lower])
            ref = whole.at[z, slot]
            self.core[k, 3, step] = wires.put(ref, ref, place.at_core())

    def finish(self, k):
        place = self.place
        for part, (flip_y, flip_x) in enumerate(FLIPS):
            slot = place.slot(flip_y=flip_y, flip_c=1, flip_x=flip_x)
            for step in range(self.steps):
                ref = self.wholes[k].at[place.z_back(step), slot]
                self.wires.landed(self.core[k, part, step], ref)


class Scatter:
    def __init__(self, wires, place, grads, from_core, from_x, from_y, last_x, last_y, from_z):
        self.wires, self.place, self.grads = wires, place, grads
        self.from_core, self.from_x, self.from_y = from_core, from_x, from_y
        self.last_x, self.last_y, self.from_z = last_x, last_y, from_z
        self.steps = place.groups
        self.core, self.first, self.second, self.third = {}, {}, {}, {}

    def halves(self, k):
        some = SCATTER_X[k]
        return pl.ds(0, some), pl.ds(some, SIZES[k] - some)

    def own(self, k, part, rows):
        flip_y, flip_x = FLIPS[part]
        return self.grads[k].at[:, self.place.slot(flip_y=flip_y, flip_x=flip_x), rows]

    def send_core(self, k):
        place = self.place
        for part in (3, 1, 2, 0):
            flip_y, flip_x = FLIPS[part]
            slot = place.slot(flip_y=flip_y, flip_c=1, flip_x=flip_x)
            self.core[k, part] = self.wires.put(
                self.grads[k].at[:, slot], self.from_core[k].at[part], place.at_core()
            )

    def add(self, into, other):
        def one(z, carry):
            total = into[z].astype(jnp.float32) + other[z].astype(jnp.float32)
            into[z] = total.astype(into.dtype)
            return carry

        lax.fori_loop(0, self.steps, one, 0)

    def after_core(self, k):
        upper, lower = self.halves(k)
        whole = pl.ds(0, SIZES[k])
        wires, place = self.wires, self.place
        for part in (3, 1, 2, 0):
            wires.landed(self.core[k, part], self.from_core[k].at[part])
            self.add(self.own(k, part, whole), self.from_core[k].at[part])
            if part == 3:
                self.first[k, "x", 1] = wires.put(
                    self.own(k, 3, upper), self.from_x[k].at[1], place.at_x()
                )
                self.first[k, "y", 1] = wires.put(
                    self.own(k, 3, lower), self.from_y[k].at[1], place.at_y()
                )
            elif part == 1:
                self.first[k, "x", 0] = wires.put(
                    self.own(k, 1, upper), self.from_x[k].at[0], place.at_x()
                )
            elif part == 2:
                self.first[k, "y", 0] = wires.put(
                    self.own(k, 2, lower), self.from_y[k].at[0], place.at_y()
                )

    def after_first(self, k):
        upper, lower = self.halves(k)
        wires, place = self.wires, self.place
        wires.landed(self.first[k, "x", 1], self.from_x[k].at[1])
        self.add(self.own(k, 2, upper), self.from_x[k].at[1])
        self.second[k, "y"] = wires.put(self.own(k, 2, upper), self.last_y[k], place.at_y())
        wires.landed(self.first[k, "y", 1], self.from_y[k].at[1])
        self.add(self.own(k, 1, lower), self.from_y[k].at[1])
        self.second[k, "x"] = wires.put(self.own(k, 1, lower), self.last_x[k], place.at_x())
        wires.landed(self.first[k, "x", 0], self.from_x[k].at[0])
        self.add(self.own(k, 0, upper), self.from_x[k].at[0])
        wires.landed(self.first[k, "y", 0], self.from_y[k].at[0])
        self.add(self.own(k, 0, lower), self.from_y[k].at[0])

    def after_second(self, k):
        upper, lower = self.halves(k)
        wires, place = self.wires, self.place
        wires.landed(self.second[k, "y"], self.last_y[k])
        self.add(self.own(k, 0, upper), self.last_y[k])
        wires.landed(self.second[k, "x"], self.last_x[k])
        self.add(self.own(k, 0, lower), self.last_x[k])
        for step in range(1, self.steps):
            z = lax.rem(place.z + step, self.steps)
            self.third[k, step] = wires.put(
                self.grads[k].at[z, place.slot()], self.from_z[k].at[step - 1], place.at_z(step)
            )

    def finish(self, k):
        place = self.place
        total = self.grads[k][place.z, place.slot()].astype(jnp.float32)
        for step in range(1, self.steps):
            self.wires.landed(self.third[k, step], self.from_z[k].at[step - 1])
            total = total + self.from_z[k][step - 1].astype(jnp.float32)
        return total


def times(a, b):
    return lax.dot_general(a, b, (((1,), (0,)), ((), ())), preferred_element_type=jnp.float32)


def times_turned(a, b):
    return lax.dot_general(a, b, (((1,), (1,)), ((), ())), preferred_element_type=jnp.float32)


def turned_times(a, b):
    return lax.dot_general(a, b, (((0,), (0,)), ((), ())), preferred_element_type=jnp.float32)


def aligned(index, size):
    return pl.ds(pl.multiple_of(index * size, size), size)


def head_masks(lanes, head_dim):
    lane = lax.broadcasted_iota(jnp.int32, (1, lanes), 1)
    return [
        jnp.where((lane >= h * head_dim) & (lane < (h + 1) * head_dim), 1.0, 0.0).astype(jnp.bfloat16)
        for h in range(lanes // head_dim)
    ]


def gelu_and_slope(u):
    near = 1.0 / (1.0 + (0.3275911 * math.sqrt(0.5)) * jnp.abs(u))
    bell = jnp.exp(-0.5 * (u * u))
    series = near * (
        0.127414796
        + near * (-0.142248368 + near * (0.7107068705 + near * (-0.7265760135 + near * 0.5307027145)))
    )
    tail = series * bell
    below = jnp.where(u < 0.0, tail, 1.0 - tail)
    return u * below, below + u * (bell * (1.0 / math.sqrt(2.0 * math.pi)))


def assemble(source, first, blocks, target):
    per_z, size = source.shape[1] // 2, 24

    def one(i, carry):
        z, pair = lax.div(i, per_z), lax.rem(i, per_z)
        left = source[z, 2 * pair].astype(jnp.float32)
        right = source[z, 2 * pair + 1].astype(jnp.float32)
        for b in range(blocks):
            rows = slice(first + b * size, first + (b + 1) * size)
            both = jnp.concatenate([left[rows], right[rows]], axis=0)
            target[b, aligned(i, 2 * size), :] = both.astype(target.dtype)
        return carry

    lax.fori_loop(0, source.shape[0] * per_z, one, 0)


def sum_slabs(source, first):
    def one(i, total):
        per_z = source.shape[1]
        slab = source[lax.div(i, per_z), lax.rem(i, per_z)].astype(jnp.float32)
        return total + slab[first : first + 8]

    count = source.shape[0] * source.shape[1]
    return lax.fori_loop(0, count, one, jnp.zeros((8, source.shape[-1]), jnp.float32))


def normalize(row_data):
    center = row_data - jnp.mean(row_data, axis=-1, keepdims=True)
    spread = jnp.mean(center * center, axis=-1, keepdims=True)
    scale = lax.rsqrt(spread + EPS)
    return center * scale, scale


def weights_forward(queries, keys_all, live):
    scores = jnp.where(live, times_turned(queries, keys_all), -1e30)
    exponent = jnp.exp(scores - jnp.max(scores, axis=-1, keepdims=True))
    return (exponent * (1.0 / jnp.sum(exponent, axis=-1, keepdims=True))).astype(jnp.bfloat16)


def forward_kernel(
    limits, slab0, slab1, slab2, slab3, short_tok, long_tok, short_cot, long_cot, short_pool, pool,
    out_down, out_wq, out_wu, out_rows, out_cot, out_qkv, out_short_probs, out_long_probs, out_mixed,
    out_first, out_hat, out_scale, out_low, out_acted, out_slope, vectors, share,
    whole0, whole1, whole2, wq, wu, rows_in, qkv, short_probs, long_probs, mixed,
    first, hat, scale, low, acted, slope, pool_in,
    send, recv, here,
):
    place = Place()
    x, other = place.x, 1 - place.x
    short_rows, half = short_tok.shape[0], long_tok.shape[1]
    total_rows, width = rows_in.shape
    long_rows = 2 * half
    cap = short_probs.shape[-1]
    count = short_rows // cap
    mine = pl.ds(pl.multiple_of(short_rows + x * half, half), half)
    theirs = pl.ds(pl.multiple_of(short_rows + other * half, half), half)
    slabs = (slab0, slab1, slab2, slab3)
    wholes = (whole0, whole1, whole2, out_down)
    local = []

    def move(src, dst):
        copy = pltpu.make_async_copy(src, dst, here.at[len(local)])
        copy.start()
        local.append(copy)
        return copy

    for k in range(4):
        move(slabs[k], wholes[k].at[place.z, place.slot()])
    for src, dst in (
        (short_tok, rows_in.at[pl.ds(0, short_rows)]),
        (long_tok.at[x], rows_in.at[mine]),
        (pool.at[x], pool_in.at[x]),
        (short_cot, out_cot.at[pl.ds(0, short_rows)]),
        (long_cot.at[x], out_cot.at[mine]),
    ):
        move(src, dst)
    arrived = len(local)
    place.greet()
    wires = Wires(send, recv)
    net = Gather(wires, place, slabs, wholes)
    net.start(0)
    tok = wires.put(long_tok.at[other], rows_in.at[mine], place.at_x())
    pooled = wires.put(pool.at[other], pool_in.at[x], place.at_x())
    net.start(1)
    net.relay_z(0)
    net.start(2)
    net.relay_plane(0)
    net.relay_corner(0)
    net.relay_z(1)
    net.relay_plane(1)
    net.relay_corner(1)
    net.start(3)
    for copy in local:
        copy.wait()
    net.finish(0)
    assemble(whole0, 0, 3, wq)
    vectors[0:8, :] = sum_slabs(whole0, 72)
    wires.landed(tok, rows_in.at[theirs])
    net.relay_z(2)

    head_dim = width // HEADS
    score_scale = 1.0 / math.sqrt(head_dim)

    def project(i, carry):
        rows = aligned(i, 256)
        data = rows_in[rows, :]
        queries = times(data, wq[0]) + vectors[0:1, :]
        qkv[0, rows, :] = (queries.astype(jnp.bfloat16).astype(jnp.float32) * score_scale).astype(jnp.bfloat16)
        qkv[1, rows, :] = times(data, wq[1]).astype(jnp.bfloat16)
        qkv[2, rows, :] = (times(data, wq[2]) + vectors[1:2, :]).astype(jnp.bfloat16)
        return carry

    lax.fori_loop(0, total_rows // 256, project, 0)
    move(qkv, out_qkv)
    move(rows_in, out_rows)

    wires.landed(pooled, pool_in.at[other])
    place_in_block = lax.broadcasted_iota(jnp.int32, (1, cap), 1)
    chosen = []
    for block in range(total_rows // cap):
        if block < count:
            mask, start = short_pool[block : block + 1, :], 0
        else:
            step = block - count
            per_half = half // cap
            mask, start = pool_in[step // per_half, step % per_half : step % per_half + 1, :], step * cap
        live = place_in_block < limits[block]
        keep = live & ((mask > 0) | (place_in_block + start == 0))
        chosen.append(jnp.where(keep, 1.0, 0.0))
    for block in range(count):
        share[block : block + 1, :] = chosen[block] / jnp.sum(chosen[block], axis=-1, keepdims=True)
    long_total = sum(jnp.sum(row, axis=-1, keepdims=True) for row in chosen[count:])
    for block in range(count, total_rows // cap):
        share[block : block + 1, :] = chosen[block] / long_total
    masks = head_masks(2 * head_dim, head_dim)
    keep_first = lax.broadcasted_iota(jnp.int32, (1, 2 * head_dim), 1) < head_dim
    short_live = [place_in_block < limits[i] for i in range(count)]
    long_live = lax.broadcasted_iota(jnp.int32, (1, long_rows), 1) < limits[count]

    def attend(pair, carry):
        lanes = aligned(pair, 2 * head_dim)
        for i in range(count):
            rows = pl.ds(i * cap, cap)
            queries, keys_all, values = qkv[0, rows, lanes], qkv[1, rows, lanes], qkv[2, rows, lanes]
            parts = []
            for h in range(2):
                probs = weights_forward(queries * masks[h], keys_all, short_live[i])
                short_probs[i, 2 * pair + h] = probs
                parts.append(times(probs, values))
            mixed[rows, lanes] = jnp.where(keep_first, parts[0], parts[1]).astype(jnp.bfloat16)
        rows = pl.ds(short_rows, long_rows)
        keys_all, values = qkv[1, rows, lanes], qkv[2, rows, lanes]
        for block in range(long_rows // 256):
            inner = pl.ds(block * 256, 256)
            rows = pl.ds(short_rows + block * 256, 256)
            queries = qkv[0, rows, lanes]
            parts = []
            for h in range(2):
                probs = weights_forward(queries * masks[h], keys_all, long_live)
                long_probs[2 * pair + h, inner, :] = probs
                parts.append(times(probs, values))
            mixed[rows, lanes] = jnp.where(keep_first, parts[0], parts[1]).astype(jnp.bfloat16)
        return carry

    pairs = width // (2 * head_dim)
    lax.fori_loop(0, pairs // 3, attend, 0)
    net.relay_plane(2)
    lax.fori_loop(pairs // 3, 2 * pairs // 3, attend, 0)
    net.relay_corner(2)
    net.relay_z(3)
    cot = wires.put(long_cot.at[other], out_cot.at[mine], place.at_x())
    lax.fori_loop(2 * pairs // 3, pairs, attend, 0)
    move(short_probs, out_short_probs)
    move(long_probs, out_long_probs)
    move(mixed, out_mixed)
    net.finish(1)
    assemble(whole1, 0, 1, wq.at[pl.ds(3, 1)])
    vectors[8:16, :] = sum_slabs(whole1, 24)
    move(wq, out_wq)
    net.relay_plane(3)

    def attach(i, carry):
        rows = aligned(i, 256)
        first_in = rows_in[rows, :].astype(jnp.float32) + (times(mixed[rows, :], wq[3]) + vectors[2:3, :])
        normal, factor = normalize(first_in)
        out = normal * vectors[4:5, :] + vectors[6:7, :]
        first[rows, :] = out
        low[rows, :] = out.astype(jnp.bfloat16)
        hat[rows, :] = normal.astype(jnp.bfloat16)
        scale[rows, :] = jnp.broadcast_to(factor, (256, scale.shape[1]))
        return carry

    lax.fori_loop(0, total_rows // 256, attach, 0)
    move(first, out_first)
    move(low, out_low)
    move(hat, out_hat)
    move(scale, out_scale)
    net.finish(2)
    assemble(whole2, 0, 4, wu)
    move(wu, out_wu)

    def expand(i, carry):
        j, rows = lax.div(i, 4), aligned(lax.rem(i, 4), 256)
        inner = times(low[rows, :], wu[j]) + vectors[pl.ds(8 + j, 1), :]
        value, grad = gelu_and_slope(inner)
        acted[j, rows, :] = value.astype(jnp.bfloat16)
        slope[j, rows, :] = grad.astype(jnp.bfloat16)
        return carry

    lax.fori_loop(0, 8, expand, 0)
    net.relay_corner(3)
    lax.fori_loop(8, 16, expand, 0)
    move(acted, out_acted)
    move(slope, out_slope)
    net.finish(3)
    wires.landed(cot, out_cot.at[theirs])
    wires.close()
    for copy in local[arrived:]:
        copy.wait()


def forward(limits, slabs, short_tok, long_tok, short_cot, long_cot, short_pool, pool, groups):
    short_rows, width = short_tok.shape
    half = long_tok.shape[1]
    long_rows = 2 * half
    rows = short_rows + long_rows
    count, cap = short_pool.shape
    inner = 4 * width
    copies = 4 * ((groups - 1) + 4 * groups + 4 * groups) + 3
    low = jnp.bfloat16
    shape = jax.ShapeDtypeStruct
    outs = (
        shape((groups, 8, SIZES[3], width), low),
        shape((4, width, width), low),
        shape((4, width, width), low),
        shape((rows, width), low),
        shape((rows, width), low),
        shape((3, rows, width), low),
        shape((count, HEADS, cap, cap), low),
        shape((HEADS, long_rows, long_rows), low),
        shape((rows, width), low),
        shape((rows, width), jnp.float32),
        shape((rows, width), low),
        shape((rows, 128), jnp.float32),
        shape((rows, width), low),
        shape((inner // width, rows, width), low),
        shape((inner // width, rows, width), low),
        shape((16, width), jnp.float32),
        shape((rows // cap, cap), jnp.float32),
    )
    anywhere, near = pl.BlockSpec(memory_space=pl.ANY), pl.BlockSpec(memory_space=pltpu.VMEM)
    kept = [pltpu.VMEM(out.shape, out.dtype) for out in (outs[1:4] + outs[5:15])]
    return pl.pallas_call(
        forward_kernel,
        name="forward",
        out_shape=outs,
        in_specs=[pl.BlockSpec(memory_space=pltpu.SMEM)] + [anywhere] * 8 + [near] + [anywhere],
        out_specs=[anywhere] * 15 + [near] * 2,
        scratch_shapes=[pltpu.VMEM((groups, 8, SIZES[k], width), low) for k in range(3)]
        + kept
        + [
            pltpu.VMEM(pool.shape, pool.dtype),
            pltpu.SemaphoreType.DMA((copies,)),
            pltpu.SemaphoreType.DMA((copies,)),
            pltpu.SemaphoreType.DMA((24,)),
        ],
        compiler_params=pltpu.CompilerParams(
            collective_id=0, has_side_effects=True, vmem_limit_bytes=60 * 1024 * 1024
        ),
    )(limits, *slabs, short_tok, long_tok, short_cot, long_cot, short_pool, pool)


def backward_kernel(
    limits, vectors, share, short_pool_cot, long_pool_cot,
    in_down, in_wq, in_wu, in_rows, in_cot, in_qkv, in_short_probs, in_long_probs, in_mixed,
    in_first, in_hat, in_scale, in_low, in_acted, in_slope,
    short_out, long_out, short_grad, long_grad, short_pooled, long_pooled,
    grad_qkv, grad_out, grad_up, grad_down, grad_vectors, grad_up_vector,
    wide, pair, w_up, w_far, hat, sums, branch, low, scale, halves, probs_short,
    vector_sums, pool_cots, pooled_rows, pooled_own, pooled_far,
    grads0, grads1, grads2, grads3, core0, core1, core2, core3,
    x0, x1, x2, x3, y0, y1, y2, y3, lx0, lx1, lx2, lx3, ly0, ly1, ly2, ly3, z0, z1, z2, z3,
    send, recv, here, blocks, fetch,
):
    place = Place()
    x, other = place.x, 1 - place.x
    total_rows, width = sums.shape
    short_rows = short_out.shape[0]
    count, cap = probs_short.shape[1], probs_short.shape[-1]
    long_rows = total_rows - short_rows
    half = long_rows // 2
    head_dim = width // HEADS
    steps = total_rows // 256
    low_type = jnp.bfloat16
    local = []

    def move(src, dst):
        copy = pltpu.make_async_copy(src, dst, here.at[len(local)])
        copy.start()
        local.append(copy)
        return copy

    load_down = [move(in_down.at[j], w_far.at[j]) for j in range(4)]

    def block_copies(i):
        rows = aligned(i, 256)
        return (
            pltpu.make_async_copy(in_acted.at[:, rows], wide.at[:, rows], blocks.at[0, i]),
            pltpu.make_async_copy(in_first.at[rows], sums.at[rows], blocks.at[1, i]),
            pltpu.make_async_copy(in_cot.at[rows], branch.at[rows], blocks.at[2, i]),
        )

    for i in range(steps):
        for copy in block_copies(i):
            copy.start()
    load_slope = [move(in_slope.at[0], pair.at[0])]
    load_low = move(in_low, low)
    load_up = move(in_wu, w_up)
    load_hat, load_scale = move(in_hat, hat), move(in_scale, scale)
    vector_sums[...] = jnp.zeros_like(vector_sums)
    pool_cots[0:count, :] = short_pool_cot[...]
    pool_cots[count : 2 * count, :] = jnp.broadcast_to(long_pool_cot[pl.ds(x, 1), :], (count, width))
    place.greet()
    wires = Wires(send, recv)
    net = Scatter(
        wires, place, (grads0, grads1, grads2, grads3), (core0, core1, core2, core3),
        (x0, x1, x2, x3), (y0, y1, y2, y3), (lx0, lx1, lx2, lx3), (ly0, ly1, ly2, ly3), (z0, z1, z2, z3),
    )
    for copy in load_down:
        copy.wait()
    tall = lax.broadcasted_iota(jnp.int32, (256, 1), 0)
    diagonal = lax.broadcasted_iota(jnp.int32, (cap, cap), 0) == lax.broadcasted_iota(jnp.int32, (cap, cap), 1)

    def add_vector(row, rows):
        vector_sums[row : row + 1, :] += jnp.sum(rows, axis=0, keepdims=True)

    def second(i, carry):
        rows = aligned(i, 256)
        for copy in block_copies(i):
            copy.wait()
        product = times(wide[0, rows, :], w_far[0])
        for j in range(1, 4):
            product += times(wide[j, rows, :], w_far[j])
        normal, factor = normalize(sums[rows, :] + (product + vectors[3:4, :]))
        live = tall < jnp.where(tall < cap, limits[2 * i], limits[2 * i + 1] + cap)
        final = jnp.where(live, normal * vectors[5:6, :] + vectors[7:8, :], 0.0)
        pair[1, rows, :] = final.astype(low_type)
        spread = []
        for part in range(2):
            share_row = share[pl.ds(2 * i + part, 1), :]
            column = jnp.sum(jnp.where(diagonal, share_row, 0.0), axis=1, keepdims=True)
            piece = final[part * cap : (part + 1) * cap]
            pooled_rows[pl.ds(2 * i + part, 1), :] = jnp.sum(piece * column, axis=0, keepdims=True)
            spread.append(column * pool_cots[pl.ds(2 * i + part, 1), :])
        grad_final = jnp.where(live, branch[rows, :].astype(jnp.float32), 0.0) + jnp.concatenate(spread, axis=0)
        add_vector(5, grad_final * normal)
        add_vector(7, grad_final)
        scaled = grad_final * vectors[5:6, :]
        mean_one = jnp.mean(scaled, axis=-1, keepdims=True)
        mean_two = jnp.mean(scaled * normal, axis=-1, keepdims=True)
        grad_second = factor * (scaled - mean_one - normal * mean_two)
        sums[rows, :] = grad_second
        grad_branch = grad_second.astype(low_type)
        branch[rows, :] = grad_branch
        add_vector(3, grad_branch.astype(jnp.float32))
        return carry

    lax.fori_loop(0, steps, second, 0)
    short_pooled[...] = pooled_rows[0:count, :]
    own_pooled = jnp.sum(pooled_rows[count : 2 * count, :], axis=0, keepdims=True)
    pooled_own[...] = jnp.broadcast_to(own_pooled, pooled_own.shape)
    long_pooled[pl.ds(x, 1), :] = own_pooled
    mine = pl.ds(pl.multiple_of(short_rows + x * half, half), half)
    theirs = pl.ds(pl.multiple_of(short_rows + other * half, half), half)
    out_copies = [
        move(pair.at[1, pl.ds(0, short_rows)], short_out),
        move(pair.at[1, mine], long_out.at[x]),
    ]

    def down_step(i, carry):
        j, part = lax.div(i, 2), lax.rem(i, 2)
        product = turned_times(wide[j, :, aligned(part, width // 2)], branch[...])
        grads3[j, aligned(part, 4)] = product.reshape(4, SIZES[3], width).astype(low_type)
        return carry

    lax.fori_loop(0, 8, down_step, 0)
    net.send_core(3)
    swap_out = wires.put(pair.at[1, theirs], long_out.at[x], place.at_x())
    swap_pooled = wires.put(pooled_own, pooled_far, place.at_x())

    def inner_block(j):
        def inner(i, carry):
            rows = aligned(i, 256)
            product = times_turned(branch[rows, :], w_far[j]) * pair[j % 2, rows, :].astype(jnp.float32)
            grad_inner = product.astype(low_type)
            wide[j, rows, :] = grad_inner
            add_vector(8 + j, grad_inner.astype(jnp.float32))
            return carry

        lax.fori_loop(0, steps, inner, 0)

    load_slope[0].wait()
    inner_block(0)
    for copy in out_copies:
        copy.wait()
    wires.has_left(swap_out)
    load_slope.append(move(in_slope.at[1], pair.at[1]))
    load_slope.append(move(in_slope.at[2], pair.at[0]))
    load_slope[1].wait()
    inner_block(1)
    load_slope.append(move(in_slope.at[3], pair.at[1]))
    net.after_core(3)
    load_slope[2].wait()
    inner_block(2)
    load_mixed = move(in_mixed, pair.at[0])
    load_slope[3].wait()
    inner_block(3)
    load_wq = move(in_wq, w_far)

    def pack(target, first, r, tail):
        def one(i, carry):
            rows = pl.ds(pl.multiple_of(i * 24, 8), 24)
            pieces = [halves[0, rows, :], halves[1, rows, :]] if tail is None else [halves[0, rows, :], tail]
            data = jnp.concatenate(pieces, axis=0).astype(low_type)
            target[2 * r + lax.div(i, 8), lax.rem(i, 8), first : first + data.shape[0], :] = data
            return carry

        lax.fori_loop(0, 16, one, 0)

    def up_step(i, carry):
        r, both = lax.div(i, 2), lax.rem(i, 2)
        data = low[:, aligned(r, width // 2)]
        halves[0] = turned_times(data, wide[2 * both])
        halves[1] = turned_times(data, wide[2 * both + 1])

        def one(k, carry):
            rows = pl.ds(pl.multiple_of(k * 24, 8), 24)
            data = jnp.concatenate([halves[0, rows, :], halves[1, rows, :]], axis=0)
            grads2[2 * r + lax.div(k, 8), lax.rem(k, 8), aligned(both, 48), :] = data.astype(low_type)
            return carry

        return lax.fori_loop(0, 16, one, carry)

    load_low.wait()
    lax.fori_loop(0, 4, up_step, 0)
    net.send_core(2)

    load_up.wait()
    load_hat.wait()
    load_scale.wait()

    def first_back(i, carry):
        rows = aligned(i, 256)
        grad_first = sums[rows, :]
        for j in range(4):
            grad_first += times_turned(wide[j, rows, :], w_up[j])
        normal = hat[rows, :].astype(jnp.float32)
        add_vector(4, grad_first * normal)
        add_vector(6, grad_first)
        scaled = grad_first * vectors[4:5, :]
        mean_one = jnp.mean(scaled, axis=-1, keepdims=True)
        mean_two = jnp.mean(scaled * normal, axis=-1, keepdims=True)
        grad_in = scale[rows, 0:1] * (scaled - mean_one - normal * mean_two)
        sums[rows, :] = grad_in
        grad_attn = grad_in.astype(low_type)
        branch[rows, :] = grad_attn
        add_vector(2, grad_attn.astype(jnp.float32))
        return carry

    lax.fori_loop(0, steps, first_back, 0)
    load_qkv = move(in_qkv, wide.at[pl.ds(0, 3)])
    load_rows = move(in_rows, wide.at[3])
    net.after_core(2)
    net.after_first(3)

    load_mixed.wait()
    load_wq.wait()
    for r in range(2):
        halves[0] = turned_times(pair[0, :, r * (width // 2) : (r + 1) * (width // 2)], branch[...])
        pack(grads1, 0, r, vector_sums[8:16, :])
    net.send_core(1)

    def mixed_back(i, carry):
        rows = aligned(i, 256)
        pair[1, rows, :] = times_turned(branch[rows, :], w_far[3]).astype(low_type)
        return carry

    lax.fori_loop(0, steps, mixed_back, 0)

    def probs_copies(p, slot):
        lanes = pl.ds(2 * p, 2)
        return (
            pltpu.make_async_copy(in_short_probs.at[:, lanes], probs_short.at[slot], fetch.at[0, slot]),
            pltpu.make_async_copy(
                in_long_probs.at[lanes],
                w_up.at[pl.ds(2 * slot, 2), pl.ds(0, long_rows), pl.ds(0, long_rows)],
                fetch.at[1, slot],
            ),
        )

    for copy in probs_copies(0, 0):
        copy.start()
    load_qkv.wait()
    score_scale = 1.0 / math.sqrt(head_dim)
    masks = head_masks(2 * head_dim, head_dim)
    pairs = width // (2 * head_dim)

    def attend_back(rows, lanes, queries_rows, probs_of, keys_all, values, carry_k, carry_v):
        queries, grad_mixed = wide[0, queries_rows, lanes], pair[1, queries_rows, lanes]
        overlap = grad_mixed.astype(jnp.float32) * pair[0, queries_rows, lanes].astype(jnp.float32)
        grad_queries = None
        for h in range(2):
            center = jnp.sum(overlap * masks[h].astype(jnp.float32), axis=-1, keepdims=True)
            grad_head = grad_mixed * masks[h]
            probs = probs_of(h)
            grad_probs = times_turned(grad_head, values)
            grad_scores = (probs.astype(jnp.float32) * (grad_probs - center)).astype(low_type)
            part = times(grad_scores, keys_all * masks[h])
            grad_queries = part if grad_queries is None else grad_queries + part
            part = turned_times(grad_scores, queries * masks[h])
            carry_k = part if carry_k is None else carry_k + part
            part = turned_times(probs, grad_head)
            carry_v = part if carry_v is None else carry_v + part
        wide[0, queries_rows, lanes] = (grad_queries * score_scale).astype(low_type)
        return carry_k, carry_v

    def attention_back(p, carry):
        slot = lax.rem(p, 2)
        for copy in probs_copies(p, slot):
            copy.wait()

        @pl.when(p + 1 < pairs)
        def _():
            for copy in probs_copies(p + 1, 1 - slot):
                copy.start()

        lanes = aligned(p, 2 * head_dim)
        for i in range(count):
            rows = pl.ds(i * cap, cap)
            grad_k, grad_v = attend_back(
                rows, lanes, rows, lambda h, i=i: probs_short[slot, i, h],
                wide[1, rows, lanes], wide[2, rows, lanes], None, None,
            )
            wide[1, rows, lanes] = grad_k.astype(low_type)
            wide[2, rows, lanes] = grad_v.astype(low_type)
        rows = pl.ds(short_rows, long_rows)
        keys_all, values = wide[1, rows, lanes], wide[2, rows, lanes]
        grad_k, grad_v = None, None
        for block in range(long_rows // 256):
            inner = pl.ds(block * 256, 256)
            grad_k, grad_v = attend_back(
                rows, lanes, pl.ds(short_rows + block * 256, 256),
                lambda h, inner=inner: w_up[2 * slot + h, inner, 0:long_rows],
                keys_all, values, grad_k, grad_v,
            )
        wide[1, rows, lanes] = grad_k.astype(low_type)
        wide[2, rows, lanes] = grad_v.astype(low_type)
        return carry

    lax.fori_loop(0, pairs // 3, attention_back, 0)
    net.after_second(3)
    net.after_core(1)
    lax.fori_loop(pairs // 3, 2 * pairs // 3, attention_back, 0)
    net.after_first(2)
    lax.fori_loop(2 * pairs // 3, pairs, attention_back, 0)
    net.after_first(1)
    net.after_second(2)

    def bias_sums(i, carry):
        rows = aligned(i, 256)
        add_vector(0, wide[0, rows, :].astype(jnp.float32))
        add_vector(1, wide[2, rows, :].astype(jnp.float32))
        return carry

    lax.fori_loop(0, steps, bias_sums, 0)
    load_rows.wait()
    for r in range(2):
        data = wide[3, :, r * (width // 2) : (r + 1) * (width // 2)]
        halves[0] = turned_times(data, wide[0])
        halves[1] = turned_times(data, wide[1])
        pack(grads0, 0, r, None)
        halves[0] = turned_times(data, wide[2])
        pack(grads0, 48, r, vector_sums[0:8, :])
    net.send_core(0)
    net.after_second(1)

    def tokens_back(rows):
        grad_in = sums[rows, :]
        for b in range(3):
            grad_in += times_turned(wide[b, rows, :], w_far[b])
        return grad_in

    far_low, far_in = low.at[pl.ds(0, half)], low.at[pl.ds(half, half)]
    far_low[...] = tokens_back(theirs).astype(low_type)
    swap_grad = wires.put(far_low, far_in, place.at_x())
    net.after_core(0)

    def tokens_step(i, carry):
        rows = pl.ds(pl.multiple_of(jnp.where(i < 2, i * 256, short_rows + x * half), 256), 256)
        sums[rows, :] = tokens_back(rows)
        return carry

    lax.fori_loop(0, 3, tokens_step, 0)
    move(sums.at[pl.ds(0, short_rows)], short_grad)
    move(sums.at[mine], long_grad.at[x])
    net.after_first(0)
    grad_down[...] = net.finish(3)
    total = net.finish(2)
    for j in range(4):
        grad_up[:, j * width : (j + 1) * width] = total[24 * j : 24 * j + 24]
    total = net.finish(1)
    grad_out[...] = total[0:24]
    grad_up_vector[...] = total[24:32]
    wires.landed(swap_pooled, pooled_far)
    long_pooled[pl.ds(other, 1), :] = pooled_far[0:1, :]
    wires.landed(swap_grad, far_in)
    sums[theirs, :] = far_in[...].astype(jnp.float32)
    move(sums.at[theirs], long_grad.at[other])
    wires.landed(swap_out, long_out.at[other])
    net.after_second(0)
    total = net.finish(0)
    for b in range(3):
        grad_qkv[:, b * width : (b + 1) * width] = total[24 * b : 24 * b + 24]
    grad_vectors[...] = total[72:80]
    wires.close()
    for copy in local[-3:]:
        copy.wait()


def backward(limits, vectors, share, short_pool_cot, long_pool_cot, arrays, groups):
    width = vectors.shape[1]
    rows = arrays[3].shape[0]
    count, _, cap, _ = arrays[6].shape
    short_rows = count * cap
    half = (rows - short_rows) // 2
    low, wide_type = jnp.bfloat16, jnp.float32
    shape = jax.ShapeDtypeStruct
    rows24 = 24
    outs = (
        shape((short_rows, width), low),
        shape((2, half, width), low),
        shape((short_rows, width), wide_type),
        shape((2, half, width), wide_type),
        shape((count, width), wide_type),
        shape((2, width), wide_type),
        shape((rows24, 3 * width), wide_type),
        shape((rows24, width), wide_type),
        shape((rows24, 4 * width), wide_type),
        shape((4 * rows24, width), wide_type),
        shape((8, width), wide_type),
        shape((8, width), wide_type),
    )
    anywhere, near = pl.BlockSpec(memory_space=pl.ANY), pl.BlockSpec(memory_space=pltpu.VMEM)
    copies = 4 * (4 + 6 + (groups - 1)) + 3

    def chunks(parts, sizes):
        return [pltpu.VMEM(parts + (size, width), low) for size in sizes]

    rest = tuple(size - some for size, some in zip(SIZES, SCATTER_X))
    scratch = [
        pltpu.VMEM((4, rows, width), low),
        pltpu.VMEM((2, rows, width), low),
        pltpu.VMEM((4, width, width), low),
        pltpu.VMEM((4, width, width), low),
        pltpu.VMEM((rows, width), low),
        pltpu.VMEM((rows, width), wide_type),
        pltpu.VMEM((rows, width), low),
        pltpu.VMEM((rows, width), low),
        pltpu.VMEM((rows, 128), wide_type),
        pltpu.VMEM((2, width // 2, width), wide_type),
        pltpu.VMEM((2, count, 2, cap, cap), low),
        pltpu.VMEM((16, width), wide_type),
        pltpu.VMEM((2 * count, width), wide_type),
        pltpu.VMEM((2 * count, width), wide_type),
        pltpu.VMEM((8, width), wide_type),
        pltpu.VMEM((8, width), wide_type),
        *chunks((groups, 8), SIZES),
        *chunks((4, groups), SIZES),
        *chunks((2, groups), SCATTER_X),
        *chunks((2, groups), rest),
        *chunks((groups,), rest),
        *chunks((groups,), SCATTER_X),
        *chunks((groups - 1,), SIZES),
        pltpu.SemaphoreType.DMA((copies,)),
        pltpu.SemaphoreType.DMA((copies,)),
        pltpu.SemaphoreType.DMA((24,)),
        pltpu.SemaphoreType.DMA((3, rows // 256)),
        pltpu.SemaphoreType.DMA((2, 2)),
    ]
    return pl.pallas_call(
        backward_kernel,
        name="backward",
        out_shape=outs,
        in_specs=[pl.BlockSpec(memory_space=pltpu.SMEM)] + [near] * 4 + [anywhere] * 15,
        out_specs=[anywhere] * 4 + [near] * 8,
        scratch_shapes=scratch,
        compiler_params=pltpu.CompilerParams(
            collective_id=1, has_side_effects=True, vmem_limit_bytes=63 * 1024 * 1024
        ),
    )(limits, vectors, share, short_pool_cot, long_pool_cot, *arrays)


def layer_norm(row_data, gain_vec, shift_vec):
    center = row_data - jnp.mean(row_data, axis=-1, keepdims=True)
    spread = jnp.mean(center * center, axis=-1, keepdims=True)
    return center * lax.rsqrt(spread + EPS) * gain_vec + shift_vec


def exact_gelu(inner_act):
    return jax.nn.gelu(inner_act, approximate=False)


def outer_sum(left_rows, right_rows):
    return lax.dot_general(
        left_rows, right_rows, (((0,), (0,)), ((), ())), preferred_element_type=jnp.float32
    )


def times_transposed(left_rows, matrix):
    return lax.dot_general(
        left_rows, matrix, (((1,), (1,)), ((), ())), preferred_element_type=jnp.float32
    )


def masked_scores(queries, keys_all, key_live, score_scale):
    scores = (
        jnp.einsum("bqhe,bkhe->bhqk", queries, keys_all, preferred_element_type=jnp.float32)
        * score_scale
    )
    return jnp.where(key_live[:, None, None, :], scores, -1e30)


def attend_forward(pieces, score_scale):
    queries, keys_all, values, key_live = pieces
    scores = masked_scores(queries, keys_all, key_live, score_scale)
    highest = jnp.max(scores, axis=-1, keepdims=True)
    exponent = jnp.exp(scores - highest)
    totals = jnp.sum(exponent, axis=-1, keepdims=True)
    soft_probs = (exponent / totals).astype(jnp.bfloat16)
    mixed_heads = jnp.einsum(
        "bhqk,bkhe->bqhe", soft_probs, values, preferred_element_type=jnp.float32
    )
    return (mixed_heads.astype(jnp.bfloat16), (highest + jnp.log(totals))[..., 0])


def attend_backward(pieces, score_scale):
    queries, keys_all, values, key_live, grad_mixed, log_total = pieces
    scores = masked_scores(queries, keys_all, key_live, score_scale)
    soft_probs = jnp.exp(scores - log_total[..., None])
    grad_probs = jnp.einsum(
        "bqhe,bkhe->bhqk", grad_mixed, values, preferred_element_type=jnp.float32
    )
    grad_values = jnp.einsum(
        "bhqk,bqhe->bkhe",
        soft_probs.astype(jnp.bfloat16),
        grad_mixed,
        preferred_element_type=jnp.float32,
    )
    center = jnp.sum(soft_probs * grad_probs, axis=-1, keepdims=True)
    grad_scores = (soft_probs * (grad_probs - center)).astype(jnp.bfloat16)
    grad_queries = (
        jnp.einsum("bhqk,bkhe->bqhe", grad_scores, keys_all, preferred_element_type=jnp.float32)
        * score_scale
    )
    grad_keys = (
        jnp.einsum("bhqk,bqhe->bkhe", grad_scores, queries, preferred_element_type=jnp.float32)
        * score_scale
    )
    return (grad_queries, grad_keys, grad_values)


def by_blocks(function, per_block, arrays):
    blocks = arrays[0].shape[0] // per_block
    stacked = tuple((member.reshape((blocks, per_block) + member.shape[1:]) for member in arrays))
    results = lax.map(function, stacked)
    return jax.tree.map(
        lambda member: member.reshape((blocks * per_block,) + member.shape[2:]), results
    )


def general_shards(
    short_tokens,
    long_tokens,
    short_len,
    long_len,
    short_pool,
    long_pool,
    short_cot,
    long_cot,
    short_pool_cot,
    long_pool_cot,
    w_qkv,
    w_out,
    w_up,
    w_down,
    qv_bias,
    out_bias,
    up_bias,
    norm_gain,
    norm_shift,
):
    gathered = (
        lax.all_gather(w_qkv, ("dp", "seq"), axis=0, tiled=True),
        lax.all_gather(w_out, ("dp", "seq"), axis=0, tiled=True),
        lax.all_gather(w_up, ("dp", "seq"), axis=0, tiled=True),
        lax.all_gather(w_down, ("dp", "seq"), axis=0, tiled=True),
        lax.all_gather(qv_bias, ("dp", "seq"), axis=0, tiled=True),
        lax.all_gather(out_bias, ("dp", "seq"), axis=0, tiled=True),
        lax.all_gather(up_bias, ("dp", "seq"), axis=0, tiled=True),
        lax.all_gather(norm_gain, ("dp", "seq"), axis=0, tiled=True),
        lax.all_gather(norm_shift, ("dp", "seq"), axis=0, tiled=True),
    )
    qkv_matrix, out_matrix, up_matrix, down_matrix, qv_vec, out_vec, up_vec, gains, shifts = (
        gathered
    )
    gains = gains.astype(jnp.float32)
    shifts = shifts.astype(jnp.float32)
    short_count, short_cap, model_width = short_tokens.shape
    long_count, long_half = (long_tokens.shape[0], long_tokens.shape[1])
    head_count = HEADS
    head_dim = model_width // head_count
    score_scale = 1.0 / math.sqrt(head_dim)
    short_rows = short_count * short_cap
    long_rows = long_count * long_half
    short_place = jnp.arange(short_cap, dtype=jnp.int32)
    short_live = short_place[None, :] < short_len[:, None]
    long_place = lax.axis_index("seq") * long_half + jnp.arange(long_half, dtype=jnp.int32)
    long_live = long_place[None, :] < long_len[:, None]
    short_weight = (short_live & ((short_pool > 0) | (short_place[None, :] == 0))).astype(
        jnp.float32
    )
    long_weight = (long_live & ((long_pool > 0) | (long_place[None, :] == 0))).astype(jnp.float32)
    row_live = jnp.concatenate([short_live.reshape(-1), long_live.reshape(-1)]).astype(jnp.float32)
    inputs = jnp.concatenate(
        [
            short_tokens.reshape(short_rows, model_width),
            long_tokens.reshape(long_rows, model_width),
        ],
        axis=0,
    )
    joined = jnp.dot(inputs, qkv_matrix, preferred_element_type=jnp.float32)
    queries = (joined[:, :model_width] + qv_vec[:, 0]).astype(jnp.bfloat16)
    keys_all = joined[:, model_width : 2 * model_width].astype(jnp.bfloat16)
    values = (joined[:, 2 * model_width :] + qv_vec[:, 1]).astype(jnp.bfloat16)
    short_shape = (short_count, short_cap, head_count, head_dim)
    long_shape = (long_count, long_half, head_count, head_dim)
    short_q = queries[:short_rows].reshape(short_shape)
    short_k = keys_all[:short_rows].reshape(short_shape)
    short_v = values[:short_rows].reshape(short_shape)
    long_q = queries[short_rows:].reshape(long_shape)
    long_k = keys_all[short_rows:].reshape(long_count, long_half, model_width)
    long_v = values[short_rows:].reshape(long_count, long_half, model_width)
    short_block = math.gcd(short_count, max(1, 512 // short_cap))
    long_block = math.gcd(long_count, max(1, 512 // long_half))

    def forward_blocks(pieces):
        return attend_forward(pieces, score_scale)

    def backward_blocks(pieces):
        return attend_backward(pieces, score_scale)

    short_mixed, short_logsum = by_blocks(
        forward_blocks, short_block, (short_q, short_k, short_v, short_live)
    )
    gathered_k, gathered_v = (
        lax.all_gather(long_k, "seq", axis=1, tiled=True),
        lax.all_gather(long_v, "seq", axis=1, tiled=True),
    )
    full_len = gathered_k.shape[1]
    full_shape = (long_count, full_len, head_count, head_dim)
    long_key_live = jnp.arange(full_len, dtype=jnp.int32)[None, :] < long_len[:, None]
    long_mixed, long_logsum = by_blocks(
        forward_blocks,
        long_block,
        (long_q, gathered_k.reshape(full_shape), gathered_v.reshape(full_shape), long_key_live),
    )
    mixed_heads = jnp.concatenate(
        [short_mixed.reshape(short_rows, model_width), long_mixed.reshape(long_rows, model_width)],
        axis=0,
    )
    attn_out = jnp.dot(mixed_heads, out_matrix, preferred_element_type=jnp.float32) + out_vec[:, 0]
    first_in = inputs.astype(jnp.float32) + attn_out
    first_norm = layer_norm(first_in, gains[:, 0], shifts[:, 0])
    first_low = first_norm.astype(jnp.bfloat16)
    inner_act = jnp.dot(first_low, up_matrix, preferred_element_type=jnp.float32) + up_vec
    activated = exact_gelu(inner_act).astype(jnp.bfloat16)
    branch = jnp.dot(activated, down_matrix, preferred_element_type=jnp.float32) + out_vec[:, 1]
    second_in = first_norm + branch
    final_norm = layer_norm(second_in, gains[:, 1], shifts[:, 1]) * row_live[:, None]
    short_final = final_norm[:short_rows].reshape(short_count, short_cap, model_width)
    long_final = final_norm[short_rows:].reshape(long_count, long_half, model_width)
    short_total = jnp.sum(short_weight, axis=1)
    short_pooled = jnp.sum(short_final * short_weight[..., None], axis=1) / short_total[:, None]
    long_partial = jnp.sum(long_final * long_weight[..., None], axis=1)
    long_sum, long_total = lax.psum((long_partial, jnp.sum(long_weight, axis=1)), "seq")
    long_pooled = long_sum / long_total[:, None]
    grad_short = (
        short_cot.astype(jnp.float32) * short_live[..., None]
        + short_weight[..., None] * short_pool_cot[:, None, :] / short_total[:, None, None]
    )
    grad_long = (
        long_cot.astype(jnp.float32) * long_live[..., None]
        + long_weight[..., None] * long_pool_cot[:, None, :] / long_total[:, None, None]
    )
    grad_top = jnp.concatenate(
        [grad_short.reshape(short_rows, model_width), grad_long.reshape(long_rows, model_width)],
        axis=0,
    )
    _, second_back = jax.vjp(layer_norm, second_in, gains[:, 1], shifts[:, 1])
    grad_second, grad_gain_two, grad_shift_two = second_back(grad_top)
    grad_branch = grad_second.astype(jnp.bfloat16)
    grad_down = outer_sum(activated, grad_branch)
    grad_bias_two = jnp.sum(grad_branch.astype(jnp.float32), axis=0)
    grad_acted = times_transposed(grad_branch, down_matrix)
    _, gelu_back = jax.vjp(exact_gelu, inner_act)
    grad_inner = gelu_back(grad_acted)[0].astype(jnp.bfloat16)
    grad_up = outer_sum(first_low, grad_inner)
    grad_up_bias = jnp.sum(grad_inner.astype(jnp.float32), axis=0)
    grad_first = grad_second + times_transposed(grad_inner, up_matrix)
    _, first_back = jax.vjp(layer_norm, first_in, gains[:, 0], shifts[:, 0])
    grad_first_in, grad_gain_one, grad_shift_one = first_back(grad_first)
    grad_attn = grad_first_in.astype(jnp.bfloat16)
    grad_out = outer_sum(mixed_heads, grad_attn)
    grad_bias_one = jnp.sum(grad_attn.astype(jnp.float32), axis=0)
    grad_mixed = times_transposed(grad_attn, out_matrix).astype(jnp.bfloat16)
    short_dq, short_dk, short_dv = by_blocks(
        backward_blocks,
        short_block,
        (
            short_q,
            short_k,
            short_v,
            short_live,
            grad_mixed[:short_rows].reshape(short_shape),
            short_logsum,
        ),
    )
    again_k, again_v = (gathered_k, gathered_v)
    long_dq, long_dk, long_dv = by_blocks(
        backward_blocks,
        long_block,
        (
            long_q,
            again_k.reshape(full_shape),
            again_v.reshape(full_shape),
            long_key_live,
            grad_mixed[short_rows:].reshape(long_shape),
            long_logsum,
        ),
    )
    own_dk, own_dv = (
        lax.psum_scatter(
            long_dk.reshape(long_count, full_len, model_width).astype(jnp.bfloat16),
            "seq",
            scatter_dimension=1,
            tiled=True,
        ).astype(jnp.float32),
        lax.psum_scatter(
            long_dv.reshape(long_count, full_len, model_width).astype(jnp.bfloat16),
            "seq",
            scatter_dimension=1,
            tiled=True,
        ).astype(jnp.float32),
    )
    grad_queries = jnp.concatenate(
        [short_dq.reshape(short_rows, model_width), long_dq.reshape(long_rows, model_width)], axis=0
    ).astype(jnp.bfloat16)
    grad_keys = jnp.concatenate(
        [short_dk.reshape(short_rows, model_width), own_dk.reshape(long_rows, model_width)], axis=0
    ).astype(jnp.bfloat16)
    grad_values = jnp.concatenate(
        [short_dv.reshape(short_rows, model_width), own_dv.reshape(long_rows, model_width)], axis=0
    ).astype(jnp.bfloat16)
    grad_joined = jnp.concatenate([grad_queries, grad_keys, grad_values], axis=1)
    grad_qkv = outer_sum(inputs, grad_joined)
    grad_qv = jnp.stack(
        [
            jnp.sum(grad_queries.astype(jnp.float32), axis=0),
            jnp.sum(grad_values.astype(jnp.float32), axis=0),
        ],
        axis=1,
    )
    grad_inputs = grad_first_in + times_transposed(grad_joined, qkv_matrix)
    grad_out_vec = jnp.stack([grad_bias_one, grad_bias_two], axis=1)
    grad_gains = jnp.stack([grad_gain_one, grad_gain_two], axis=1)
    grad_shifts = jnp.stack([grad_shift_one, grad_shift_two], axis=1)
    shard_grads = (
        lax.psum_scatter(grad_qkv, ("dp", "seq"), scatter_dimension=0, tiled=True),
        lax.psum_scatter(grad_out, ("dp", "seq"), scatter_dimension=0, tiled=True),
        lax.psum_scatter(grad_up, ("dp", "seq"), scatter_dimension=0, tiled=True),
        lax.psum_scatter(grad_down, ("dp", "seq"), scatter_dimension=0, tiled=True),
        lax.psum_scatter(grad_qv, ("dp", "seq"), scatter_dimension=0, tiled=True),
        lax.psum_scatter(grad_out_vec, ("dp", "seq"), scatter_dimension=0, tiled=True),
        lax.psum_scatter(grad_up_bias, ("dp", "seq"), scatter_dimension=0, tiled=True),
        lax.psum_scatter(grad_gains, ("dp", "seq"), scatter_dimension=0, tiled=True),
        lax.psum_scatter(grad_shifts, ("dp", "seq"), scatter_dimension=0, tiled=True),
    )
    short_out = short_final.astype(jnp.bfloat16)
    long_out = long_final.astype(jnp.bfloat16)
    short_grad_in = grad_inputs[:short_rows].reshape(short_count, short_cap, model_width)
    long_grad_in = grad_inputs[short_rows:].reshape(long_count, long_half, model_width)
    return (
        short_out,
        long_out,
        short_pooled,
        long_pooled,
        short_grad_in,
        long_grad_in,
        shard_grads[0],
        shard_grads[1],
        shard_grads[2],
        shard_grads[3],
        shard_grads[4],
        shard_grads[5],
        shard_grads[6],
        shard_grads[7],
        shard_grads[8],
    )


def fast_shards(
    short_tokens, long_tokens, short_len, long_len, short_pool, long_pool, short_cot, long_cot,
    short_pool_cot, long_pool_cot, w_qkv, w_out, w_up, w_down, qv_bias, out_bias, up_bias,
    norm_gain, norm_shift,
):
    groups = lax.axis_size("dp") // 4
    rows, width = w_out.shape
    seq = lax.axis_index("seq")
    device = lax.axis_index("dp") * 2 + seq
    count, cap, _ = short_tokens.shape
    half = long_tokens.shape[1]
    short_rows = count * cap

    pairs = jnp.concatenate([member.T for member in (qv_bias, out_bias, norm_gain, norm_shift)], axis=0)
    empty = jnp.zeros((8, width), w_out.dtype)
    lane = lax.rem(device, 8) * (4 * rows)
    pairs = lax.dynamic_update_slice(empty, pairs, (0, device * rows))
    ups = lax.dynamic_update_slice(empty, up_bias[None, :], (lax.div(device, 8), lane))
    slabs = (
        jnp.concatenate([w_qkv[:, i * width : (i + 1) * width] for i in range(3)] + [pairs], axis=0),
        jnp.concatenate([w_out, ups], axis=0),
        jnp.concatenate([w_up[:, i * width : (i + 1) * width] for i in range(4)], axis=0),
        w_down,
    )
    passage_len = lax.dynamic_slice_in_dim(long_len, seq, 1)
    limits = jnp.concatenate([short_len, passage_len - cap * jnp.arange(2 * half // cap, dtype=jnp.int32)])
    pool = jnp.pad(long_pool.reshape(2, half // cap, cap), ((0, 0), (0, 8 - half // cap), (0, 0)))
    (down, *kept, vectors, share) = forward(
        limits,
        slabs,
        short_tokens.reshape(short_rows, width),
        long_tokens,
        short_cot.reshape(short_rows, width),
        long_cot,
        short_pool,
        pool,
        groups,
    )
    (
        short_out, long_out, short_grad, long_grad, short_pooled, long_pooled,
        grad_qkv, grad_out, grad_up, grad_down, grad_vectors, grad_ups,
    ) = backward(
        limits, vectors, share, short_pool_cot, long_pool_cot, (down.reshape(4, width, width), *kept), groups
    )
    small = lax.dynamic_slice(grad_vectors, (0, device * rows), (8, rows))
    return (
        short_out.reshape(short_tokens.shape),
        long_out,
        short_pooled,
        long_pooled,
        short_grad.reshape(short_tokens.shape),
        long_grad,
        grad_qkv,
        grad_out,
        grad_up,
        grad_down,
        small[0:2].T,
        small[2:4].T,
        lax.dynamic_slice(grad_ups, (lax.div(device, 8), lane), (1, 4 * rows))[0],
        small[4:6].T,
        small[6:8].T,
    )


def solution(mesh):
    short_spec, long_spec, spread = P(("dp", "seq"), None, None), P("dp", "seq", None), P(("dp", "seq"), None)
    vector, parameters = P(("dp", "seq")), [P(("dp", "seq"), None)] * 6
    in_specs = (
        short_spec, long_spec, vector, P("dp"), spread, P("dp", "seq"), short_spec, long_spec,
        spread, P("dp", None), *parameters, vector, spread, spread,
    )
    out_specs = (
        short_spec, long_spec, spread, P("dp", None), short_spec, long_spec, *parameters, vector,
        spread, spread,
    )
    dp, seq = mesh.shape["dp"], mesh.shape["seq"]

    def run(*arrays):
        width = arrays[11].shape[1]
        passages = arrays[1].shape[0] // dp
        regular = dp == 16 and seq == 2 and passages == 2 and width == 24 * dp * seq
        body = fast_shards if regular else general_shards
        return jax.shard_map(body, mesh=mesh, in_specs=in_specs, out_specs=out_specs, check_vma=False)(*arrays)

    return run
```

```python
import functools
import math

import jax
import jax.numpy as jnp
from jax import lax
from jax.experimental import pallas as pl
from jax.experimental.pallas import tpu as pltpu
from jax.sharding import PartitionSpec as P

HEADS = 12
EPS = 1e-12
MESH = pl.DeviceIdType.MESH

SIZES = (80, 32, 96, 96)
GATHER_X = (48, 16, 48, 48)
SUMS = (80, 80, 80, 32, 96, 96)
SUMS_X = (32, 32, 32, 16, 32, 32)


FLIPS = ((0, 0), (0, 1), (1, 0), (1, 1))


class Place:
    def __init__(self):
        dp = lax.axis_index("dp")
        self.x = lax.axis_index("seq")
        self.groups = lax.axis_size("dp") // 4
        self.z = lax.div(dp, 4)
        self.y = lax.rem(lax.div(dp, 2), 2)
        self.c = lax.rem(dp, 2)
        self.dp = dp

    def at_z(self, step):
        z = lax.rem(self.z + step, self.groups)
        return (z * 4 + self.y * 2 + self.c, self.x)

    def at_x(self):
        return (self.dp, 1 - self.x)

    def at_y(self):
        return (self.z * 4 + (1 - self.y) * 2 + self.c, self.x)

    def at_core(self):
        return (self.z * 4 + self.y * 2 + 1 - self.c, self.x)

    def slot(self, flip_y=0, flip_c=0, flip_x=0):
        y = 1 - self.y if flip_y else self.y
        c = 1 - self.c if flip_c else self.c
        x = 1 - self.x if flip_x else self.x
        return y * 4 + c * 2 + x

    def z_back(self, step):
        return lax.rem(self.z + self.groups - step, self.groups)

    def partners(self):
        return [self.at_z(step) for step in range(1, self.groups)] + [
            self.at_x(),
            self.at_y(),
            self.at_core(),
        ]

    def greet_start(self):
        for partner in self.partners():
            pl.semaphore_signal(
                pltpu.get_barrier_semaphore(), inc=1, device_id=partner, device_id_type=MESH
            )

    def greet_wait(self):
        pl.semaphore_wait(pltpu.get_barrier_semaphore(), len(self.partners()))


class Wires:
    def __init__(self, send, recv):
        self.send, self.recv, self.sent, self.left = send, recv, [], set()

    def put(self, src, dst, to):
        number = len(self.sent)
        copy = pltpu.make_async_remote_copy(
            src_ref=src,
            dst_ref=dst,
            send_sem=self.send.at[number],
            recv_sem=self.recv.at[number],
            device_id=to,
            device_id_type=MESH,
        )
        copy.start()
        self.sent.append(copy)
        return (number, to)

    def landed(self, ticket, ref):
        number, to = ticket
        pltpu.make_async_remote_copy(
            src_ref=ref,
            dst_ref=ref,
            send_sem=self.send.at[number],
            recv_sem=self.recv.at[number],
            device_id=to,
            device_id_type=MESH,
        ).wait_recv()

    def has_left(self, ticket):
        self.sent[ticket[0]].wait_send()
        self.left.add(ticket[0])

    def close(self):
        for number, copy in enumerate(self.sent):
            if number not in self.left:
                copy.wait_send()


class Gather:
    def __init__(self, wires, place, wholes, last):
        self.wires, self.place, self.wholes, self.last = wires, place, wholes, last
        self.steps = place.groups
        self.along_z, self.along_x, self.along_y = {}, {}, {}
        self.by_x, self.by_y, self.core = {}, {}, {}

    def halves(self, k):
        some = GATHER_X[k]
        return pl.ds(0, some), pl.ds(some, SIZES[k] - some)

    def start(self, k):
        place, wires = self.place, self.wires
        dst = self.wholes[k].at[place.z, place.slot()]
        src = self.last if k == 3 else dst
        for step in range(1, self.steps):
            self.along_z[k, step] = wires.put(src, dst, place.at_z(step))

    def start_plane(self, k):
        place, wires = self.place, self.wires
        dst = self.wholes[k].at[place.z, place.slot()]
        src = self.last if k == 3 else dst
        self.along_x[k, 0] = wires.put(src, dst, place.at_x())
        self.along_y[k, 0] = wires.put(src, dst, place.at_y())
        self.core[k, 0, 0] = wires.put(src, dst, place.at_core())

    def relay_z(self, k):
        place, wires = self.place, self.wires
        for step in range(1, self.steps):
            ref = self.wholes[k].at[place.z_back(step), place.slot()]
            wires.landed(self.along_z[k, step], ref)
            self.along_x[k, step] = wires.put(ref, ref, place.at_x())
            self.along_y[k, step] = wires.put(ref, ref, place.at_y())
            self.core[k, 0, step] = wires.put(ref, ref, place.at_core())

    def relay_plane(self, k):
        upper, lower = self.halves(k)
        place, wires, whole = self.place, self.wires, self.wholes[k]
        for step in range(self.steps):
            z = place.z_back(step)
            slot = place.slot(flip_x=1)
            ref = whole.at[z, slot]
            wires.landed(self.along_x[k, step], ref)
            half = whole.at[z, slot, upper]
            self.by_y[k, step] = wires.put(half, half, place.at_y())
            self.core[k, 1, step] = wires.put(ref, ref, place.at_core())
            slot = place.slot(flip_y=1)
            ref = whole.at[z, slot]
            wires.landed(self.along_y[k, step], ref)
            half = whole.at[z, slot, lower]
            self.by_x[k, step] = wires.put(half, half, place.at_x())
            self.core[k, 2, step] = wires.put(ref, ref, place.at_core())

    def relay_corner(self, k):
        upper, lower = self.halves(k)
        place, wires, whole = self.place, self.wires, self.wholes[k]
        slot = place.slot(flip_x=1, flip_y=1)
        for step in range(self.steps):
            z = place.z_back(step)
            wires.landed(self.by_y[k, step], whole.at[z, slot, upper])
            wires.landed(self.by_x[k, step], whole.at[z, slot, lower])
            ref = whole.at[z, slot]
            self.core[k, 3, step] = wires.put(ref, ref, place.at_core())

    def finish(self, k):
        place = self.place
        for part, (flip_y, flip_x) in enumerate(FLIPS):
            slot = place.slot(flip_y=flip_y, flip_c=1, flip_x=flip_x)
            for step in range(self.steps):
                ref = self.wholes[k].at[place.z_back(step), slot]
                self.wires.landed(self.core[k, part, step], ref)


class Scatter:
    def __init__(self, wires, place, grads, from_core, from_x, from_y, last_x, last_y, from_z):
        self.wires, self.place, self.grads = wires, place, grads
        self.from_core, self.from_x, self.from_y = from_core, from_x, from_y
        self.last_x, self.last_y, self.from_z = last_x, last_y, from_z
        self.steps = place.groups
        self.core, self.first, self.second, self.third = {}, {}, {}, {}

    def halves(self, k):
        some = SUMS_X[k]
        return pl.ds(0, some), pl.ds(some, SUMS[k] - some)

    def own(self, k, part, rows):
        flip_y, flip_x = FLIPS[part]
        return self.grads[k].at[:, self.place.slot(flip_y=flip_y, flip_x=flip_x), rows]

    def send_core(self, k):
        place = self.place
        for part in (3, 1, 2, 0):
            flip_y, flip_x = FLIPS[part]
            slot = place.slot(flip_y=flip_y, flip_c=1, flip_x=flip_x)
            self.core[k, part] = self.wires.put(
                self.grads[k].at[:, slot], self.from_core[k].at[part], place.at_core()
            )

    def add(self, into, other):
        def one(z, carry):
            total = into[z].astype(jnp.float32) + other[z].astype(jnp.float32)
            into[z] = total.astype(into.dtype)
            return carry

        lax.fori_loop(0, self.steps, one, 0)

    def after_core(self, k):
        upper, lower = self.halves(k)
        whole = pl.ds(0, SUMS[k])
        wires, place = self.wires, self.place
        for part in (3, 1, 2, 0):
            wires.landed(self.core[k, part], self.from_core[k].at[part])
            self.add(self.own(k, part, whole), self.from_core[k].at[part])
            if part == 3:
                self.first[k, "x", 1] = wires.put(
                    self.own(k, 3, upper), self.from_x[k].at[1], place.at_x()
                )
                self.first[k, "y", 1] = wires.put(
                    self.own(k, 3, lower), self.from_y[k].at[1], place.at_y()
                )
            elif part == 1:
                self.first[k, "x", 0] = wires.put(
                    self.own(k, 1, upper), self.from_x[k].at[0], place.at_x()
                )
            elif part == 2:
                self.first[k, "y", 0] = wires.put(
                    self.own(k, 2, lower), self.from_y[k].at[0], place.at_y()
                )

    def after_first(self, k):
        upper, lower = self.halves(k)
        wires, place = self.wires, self.place
        wires.landed(self.first[k, "x", 1], self.from_x[k].at[1])
        self.add(self.own(k, 2, upper), self.from_x[k].at[1])
        self.second[k, "y"] = wires.put(self.own(k, 2, upper), self.last_y[k], place.at_y())
        wires.landed(self.first[k, "y", 1], self.from_y[k].at[1])
        self.add(self.own(k, 1, lower), self.from_y[k].at[1])
        self.second[k, "x"] = wires.put(self.own(k, 1, lower), self.last_x[k], place.at_x())
        wires.landed(self.first[k, "x", 0], self.from_x[k].at[0])
        self.add(self.own(k, 0, upper), self.from_x[k].at[0])
        wires.landed(self.first[k, "y", 0], self.from_y[k].at[0])
        self.add(self.own(k, 0, lower), self.from_y[k].at[0])

    def after_second(self, k):
        upper, lower = self.halves(k)
        wires, place = self.wires, self.place
        wires.landed(self.second[k, "y"], self.last_y[k])
        self.add(self.own(k, 0, upper), self.last_y[k])
        wires.landed(self.second[k, "x"], self.last_x[k])
        self.add(self.own(k, 0, lower), self.last_x[k])
        for step in range(1, self.steps):
            z = lax.rem(place.z + step, self.steps)
            self.third[k, step] = wires.put(
                self.grads[k].at[z, place.slot()], self.from_z[k].at[step - 1], place.at_z(step)
            )

    def finish(self, k):
        place = self.place
        total = self.grads[k][place.z, place.slot()].astype(jnp.float32)
        for step in range(1, self.steps):
            self.wires.landed(self.third[k, step], self.from_z[k].at[step - 1])
            total = total + self.from_z[k][step - 1].astype(jnp.float32)
        return total


def times(a, b):
    return lax.dot_general(a, b, (((1,), (0,)), ((), ())), preferred_element_type=jnp.float32)


def times_turned(a, b):
    return lax.dot_general(a, b, (((1,), (1,)), ((), ())), preferred_element_type=jnp.float32)


def turned_times(a, b):
    return lax.dot_general(a, b, (((0,), (0,)), ((), ())), preferred_element_type=jnp.float32)


def aligned(index, size):
    return pl.ds(pl.multiple_of(index * size, size), size)


def head_masks(lanes, head_dim):
    lane = lax.broadcasted_iota(jnp.int32, (1, lanes), 1)
    return [
        jnp.where((lane >= h * head_dim) & (lane < (h + 1) * head_dim), 1.0, 0.0).astype(jnp.bfloat16)
        for h in range(lanes // head_dim)
    ]


def gelu_and_slope(u):
    near = 1.0 / (1.0 + (0.3275911 * math.sqrt(0.5)) * jnp.abs(u))
    bell = jnp.exp(-0.5 * (u * u))
    series = near * (
        0.127414796
        + near * (-0.142248368 + near * (0.7107068705 + near * (-0.7265760135 + near * 0.5307027145)))
    )
    tail = series * bell
    below = jnp.where(u < 0.0, tail, 1.0 - tail)
    return u * below, below + u * (bell * (1.0 / math.sqrt(2.0 * math.pi)))


def assemble(source, first, blocks, target):
    per_z, size = source.shape[1] // 2, 24

    def one(i, carry):
        z, pair = lax.div(i, per_z), lax.rem(i, per_z)
        left = source[z, 2 * pair].astype(jnp.float32)
        right = source[z, 2 * pair + 1].astype(jnp.float32)
        for b in range(blocks):
            rows = slice(first + b * size, first + (b + 1) * size)
            both = jnp.concatenate([left[rows], right[rows]], axis=0)
            target[b, aligned(i, 2 * size), :] = both.astype(target.dtype)
        return carry

    lax.fori_loop(0, source.shape[0] * per_z, one, 0)


def sum_slabs(source, first):
    def one(i, total):
        per_z = source.shape[1]
        slab = source[lax.div(i, per_z), lax.rem(i, per_z)].astype(jnp.float32)
        return total + slab[first : first + 8]

    count = source.shape[0] * source.shape[1]
    return lax.fori_loop(0, count, one, jnp.zeros((8, source.shape[-1]), jnp.float32))


def normalize(row_data):
    center = row_data - jnp.mean(row_data, axis=-1, keepdims=True)
    spread = jnp.mean(center * center, axis=-1, keepdims=True)
    scale = lax.rsqrt(spread + EPS)
    return center * scale, scale


def weights_forward(queries, keys_all, live):
    scores = jnp.where(live, times_turned(queries, keys_all), -1e30)
    exponent = jnp.exp(scores - jnp.max(scores, axis=-1, keepdims=True))
    return (exponent * (1.0 / jnp.sum(exponent, axis=-1, keepdims=True))).astype(jnp.bfloat16)


def as_column(row):
    size = row.shape[1]
    down = lax.broadcasted_iota(jnp.int32, (size, size), 0)
    across = lax.broadcasted_iota(jnp.int32, (size, size), 1)
    return jnp.sum(jnp.where(down == across, row, 0.0), axis=1, keepdims=True)


def put_at(row, start, width):
    size = row.shape[1]
    down = lax.broadcasted_iota(jnp.int32, (size, width), 0)
    across = lax.broadcasted_iota(jnp.int32, (size, width), 1)
    return jnp.sum(jnp.where(across == down + start, as_column(row), 0.0), axis=0, keepdims=True)


def forward_kernel(
    short_len, long_len, w_qkv, w_out, w_up, w_down, qv_bias, out_bias, gains, shifts, up_bias,
    short_pool, long_pool, short_tok, long_tok,
    out_down, out_wq, out_wu, out_rows, out_qkv, out_short_probs, out_long_probs, out_mixed,
    out_first, out_hat, out_scale, out_low, out_acted, out_slope, vectors, share,
    whole0, whole1, whole2, wq, wu, rows_in, qkv, short_probs, long_probs, mixed,
    first, hat, scale, low, acted, slope, far_pool,
    send, recv, here, leave,
):
    place = Place()
    x, other = place.x, 1 - place.x
    short_rows, half = short_tok.shape[0], long_tok.shape[1]
    total_rows, width = rows_in.shape
    long_rows = 2 * half
    count, cap = short_pool.shape
    mine = pl.ds(pl.multiple_of(short_rows + x * half, half), half)
    theirs = pl.ds(pl.multiple_of(short_rows + other * half, half), half)
    local = []

    def move(src, dst):
        copy = pltpu.make_async_copy(src, dst, here.at[len(local)])
        copy.start()
        local.append(copy)
        return copy

    move(w_down, out_down.at[place.z, place.slot()])
    loads = [
        move(short_tok, rows_in.at[pl.ds(0, short_rows)]),
        move(long_tok.at[x], rows_in.at[mine]),
    ]
    place.greet_start()

    device = place.dp * 2 + x
    size = w_out.shape[0]

    def blocks(matrix):
        data = matrix[...].astype(jnp.float32)
        return [data[:, i * width : (i + 1) * width] for i in range(data.shape[1] // width)]

    pairs = [
        put_at(member[i : i + 1, :].astype(jnp.float32), device * size, width)
        for member in (qv_bias, out_bias, gains, shifts)
        for i in range(2)
    ]
    ups = put_at(up_bias[...].astype(jnp.float32), lax.rem(device, 8) * (4 * size), width)
    ups = jnp.where(lax.broadcasted_iota(jnp.int32, (8, 1), 0) == lax.div(device, 8), ups, 0.0)
    z, slot = place.z, place.slot()
    whole0[z, slot] = jnp.concatenate(blocks(w_qkv) + pairs, axis=0).astype(jnp.bfloat16)
    whole1[z, slot] = jnp.concatenate(blocks(w_out) + [ups], axis=0).astype(jnp.bfloat16)
    whole2[z, slot] = jnp.concatenate(blocks(w_up), axis=0).astype(jnp.bfloat16)

    place.greet_wait()
    wires = Wires(send, recv)
    net = Gather(wires, place, (whole0, whole1, whole2, out_down), w_down)
    net.start(0)
    net.start(1)
    net.start_plane(2)
    net.start(2)
    net.start_plane(1)
    net.start_plane(0)
    pooled = wires.put(long_pool, far_pool, place.at_x())
    net.relay_z(0)
    net.relay_plane(0)
    tok = wires.put(long_tok.at[other], rows_in.at[mine], place.at_x())
    net.relay_z(1)
    net.relay_corner(0)
    for copy in loads:
        copy.wait()
    net.finish(0)
    assemble(whole0, 0, 3, wq)
    vectors[0:8, :] = sum_slabs(whole0, 72)

    head_dim = width // HEADS
    score_scale = 1.0 / math.sqrt(head_dim)

    def project(i, carry):
        rows = aligned(i, 256)
        data = rows_in[rows, :]
        queries = times(data, wq[0]) + vectors[0:1, :]
        qkv[0, rows, :] = (queries.astype(jnp.bfloat16).astype(jnp.float32) * score_scale).astype(jnp.bfloat16)
        qkv[1, rows, :] = times(data, wq[1]).astype(jnp.bfloat16)
        qkv[2, rows, :] = (times(data, wq[2]) + vectors[1:2, :]).astype(jnp.bfloat16)
        return carry

    lax.fori_loop(0, short_rows // 256, project, 0)

    masks = head_masks(2 * head_dim, head_dim)
    keep_first = lax.broadcasted_iota(jnp.int32, (1, 2 * head_dim), 1) < head_dim
    place_in_block = lax.broadcasted_iota(jnp.int32, (1, cap), 1)
    short_live = [place_in_block < short_len[i] for i in range(count)]
    passage_len = long_len[x]
    long_live = lax.broadcasted_iota(jnp.int32, (1, long_rows), 1) < passage_len
    pairs = width // (2 * head_dim)

    def attend_short(pair, carry):
        lanes = aligned(pair, 2 * head_dim)
        blocks_of = [pl.ds(i * cap, cap) for i in range(count)]
        queries, keys_all, values = [[qkv[b, rows, lanes] for rows in blocks_of] for b in range(3)]
        units = [(i, h) for i in range(count) for h in range(2)]
        scores = [times_turned(queries[i] * masks[h], keys_all[i]) for i, h in units]
        scores = [jnp.where(short_live[i], part, -1e30) for (i, h), part in zip(units, scores)]
        tops = [jnp.max(part, axis=-1, keepdims=True) for part in scores]
        exponents = [jnp.exp(part - top) for part, top in zip(scores, tops)]
        totals = [jnp.sum(part, axis=-1, keepdims=True) for part in exponents]
        probs = [(part * (1.0 / total)).astype(jnp.bfloat16) for part, total in zip(exponents, totals)]
        parts = [times(part, values[i]) for (i, h), part in zip(units, probs)]
        for (i, h), part in zip(units, probs):
            short_probs[i, 2 * pair + h] = part
        for i in range(count):
            mixed[blocks_of[i], lanes] = jnp.where(keep_first, parts[2 * i], parts[2 * i + 1]).astype(jnp.bfloat16)
        return carry

    lax.fori_loop(0, pairs // 2, attend_short, 0)
    net.relay_z(2)
    lax.fori_loop(pairs // 2, pairs - 1, attend_short, 0)
    net.start(3)
    net.relay_plane(1)
    lax.fori_loop(pairs - 1, pairs, attend_short, 0)
    net.start_plane(3)
    move(short_probs, out_short_probs)
    wires.landed(tok, rows_in.at[theirs])
    lax.fori_loop(short_rows // 256, total_rows // 256, project, 0)
    move(qkv, out_qkv)
    move(rows_in, out_rows)

    wires.landed(pooled, far_pool)
    chosen = []
    for block in range(total_rows // cap):
        if block < count:
            mask, start = short_pool[block : block + 1, :], 0
            limit = short_len[block]
        else:
            step = block - count
            in_half, start = step % (half // cap) * cap, step * cap
            at = slice(in_half, in_half + cap)
            own = jnp.where(x == 0, long_pool[0:1, at], long_pool[1:2, at])
            far = jnp.where(x == 0, far_pool[0:1, at], far_pool[1:2, at])
            mask = jnp.where(x == step // (half // cap), own, far)
            limit = passage_len - start
        keep = (place_in_block < limit) & ((mask > 0) | (place_in_block + start == 0))
        chosen.append(jnp.where(keep, 1.0, 0.0))
    for block in range(count):
        share[block : block + 1, :] = chosen[block] / jnp.sum(chosen[block], axis=-1, keepdims=True)
    long_total = sum(jnp.sum(row, axis=-1, keepdims=True) for row in chosen[count:])
    for block in range(count, total_rows // cap):
        share[block : block + 1, :] = chosen[block] / long_total

    def attend_long(pair, carry):
        lanes = aligned(pair, 2 * head_dim)
        rows = pl.ds(short_rows, long_rows)
        keys_all, values = qkv[1, rows, lanes], qkv[2, rows, lanes]
        for block in range(long_rows // 256):
            inner = pl.ds(block * 256, 256)
            rows = pl.ds(short_rows + block * 256, 256)
            queries = qkv[0, rows, lanes]
            parts = []
            for h in range(2):
                probs = weights_forward(queries * masks[h], keys_all, long_live)
                long_probs[2 * pair + h, inner, :] = probs
                parts.append(times(probs, values))
            mixed[rows, lanes] = jnp.where(keep_first, parts[0], parts[1]).astype(jnp.bfloat16)
        return carry

    lax.fori_loop(0, pairs - 2, attend_long, 0)
    net.relay_plane(2)
    net.relay_corner(1)
    lax.fori_loop(pairs - 2, pairs - 1, attend_long, 0)
    net.relay_z(3)
    lax.fori_loop(pairs - 1, pairs, attend_long, 0)
    move(long_probs, out_long_probs)
    move(mixed, out_mixed)
    net.finish(1)
    assemble(whole1, 0, 1, wq.at[pl.ds(3, 1)])
    vectors[8:16, :] = sum_slabs(whole1, 24)
    move(wq, out_wq)

    def attach(i, carry):
        rows = aligned(i, 256)
        first_in = rows_in[rows, :].astype(jnp.float32) + (times(mixed[rows, :], wq[3]) + vectors[2:3, :])
        normal, factor = normalize(first_in)
        out = normal * vectors[4:5, :] + vectors[6:7, :]
        first[rows, :] = out
        low[rows, :] = out.astype(jnp.bfloat16)
        hat[rows, :] = normal.astype(jnp.bfloat16)
        scale[rows, :] = jnp.broadcast_to(factor, (256, scale.shape[1]))
        return carry

    lax.fori_loop(0, total_rows // 256, attach, 0)
    move(first, out_first)
    move(low, out_low)
    move(hat, out_hat)
    move(scale, out_scale)
    net.relay_corner(2)
    net.finish(2)
    assemble(whole2, 0, 4, wu)
    move(wu, out_wu)

    def leaving(i):
        j, rows = lax.div(i, 4), aligned(lax.rem(i, 4), 256)
        return (
            pltpu.make_async_copy(acted.at[j, rows], out_acted.at[j, rows], leave.at[0, i]),
            pltpu.make_async_copy(slope.at[j, rows], out_slope.at[j, rows], leave.at[1, i]),
        )

    def expand(i, carry):
        j, rows = lax.div(i, 4), aligned(lax.rem(i, 4), 256)
        inner = times(low[rows, :], wu[j]) + vectors[pl.ds(8 + j, 1), :]
        value, grad = gelu_and_slope(inner)
        acted[j, rows, :] = value.astype(jnp.bfloat16)
        slope[j, rows, :] = grad.astype(jnp.bfloat16)
        for copy in leaving(i):
            copy.start()
        return carry

    def left(i, carry):
        for copy in leaving(i):
            copy.wait()
        return carry

    lax.fori_loop(0, 7, expand, 0)
    net.relay_plane(3)
    lax.fori_loop(7, 14, expand, 0)
    net.relay_corner(3)
    lax.fori_loop(14, 16, expand, 0)
    net.finish(3)
    wires.close()
    lax.fori_loop(0, 16, left, 0)
    for copy in [local[0]] + local[3:]:
        copy.wait()


def forward(lengths, parameters, pools, short_tok, long_tok, groups):
    short_rows, width = short_tok.shape
    half = long_tok.shape[1]
    long_rows = 2 * half
    rows = short_rows + long_rows
    count, cap = pools[0].shape
    inner = 4 * width
    copies = 4 * ((groups - 1) + 4 * groups + 4 * groups) + 2
    low = jnp.bfloat16
    shape = jax.ShapeDtypeStruct
    outs = (
        shape((groups, 8, SIZES[3], width), low),
        shape((4, width, width), low),
        shape((4, width, width), low),
        shape((rows, width), low),
        shape((3, rows, width), low),
        shape((count, HEADS, cap, cap), low),
        shape((HEADS, long_rows, long_rows), low),
        shape((rows, width), low),
        shape((rows, width), jnp.float32),
        shape((rows, width), low),
        shape((rows, 128), jnp.float32),
        shape((rows, width), low),
        shape((inner // width, rows, width), low),
        shape((inner // width, rows, width), low),
        shape((16, width), jnp.float32),
        shape((rows // cap, cap), jnp.float32),
    )
    anywhere, near = pl.BlockSpec(memory_space=pl.ANY), pl.BlockSpec(memory_space=pltpu.VMEM)
    scalars = pl.BlockSpec(memory_space=pltpu.SMEM)
    kept = [pltpu.VMEM(out.shape, out.dtype) for out in outs[1:14]]
    return pl.pallas_call(
        forward_kernel,
        name="forward",
        out_shape=outs,
        in_specs=[scalars] * 2 + [near] * 11 + [anywhere] * 2,
        out_specs=[anywhere] * 14 + [near] * 2,
        scratch_shapes=[pltpu.VMEM((groups, 8, SIZES[k], width), low) for k in range(3)]
        + kept
        + [
            pltpu.VMEM(pools[1].shape, pools[1].dtype),
            pltpu.SemaphoreType.DMA((copies,)),
            pltpu.SemaphoreType.DMA((copies,)),
            pltpu.SemaphoreType.DMA((24,)),
            pltpu.SemaphoreType.DMA((2, 16)),
        ],
        compiler_params=pltpu.CompilerParams(
            collective_id=0, has_side_effects=True, vmem_limit_bytes=60 * 1024 * 1024
        ),
    )(*lengths, *parameters, *pools, short_tok, long_tok)


def backward_kernel(
    short_len, long_len, vectors, share, short_pool_cot, long_pool_cot, short_cot, long_cot,
    in_down, in_wq, in_wu, in_rows, in_qkv, in_short_probs, in_long_probs, in_mixed,
    in_first, in_hat, in_scale, in_low, in_acted, in_slope,
    short_out, long_out, short_grad, long_grad, short_pooled, long_pooled,
    grad_qkv, grad_out, grad_up, grad_down, grad_vectors, grad_up_vector,
    wide, pair, w_up, w_far, hat, sums, branch, low, scale, halves, probs_short,
    vector_sums, pool_cots, pooled_rows, pooled_own, pooled_far,
    *more,
):
    place = Place()
    x, other = place.x, 1 - place.x
    *chunks, send, recv, here, blocks, fetch = more
    parts = len(SUMS)
    grads, *received = [chunks[i * parts : (i + 1) * parts] for i in range(7)]
    total_rows, width = sums.shape
    short_rows = short_out.shape[0]
    count, cap = probs_short.shape[1], probs_short.shape[-1]
    long_rows = total_rows - short_rows
    half = long_rows // 2
    head_dim = width // HEADS
    steps = total_rows // 256
    low_type = jnp.bfloat16
    local = []

    def move(src, dst):
        copy = pltpu.make_async_copy(src, dst, here.at[len(local)])
        copy.start()
        local.append(copy)
        return copy

    mine = pl.ds(pl.multiple_of(short_rows + x * half, half), half)
    theirs = pl.ds(pl.multiple_of(short_rows + other * half, half), half)
    place.greet_start()
    load_down = [move(in_down.at[j], w_far.at[j]) for j in range(4)]
    load_down += [
        move(short_cot, branch.at[pl.ds(0, short_rows)]),
        move(long_cot.at[x], branch.at[mine]),
    ]
    passage_len = long_len[x]

    def block_copies(i):
        rows = aligned(i, 256)
        return (
            pltpu.make_async_copy(in_acted.at[:, rows], wide.at[:, rows], blocks.at[0, i]),
            pltpu.make_async_copy(in_first.at[rows], sums.at[rows], blocks.at[1, i]),
        )

    for i in range(steps):
        for copy in block_copies(i):
            copy.start()
    vector_sums[...] = jnp.zeros_like(vector_sums)
    pool_cots[0:count, :] = short_pool_cot[...]
    pool_cots[count : 2 * count, :] = jnp.broadcast_to(long_pool_cot[pl.ds(x, 1), :], (count, width))
    place.greet_wait()
    wires = Wires(send, recv)
    swap_cot = wires.put(long_cot.at[other], branch.at[mine], place.at_x())
    net = Scatter(wires, place, grads, *received)
    for copy in load_down:
        copy.wait()
    tall = lax.broadcasted_iota(jnp.int32, (256, 1), 0)
    diagonal = lax.broadcasted_iota(jnp.int32, (cap, cap), 0) == lax.broadcasted_iota(jnp.int32, (cap, cap), 1)

    def add_vector(row, rows):
        vector_sums[row : row + 1, :] += jnp.sum(rows, axis=0, keepdims=True)

    def second(step, carry):
        i = jnp.where(step < 2, step, 2 + lax.rem(step + x, 2))

        @pl.when(step == steps - 1)
        def _():
            wires.landed(swap_cot, branch.at[theirs])

        rows = aligned(i, 256)
        for copy in block_copies(i):
            copy.wait()
        product = times(wide[0, rows, :], w_far[0])
        for j in range(1, 4):
            product += times(wide[j, rows, :], w_far[j])
        normal, factor = normalize(sums[rows, :] + (product + vectors[3:4, :]))
        lens = [
            jnp.where(2 * i + part < count, short_len[lax.rem(2 * i + part, count)], passage_len - (2 * i + part - count) * cap)
            for part in range(2)
        ]
        live = tall < jnp.where(tall < cap, lens[0], lens[1] + cap)
        final = jnp.where(live, normal * vectors[5:6, :] + vectors[7:8, :], 0.0)
        low[rows, :] = final.astype(low_type)
        spread = []
        for part in range(2):
            share_row = share[pl.ds(2 * i + part, 1), :]
            column = jnp.sum(jnp.where(diagonal, share_row, 0.0), axis=1, keepdims=True)
            piece = final[part * cap : (part + 1) * cap]
            pooled_rows[pl.ds(2 * i + part, 1), :] = jnp.sum(piece * column, axis=0, keepdims=True)
            spread.append(column * pool_cots[pl.ds(2 * i + part, 1), :])
        grad_final = jnp.where(live, branch[rows, :].astype(jnp.float32), 0.0) + jnp.concatenate(spread, axis=0)
        add_vector(5, grad_final * normal)
        add_vector(7, grad_final)
        scaled = grad_final * vectors[5:6, :]
        mean_one = jnp.mean(scaled, axis=-1, keepdims=True)
        mean_two = jnp.mean(scaled * normal, axis=-1, keepdims=True)
        grad_second = factor * (scaled - mean_one - normal * mean_two)
        sums[rows, :] = grad_second
        grad_branch = grad_second.astype(low_type)
        branch[rows, :] = grad_branch
        add_vector(3, grad_branch.astype(jnp.float32))
        return carry

    lax.fori_loop(0, steps, second, 0)
    short_pooled[...] = pooled_rows[0:count, :]
    own_pooled = jnp.sum(pooled_rows[count : 2 * count, :], axis=0, keepdims=True)
    pooled_own[...] = jnp.broadcast_to(own_pooled, pooled_own.shape)
    long_pooled[pl.ds(x, 1), :] = own_pooled
    out_copies = [
        move(low.at[pl.ds(0, short_rows)], short_out),
        move(low.at[mine], long_out.at[x]),
    ]
    load_slope = [move(in_slope.at[0], pair.at[0]), move(in_slope.at[1], pair.at[1])]
    load_up = move(in_wu, w_up)
    load_hat, load_scale = move(in_hat, hat), move(in_scale, scale)

    def down_step(i, carry):
        j, part = lax.div(i, 2), lax.rem(i, 2)
        product = turned_times(wide[j, :, aligned(part, width // 2)], branch[...])
        grads[5][j, aligned(part, 4)] = product.reshape(4, SUMS[5], width).astype(low_type)
        return carry

    lax.fori_loop(0, 8, down_step, 0, unroll=2)
    net.send_core(5)
    swap_out = wires.put(low.at[theirs], long_out.at[x], place.at_x())
    swap_pooled = wires.put(pooled_own, pooled_far, place.at_x())

    def inner_block(j):
        def inner(i, carry):
            rows = aligned(i, 256)
            product = times_turned(branch[rows, :], w_far[j]) * pair[j % 2, rows, :].astype(jnp.float32)
            grad_inner = product.astype(low_type)
            wide[j, rows, :] = grad_inner
            add_vector(8 + j, grad_inner.astype(jnp.float32))
            return carry

        lax.fori_loop(0, steps, inner, 0, unroll=2)

    load_slope[0].wait()
    inner_block(0)
    load_slope.append(move(in_slope.at[2], pair.at[0]))
    load_slope[1].wait()
    inner_block(1)
    load_slope.append(move(in_slope.at[3], pair.at[1]))
    for copy in out_copies:
        copy.wait()
    wires.has_left(swap_out)
    load_low = move(in_low, low)
    net.after_core(5)
    load_slope[2].wait()
    inner_block(2)
    load_mixed = move(in_mixed, pair.at[0])
    load_slope[3].wait()
    inner_block(3)
    load_wq = move(in_wq, w_far)

    def up_step(i, carry):
        r, both = lax.div(i, 2), lax.rem(i, 2)
        data = low[:, aligned(r, width // 2)]
        halves[0] = turned_times(data, wide[2 * both])
        halves[1] = turned_times(data, wide[2 * both + 1])

        def one(k, carry):
            rows = pl.ds(pl.multiple_of(k * 24, 8), 24)
            data = jnp.concatenate([halves[0, rows, :], halves[1, rows, :]], axis=0)
            grads[4][2 * r + lax.div(k, 8), lax.rem(k, 8), aligned(both, 48), :] = data.astype(low_type)
            return carry

        return lax.fori_loop(0, 16, one, carry)

    load_low.wait()
    lax.fori_loop(0, 4, up_step, 0)
    net.send_core(4)

    load_up.wait()
    load_hat.wait()
    load_scale.wait()

    def first_back(i, carry):
        rows = aligned(i, 256)
        grad_first = sums[rows, :]
        for j in range(4):
            grad_first += times_turned(wide[j, rows, :], w_up[j])
        normal = hat[rows, :].astype(jnp.float32)
        add_vector(4, grad_first * normal)
        add_vector(6, grad_first)
        scaled = grad_first * vectors[4:5, :]
        mean_one = jnp.mean(scaled, axis=-1, keepdims=True)
        mean_two = jnp.mean(scaled * normal, axis=-1, keepdims=True)
        grad_in = scale[rows, 0:1] * (scaled - mean_one - normal * mean_two)
        sums[rows, :] = grad_in
        grad_attn = grad_in.astype(low_type)
        branch[rows, :] = grad_attn
        add_vector(2, grad_attn.astype(jnp.float32))
        return carry

    lax.fori_loop(0, steps // 2, first_back, 0)
    net.after_first(5)
    lax.fori_loop(steps // 2, steps, first_back, 0)
    load_qkv = move(in_qkv, wide.at[pl.ds(0, 3)])
    load_rows = move(in_rows, wide.at[3])
    net.after_core(4)

    load_mixed.wait()
    load_wq.wait()
    def out_step(r, carry):
        halves[0] = turned_times(pair[0, :, aligned(r, width // 2)], branch[...])

        def one(k, carry):
            rows = pl.ds(pl.multiple_of(k * 24, 8), 24)
            data = jnp.concatenate([halves[0, rows, :], vector_sums[8:16, :]], axis=0)
            grads[3][2 * r + lax.div(k, 8), lax.rem(k, 8)] = data.astype(low_type)
            return carry

        return lax.fori_loop(0, 16, one, carry)

    lax.fori_loop(0, 2, out_step, 0)
    net.send_core(3)

    def mixed_back(i, carry):
        rows = aligned(i, 256)
        pair[1, rows, :] = times_turned(branch[rows, :], w_far[3]).astype(low_type)
        return carry

    lax.fori_loop(0, steps, mixed_back, 0)

    def probs_copies(p, slot):
        lanes = pl.ds(2 * p, 2)
        return (
            pltpu.make_async_copy(in_short_probs.at[:, lanes], probs_short.at[slot], fetch.at[0, slot]),
            pltpu.make_async_copy(
                in_long_probs.at[lanes],
                w_up.at[pl.ds(2 * slot, 2), pl.ds(0, long_rows), pl.ds(0, long_rows)],
                fetch.at[1, slot],
            ),
        )

    for copy in probs_copies(0, 0):
        copy.start()
    load_qkv.wait()
    score_scale = 1.0 / math.sqrt(head_dim)
    masks = head_masks(2 * head_dim, head_dim)
    pairs = width // (2 * head_dim)

    def attend_back(lanes, units):
        heads = [(u, h) for u in range(len(units)) for h in range(2)]
        queries = [wide[0, rows, lanes] for rows, _, _, _ in units]
        grads_mixed = [pair[1, rows, lanes] for rows, _, _, _ in units]
        overlaps = [
            grad.astype(jnp.float32) * pair[0, rows, lanes].astype(jnp.float32)
            for grad, (rows, _, _, _) in zip(grads_mixed, units)
        ]
        centers = [
            jnp.sum(overlaps[u] * masks[h].astype(jnp.float32), axis=-1, keepdims=True) for u, h in heads
        ]
        grads_head = [grads_mixed[u] * masks[h] for u, h in heads]
        probs = [units[u][1](h) for u, h in heads]
        grads_probs = [times_turned(grad, units[u][3]) for grad, (u, h) in zip(grads_head, heads)]
        scores = [
            (part.astype(jnp.float32) * (grad - center)).astype(low_type)
            for part, grad, center in zip(probs, grads_probs, centers)
        ]
        grads_q = [times(part, units[u][2] * masks[h]) for part, (u, h) in zip(scores, heads)]
        grads_k = [turned_times(part, queries[u] * masks[h]) for part, (u, h) in zip(scores, heads)]
        grads_v = [turned_times(part, grad) for part, grad in zip(probs, grads_head)]
        for u, (rows, _, _, _) in enumerate(units):
            total = grads_q[2 * u] + grads_q[2 * u + 1]
            wide[0, rows, lanes] = (total * score_scale).astype(low_type)
        return [
            [grads[2 * u] + grads[2 * u + 1] for u in range(len(units))] for grads in (grads_k, grads_v)
        ]

    def attention_back(p, carry):
        slot = lax.rem(p, 2)
        for copy in probs_copies(p, slot):
            copy.wait()

        @pl.when(p + 1 < pairs)
        def _():
            for copy in probs_copies(p + 1, 1 - slot):
                copy.start()

        lanes = aligned(p, 2 * head_dim)
        blocks_of = [pl.ds(i * cap, cap) for i in range(count)]
        units = [
            (rows, lambda h, i=i: probs_short[slot, i, h], wide[1, rows, lanes], wide[2, rows, lanes])
            for i, rows in enumerate(blocks_of)
        ]
        grads_k, grads_v = attend_back(lanes, units)
        for rows, grad_k, grad_v in zip(blocks_of, grads_k, grads_v):
            wide[1, rows, lanes] = grad_k.astype(low_type)
            wide[2, rows, lanes] = grad_v.astype(low_type)
        rows = pl.ds(short_rows, long_rows)
        keys_all, values = wide[1, rows, lanes], wide[2, rows, lanes]
        total_k, total_v = None, None
        for block in range(long_rows // 256):
            inner = pl.ds(block * 256, 256)
            unit = (
                pl.ds(short_rows + block * 256, 256),
                lambda h, inner=inner: w_up[2 * slot + h, inner, 0:long_rows],
                keys_all,
                values,
            )
            (grad_k,), (grad_v,) = attend_back(lanes, [unit])
            total_k = grad_k if total_k is None else total_k + grad_k
            total_v = grad_v if total_v is None else total_v + grad_v
        wide[1, rows, lanes] = total_k.astype(low_type)
        wide[2, rows, lanes] = total_v.astype(low_type)
        return carry

    third = width // 3

    def qkv_step(group):
        lanes = pl.ds(group * third, third)

        def bias(i, carry):
            rows = aligned(i, 256)
            for row, b in ((0, 0), (1, 2)):
                piece = wide[b, rows, lanes].astype(jnp.float32)
                vector_sums[row : row + 1, lanes] += jnp.sum(piece, axis=0, keepdims=True)
            return carry

        lax.fori_loop(0, steps, bias, 0)

        def step(r, carry):
            data = wide[3, :, aligned(r, width // 2)]
            for b in range(3):
                halves[0, :, b * third : (b + 1) * third] = turned_times(data, wide[b, :, lanes])

            def one(k, carry):
                rows = pl.ds(pl.multiple_of(k * 24, 8), 24)
                pieces = [halves[0, rows, b * third : (b + 1) * third] for b in range(3)]
                data = jnp.concatenate(pieces + [vector_sums[0:8, lanes]], axis=0)
                grads[group][2 * r + lax.div(k, 8), lax.rem(k, 8)] = data.astype(low_type)
                return carry

            return lax.fori_loop(0, 16, one, carry)

        lax.fori_loop(0, 2, step, 0)
        net.send_core(group)

    lax.fori_loop(0, pairs // 3, attention_back, 0)
    load_rows.wait()
    qkv_step(0)
    net.after_core(3)
    net.after_second(5)
    net.after_first(4)
    lax.fori_loop(pairs // 3, 2 * pairs // 3, attention_back, 0)
    qkv_step(1)
    net.after_core(0)
    net.after_first(3)
    net.after_second(4)
    lax.fori_loop(2 * pairs // 3, pairs, attention_back, 0)
    qkv_step(2)
    net.after_core(1)
    net.after_first(0)
    net.after_second(3)

    def tokens_back(rows):
        grad_in = sums[rows, :]
        for b in range(3):
            grad_in += times_turned(wide[b, rows, :], w_far[b])
        return grad_in

    far_low, far_in = low.at[pl.ds(0, half)], low.at[pl.ds(half, half)]
    far_low[...] = tokens_back(theirs).astype(low_type)
    swap_grad = wires.put(far_low, far_in, place.at_x())
    net.after_core(2)
    net.after_first(1)
    net.after_second(0)

    def tokens_step(i, carry):
        rows = pl.ds(pl.multiple_of(jnp.where(i < 2, i * 256, short_rows + x * half), 256), 256)
        sums[rows, :] = tokens_back(rows)
        return carry

    lax.fori_loop(0, 3, tokens_step, 0)
    move(sums.at[pl.ds(0, short_rows)], short_grad)
    move(sums.at[mine], long_grad.at[x])
    net.after_first(2)
    net.after_second(1)
    grad_down[...] = net.finish(5)
    total = net.finish(4)
    for j in range(4):
        grad_up[:, j * width : (j + 1) * width] = total[24 * j : 24 * j + 24]
    total = net.finish(3)
    grad_out[...] = total[0:24]
    grad_up_vector[...] = total[24:32]
    wires.landed(swap_pooled, pooled_far)
    long_pooled[pl.ds(other, 1), :] = pooled_far[0:1, :]
    wires.landed(swap_grad, far_in)
    sums[theirs, :] = far_in[...].astype(jnp.float32)
    move(sums.at[theirs], long_grad.at[other])
    wires.landed(swap_out, long_out.at[other])
    net.after_second(2)
    for group in range(3):
        total = net.finish(group)
        for b in range(3):
            columns = slice(b * width + group * third, b * width + (group + 1) * third)
            grad_qkv[:, columns] = total[24 * b : 24 * b + 24]
        grad_vectors[:, group * third : (group + 1) * third] = total[72:80]
    wires.close()
    for copy in local[-3:]:
        copy.wait()


def backward(lengths, vectors, share, pool_cots, cots, arrays, groups):
    width = vectors.shape[1]
    rows = arrays[3].shape[0]
    count, _, cap, _ = arrays[5].shape
    short_rows = count * cap
    half = (rows - short_rows) // 2
    low, wide_type = jnp.bfloat16, jnp.float32
    shape = jax.ShapeDtypeStruct
    rows24 = 24
    outs = (
        shape((short_rows, width), low),
        shape((2, half, width), low),
        shape((short_rows, width), wide_type),
        shape((2, half, width), wide_type),
        shape((count, width), wide_type),
        shape((2, width), wide_type),
        shape((rows24, 3 * width), wide_type),
        shape((rows24, width), wide_type),
        shape((rows24, 4 * width), wide_type),
        shape((4 * rows24, width), wide_type),
        shape((8, width), wide_type),
        shape((8, width), wide_type),
    )
    anywhere, near = pl.BlockSpec(memory_space=pl.ANY), pl.BlockSpec(memory_space=pltpu.VMEM)
    copies = len(SUMS) * (4 + 6 + (groups - 1)) + 4

    widths = (width // 3,) * 3 + (width,) * 3

    def chunks(parts, sizes):
        return [pltpu.VMEM(parts + (size, columns), low) for size, columns in zip(sizes, widths)]

    rest = tuple(size - some for size, some in zip(SUMS, SUMS_X))
    scratch = [
        pltpu.VMEM((4, rows, width), low),
        pltpu.VMEM((2, rows, width), low),
        pltpu.VMEM((4, width, width), low),
        pltpu.VMEM((4, width, width), low),
        pltpu.VMEM((rows, width), low),
        pltpu.VMEM((rows, width), wide_type),
        pltpu.VMEM((rows, width), low),
        pltpu.VMEM((rows, width), low),
        pltpu.VMEM((rows, 128), wide_type),
        pltpu.VMEM((2, width // 2, width), wide_type),
        pltpu.VMEM((2, count, 2, cap, cap), low),
        pltpu.VMEM((16, width), wide_type),
        pltpu.VMEM((2 * count, width), wide_type),
        pltpu.VMEM((2 * count, width), wide_type),
        pltpu.VMEM((8, width), wide_type),
        pltpu.VMEM((8, width), wide_type),
        *chunks((groups, 8), SUMS),
        *chunks((4, groups), SUMS),
        *chunks((2, groups), SUMS_X),
        *chunks((2, groups), rest),
        *chunks((groups,), rest),
        *chunks((groups,), SUMS_X),
        *chunks((groups - 1,), SUMS),
        pltpu.SemaphoreType.DMA((copies,)),
        pltpu.SemaphoreType.DMA((copies,)),
        pltpu.SemaphoreType.DMA((24,)),
        pltpu.SemaphoreType.DMA((2, rows // 256)),
        pltpu.SemaphoreType.DMA((2, 2)),
    ]
    return pl.pallas_call(
        backward_kernel,
        name="backward",
        out_shape=outs,
        in_specs=[pl.BlockSpec(memory_space=pltpu.SMEM)] * 2 + [near] * 4 + [anywhere] * 16,
        out_specs=[anywhere] * 4 + [near] * 8,
        scratch_shapes=scratch,
        compiler_params=pltpu.CompilerParams(
            collective_id=1, has_side_effects=True, vmem_limit_bytes=63 * 1024 * 1024
        ),
    )(*lengths, vectors, share, *pool_cots, *cots, *arrays)


def results_kernel(
    in_0, in_1, in_2, in_3, in_4, in_5, in_6, in_7, in_8, in_9, grad_vectors, grad_ups,
    out_0, out_1, out_2, out_3, out_4, out_5, out_6, out_7, out_8, out_9, pair_0, pair_1, ups, pair_2, pair_3,
    *more,
):
    *held, come, leave = more
    sources = (in_0, in_1, in_2, in_3, in_4, in_5, in_6, in_7, in_8, in_9)
    places = (out_0, out_1, out_4, out_5, out_2, out_3, out_6, out_7, out_8, out_9)
    ins = [pltpu.make_async_copy(sources[i], held[i], come.at[i]) for i in range(10)]
    outs = [pltpu.make_async_copy(held[i], places[i], leave.at[i]) for i in range(10)]
    for copy in ins:
        copy.start()
    device = lax.axis_index("dp") * 2 + lax.axis_index("seq")
    size, width = in_7.shape
    rows = pltpu.roll(grad_vectors[...], lax.rem(width - device * size, width), 1)
    for i, ref in enumerate((pair_0, pair_1, pair_2, pair_3)):
        ref[...] = rows[2 * i : 2 * i + 2, 0:size]
    start = lax.rem(device, 8) * (4 * size)
    row = grad_ups[pl.ds(lax.div(device, 8), 1), :]
    row = pltpu.roll(jnp.broadcast_to(row, (8, width)), lax.rem(width - start, width), 1)
    ups[...] = row[0:1, 0 : 4 * size]
    for i in range(10):
        ins[i].wait()
        outs[i].start()
    for copy in outs:
        copy.wait()


def results(arrays):
    size = arrays[7].shape[0]
    order = (0, 1, 4, 5, 2, 3, 6, 7, 8, 9)
    shape = jax.ShapeDtypeStruct
    pair = shape((2, size), jnp.float32)
    outs = tuple(shape(arrays[i].shape, arrays[i].dtype) for i in order)
    anywhere, near = pl.BlockSpec(memory_space=pl.ANY), pl.BlockSpec(memory_space=pltpu.VMEM)
    return pl.pallas_call(
        results_kernel,
        name="results",
        out_shape=outs + (pair, pair, shape((1, 4 * size), jnp.float32), pair, pair),
        in_specs=[anywhere] * 10 + [near] * 2,
        out_specs=[anywhere] * 10 + [near] * 5,
        scratch_shapes=[pltpu.VMEM(array.shape, array.dtype) for array in arrays[:10]]
        + [pltpu.SemaphoreType.DMA((10,)), pltpu.SemaphoreType.DMA((10,))],
        compiler_params=pltpu.CompilerParams(vmem_limit_bytes=56 * 1024 * 1024),
    )(*arrays)


def layer_norm(row_data, gain_vec, shift_vec):
    center = row_data - jnp.mean(row_data, axis=-1, keepdims=True)
    spread = jnp.mean(center * center, axis=-1, keepdims=True)
    return center * lax.rsqrt(spread + EPS) * gain_vec + shift_vec


def exact_gelu(inner_act):
    return jax.nn.gelu(inner_act, approximate=False)


def outer_sum(left_rows, right_rows):
    return lax.dot_general(
        left_rows, right_rows, (((0,), (0,)), ((), ())), preferred_element_type=jnp.float32
    )


def times_transposed(left_rows, matrix):
    return lax.dot_general(
        left_rows, matrix, (((1,), (1,)), ((), ())), preferred_element_type=jnp.float32
    )


def masked_scores(queries, keys_all, key_live, score_scale):
    scores = (
        jnp.einsum("bqhe,bkhe->bhqk", queries, keys_all, preferred_element_type=jnp.float32)
        * score_scale
    )
    return jnp.where(key_live[:, None, None, :], scores, -1e30)


def attend_forward(pieces, score_scale):
    queries, keys_all, values, key_live = pieces
    scores = masked_scores(queries, keys_all, key_live, score_scale)
    highest = jnp.max(scores, axis=-1, keepdims=True)
    exponent = jnp.exp(scores - highest)
    totals = jnp.sum(exponent, axis=-1, keepdims=True)
    soft_probs = (exponent / totals).astype(jnp.bfloat16)
    mixed_heads = jnp.einsum(
        "bhqk,bkhe->bqhe", soft_probs, values, preferred_element_type=jnp.float32
    )
    return (mixed_heads.astype(jnp.bfloat16), (highest + jnp.log(totals))[..., 0])


def attend_backward(pieces, score_scale):
    queries, keys_all, values, key_live, grad_mixed, log_total = pieces
    scores = masked_scores(queries, keys_all, key_live, score_scale)
    soft_probs = jnp.exp(scores - log_total[..., None])
    grad_probs = jnp.einsum(
        "bqhe,bkhe->bhqk", grad_mixed, values, preferred_element_type=jnp.float32
    )
    grad_values = jnp.einsum(
        "bhqk,bqhe->bkhe",
        soft_probs.astype(jnp.bfloat16),
        grad_mixed,
        preferred_element_type=jnp.float32,
    )
    center = jnp.sum(soft_probs * grad_probs, axis=-1, keepdims=True)
    grad_scores = (soft_probs * (grad_probs - center)).astype(jnp.bfloat16)
    grad_queries = (
        jnp.einsum("bhqk,bkhe->bqhe", grad_scores, keys_all, preferred_element_type=jnp.float32)
        * score_scale
    )
    grad_keys = (
        jnp.einsum("bhqk,bqhe->bkhe", grad_scores, queries, preferred_element_type=jnp.float32)
        * score_scale
    )
    return (grad_queries, grad_keys, grad_values)


def by_blocks(function, per_block, arrays):
    blocks = arrays[0].shape[0] // per_block
    stacked = tuple((member.reshape((blocks, per_block) + member.shape[1:]) for member in arrays))
    results = lax.map(function, stacked)
    return jax.tree.map(
        lambda member: member.reshape((blocks * per_block,) + member.shape[2:]), results
    )


def general_shards(
    short_tokens,
    long_tokens,
    short_len,
    long_len,
    short_pool,
    long_pool,
    short_cot,
    long_cot,
    short_pool_cot,
    long_pool_cot,
    w_qkv,
    w_out,
    w_up,
    w_down,
    qv_bias,
    out_bias,
    up_bias,
    norm_gain,
    norm_shift,
):
    gathered = (
        lax.all_gather(w_qkv, ("dp", "seq"), axis=0, tiled=True),
        lax.all_gather(w_out, ("dp", "seq"), axis=0, tiled=True),
        lax.all_gather(w_up, ("dp", "seq"), axis=0, tiled=True),
        lax.all_gather(w_down, ("dp", "seq"), axis=0, tiled=True),
        lax.all_gather(qv_bias, ("dp", "seq"), axis=0, tiled=True),
        lax.all_gather(out_bias, ("dp", "seq"), axis=0, tiled=True),
        lax.all_gather(up_bias, ("dp", "seq"), axis=0, tiled=True),
        lax.all_gather(norm_gain, ("dp", "seq"), axis=0, tiled=True),
        lax.all_gather(norm_shift, ("dp", "seq"), axis=0, tiled=True),
    )
    qkv_matrix, out_matrix, up_matrix, down_matrix, qv_vec, out_vec, up_vec, gains, shifts = (
        gathered
    )
    gains = gains.astype(jnp.float32)
    shifts = shifts.astype(jnp.float32)
    short_count, short_cap, model_width = short_tokens.shape
    long_count, long_half = (long_tokens.shape[0], long_tokens.shape[1])
    head_count = HEADS
    head_dim = model_width // head_count
    score_scale = 1.0 / math.sqrt(head_dim)
    short_rows = short_count * short_cap
    long_rows = long_count * long_half
    short_place = jnp.arange(short_cap, dtype=jnp.int32)
    short_live = short_place[None, :] < short_len[:, None]
    long_place = lax.axis_index("seq") * long_half + jnp.arange(long_half, dtype=jnp.int32)
    long_live = long_place[None, :] < long_len[:, None]
    short_weight = (short_live & ((short_pool > 0) | (short_place[None, :] == 0))).astype(
        jnp.float32
    )
    long_weight = (long_live & ((long_pool > 0) | (long_place[None, :] == 0))).astype(jnp.float32)
    row_live = jnp.concatenate([short_live.reshape(-1), long_live.reshape(-1)]).astype(jnp.float32)
    inputs = jnp.concatenate(
        [
            short_tokens.reshape(short_rows, model_width),
            long_tokens.reshape(long_rows, model_width),
        ],
        axis=0,
    )
    joined = jnp.dot(inputs, qkv_matrix, preferred_element_type=jnp.float32)
    queries = (joined[:, :model_width] + qv_vec[:, 0]).astype(jnp.bfloat16)
    keys_all = joined[:, model_width : 2 * model_width].astype(jnp.bfloat16)
    values = (joined[:, 2 * model_width :] + qv_vec[:, 1]).astype(jnp.bfloat16)
    short_shape = (short_count, short_cap, head_count, head_dim)
    long_shape = (long_count, long_half, head_count, head_dim)
    short_q = queries[:short_rows].reshape(short_shape)
    short_k = keys_all[:short_rows].reshape(short_shape)
    short_v = values[:short_rows].reshape(short_shape)
    long_q = queries[short_rows:].reshape(long_shape)
    long_k = keys_all[short_rows:].reshape(long_count, long_half, model_width)
    long_v = values[short_rows:].reshape(long_count, long_half, model_width)
    short_block = math.gcd(short_count, max(1, 512 // short_cap))
    long_block = math.gcd(long_count, max(1, 512 // long_half))

    def forward_blocks(pieces):
        return attend_forward(pieces, score_scale)

    def backward_blocks(pieces):
        return attend_backward(pieces, score_scale)

    short_mixed, short_logsum = by_blocks(
        forward_blocks, short_block, (short_q, short_k, short_v, short_live)
    )
    gathered_k, gathered_v = (
        lax.all_gather(long_k, "seq", axis=1, tiled=True),
        lax.all_gather(long_v, "seq", axis=1, tiled=True),
    )
    full_len = gathered_k.shape[1]
    full_shape = (long_count, full_len, head_count, head_dim)
    long_key_live = jnp.arange(full_len, dtype=jnp.int32)[None, :] < long_len[:, None]
    long_mixed, long_logsum = by_blocks(
        forward_blocks,
        long_block,
        (long_q, gathered_k.reshape(full_shape), gathered_v.reshape(full_shape), long_key_live),
    )
    mixed_heads = jnp.concatenate(
        [short_mixed.reshape(short_rows, model_width), long_mixed.reshape(long_rows, model_width)],
        axis=0,
    )
    attn_out = jnp.dot(mixed_heads, out_matrix, preferred_element_type=jnp.float32) + out_vec[:, 0]
    first_in = inputs.astype(jnp.float32) + attn_out
    first_norm = layer_norm(first_in, gains[:, 0], shifts[:, 0])
    first_low = first_norm.astype(jnp.bfloat16)
    inner_act = jnp.dot(first_low, up_matrix, preferred_element_type=jnp.float32) + up_vec
    activated = exact_gelu(inner_act).astype(jnp.bfloat16)
    branch = jnp.dot(activated, down_matrix, preferred_element_type=jnp.float32) + out_vec[:, 1]
    second_in = first_norm + branch
    final_norm = layer_norm(second_in, gains[:, 1], shifts[:, 1]) * row_live[:, None]
    short_final = final_norm[:short_rows].reshape(short_count, short_cap, model_width)
    long_final = final_norm[short_rows:].reshape(long_count, long_half, model_width)
    short_total = jnp.sum(short_weight, axis=1)
    short_pooled = jnp.sum(short_final * short_weight[..., None], axis=1) / short_total[:, None]
    long_partial = jnp.sum(long_final * long_weight[..., None], axis=1)
    long_sum, long_total = lax.psum((long_partial, jnp.sum(long_weight, axis=1)), "seq")
    long_pooled = long_sum / long_total[:, None]
    grad_short = (
        short_cot.astype(jnp.float32) * short_live[..., None]
        + short_weight[..., None] * short_pool_cot[:, None, :] / short_total[:, None, None]
    )
    grad_long = (
        long_cot.astype(jnp.float32) * long_live[..., None]
        + long_weight[..., None] * long_pool_cot[:, None, :] / long_total[:, None, None]
    )
    grad_top = jnp.concatenate(
        [grad_short.reshape(short_rows, model_width), grad_long.reshape(long_rows, model_width)],
        axis=0,
    )
    _, second_back = jax.vjp(layer_norm, second_in, gains[:, 1], shifts[:, 1])
    grad_second, grad_gain_two, grad_shift_two = second_back(grad_top)
    grad_branch = grad_second.astype(jnp.bfloat16)
    grad_down = outer_sum(activated, grad_branch)
    grad_bias_two = jnp.sum(grad_branch.astype(jnp.float32), axis=0)
    grad_acted = times_transposed(grad_branch, down_matrix)
    _, gelu_back = jax.vjp(exact_gelu, inner_act)
    grad_inner = gelu_back(grad_acted)[0].astype(jnp.bfloat16)
    grad_up = outer_sum(first_low, grad_inner)
    grad_up_bias = jnp.sum(grad_inner.astype(jnp.float32), axis=0)
    grad_first = grad_second + times_transposed(grad_inner, up_matrix)
    _, first_back = jax.vjp(layer_norm, first_in, gains[:, 0], shifts[:, 0])
    grad_first_in, grad_gain_one, grad_shift_one = first_back(grad_first)
    grad_attn = grad_first_in.astype(jnp.bfloat16)
    grad_out = outer_sum(mixed_heads, grad_attn)
    grad_bias_one = jnp.sum(grad_attn.astype(jnp.float32), axis=0)
    grad_mixed = times_transposed(grad_attn, out_matrix).astype(jnp.bfloat16)
    short_dq, short_dk, short_dv = by_blocks(
        backward_blocks,
        short_block,
        (
            short_q,
            short_k,
            short_v,
            short_live,
            grad_mixed[:short_rows].reshape(short_shape),
            short_logsum,
        ),
    )
    again_k, again_v = (gathered_k, gathered_v)
    long_dq, long_dk, long_dv = by_blocks(
        backward_blocks,
        long_block,
        (
            long_q,
            again_k.reshape(full_shape),
            again_v.reshape(full_shape),
            long_key_live,
            grad_mixed[short_rows:].reshape(long_shape),
            long_logsum,
        ),
    )
    own_dk, own_dv = (
        lax.psum_scatter(
            long_dk.reshape(long_count, full_len, model_width).astype(jnp.bfloat16),
            "seq",
            scatter_dimension=1,
            tiled=True,
        ).astype(jnp.float32),
        lax.psum_scatter(
            long_dv.reshape(long_count, full_len, model_width).astype(jnp.bfloat16),
            "seq",
            scatter_dimension=1,
            tiled=True,
        ).astype(jnp.float32),
    )
    grad_queries = jnp.concatenate(
        [short_dq.reshape(short_rows, model_width), long_dq.reshape(long_rows, model_width)], axis=0
    ).astype(jnp.bfloat16)
    grad_keys = jnp.concatenate(
        [short_dk.reshape(short_rows, model_width), own_dk.reshape(long_rows, model_width)], axis=0
    ).astype(jnp.bfloat16)
    grad_values = jnp.concatenate(
        [short_dv.reshape(short_rows, model_width), own_dv.reshape(long_rows, model_width)], axis=0
    ).astype(jnp.bfloat16)
    grad_joined = jnp.concatenate([grad_queries, grad_keys, grad_values], axis=1)
    grad_qkv = outer_sum(inputs, grad_joined)
    grad_qv = jnp.stack(
        [
            jnp.sum(grad_queries.astype(jnp.float32), axis=0),
            jnp.sum(grad_values.astype(jnp.float32), axis=0),
        ],
        axis=1,
    )
    grad_inputs = grad_first_in + times_transposed(grad_joined, qkv_matrix)
    grad_out_vec = jnp.stack([grad_bias_one, grad_bias_two], axis=1)
    grad_gains = jnp.stack([grad_gain_one, grad_gain_two], axis=1)
    grad_shifts = jnp.stack([grad_shift_one, grad_shift_two], axis=1)
    shard_grads = (
        lax.psum_scatter(grad_qkv, ("dp", "seq"), scatter_dimension=0, tiled=True),
        lax.psum_scatter(grad_out, ("dp", "seq"), scatter_dimension=0, tiled=True),
        lax.psum_scatter(grad_up, ("dp", "seq"), scatter_dimension=0, tiled=True),
        lax.psum_scatter(grad_down, ("dp", "seq"), scatter_dimension=0, tiled=True),
        lax.psum_scatter(grad_qv, ("dp", "seq"), scatter_dimension=0, tiled=True),
        lax.psum_scatter(grad_out_vec, ("dp", "seq"), scatter_dimension=0, tiled=True),
        lax.psum_scatter(grad_up_bias, ("dp", "seq"), scatter_dimension=0, tiled=True),
        lax.psum_scatter(grad_gains, ("dp", "seq"), scatter_dimension=0, tiled=True),
        lax.psum_scatter(grad_shifts, ("dp", "seq"), scatter_dimension=0, tiled=True),
    )
    short_out = short_final.astype(jnp.bfloat16)
    long_out = long_final.astype(jnp.bfloat16)
    short_grad_in = grad_inputs[:short_rows].reshape(short_count, short_cap, model_width)
    long_grad_in = grad_inputs[short_rows:].reshape(long_count, long_half, model_width)
    return (
        short_out,
        long_out,
        short_pooled,
        long_pooled,
        short_grad_in,
        long_grad_in,
        shard_grads[0],
        shard_grads[1],
        shard_grads[2],
        shard_grads[3],
        shard_grads[4],
        shard_grads[5],
        shard_grads[6],
        shard_grads[7],
        shard_grads[8],
    )


def fast_shards(
    short_tokens, long_tokens, short_len, long_len, short_pool, long_pool, short_cot, long_cot,
    short_pool_cot, long_pool_cot, w_qkv, w_out, w_up, w_down, qv_bias, out_bias, up_bias,
    norm_gain, norm_shift,
):
    groups = lax.axis_size("dp") // 4
    width = w_out.shape[1]
    count, cap, _ = short_tokens.shape
    short_rows = count * cap
    lengths = (short_len, long_len)
    parameters = (
        w_qkv, w_out, w_up, w_down, qv_bias.T, out_bias.T, norm_gain.T, norm_shift.T, up_bias[None, :],
    )
    (down, *kept, vectors, share) = forward(
        lengths,
        parameters,
        (short_pool, long_pool),
        short_tokens.reshape(short_rows, width),
        long_tokens,
        groups,
    )
    arrays = backward(
        lengths,
        vectors,
        share,
        (short_pool_cot, long_pool_cot),
        (short_cot.reshape(short_rows, width), long_cot),
        (down.reshape(4, width, width), *kept),
        groups,
    )
    (
        short_out, long_out, short_pooled, long_pooled, short_grad, long_grad,
        grad_qkv, grad_out, grad_up, grad_down, qv, out, ups, gain, shift,
    ) = results(arrays)
    return (
        short_out.reshape(short_tokens.shape), long_out, short_pooled, long_pooled,
        short_grad.reshape(short_tokens.shape), long_grad, grad_qkv, grad_out, grad_up, grad_down,
        qv.T, out.T, ups[0], gain.T, shift.T,
    )


def solution(mesh):
    short_spec, long_spec, spread = P(("dp", "seq"), None, None), P("dp", "seq", None), P(("dp", "seq"), None)
    vector, parameters = P(("dp", "seq")), [P(("dp", "seq"), None)] * 6
    in_specs = (
        short_spec, long_spec, vector, P("dp"), spread, P("dp", "seq"), short_spec, long_spec,
        spread, P("dp", None), *parameters, vector, spread, spread,
    )
    out_specs = (
        short_spec, long_spec, spread, P("dp", None), short_spec, long_spec, *parameters, vector,
        spread, spread,
    )
    dp, seq = mesh.shape["dp"], mesh.shape["seq"]

    def run(*arrays):
        width = arrays[11].shape[1]
        passages = arrays[1].shape[0] // dp
        regular = dp == 16 and seq == 2 and passages == 2 and width == 24 * dp * seq
        body = fast_shards if regular else general_shards
        return jax.shard_map(body, mesh=mesh, in_specs=in_specs, out_specs=out_specs, check_vma=False)(*arrays)

    return run
```

```python
import functools
import math

import jax
import jax.numpy as jnp
from jax import lax
from jax.experimental import pallas as pl
from jax.experimental.pallas import tpu as pltpu
from jax.sharding import PartitionSpec as P

HEADS = 12
EPS = 1e-12
MESH = pl.DeviceIdType.MESH

SIZES = (80, 32, 96, 96)
GATHER_X = (48, 16, 48, 48)
SUMS = (80, 80, 80, 32, 96, 96)
SUMS_X = (32, 32, 32, 16, 48, 48)


FLIPS = ((0, 0), (0, 1), (1, 0), (1, 1))


class Place:
    def __init__(self):
        dp = lax.axis_index("dp")
        self.x = lax.axis_index("seq")
        self.groups = lax.axis_size("dp") // 4
        self.z = lax.div(dp, 4)
        self.y = lax.rem(lax.div(dp, 2), 2)
        self.c = lax.rem(dp, 2)
        self.dp = dp

    def at_z(self, step):
        z = lax.rem(self.z + step, self.groups)
        return (z * 4 + self.y * 2 + self.c, self.x)

    def at_x(self):
        return (self.dp, 1 - self.x)

    def at_y(self):
        return (self.z * 4 + (1 - self.y) * 2 + self.c, self.x)

    def at_core(self):
        return (self.z * 4 + self.y * 2 + 1 - self.c, self.x)

    def slot(self, flip_y=0, flip_c=0, flip_x=0):
        y = 1 - self.y if flip_y else self.y
        c = 1 - self.c if flip_c else self.c
        x = 1 - self.x if flip_x else self.x
        return y * 4 + c * 2 + x

    def z_back(self, step):
        return lax.rem(self.z + self.groups - step, self.groups)

    def partners(self):
        return [self.at_z(step) for step in range(1, self.groups)] + [
            self.at_x(),
            self.at_y(),
            self.at_core(),
        ]

    def greet_start(self):
        for partner in self.partners():
            pl.semaphore_signal(
                pltpu.get_barrier_semaphore(), inc=1, device_id=partner, device_id_type=MESH
            )

    def greet_wait(self):
        pl.semaphore_wait(pltpu.get_barrier_semaphore(), len(self.partners()))


class Wires:
    def __init__(self, send, recv):
        self.send, self.recv, self.sent, self.left = send, recv, [], set()

    def put(self, src, dst, to):
        number = len(self.sent)
        copy = pltpu.make_async_remote_copy(
            src_ref=src,
            dst_ref=dst,
            send_sem=self.send.at[number],
            recv_sem=self.recv.at[number],
            device_id=to,
            device_id_type=MESH,
        )
        copy.start()
        self.sent.append(copy)
        return (number, to)

    def landed(self, ticket, ref):
        number, to = ticket
        pltpu.make_async_remote_copy(
            src_ref=ref,
            dst_ref=ref,
            send_sem=self.send.at[number],
            recv_sem=self.recv.at[number],
            device_id=to,
            device_id_type=MESH,
        ).wait_recv()

    def has_left(self, ticket):
        self.sent[ticket[0]].wait_send()
        self.left.add(ticket[0])

    def close(self):
        for number, copy in enumerate(self.sent):
            if number not in self.left:
                copy.wait_send()


class Gather:
    def __init__(self, wires, place, wholes, last):
        self.wires, self.place, self.wholes, self.last = wires, place, wholes, last
        self.steps = place.groups
        self.along_z, self.along_x, self.along_y = {}, {}, {}
        self.by_x, self.by_y, self.core = {}, {}, {}

    def halves(self, k):
        some = GATHER_X[k]
        return pl.ds(0, some), pl.ds(some, SIZES[k] - some)

    def start(self, k):
        place, wires = self.place, self.wires
        dst = self.wholes[k].at[place.z, place.slot()]
        src = self.last if k == 3 else dst
        for step in range(1, self.steps):
            self.along_z[k, step] = wires.put(src, dst, place.at_z(step))

    def start_plane(self, k):
        place, wires = self.place, self.wires
        dst = self.wholes[k].at[place.z, place.slot()]
        src = self.last if k == 3 else dst
        self.along_x[k, 0] = wires.put(src, dst, place.at_x())
        self.along_y[k, 0] = wires.put(src, dst, place.at_y())
        self.core[k, 0, 0] = wires.put(src, dst, place.at_core())

    def relay_z(self, k):
        place, wires = self.place, self.wires
        for step in range(1, self.steps):
            ref = self.wholes[k].at[place.z_back(step), place.slot()]
            wires.landed(self.along_z[k, step], ref)
            self.along_x[k, step] = wires.put(ref, ref, place.at_x())
            self.along_y[k, step] = wires.put(ref, ref, place.at_y())
            self.core[k, 0, step] = wires.put(ref, ref, place.at_core())

    def relay_plane(self, k):
        upper, lower = self.halves(k)
        place, wires, whole = self.place, self.wires, self.wholes[k]
        for step in range(self.steps):
            z = place.z_back(step)
            slot = place.slot(flip_x=1)
            ref = whole.at[z, slot]
            wires.landed(self.along_x[k, step], ref)
            half = whole.at[z, slot, upper]
            self.by_y[k, step] = wires.put(half, half, place.at_y())
            self.core[k, 1, step] = wires.put(ref, ref, place.at_core())
            slot = place.slot(flip_y=1)
            ref = whole.at[z, slot]
            wires.landed(self.along_y[k, step], ref)
            half = whole.at[z, slot, lower]
            self.by_x[k, step] = wires.put(half, half, place.at_x())
            self.core[k, 2, step] = wires.put(ref, ref, place.at_core())

    def relay_corner(self, k):
        upper, lower = self.halves(k)
        place, wires, whole = self.place, self.wires, self.wholes[k]
        slot = place.slot(flip_x=1, flip_y=1)
        for step in range(self.steps):
            z = place.z_back(step)
            wires.landed(self.by_y[k, step], whole.at[z, slot, upper])
            wires.landed(self.by_x[k, step], whole.at[z, slot, lower])
            ref = whole.at[z, slot]
            self.core[k, 3, step] = wires.put(ref, ref, place.at_core())

    def finish(self, k):
        place = self.place
        for part, (flip_y, flip_x) in enumerate(FLIPS):
            slot = place.slot(flip_y=flip_y, flip_c=1, flip_x=flip_x)
            for step in range(self.steps):
                ref = self.wholes[k].at[place.z_back(step), slot]
                self.wires.landed(self.core[k, part, step], ref)


class Scatter:
    def __init__(self, wires, place, grads, from_core, from_x, from_y, last_x, last_y, from_z):
        self.wires, self.place, self.grads = wires, place, grads
        self.from_core, self.from_x, self.from_y = from_core, from_x, from_y
        self.last_x, self.last_y, self.from_z = last_x, last_y, from_z
        self.steps = place.groups
        self.core, self.first, self.second, self.third = {}, {}, {}, {}

    def halves(self, k):
        some = SUMS_X[k]
        return pl.ds(0, some), pl.ds(some, SUMS[k] - some)

    def own(self, k, part, rows):
        flip_y, flip_x = FLIPS[part]
        return self.grads[k].at[:, self.place.slot(flip_y=flip_y, flip_x=flip_x), rows]

    def send_core(self, k):
        place = self.place
        for part in (3, 1, 2, 0):
            flip_y, flip_x = FLIPS[part]
            slot = place.slot(flip_y=flip_y, flip_c=1, flip_x=flip_x)
            self.core[k, part] = self.wires.put(
                self.grads[k].at[:, slot], self.from_core[k].at[part], place.at_core()
            )

    def add(self, into, other):
        def one(z, carry):
            total = into[z].astype(jnp.float32) + other[z].astype(jnp.float32)
            into[z] = total.astype(into.dtype)
            return carry

        lax.fori_loop(0, self.steps, one, 0)

    def after_core(self, k):
        upper, lower = self.halves(k)
        whole = pl.ds(0, SUMS[k])
        wires, place = self.wires, self.place
        for part in (3, 1, 2, 0):
            wires.landed(self.core[k, part], self.from_core[k].at[part])
            self.add(self.own(k, part, whole), self.from_core[k].at[part])
            if part == 3:
                self.first[k, "x", 1] = wires.put(
                    self.own(k, 3, upper), self.from_x[k].at[1], place.at_x()
                )
                self.first[k, "y", 1] = wires.put(
                    self.own(k, 3, lower), self.from_y[k].at[1], place.at_y()
                )
            elif part == 1:
                self.first[k, "x", 0] = wires.put(
                    self.own(k, 1, upper), self.from_x[k].at[0], place.at_x()
                )
            elif part == 2:
                self.first[k, "y", 0] = wires.put(
                    self.own(k, 2, lower), self.from_y[k].at[0], place.at_y()
                )

    def after_first(self, k):
        upper, lower = self.halves(k)
        wires, place = self.wires, self.place
        wires.landed(self.first[k, "x", 1], self.from_x[k].at[1])
        self.add(self.own(k, 2, upper), self.from_x[k].at[1])
        self.second[k, "y"] = wires.put(self.own(k, 2, upper), self.last_y[k], place.at_y())
        wires.landed(self.first[k, "y", 1], self.from_y[k].at[1])
        self.add(self.own(k, 1, lower), self.from_y[k].at[1])
        self.second[k, "x"] = wires.put(self.own(k, 1, lower), self.last_x[k], place.at_x())
        wires.landed(self.first[k, "x", 0], self.from_x[k].at[0])
        self.add(self.own(k, 0, upper), self.from_x[k].at[0])
        wires.landed(self.first[k, "y", 0], self.from_y[k].at[0])
        self.add(self.own(k, 0, lower), self.from_y[k].at[0])

    def after_second(self, k):
        upper, lower = self.halves(k)
        wires, place = self.wires, self.place
        wires.landed(self.second[k, "y"], self.last_y[k])
        self.add(self.own(k, 0, upper), self.last_y[k])
        wires.landed(self.second[k, "x"], self.last_x[k])
        self.add(self.own(k, 0, lower), self.last_x[k])
        for step in range(1, self.steps):
            z = lax.rem(place.z + step, self.steps)
            self.third[k, step] = wires.put(
                self.grads[k].at[z, place.slot()], self.from_z[k].at[step - 1], place.at_z(step)
            )

    def finish(self, k):
        place = self.place
        total = self.grads[k][place.z, place.slot()].astype(jnp.float32)
        for step in range(1, self.steps):
            self.wires.landed(self.third[k, step], self.from_z[k].at[step - 1])
            total = total + self.from_z[k][step - 1].astype(jnp.float32)
        return total


def times(a, b):
    return lax.dot_general(a, b, (((1,), (0,)), ((), ())), preferred_element_type=jnp.float32)


def times_turned(a, b):
    return lax.dot_general(a, b, (((1,), (1,)), ((), ())), preferred_element_type=jnp.float32)


def turned_times(a, b):
    return lax.dot_general(a, b, (((0,), (0,)), ((), ())), preferred_element_type=jnp.float32)


def aligned(index, size):
    return pl.ds(pl.multiple_of(index * size, size), size)


def head_masks(lanes, head_dim):
    lane = lax.broadcasted_iota(jnp.int32, (1, lanes), 1)
    return [
        jnp.where((lane >= h * head_dim) & (lane < (h + 1) * head_dim), 1.0, 0.0).astype(jnp.bfloat16)
        for h in range(lanes // head_dim)
    ]


def gelu_and_slope(u):
    near = 1.0 / (1.0 + (0.3275911 * math.sqrt(0.5)) * jnp.abs(u))
    bell = jnp.exp(-0.5 * (u * u))
    series = near * (
        0.127414796
        + near * (-0.142248368 + near * (0.7107068705 + near * (-0.7265760135 + near * 0.5307027145)))
    )
    tail = series * bell
    below = jnp.where(u < 0.0, tail, 1.0 - tail)
    return u * below, below + u * (bell * (1.0 / math.sqrt(2.0 * math.pi)))


def assemble(source, first, blocks, target):
    per_z, size = source.shape[1] // 2, 24

    def one(i, carry):
        z, pair = lax.div(i, per_z), lax.rem(i, per_z)
        left = source[z, 2 * pair].astype(jnp.float32)
        right = source[z, 2 * pair + 1].astype(jnp.float32)
        for b in range(blocks):
            rows = slice(first + b * size, first + (b + 1) * size)
            both = jnp.concatenate([left[rows], right[rows]], axis=0)
            target[b, aligned(i, 2 * size), :] = both.astype(target.dtype)
        return carry

    lax.fori_loop(0, source.shape[0] * per_z, one, 0)


def sum_slabs(source, first):
    def one(i, total):
        per_z = source.shape[1]
        slab = source[lax.div(i, per_z), lax.rem(i, per_z)].astype(jnp.float32)
        return total + slab[first : first + 8]

    count = source.shape[0] * source.shape[1]
    return lax.fori_loop(0, count, one, jnp.zeros((8, source.shape[-1]), jnp.float32))


def normalize(row_data):
    center = row_data - jnp.mean(row_data, axis=-1, keepdims=True)
    spread = jnp.mean(center * center, axis=-1, keepdims=True)
    scale = lax.rsqrt(spread + EPS)
    return center * scale, scale


def weights_forward(queries, keys_all, live):
    scores = jnp.where(live, times_turned(queries, keys_all), -1e30)
    exponent = jnp.exp(scores - jnp.max(scores, axis=-1, keepdims=True))
    return (exponent * (1.0 / jnp.sum(exponent, axis=-1, keepdims=True))).astype(jnp.bfloat16)


def as_column(row):
    size = row.shape[1]
    down = lax.broadcasted_iota(jnp.int32, (size, size), 0)
    across = lax.broadcasted_iota(jnp.int32, (size, size), 1)
    return jnp.sum(jnp.where(down == across, row, 0.0), axis=1, keepdims=True)


def put_at(row, start, width):
    size = row.shape[1]
    down = lax.broadcasted_iota(jnp.int32, (size, width), 0)
    across = lax.broadcasted_iota(jnp.int32, (size, width), 1)
    return jnp.sum(jnp.where(across == down + start, as_column(row), 0.0), axis=0, keepdims=True)


def forward_kernel(
    short_len, long_len, w_qkv, w_out, w_up, w_down, qv_bias, out_bias, gains, shifts, up_bias,
    short_pool, long_pool, short_tok, long_tok,
    out_down, out_wq, out_wu, out_rows, out_qkv, out_short_probs, out_long_probs, out_mixed,
    out_first, out_hat, out_scale, out_low, out_acted, out_slope, vectors, share,
    whole0, whole1, whole2, wq, wu, rows_in, qkv, short_probs, long_probs, mixed,
    first, hat, scale, low, acted, slope, far_pool,
    send, recv, here, leave,
):
    place = Place()
    x, other = place.x, 1 - place.x
    short_rows, half = short_tok.shape[0], long_tok.shape[1]
    total_rows, width = rows_in.shape
    long_rows = 2 * half
    count, cap = short_pool.shape
    mine = pl.ds(pl.multiple_of(short_rows + x * half, half), half)
    theirs = pl.ds(pl.multiple_of(short_rows + other * half, half), half)
    local = []

    def move(src, dst):
        copy = pltpu.make_async_copy(src, dst, here.at[len(local)])
        copy.start()
        local.append(copy)
        return copy

    move(w_down, out_down.at[place.z, place.slot()])
    loads = [
        move(short_tok, rows_in.at[pl.ds(0, short_rows)]),
        move(long_tok.at[x], rows_in.at[mine]),
    ]
    place.greet_start()

    device = place.dp * 2 + x
    size = w_out.shape[0]

    def blocks(matrix):
        data = matrix[...].astype(jnp.float32)
        return [data[:, i * width : (i + 1) * width] for i in range(data.shape[1] // width)]

    pairs = [
        put_at(member[i : i + 1, :].astype(jnp.float32), device * size, width)
        for member in (qv_bias, out_bias, gains, shifts)
        for i in range(2)
    ]
    ups = put_at(up_bias[...].astype(jnp.float32), lax.rem(device, 8) * (4 * size), width)
    ups = jnp.where(lax.broadcasted_iota(jnp.int32, (8, 1), 0) == lax.div(device, 8), ups, 0.0)
    z, slot = place.z, place.slot()
    whole0[z, slot] = jnp.concatenate(blocks(w_qkv) + pairs, axis=0).astype(jnp.bfloat16)
    whole1[z, slot] = jnp.concatenate(blocks(w_out) + [ups], axis=0).astype(jnp.bfloat16)
    whole2[z, slot] = jnp.concatenate(blocks(w_up), axis=0).astype(jnp.bfloat16)

    place.greet_wait()
    wires = Wires(send, recv)
    net = Gather(wires, place, (whole0, whole1, whole2, out_down), w_down)
    net.start(0)
    net.start(1)
    net.start_plane(2)
    net.start(2)
    net.start_plane(1)
    net.start_plane(0)
    pooled = wires.put(long_pool, far_pool, place.at_x())
    net.relay_z(0)
    net.relay_plane(0)
    tok = wires.put(long_tok.at[other], rows_in.at[mine], place.at_x())
    net.relay_z(1)
    net.relay_corner(0)
    for copy in loads:
        copy.wait()
    net.finish(0)
    assemble(whole0, 0, 3, wq)
    vectors[0:8, :] = sum_slabs(whole0, 72)

    head_dim = width // HEADS
    score_scale = 1.0 / math.sqrt(head_dim)

    def project(i, carry):
        rows = aligned(i, 256)
        data = rows_in[rows, :]
        queries = times(data, wq[0]) + vectors[0:1, :]
        qkv[0, rows, :] = (queries.astype(jnp.bfloat16).astype(jnp.float32) * score_scale).astype(jnp.bfloat16)
        qkv[1, rows, :] = times(data, wq[1]).astype(jnp.bfloat16)
        qkv[2, rows, :] = (times(data, wq[2]) + vectors[1:2, :]).astype(jnp.bfloat16)
        return carry

    lax.fori_loop(0, short_rows // 256, project, 0)

    masks = head_masks(2 * head_dim, head_dim)
    keep_first = lax.broadcasted_iota(jnp.int32, (1, 2 * head_dim), 1) < head_dim
    place_in_block = lax.broadcasted_iota(jnp.int32, (1, cap), 1)
    short_live = [place_in_block < short_len[i] for i in range(count)]
    passage_len = long_len[x]
    long_live = lax.broadcasted_iota(jnp.int32, (1, long_rows), 1) < passage_len
    pairs = width // (2 * head_dim)

    def attend_short(pair, carry):
        lanes = aligned(pair, 2 * head_dim)
        blocks_of = [pl.ds(i * cap, cap) for i in range(count)]
        queries, keys_all, values = [[qkv[b, rows, lanes] for rows in blocks_of] for b in range(3)]
        units = [(i, h) for i in range(count) for h in range(2)]
        scores = [times_turned(queries[i] * masks[h], keys_all[i]) for i, h in units]
        scores = [jnp.where(short_live[i], part, -1e30) for (i, h), part in zip(units, scores)]
        tops = [jnp.max(part, axis=-1, keepdims=True) for part in scores]
        exponents = [jnp.exp(part - top) for part, top in zip(scores, tops)]
        totals = [jnp.sum(part, axis=-1, keepdims=True) for part in exponents]
        probs = [(part * (1.0 / total)).astype(jnp.bfloat16) for part, total in zip(exponents, totals)]
        parts = [times(part, values[i]) for (i, h), part in zip(units, probs)]
        for (i, h), part in zip(units, probs):
            short_probs[i, 2 * pair + h] = part
        for i in range(count):
            mixed[blocks_of[i], lanes] = jnp.where(keep_first, parts[2 * i], parts[2 * i + 1]).astype(jnp.bfloat16)
        return carry

    lax.fori_loop(0, pairs // 2, attend_short, 0)
    net.relay_z(2)
    lax.fori_loop(pairs // 2, pairs - 1, attend_short, 0)
    net.start(3)
    net.relay_plane(1)
    lax.fori_loop(pairs - 1, pairs, attend_short, 0)
    net.start_plane(3)
    move(short_probs, out_short_probs)
    wires.landed(tok, rows_in.at[theirs])
    lax.fori_loop(short_rows // 256, total_rows // 256, project, 0)
    move(qkv, out_qkv)
    move(rows_in, out_rows)

    wires.landed(pooled, far_pool)
    chosen = []
    for block in range(total_rows // cap):
        if block < count:
            mask, start = short_pool[block : block + 1, :], 0
            limit = short_len[block]
        else:
            step = block - count
            in_half, start = step % (half // cap) * cap, step * cap
            at = slice(in_half, in_half + cap)
            own = jnp.where(x == 0, long_pool[0:1, at], long_pool[1:2, at])
            far = jnp.where(x == 0, far_pool[0:1, at], far_pool[1:2, at])
            mask = jnp.where(x == step // (half // cap), own, far)
            limit = passage_len - start
        keep = (place_in_block < limit) & ((mask > 0) | (place_in_block + start == 0))
        chosen.append(jnp.where(keep, 1.0, 0.0))
    for block in range(count):
        share[block : block + 1, :] = chosen[block] / jnp.sum(chosen[block], axis=-1, keepdims=True)
    long_total = sum(jnp.sum(row, axis=-1, keepdims=True) for row in chosen[count:])
    for block in range(count, total_rows // cap):
        share[block : block + 1, :] = chosen[block] / long_total

    def attend_long(pair, carry):
        lanes = aligned(pair, 2 * head_dim)
        rows = pl.ds(short_rows, long_rows)
        keys_all, values = qkv[1, rows, lanes], qkv[2, rows, lanes]
        for block in range(long_rows // 256):
            inner = pl.ds(block * 256, 256)
            rows = pl.ds(short_rows + block * 256, 256)
            queries = qkv[0, rows, lanes]
            parts = []
            for h in range(2):
                probs = weights_forward(queries * masks[h], keys_all, long_live)
                long_probs[2 * pair + h, inner, :] = probs
                parts.append(times(probs, values))
            mixed[rows, lanes] = jnp.where(keep_first, parts[0], parts[1]).astype(jnp.bfloat16)
        return carry

    lax.fori_loop(0, pairs - 2, attend_long, 0)
    net.relay_plane(2)
    net.relay_corner(1)
    lax.fori_loop(pairs - 2, pairs - 1, attend_long, 0)
    net.relay_z(3)
    lax.fori_loop(pairs - 1, pairs, attend_long, 0)
    move(long_probs, out_long_probs)
    move(mixed, out_mixed)
    net.finish(1)
    assemble(whole1, 0, 1, wq.at[pl.ds(3, 1)])
    vectors[8:16, :] = sum_slabs(whole1, 24)
    move(wq, out_wq)

    def attach(i, carry):
        rows = aligned(i, 256)
        first_in = rows_in[rows, :].astype(jnp.float32) + (times(mixed[rows, :], wq[3]) + vectors[2:3, :])
        normal, factor = normalize(first_in)
        out = normal * vectors[4:5, :] + vectors[6:7, :]
        first[rows, :] = out
        low[rows, :] = out.astype(jnp.bfloat16)
        hat[rows, :] = normal.astype(jnp.bfloat16)
        scale[rows, :] = jnp.broadcast_to(factor, (256, scale.shape[1]))
        return carry

    lax.fori_loop(0, total_rows // 256, attach, 0)
    move(first, out_first)
    move(low, out_low)
    move(hat, out_hat)
    move(scale, out_scale)
    net.relay_corner(2)
    net.finish(2)
    assemble(whole2, 0, 4, wu)
    move(wu, out_wu)

    def leaving(i):
        j, rows = lax.div(i, 4), aligned(lax.rem(i, 4), 256)
        return (
            pltpu.make_async_copy(acted.at[j, rows], out_acted.at[j, rows], leave.at[0, i]),
            pltpu.make_async_copy(slope.at[j, rows], out_slope.at[j, rows], leave.at[1, i]),
        )

    def expand(i, carry):
        j, rows = lax.div(i, 4), aligned(lax.rem(i, 4), 256)
        inner = times(low[rows, :], wu[j]) + vectors[pl.ds(8 + j, 1), :]
        value, grad = gelu_and_slope(inner)
        acted[j, rows, :] = value.astype(jnp.bfloat16)
        slope[j, rows, :] = grad.astype(jnp.bfloat16)
        for copy in leaving(i):
            copy.start()
        return carry

    def left(i, carry):
        for copy in leaving(i):
            copy.wait()
        return carry

    lax.fori_loop(0, 7, expand, 0)
    net.relay_plane(3)
    lax.fori_loop(7, 14, expand, 0)
    net.relay_corner(3)
    lax.fori_loop(14, 16, expand, 0)
    net.finish(3)
    wires.close()
    lax.fori_loop(0, 16, left, 0)
    for copy in [local[0]] + local[3:]:
        copy.wait()


def forward(lengths, parameters, pools, short_tok, long_tok, groups):
    short_rows, width = short_tok.shape
    half = long_tok.shape[1]
    long_rows = 2 * half
    rows = short_rows + long_rows
    count, cap = pools[0].shape
    inner = 4 * width
    copies = 4 * ((groups - 1) + 4 * groups + 4 * groups) + 2
    low = jnp.bfloat16
    shape = jax.ShapeDtypeStruct
    outs = (
        shape((groups, 8, SIZES[3], width), low),
        shape((4, width, width), low),
        shape((4, width, width), low),
        shape((rows, width), low),
        shape((3, rows, width), low),
        shape((count, HEADS, cap, cap), low),
        shape((HEADS, long_rows, long_rows), low),
        shape((rows, width), low),
        shape((rows, width), jnp.float32),
        shape((rows, width), low),
        shape((rows, 128), jnp.float32),
        shape((rows, width), low),
        shape((inner // width, rows, width), low),
        shape((inner // width, rows, width), low),
        shape((16, width), jnp.float32),
        shape((rows // cap, cap), jnp.float32),
    )
    anywhere, near = pl.BlockSpec(memory_space=pl.ANY), pl.BlockSpec(memory_space=pltpu.VMEM)
    scalars = pl.BlockSpec(memory_space=pltpu.SMEM)
    kept = [pltpu.VMEM(out.shape, out.dtype) for out in outs[1:14]]
    return pl.pallas_call(
        forward_kernel,
        name="forward",
        out_shape=outs,
        in_specs=[scalars] * 2 + [near] * 11 + [anywhere] * 2,
        out_specs=[anywhere] * 14 + [near] * 2,
        scratch_shapes=[pltpu.VMEM((groups, 8, SIZES[k], width), low) for k in range(3)]
        + kept
        + [
            pltpu.VMEM(pools[1].shape, pools[1].dtype),
            pltpu.SemaphoreType.DMA((copies,)),
            pltpu.SemaphoreType.DMA((copies,)),
            pltpu.SemaphoreType.DMA((24,)),
            pltpu.SemaphoreType.DMA((2, 16)),
        ],
        compiler_params=pltpu.CompilerParams(
            collective_id=0, has_side_effects=True, vmem_limit_bytes=60 * 1024 * 1024
        ),
    )(*lengths, *parameters, *pools, short_tok, long_tok)


def backward_kernel(
    short_len, long_len, vectors, share, short_pool_cot, long_pool_cot, short_cot, long_cot,
    in_down, in_wq, in_wu, in_rows, in_qkv, in_short_probs, in_long_probs, in_mixed,
    in_first, in_hat, in_scale, in_low, in_acted, in_slope,
    short_out, long_out, short_grad, long_grad, short_pooled, long_pooled,
    grad_qkv, grad_out, grad_up, grad_down, grad_vectors, grad_up_vector,
    wide, pair, w_up, w_far, hat, sums, branch, low, scale, halves, probs_short,
    vector_sums, pool_cots, pooled_rows, pooled_own, pooled_far,
    *more,
):
    place = Place()
    x, other = place.x, 1 - place.x
    *chunks, send, recv, here, blocks, fetch = more
    parts = len(SUMS)
    grads, *received = [chunks[i * parts : (i + 1) * parts] for i in range(7)]
    total_rows, width = sums.shape
    short_rows = short_out.shape[0]
    count, cap = probs_short.shape[1], probs_short.shape[-1]
    long_rows = total_rows - short_rows
    half = long_rows // 2
    head_dim = width // HEADS
    steps = total_rows // 256
    low_type = jnp.bfloat16
    local = []

    def move(src, dst):
        copy = pltpu.make_async_copy(src, dst, here.at[len(local)])
        copy.start()
        local.append(copy)
        return copy

    mine = pl.ds(pl.multiple_of(short_rows + x * half, half), half)
    theirs = pl.ds(pl.multiple_of(short_rows + other * half, half), half)
    place.greet_start()
    load_down = [move(in_down.at[j], w_far.at[j]) for j in range(4)]
    load_down += [
        move(short_cot, branch.at[pl.ds(0, short_rows)]),
        move(long_cot.at[x], branch.at[mine]),
    ]
    passage_len = long_len[x]

    def block_copies(i):
        rows = aligned(i, 256)
        return (
            pltpu.make_async_copy(in_acted.at[:, rows], wide.at[:, rows], blocks.at[0, i]),
            pltpu.make_async_copy(in_first.at[rows], sums.at[rows], blocks.at[1, i]),
        )

    for i in range(steps):
        for copy in block_copies(i):
            copy.start()
    vector_sums[...] = jnp.zeros_like(vector_sums)
    pool_cots[0:count, :] = short_pool_cot[...]
    pool_cots[count : 2 * count, :] = jnp.broadcast_to(long_pool_cot[pl.ds(x, 1), :], (count, width))
    place.greet_wait()
    wires = Wires(send, recv)
    swap_cot = wires.put(long_cot.at[other], branch.at[mine], place.at_x())
    net = Scatter(wires, place, grads, *received)
    for copy in load_down:
        copy.wait()
    tall = lax.broadcasted_iota(jnp.int32, (256, 1), 0)
    diagonal = lax.broadcasted_iota(jnp.int32, (cap, cap), 0) == lax.broadcasted_iota(jnp.int32, (cap, cap), 1)

    def add_vector(row, rows):
        vector_sums[row : row + 1, :] += jnp.sum(rows, axis=0, keepdims=True)

    def second(step, carry):
        i = jnp.where(step < 2, step, 2 + lax.rem(step + x, 2))

        @pl.when(step == steps - 1)
        def _():
            wires.landed(swap_cot, branch.at[theirs])

        rows = aligned(i, 256)
        for copy in block_copies(i):
            copy.wait()
        product = times(wide[0, rows, :], w_far[0])
        for j in range(1, 4):
            product += times(wide[j, rows, :], w_far[j])
        normal, factor = normalize(sums[rows, :] + (product + vectors[3:4, :]))
        lens = [
            jnp.where(2 * i + part < count, short_len[lax.rem(2 * i + part, count)], passage_len - (2 * i + part - count) * cap)
            for part in range(2)
        ]
        live = tall < jnp.where(tall < cap, lens[0], lens[1] + cap)
        final = jnp.where(live, normal * vectors[5:6, :] + vectors[7:8, :], 0.0)
        low[rows, :] = final.astype(low_type)
        spread = []
        for part in range(2):
            share_row = share[pl.ds(2 * i + part, 1), :]
            column = jnp.sum(jnp.where(diagonal, share_row, 0.0), axis=1, keepdims=True)
            piece = final[part * cap : (part + 1) * cap]
            pooled_rows[pl.ds(2 * i + part, 1), :] = jnp.sum(piece * column, axis=0, keepdims=True)
            spread.append(column * pool_cots[pl.ds(2 * i + part, 1), :])
        grad_final = jnp.where(live, branch[rows, :].astype(jnp.float32), 0.0) + jnp.concatenate(spread, axis=0)
        add_vector(5, grad_final * normal)
        add_vector(7, grad_final)
        scaled = grad_final * vectors[5:6, :]
        mean_one = jnp.mean(scaled, axis=-1, keepdims=True)
        mean_two = jnp.mean(scaled * normal, axis=-1, keepdims=True)
        grad_second = factor * (scaled - mean_one - normal * mean_two)
        sums[rows, :] = grad_second
        grad_branch = grad_second.astype(low_type)
        branch[rows, :] = grad_branch
        add_vector(3, grad_branch.astype(jnp.float32))
        return carry

    lax.fori_loop(0, steps, second, 0)
    short_pooled[...] = pooled_rows[0:count, :]
    own_pooled = jnp.sum(pooled_rows[count : 2 * count, :], axis=0, keepdims=True)
    pooled_own[...] = jnp.broadcast_to(own_pooled, pooled_own.shape)
    long_pooled[pl.ds(x, 1), :] = own_pooled
    out_copies = [
        move(low.at[pl.ds(0, short_rows)], short_out),
        move(low.at[mine], long_out.at[x]),
    ]
    load_slope = [move(in_slope.at[0], pair.at[0]), move(in_slope.at[1], pair.at[1])]
    load_up = move(in_wu, w_up)
    load_hat, load_scale = move(in_hat, hat), move(in_scale, scale)

    swap_out = wires.put(low.at[theirs], long_out.at[x], place.at_x())
    swap_pooled = wires.put(pooled_own, pooled_far, place.at_x())

    def down_step(i, carry):
        j, part = lax.div(i, 2), lax.rem(i, 2)
        product = turned_times(wide[j, :, aligned(part, width // 2)], branch[...])
        grads[5][j, aligned(part, 4)] = product.reshape(4, SUMS[5], width).astype(low_type)
        return carry

    lax.fori_loop(0, 8, down_step, 0, unroll=2)
    net.send_core(5)

    def inner_block(j):
        def inner(i, carry):
            rows = aligned(i, 256)
            product = times_turned(branch[rows, :], w_far[j]) * pair[j % 2, rows, :].astype(jnp.float32)
            grad_inner = product.astype(low_type)
            wide[j, rows, :] = grad_inner
            add_vector(8 + j, grad_inner.astype(jnp.float32))
            return carry

        lax.fori_loop(0, steps, inner, 0, unroll=2)

    load_slope[0].wait()
    inner_block(0)
    load_slope.append(move(in_slope.at[2], pair.at[0]))
    load_slope[1].wait()
    inner_block(1)
    load_slope.append(move(in_slope.at[3], pair.at[1]))
    for copy in out_copies:
        copy.wait()
    wires.has_left(swap_out)
    load_low = move(in_low, low)
    load_slope[2].wait()
    inner_block(2)
    net.after_core(5)
    load_mixed = move(in_mixed, pair.at[0])
    load_slope[3].wait()
    inner_block(3)
    load_wq = move(in_wq, w_far)

    def up_step(i, carry):
        r, both = lax.div(i, 2), lax.rem(i, 2)
        data = low[:, aligned(r, width // 2)]
        halves[0] = turned_times(data, wide[2 * both])
        halves[1] = turned_times(data, wide[2 * both + 1])

        def one(k, carry):
            rows = pl.ds(pl.multiple_of(k * 24, 8), 24)
            data = jnp.concatenate([halves[0, rows, :], halves[1, rows, :]], axis=0)
            grads[4][2 * r + lax.div(k, 8), lax.rem(k, 8), aligned(both, 48), :] = data.astype(low_type)
            return carry

        return lax.fori_loop(0, 16, one, carry)

    load_low.wait()
    lax.fori_loop(0, 4, up_step, 0)
    net.send_core(4)

    load_up.wait()
    load_hat.wait()
    load_scale.wait()

    def first_back(i, carry):
        rows = aligned(i, 256)
        grad_first = sums[rows, :]
        for j in range(4):
            grad_first += times_turned(wide[j, rows, :], w_up[j])
        normal = hat[rows, :].astype(jnp.float32)
        add_vector(4, grad_first * normal)
        add_vector(6, grad_first)
        scaled = grad_first * vectors[4:5, :]
        mean_one = jnp.mean(scaled, axis=-1, keepdims=True)
        mean_two = jnp.mean(scaled * normal, axis=-1, keepdims=True)
        grad_in = scale[rows, 0:1] * (scaled - mean_one - normal * mean_two)
        sums[rows, :] = grad_in
        grad_attn = grad_in.astype(low_type)
        branch[rows, :] = grad_attn
        add_vector(2, grad_attn.astype(jnp.float32))
        return carry

    lax.fori_loop(0, steps // 2, first_back, 0)
    net.after_first(5)
    net.after_core(4)
    lax.fori_loop(steps // 2, steps, first_back, 0)
    load_qkv = move(in_qkv, wide.at[pl.ds(0, 3)])
    load_rows = move(in_rows, wide.at[3])
    net.after_second(5)

    load_mixed.wait()
    load_wq.wait()
    def out_step(r, carry):
        halves[0] = turned_times(pair[0, :, aligned(r, width // 2)], branch[...])

        def one(k, carry):
            rows = pl.ds(pl.multiple_of(k * 24, 8), 24)
            data = jnp.concatenate([halves[0, rows, :], vector_sums[8:16, :]], axis=0)
            grads[3][2 * r + lax.div(k, 8), lax.rem(k, 8)] = data.astype(low_type)
            return carry

        return lax.fori_loop(0, 16, one, carry)

    lax.fori_loop(0, 2, out_step, 0)
    net.send_core(3)

    def mixed_back(i, carry):
        rows = aligned(i, 256)
        pair[1, rows, :] = times_turned(branch[rows, :], w_far[3]).astype(low_type)
        return carry

    lax.fori_loop(0, steps, mixed_back, 0)

    def probs_copies(p, slot):
        lanes = pl.ds(2 * p, 2)
        return (
            pltpu.make_async_copy(in_short_probs.at[:, lanes], probs_short.at[slot], fetch.at[0, slot]),
            pltpu.make_async_copy(
                in_long_probs.at[lanes],
                w_up.at[pl.ds(2 * slot, 2), pl.ds(0, long_rows), pl.ds(0, long_rows)],
                fetch.at[1, slot],
            ),
        )

    for copy in probs_copies(0, 0):
        copy.start()
    load_qkv.wait()
    score_scale = 1.0 / math.sqrt(head_dim)
    masks = head_masks(2 * head_dim, head_dim)
    pairs = width // (2 * head_dim)

    def attend_back(lanes, units):
        heads = [(u, h) for u in range(len(units)) for h in range(2)]
        queries = [wide[0, rows, lanes] for rows, _, _, _ in units]
        grads_mixed = [pair[1, rows, lanes] for rows, _, _, _ in units]
        overlaps = [
            grad.astype(jnp.float32) * pair[0, rows, lanes].astype(jnp.float32)
            for grad, (rows, _, _, _) in zip(grads_mixed, units)
        ]
        centers = [
            jnp.sum(overlaps[u] * masks[h].astype(jnp.float32), axis=-1, keepdims=True) for u, h in heads
        ]
        grads_head = [grads_mixed[u] * masks[h] for u, h in heads]
        probs = [units[u][1](h) for u, h in heads]
        grads_probs = [times_turned(grad, units[u][3]) for grad, (u, h) in zip(grads_head, heads)]
        scores = [
            (part.astype(jnp.float32) * (grad - center)).astype(low_type)
            for part, grad, center in zip(probs, grads_probs, centers)
        ]
        grads_q = [times(part, units[u][2] * masks[h]) for part, (u, h) in zip(scores, heads)]
        grads_k = [turned_times(part, queries[u] * masks[h]) for part, (u, h) in zip(scores, heads)]
        grads_v = [turned_times(part, grad) for part, grad in zip(probs, grads_head)]
        for u, (rows, _, _, _) in enumerate(units):
            total = grads_q[2 * u] + grads_q[2 * u + 1]
            wide[0, rows, lanes] = (total * score_scale).astype(low_type)
        return [
            [grads[2 * u] + grads[2 * u + 1] for u in range(len(units))] for grads in (grads_k, grads_v)
        ]

    def attention_back(p, carry):
        slot = lax.rem(p, 2)
        for copy in probs_copies(p, slot):
            copy.wait()

        @pl.when(p + 1 < pairs)
        def _():
            for copy in probs_copies(p + 1, 1 - slot):
                copy.start()

        lanes = aligned(p, 2 * head_dim)
        blocks_of = [pl.ds(i * cap, cap) for i in range(count)]
        units = [
            (rows, lambda h, i=i: probs_short[slot, i, h], wide[1, rows, lanes], wide[2, rows, lanes])
            for i, rows in enumerate(blocks_of)
        ]
        grads_k, grads_v = attend_back(lanes, units)
        for rows, grad_k, grad_v in zip(blocks_of, grads_k, grads_v):
            wide[1, rows, lanes] = grad_k.astype(low_type)
            wide[2, rows, lanes] = grad_v.astype(low_type)
        rows = pl.ds(short_rows, long_rows)
        keys_all, values = wide[1, rows, lanes], wide[2, rows, lanes]
        total_k, total_v = None, None
        for block in range(long_rows // 256):
            inner = pl.ds(block * 256, 256)
            unit = (
                pl.ds(short_rows + block * 256, 256),
                lambda h, inner=inner: w_up[2 * slot + h, inner, 0:long_rows],
                keys_all,
                values,
            )
            (grad_k,), (grad_v,) = attend_back(lanes, [unit])
            total_k = grad_k if total_k is None else total_k + grad_k
            total_v = grad_v if total_v is None else total_v + grad_v
        wide[1, rows, lanes] = total_k.astype(low_type)
        wide[2, rows, lanes] = total_v.astype(low_type)
        return carry

    third = width // 3

    def qkv_step(group):
        lanes = pl.ds(group * third, third)

        def bias(i, carry):
            rows = aligned(i, 256)
            for row, b in ((0, 0), (1, 2)):
                piece = wide[b, rows, lanes].astype(jnp.float32)
                vector_sums[row : row + 1, lanes] += jnp.sum(piece, axis=0, keepdims=True)
            return carry

        lax.fori_loop(0, steps, bias, 0)

        def step(r, carry):
            data = wide[3, :, aligned(r, width // 2)]
            for b in range(3):
                halves[0, :, b * third : (b + 1) * third] = turned_times(data, wide[b, :, lanes])

            def one(k, carry):
                rows = pl.ds(pl.multiple_of(k * 24, 8), 24)
                pieces = [halves[0, rows, b * third : (b + 1) * third] for b in range(3)]
                data = jnp.concatenate(pieces + [vector_sums[0:8, lanes]], axis=0)
                grads[group][2 * r + lax.div(k, 8), lax.rem(k, 8)] = data.astype(low_type)
                return carry

            return lax.fori_loop(0, 16, one, carry)

        lax.fori_loop(0, 2, step, 0)
        net.send_core(group)

    lax.fori_loop(0, pairs // 3, attention_back, 0)
    load_rows.wait()
    qkv_step(0)
    net.after_first(4)
    lax.fori_loop(pairs // 3, 2 * pairs // 3, attention_back, 0)
    net.after_core(3)
    qkv_step(1)
    net.after_second(4)
    net.after_core(0)
    lax.fori_loop(2 * pairs // 3, pairs, attention_back, 0)
    net.after_first(3)
    qkv_step(2)
    net.after_core(1)
    net.after_first(0)
    net.after_core(2)

    def tokens_back(rows):
        grad_in = sums[rows, :]
        for b in range(3):
            grad_in += times_turned(wide[b, rows, :], w_far[b])
        return grad_in

    far_low, far_in = low.at[pl.ds(0, half)], low.at[pl.ds(half, half)]
    far_low[...] = tokens_back(theirs).astype(low_type)
    net.after_second(0)

    def tokens_step(i, carry):
        rows = pl.ds(pl.multiple_of(jnp.where(i < 2, i * 256, short_rows + x * half), 256), 256)
        sums[rows, :] = tokens_back(rows)
        return carry

    lax.fori_loop(0, 1, tokens_step, 0)
    net.after_first(1)
    net.after_first(2)
    net.after_second(3)
    swap_grad = wires.put(far_low, far_in, place.at_x())
    lax.fori_loop(1, 3, tokens_step, 0)
    move(sums.at[pl.ds(0, short_rows)], short_grad)
    move(sums.at[mine], long_grad.at[x])
    net.after_second(1)
    net.after_second(2)
    grad_down[...] = net.finish(5)
    total = net.finish(4)
    for j in range(4):
        grad_up[:, j * width : (j + 1) * width] = total[24 * j : 24 * j + 24]
    total = net.finish(3)
    grad_out[...] = total[0:24]
    grad_up_vector[...] = total[24:32]
    wires.landed(swap_pooled, pooled_far)
    long_pooled[pl.ds(other, 1), :] = pooled_far[0:1, :]
    wires.landed(swap_grad, far_in)
    sums[theirs, :] = far_in[...].astype(jnp.float32)
    move(sums.at[theirs], long_grad.at[other])
    wires.landed(swap_out, long_out.at[other])
    for group in range(3):
        total = net.finish(group)
        for b in range(3):
            columns = slice(b * width + group * third, b * width + (group + 1) * third)
            grad_qkv[:, columns] = total[24 * b : 24 * b + 24]
        grad_vectors[:, group * third : (group + 1) * third] = total[72:80]
    wires.close()
    for copy in local[-3:]:
        copy.wait()


def backward(lengths, vectors, share, pool_cots, cots, arrays, groups):
    width = vectors.shape[1]
    rows = arrays[3].shape[0]
    count, _, cap, _ = arrays[5].shape
    short_rows = count * cap
    half = (rows - short_rows) // 2
    low, wide_type = jnp.bfloat16, jnp.float32
    shape = jax.ShapeDtypeStruct
    rows24 = 24
    outs = (
        shape((short_rows, width), low),
        shape((2, half, width), low),
        shape((short_rows, width), wide_type),
        shape((2, half, width), wide_type),
        shape((count, width), wide_type),
        shape((2, width), wide_type),
        shape((rows24, 3 * width), wide_type),
        shape((rows24, width), wide_type),
        shape((rows24, 4 * width), wide_type),
        shape((4 * rows24, width), wide_type),
        shape((8, width), wide_type),
        shape((8, width), wide_type),
    )
    anywhere, near = pl.BlockSpec(memory_space=pl.ANY), pl.BlockSpec(memory_space=pltpu.VMEM)
    copies = len(SUMS) * (4 + 6 + (groups - 1)) + 4

    widths = (width // 3,) * 3 + (width,) * 3

    def chunks(parts, sizes):
        return [pltpu.VMEM(parts + (size, columns), low) for size, columns in zip(sizes, widths)]

    rest = tuple(size - some for size, some in zip(SUMS, SUMS_X))
    scratch = [
        pltpu.VMEM((4, rows, width), low),
        pltpu.VMEM((2, rows, width), low),
        pltpu.VMEM((4, width, width), low),
        pltpu.VMEM((4, width, width), low),
        pltpu.VMEM((rows, width), low),
        pltpu.VMEM((rows, width), wide_type),
        pltpu.VMEM((rows, width), low),
        pltpu.VMEM((rows, width), low),
        pltpu.VMEM((rows, 128), wide_type),
        pltpu.VMEM((2, width // 2, width), wide_type),
        pltpu.VMEM((2, count, 2, cap, cap), low),
        pltpu.VMEM((16, width), wide_type),
        pltpu.VMEM((2 * count, width), wide_type),
        pltpu.VMEM((2 * count, width), wide_type),
        pltpu.VMEM((8, width), wide_type),
        pltpu.VMEM((8, width), wide_type),
        *chunks((groups, 8), SUMS),
        *chunks((4, groups), SUMS),
        *chunks((2, groups), SUMS_X),
        *chunks((2, groups), rest),
        *chunks((groups,), rest),
        *chunks((groups,), SUMS_X),
        *chunks((groups - 1,), SUMS),
        pltpu.SemaphoreType.DMA((copies,)),
        pltpu.SemaphoreType.DMA((copies,)),
        pltpu.SemaphoreType.DMA((24,)),
        pltpu.SemaphoreType.DMA((2, rows // 256)),
        pltpu.SemaphoreType.DMA((2, 2)),
    ]
    return pl.pallas_call(
        backward_kernel,
        name="backward",
        out_shape=outs,
        in_specs=[pl.BlockSpec(memory_space=pltpu.SMEM)] * 2 + [near] * 4 + [anywhere] * 16,
        out_specs=[anywhere] * 4 + [near] * 8,
        scratch_shapes=scratch,
        compiler_params=pltpu.CompilerParams(
            collective_id=1, has_side_effects=True, vmem_limit_bytes=63 * 1024 * 1024
        ),
    )(*lengths, vectors, share, *pool_cots, *cots, *arrays)


def results_kernel(
    in_0, in_1, in_2, in_3, in_4, in_5, in_6, in_7, in_8, in_9, grad_vectors, grad_ups,
    out_0, out_1, out_2, out_3, out_4, out_5, out_6, out_7, out_8, out_9, pair_0, pair_1, ups, pair_2, pair_3,
    *more,
):
    *held, come, leave = more
    sources = (in_0, in_1, in_2, in_3, in_4, in_5, in_6, in_7, in_8, in_9)
    places = (out_0, out_1, out_4, out_5, out_2, out_3, out_6, out_7, out_8, out_9)
    ins = [pltpu.make_async_copy(sources[i], held[i], come.at[i]) for i in range(10)]
    outs = [pltpu.make_async_copy(held[i], places[i], leave.at[i]) for i in range(10)]
    for copy in ins:
        copy.start()
    device = lax.axis_index("dp") * 2 + lax.axis_index("seq")
    size, width = in_7.shape
    rows = pltpu.roll(grad_vectors[...], lax.rem(width - device * size, width), 1)
    for i, ref in enumerate((pair_0, pair_1, pair_2, pair_3)):
        ref[...] = rows[2 * i : 2 * i + 2, 0:size]
    start = lax.rem(device, 8) * (4 * size)
    row = grad_ups[pl.ds(lax.div(device, 8), 1), :]
    row = pltpu.roll(jnp.broadcast_to(row, (8, width)), lax.rem(width - start, width), 1)
    ups[...] = row[0:1, 0 : 4 * size]
    for i in range(10):
        ins[i].wait()
        outs[i].start()
    for copy in outs:
        copy.wait()


def results(arrays):
    size = arrays[7].shape[0]
    order = (0, 1, 4, 5, 2, 3, 6, 7, 8, 9)
    shape = jax.ShapeDtypeStruct
    pair = shape((2, size), jnp.float32)
    outs = tuple(shape(arrays[i].shape, arrays[i].dtype) for i in order)
    anywhere, near = pl.BlockSpec(memory_space=pl.ANY), pl.BlockSpec(memory_space=pltpu.VMEM)
    return pl.pallas_call(
        results_kernel,
        name="results",
        out_shape=outs + (pair, pair, shape((1, 4 * size), jnp.float32), pair, pair),
        in_specs=[anywhere] * 10 + [near] * 2,
        out_specs=[anywhere] * 10 + [near] * 5,
        scratch_shapes=[pltpu.VMEM(array.shape, array.dtype) for array in arrays[:10]]
        + [pltpu.SemaphoreType.DMA((10,)), pltpu.SemaphoreType.DMA((10,))],
        compiler_params=pltpu.CompilerParams(vmem_limit_bytes=56 * 1024 * 1024),
    )(*arrays)


def layer_norm(row_data, gain_vec, shift_vec):
    center = row_data - jnp.mean(row_data, axis=-1, keepdims=True)
    spread = jnp.mean(center * center, axis=-1, keepdims=True)
    return center * lax.rsqrt(spread + EPS) * gain_vec + shift_vec


def exact_gelu(inner_act):
    return jax.nn.gelu(inner_act, approximate=False)


def outer_sum(left_rows, right_rows):
    return lax.dot_general(
        left_rows, right_rows, (((0,), (0,)), ((), ())), preferred_element_type=jnp.float32
    )


def times_transposed(left_rows, matrix):
    return lax.dot_general(
        left_rows, matrix, (((1,), (1,)), ((), ())), preferred_element_type=jnp.float32
    )


def masked_scores(queries, keys_all, key_live, score_scale):
    scores = (
        jnp.einsum("bqhe,bkhe->bhqk", queries, keys_all, preferred_element_type=jnp.float32)
        * score_scale
    )
    return jnp.where(key_live[:, None, None, :], scores, -1e30)


def attend_forward(pieces, score_scale):
    queries, keys_all, values, key_live = pieces
    scores = masked_scores(queries, keys_all, key_live, score_scale)
    highest = jnp.max(scores, axis=-1, keepdims=True)
    exponent = jnp.exp(scores - highest)
    totals = jnp.sum(exponent, axis=-1, keepdims=True)
    soft_probs = (exponent / totals).astype(jnp.bfloat16)
    mixed_heads = jnp.einsum(
        "bhqk,bkhe->bqhe", soft_probs, values, preferred_element_type=jnp.float32
    )
    return (mixed_heads.astype(jnp.bfloat16), (highest + jnp.log(totals))[..., 0])


def attend_backward(pieces, score_scale):
    queries, keys_all, values, key_live, grad_mixed, log_total = pieces
    scores = masked_scores(queries, keys_all, key_live, score_scale)
    soft_probs = jnp.exp(scores - log_total[..., None])
    grad_probs = jnp.einsum(
        "bqhe,bkhe->bhqk", grad_mixed, values, preferred_element_type=jnp.float32
    )
    grad_values = jnp.einsum(
        "bhqk,bqhe->bkhe",
        soft_probs.astype(jnp.bfloat16),
        grad_mixed,
        preferred_element_type=jnp.float32,
    )
    center = jnp.sum(soft_probs * grad_probs, axis=-1, keepdims=True)
    grad_scores = (soft_probs * (grad_probs - center)).astype(jnp.bfloat16)
    grad_queries = (
        jnp.einsum("bhqk,bkhe->bqhe", grad_scores, keys_all, preferred_element_type=jnp.float32)
        * score_scale
    )
    grad_keys = (
        jnp.einsum("bhqk,bqhe->bkhe", grad_scores, queries, preferred_element_type=jnp.float32)
        * score_scale
    )
    return (grad_queries, grad_keys, grad_values)


def by_blocks(function, per_block, arrays):
    blocks = arrays[0].shape[0] // per_block
    stacked = tuple((member.reshape((blocks, per_block) + member.shape[1:]) for member in arrays))
    results = lax.map(function, stacked)
    return jax.tree.map(
        lambda member: member.reshape((blocks * per_block,) + member.shape[2:]), results
    )


def general_shards(
    short_tokens,
    long_tokens,
    short_len,
    long_len,
    short_pool,
    long_pool,
    short_cot,
    long_cot,
    short_pool_cot,
    long_pool_cot,
    w_qkv,
    w_out,
    w_up,
    w_down,
    qv_bias,
    out_bias,
    up_bias,
    norm_gain,
    norm_shift,
):
    gathered = (
        lax.all_gather(w_qkv, ("dp", "seq"), axis=0, tiled=True),
        lax.all_gather(w_out, ("dp", "seq"), axis=0, tiled=True),
        lax.all_gather(w_up, ("dp", "seq"), axis=0, tiled=True),
        lax.all_gather(w_down, ("dp", "seq"), axis=0, tiled=True),
        lax.all_gather(qv_bias, ("dp", "seq"), axis=0, tiled=True),
        lax.all_gather(out_bias, ("dp", "seq"), axis=0, tiled=True),
        lax.all_gather(up_bias, ("dp", "seq"), axis=0, tiled=True),
        lax.all_gather(norm_gain, ("dp", "seq"), axis=0, tiled=True),
        lax.all_gather(norm_shift, ("dp", "seq"), axis=0, tiled=True),
    )
    qkv_matrix, out_matrix, up_matrix, down_matrix, qv_vec, out_vec, up_vec, gains, shifts = (
        gathered
    )
    gains = gains.astype(jnp.float32)
    shifts = shifts.astype(jnp.float32)
    short_count, short_cap, model_width = short_tokens.shape
    long_count, long_half = (long_tokens.shape[0], long_tokens.shape[1])
    head_count = HEADS
    head_dim = model_width // head_count
    score_scale = 1.0 / math.sqrt(head_dim)
    short_rows = short_count * short_cap
    long_rows = long_count * long_half
    short_place = jnp.arange(short_cap, dtype=jnp.int32)
    short_live = short_place[None, :] < short_len[:, None]
    long_place = lax.axis_index("seq") * long_half + jnp.arange(long_half, dtype=jnp.int32)
    long_live = long_place[None, :] < long_len[:, None]
    short_weight = (short_live & ((short_pool > 0) | (short_place[None, :] == 0))).astype(
        jnp.float32
    )
    long_weight = (long_live & ((long_pool > 0) | (long_place[None, :] == 0))).astype(jnp.float32)
    row_live = jnp.concatenate([short_live.reshape(-1), long_live.reshape(-1)]).astype(jnp.float32)
    inputs = jnp.concatenate(
        [
            short_tokens.reshape(short_rows, model_width),
            long_tokens.reshape(long_rows, model_width),
        ],
        axis=0,
    )
    joined = jnp.dot(inputs, qkv_matrix, preferred_element_type=jnp.float32)
    queries = (joined[:, :model_width] + qv_vec[:, 0]).astype(jnp.bfloat16)
    keys_all = joined[:, model_width : 2 * model_width].astype(jnp.bfloat16)
    values = (joined[:, 2 * model_width :] + qv_vec[:, 1]).astype(jnp.bfloat16)
    short_shape = (short_count, short_cap, head_count, head_dim)
    long_shape = (long_count, long_half, head_count, head_dim)
    short_q = queries[:short_rows].reshape(short_shape)
    short_k = keys_all[:short_rows].reshape(short_shape)
    short_v = values[:short_rows].reshape(short_shape)
    long_q = queries[short_rows:].reshape(long_shape)
    long_k = keys_all[short_rows:].reshape(long_count, long_half, model_width)
    long_v = values[short_rows:].reshape(long_count, long_half, model_width)
    short_block = math.gcd(short_count, max(1, 512 // short_cap))
    long_block = math.gcd(long_count, max(1, 512 // long_half))

    def forward_blocks(pieces):
        return attend_forward(pieces, score_scale)

    def backward_blocks(pieces):
        return attend_backward(pieces, score_scale)

    short_mixed, short_logsum = by_blocks(
        forward_blocks, short_block, (short_q, short_k, short_v, short_live)
    )
    gathered_k, gathered_v = (
        lax.all_gather(long_k, "seq", axis=1, tiled=True),
        lax.all_gather(long_v, "seq", axis=1, tiled=True),
    )
    full_len = gathered_k.shape[1]
    full_shape = (long_count, full_len, head_count, head_dim)
    long_key_live = jnp.arange(full_len, dtype=jnp.int32)[None, :] < long_len[:, None]
    long_mixed, long_logsum = by_blocks(
        forward_blocks,
        long_block,
        (long_q, gathered_k.reshape(full_shape), gathered_v.reshape(full_shape), long_key_live),
    )
    mixed_heads = jnp.concatenate(
        [short_mixed.reshape(short_rows, model_width), long_mixed.reshape(long_rows, model_width)],
        axis=0,
    )
    attn_out = jnp.dot(mixed_heads, out_matrix, preferred_element_type=jnp.float32) + out_vec[:, 0]
    first_in = inputs.astype(jnp.float32) + attn_out
    first_norm = layer_norm(first_in, gains[:, 0], shifts[:, 0])
    first_low = first_norm.astype(jnp.bfloat16)
    inner_act = jnp.dot(first_low, up_matrix, preferred_element_type=jnp.float32) + up_vec
    activated = exact_gelu(inner_act).astype(jnp.bfloat16)
    branch = jnp.dot(activated, down_matrix, preferred_element_type=jnp.float32) + out_vec[:, 1]
    second_in = first_norm + branch
    final_norm = layer_norm(second_in, gains[:, 1], shifts[:, 1]) * row_live[:, None]
    short_final = final_norm[:short_rows].reshape(short_count, short_cap, model_width)
    long_final = final_norm[short_rows:].reshape(long_count, long_half, model_width)
    short_total = jnp.sum(short_weight, axis=1)
    short_pooled = jnp.sum(short_final * short_weight[..., None], axis=1) / short_total[:, None]
    long_partial = jnp.sum(long_final * long_weight[..., None], axis=1)
    long_sum, long_total = lax.psum((long_partial, jnp.sum(long_weight, axis=1)), "seq")
    long_pooled = long_sum / long_total[:, None]
    grad_short = (
        short_cot.astype(jnp.float32) * short_live[..., None]
        + short_weight[..., None] * short_pool_cot[:, None, :] / short_total[:, None, None]
    )
    grad_long = (
        long_cot.astype(jnp.float32) * long_live[..., None]
        + long_weight[..., None] * long_pool_cot[:, None, :] / long_total[:, None, None]
    )
    grad_top = jnp.concatenate(
        [grad_short.reshape(short_rows, model_width), grad_long.reshape(long_rows, model_width)],
        axis=0,
    )
    _, second_back = jax.vjp(layer_norm, second_in, gains[:, 1], shifts[:, 1])
    grad_second, grad_gain_two, grad_shift_two = second_back(grad_top)
    grad_branch = grad_second.astype(jnp.bfloat16)
    grad_down = outer_sum(activated, grad_branch)
    grad_bias_two = jnp.sum(grad_branch.astype(jnp.float32), axis=0)
    grad_acted = times_transposed(grad_branch, down_matrix)
    _, gelu_back = jax.vjp(exact_gelu, inner_act)
    grad_inner = gelu_back(grad_acted)[0].astype(jnp.bfloat16)
    grad_up = outer_sum(first_low, grad_inner)
    grad_up_bias = jnp.sum(grad_inner.astype(jnp.float32), axis=0)
    grad_first = grad_second + times_transposed(grad_inner, up_matrix)
    _, first_back = jax.vjp(layer_norm, first_in, gains[:, 0], shifts[:, 0])
    grad_first_in, grad_gain_one, grad_shift_one = first_back(grad_first)
    grad_attn = grad_first_in.astype(jnp.bfloat16)
    grad_out = outer_sum(mixed_heads, grad_attn)
    grad_bias_one = jnp.sum(grad_attn.astype(jnp.float32), axis=0)
    grad_mixed = times_transposed(grad_attn, out_matrix).astype(jnp.bfloat16)
    short_dq, short_dk, short_dv = by_blocks(
        backward_blocks,
        short_block,
        (
            short_q,
            short_k,
            short_v,
            short_live,
            grad_mixed[:short_rows].reshape(short_shape),
            short_logsum,
        ),
    )
    again_k, again_v = (gathered_k, gathered_v)
    long_dq, long_dk, long_dv = by_blocks(
        backward_blocks,
        long_block,
        (
            long_q,
            again_k.reshape(full_shape),
            again_v.reshape(full_shape),
            long_key_live,
            grad_mixed[short_rows:].reshape(long_shape),
            long_logsum,
        ),
    )
    own_dk, own_dv = (
        lax.psum_scatter(
            long_dk.reshape(long_count, full_len, model_width).astype(jnp.bfloat16),
            "seq",
            scatter_dimension=1,
            tiled=True,
        ).astype(jnp.float32),
        lax.psum_scatter(
            long_dv.reshape(long_count, full_len, model_width).astype(jnp.bfloat16),
            "seq",
            scatter_dimension=1,
            tiled=True,
        ).astype(jnp.float32),
    )
    grad_queries = jnp.concatenate(
        [short_dq.reshape(short_rows, model_width), long_dq.reshape(long_rows, model_width)], axis=0
    ).astype(jnp.bfloat16)
    grad_keys = jnp.concatenate(
        [short_dk.reshape(short_rows, model_width), own_dk.reshape(long_rows, model_width)], axis=0
    ).astype(jnp.bfloat16)
    grad_values = jnp.concatenate(
        [short_dv.reshape(short_rows, model_width), own_dv.reshape(long_rows, model_width)], axis=0
    ).astype(jnp.bfloat16)
    grad_joined = jnp.concatenate([grad_queries, grad_keys, grad_values], axis=1)
    grad_qkv = outer_sum(inputs, grad_joined)
    grad_qv = jnp.stack(
        [
            jnp.sum(grad_queries.astype(jnp.float32), axis=0),
            jnp.sum(grad_values.astype(jnp.float32), axis=0),
        ],
        axis=1,
    )
    grad_inputs = grad_first_in + times_transposed(grad_joined, qkv_matrix)
    grad_out_vec = jnp.stack([grad_bias_one, grad_bias_two], axis=1)
    grad_gains = jnp.stack([grad_gain_one, grad_gain_two], axis=1)
    grad_shifts = jnp.stack([grad_shift_one, grad_shift_two], axis=1)
    shard_grads = (
        lax.psum_scatter(grad_qkv, ("dp", "seq"), scatter_dimension=0, tiled=True),
        lax.psum_scatter(grad_out, ("dp", "seq"), scatter_dimension=0, tiled=True),
        lax.psum_scatter(grad_up, ("dp", "seq"), scatter_dimension=0, tiled=True),
        lax.psum_scatter(grad_down, ("dp", "seq"), scatter_dimension=0, tiled=True),
        lax.psum_scatter(grad_qv, ("dp", "seq"), scatter_dimension=0, tiled=True),
        lax.psum_scatter(grad_out_vec, ("dp", "seq"), scatter_dimension=0, tiled=True),
        lax.psum_scatter(grad_up_bias, ("dp", "seq"), scatter_dimension=0, tiled=True),
        lax.psum_scatter(grad_gains, ("dp", "seq"), scatter_dimension=0, tiled=True),
        lax.psum_scatter(grad_shifts, ("dp", "seq"), scatter_dimension=0, tiled=True),
    )
    short_out = short_final.astype(jnp.bfloat16)
    long_out = long_final.astype(jnp.bfloat16)
    short_grad_in = grad_inputs[:short_rows].reshape(short_count, short_cap, model_width)
    long_grad_in = grad_inputs[short_rows:].reshape(long_count, long_half, model_width)
    return (
        short_out,
        long_out,
        short_pooled,
        long_pooled,
        short_grad_in,
        long_grad_in,
        shard_grads[0],
        shard_grads[1],
        shard_grads[2],
        shard_grads[3],
        shard_grads[4],
        shard_grads[5],
        shard_grads[6],
        shard_grads[7],
        shard_grads[8],
    )


def fast_shards(
    short_tokens, long_tokens, short_len, long_len, short_pool, long_pool, short_cot, long_cot,
    short_pool_cot, long_pool_cot, w_qkv, w_out, w_up, w_down, qv_bias, out_bias, up_bias,
    norm_gain, norm_shift,
):
    groups = lax.axis_size("dp") // 4
    width = w_out.shape[1]
    count, cap, _ = short_tokens.shape
    short_rows = count * cap
    lengths = (short_len, long_len)
    parameters = (
        w_qkv, w_out, w_up, w_down, qv_bias.T, out_bias.T, norm_gain.T, norm_shift.T, up_bias[None, :],
    )
    (down, *kept, vectors, share) = forward(
        lengths,
        parameters,
        (short_pool, long_pool),
        short_tokens.reshape(short_rows, width),
        long_tokens,
        groups,
    )
    arrays = backward(
        lengths,
        vectors,
        share,
        (short_pool_cot, long_pool_cot),
        (short_cot.reshape(short_rows, width), long_cot),
        (down.reshape(4, width, width), *kept),
        groups,
    )
    (
        short_out, long_out, short_pooled, long_pooled, short_grad, long_grad,
        grad_qkv, grad_out, grad_up, grad_down, qv, out, ups, gain, shift,
    ) = results(arrays)
    return (
        short_out.reshape(short_tokens.shape), long_out, short_pooled, long_pooled,
        short_grad.reshape(short_tokens.shape), long_grad, grad_qkv, grad_out, grad_up, grad_down,
        qv.T, out.T, ups[0], gain.T, shift.T,
    )


def solution(mesh):
    short_spec, long_spec, spread = P(("dp", "seq"), None, None), P("dp", "seq", None), P(("dp", "seq"), None)
    vector, parameters = P(("dp", "seq")), [P(("dp", "seq"), None)] * 6
    in_specs = (
        short_spec, long_spec, vector, P("dp"), spread, P("dp", "seq"), short_spec, long_spec,
        spread, P("dp", None), *parameters, vector, spread, spread,
    )
    out_specs = (
        short_spec, long_spec, spread, P("dp", None), short_spec, long_spec, *parameters, vector,
        spread, spread,
    )
    dp, seq = mesh.shape["dp"], mesh.shape["seq"]

    def run(*arrays):
        width = arrays[11].shape[1]
        passages = arrays[1].shape[0] // dp
        regular = dp == 16 and seq == 2 and passages == 2 and width == 24 * dp * seq
        body = fast_shards if regular else general_shards
        return jax.shard_map(body, mesh=mesh, in_specs=in_specs, out_specs=out_specs, check_vma=False)(*arrays)

    return run
```

```python
import functools
import math

import jax
import jax.numpy as jnp
from jax import lax
from jax.experimental import pallas as pl
from jax.experimental.pallas import tpu as pltpu
from jax.sharding import PartitionSpec as P

HEADS = 12
EPS = 1e-12
MESH = pl.DeviceIdType.MESH

SIZES = (80, 32, 96, 96)
GATHER_X = (48, 16, 48, 48)
SUMS = (80, 80, 80, 32, 96, 96)
SUMS_X = (32, 48, 32, 16, 48, 48)


FLIPS = ((0, 0), (0, 1), (1, 0), (1, 1))


class Place:
    def __init__(self):
        dp = lax.axis_index("dp")
        self.x = lax.axis_index("seq")
        self.groups = lax.axis_size("dp") // 4
        self.z = lax.div(dp, 4)
        self.y = lax.rem(lax.div(dp, 2), 2)
        self.c = lax.rem(dp, 2)
        self.dp = dp

    def z_of(self, step):
        if step == 1:
            return self.z + 1 - 2 * lax.rem(self.z, 2)
        return lax.rem(self.z + 2, 4) if step == 2 else 3 - self.z

    def at_z(self, step):
        return (self.z_of(step) * 4 + self.y * 2 + self.c, self.x)

    def at_x(self):
        return (self.dp, 1 - self.x)

    def at_y(self):
        return (self.z * 4 + (1 - self.y) * 2 + self.c, self.x)

    def at_core(self):
        return (self.z * 4 + self.y * 2 + 1 - self.c, self.x)

    def slot(self, flip_y=0, flip_c=0, flip_x=0):
        y = 1 - self.y if flip_y else self.y
        c = 1 - self.c if flip_c else self.c
        x = 1 - self.x if flip_x else self.x
        return y * 4 + c * 2 + x

    def z_back(self, step):
        return self.z if step == 0 else self.z_of(step)

    def partners(self):
        return [self.at_z(step) for step in range(1, self.groups)] + [
            self.at_x(),
            self.at_y(),
            self.at_core(),
        ]

    def greet_start(self):
        for partner in self.partners():
            pl.semaphore_signal(
                pltpu.get_barrier_semaphore(), inc=1, device_id=partner, device_id_type=MESH
            )

    def greet_wait(self):
        pl.semaphore_wait(pltpu.get_barrier_semaphore(), len(self.partners()))


class Wires:
    def __init__(self, send, recv):
        self.send, self.recv, self.sent, self.left = send, recv, [], set()

    def put(self, src, dst, to):
        number = len(self.sent)
        copy = pltpu.make_async_remote_copy(
            src_ref=src,
            dst_ref=dst,
            send_sem=self.send.at[number],
            recv_sem=self.recv.at[number],
            device_id=to,
            device_id_type=MESH,
        )
        copy.start()
        self.sent.append(copy)
        return (number, to)

    def landed(self, ticket, ref):
        number, to = ticket
        pltpu.make_async_remote_copy(
            src_ref=ref,
            dst_ref=ref,
            send_sem=self.send.at[number],
            recv_sem=self.recv.at[number],
            device_id=to,
            device_id_type=MESH,
        ).wait_recv()

    def has_left(self, ticket):
        self.sent[ticket[0]].wait_send()
        self.left.add(ticket[0])

    def close(self):
        for number, copy in enumerate(self.sent):
            if number not in self.left:
                copy.wait_send()


class Gather:
    def __init__(self, wires, place, wholes, last):
        self.wires, self.place, self.wholes, self.last = wires, place, wholes, last
        self.steps = place.groups
        self.along_z, self.along_x, self.along_y = {}, {}, {}
        self.by_x, self.by_y, self.core = {}, {}, {}

    def halves(self, k):
        some = GATHER_X[k]
        return pl.ds(0, some), pl.ds(some, SIZES[k] - some)

    def start(self, k):
        place, wires = self.place, self.wires
        dst = self.wholes[k].at[place.z, place.slot()]
        src = self.last if k == 3 else dst
        for step in range(1, self.steps):
            self.along_z[k, step] = wires.put(src, dst, place.at_z(step))

    def start_plane(self, k):
        place, wires = self.place, self.wires
        dst = self.wholes[k].at[place.z, place.slot()]
        src = self.last if k == 3 else dst
        self.along_x[k, 0] = wires.put(src, dst, place.at_x())
        self.along_y[k, 0] = wires.put(src, dst, place.at_y())
        self.core[k, 0, 0] = wires.put(src, dst, place.at_core())

    def relay_z(self, k):
        place, wires = self.place, self.wires
        for step in range(1, self.steps):
            ref = self.wholes[k].at[place.z_back(step), place.slot()]
            wires.landed(self.along_z[k, step], ref)
            self.along_x[k, step] = wires.put(ref, ref, place.at_x())
            self.along_y[k, step] = wires.put(ref, ref, place.at_y())
            self.core[k, 0, step] = wires.put(ref, ref, place.at_core())

    def relay_plane(self, k):
        upper, lower = self.halves(k)
        place, wires, whole = self.place, self.wires, self.wholes[k]
        for step in range(self.steps):
            z = place.z_back(step)
            slot = place.slot(flip_x=1)
            ref = whole.at[z, slot]
            wires.landed(self.along_x[k, step], ref)
            half = whole.at[z, slot, upper]
            self.by_y[k, step] = wires.put(half, half, place.at_y())
            self.core[k, 1, step] = wires.put(ref, ref, place.at_core())
            slot = place.slot(flip_y=1)
            ref = whole.at[z, slot]
            wires.landed(self.along_y[k, step], ref)
            half = whole.at[z, slot, lower]
            self.by_x[k, step] = wires.put(half, half, place.at_x())
            self.core[k, 2, step] = wires.put(ref, ref, place.at_core())

    def relay_corner(self, k):
        upper, lower = self.halves(k)
        place, wires, whole = self.place, self.wires, self.wholes[k]
        slot = place.slot(flip_x=1, flip_y=1)
        for step in range(self.steps):
            z = place.z_back(step)
            wires.landed(self.by_y[k, step], whole.at[z, slot, upper])
            wires.landed(self.by_x[k, step], whole.at[z, slot, lower])
            ref = whole.at[z, slot]
            self.core[k, 3, step] = wires.put(ref, ref, place.at_core())

    def finish(self, k):
        place = self.place
        for part, (flip_y, flip_x) in enumerate(FLIPS):
            slot = place.slot(flip_y=flip_y, flip_c=1, flip_x=flip_x)
            for step in range(self.steps):
                ref = self.wholes[k].at[place.z_back(step), slot]
                self.wires.landed(self.core[k, part, step], ref)


class Scatter:
    def __init__(self, wires, place, grads, from_core, from_x, from_y, last_x, last_y, from_z):
        self.wires, self.place, self.grads = wires, place, grads
        self.from_core, self.from_x, self.from_y = from_core, from_x, from_y
        self.last_x, self.last_y, self.from_z = last_x, last_y, from_z
        self.steps = place.groups
        self.core, self.first, self.second, self.third = {}, {}, {}, {}

    def halves(self, k):
        some = SUMS_X[k]
        return pl.ds(0, some), pl.ds(some, SUMS[k] - some)

    def own(self, k, part, rows):
        flip_y, flip_x = FLIPS[part]
        return self.grads[k].at[:, self.place.slot(flip_y=flip_y, flip_x=flip_x), rows]

    def send_core(self, k):
        place = self.place
        for part in (3, 1, 2, 0):
            flip_y, flip_x = FLIPS[part]
            slot = place.slot(flip_y=flip_y, flip_c=1, flip_x=flip_x)
            self.core[k, part] = self.wires.put(
                self.grads[k].at[:, slot], self.from_core[k].at[part], place.at_core()
            )

    def add(self, into, other):
        def one(z, carry):
            total = into[z].astype(jnp.float32) + other[z].astype(jnp.float32)
            into[z] = total.astype(into.dtype)
            return carry

        lax.fori_loop(0, self.steps, one, 0)

    def after_core(self, k):
        upper, lower = self.halves(k)
        whole = pl.ds(0, SUMS[k])
        wires, place = self.wires, self.place
        for part in (3, 1, 2, 0):
            wires.landed(self.core[k, part], self.from_core[k].at[part])
            self.add(self.own(k, part, whole), self.from_core[k].at[part])
            if part == 3:
                self.first[k, "x", 1] = wires.put(
                    self.own(k, 3, upper), self.from_x[k].at[1], place.at_x()
                )
                self.first[k, "y", 1] = wires.put(
                    self.own(k, 3, lower), self.from_y[k].at[1], place.at_y()
                )
            elif part == 1:
                self.first[k, "x", 0] = wires.put(
                    self.own(k, 1, upper), self.from_x[k].at[0], place.at_x()
                )
            elif part == 2:
                self.first[k, "y", 0] = wires.put(
                    self.own(k, 2, lower), self.from_y[k].at[0], place.at_y()
                )

    def after_first(self, k):
        upper, lower = self.halves(k)
        wires, place = self.wires, self.place
        wires.landed(self.first[k, "x", 1], self.from_x[k].at[1])
        self.add(self.own(k, 2, upper), self.from_x[k].at[1])
        self.second[k, "y"] = wires.put(self.own(k, 2, upper), self.last_y[k], place.at_y())
        wires.landed(self.first[k, "y", 1], self.from_y[k].at[1])
        self.add(self.own(k, 1, lower), self.from_y[k].at[1])
        self.second[k, "x"] = wires.put(self.own(k, 1, lower), self.last_x[k], place.at_x())
        wires.landed(self.first[k, "x", 0], self.from_x[k].at[0])
        self.add(self.own(k, 0, upper), self.from_x[k].at[0])
        wires.landed(self.first[k, "y", 0], self.from_y[k].at[0])
        self.add(self.own(k, 0, lower), self.from_y[k].at[0])

    def after_second(self, k):
        upper, lower = self.halves(k)
        wires, place = self.wires, self.place
        wires.landed(self.second[k, "y"], self.last_y[k])
        self.add(self.own(k, 0, upper), self.last_y[k])
        wires.landed(self.second[k, "x"], self.last_x[k])
        self.add(self.own(k, 0, lower), self.last_x[k])
        for step in range(1, self.steps):
            z = place.z_of(step)
            self.third[k, step] = wires.put(
                self.grads[k].at[z, place.slot()], self.from_z[k].at[step - 1], place.at_z(step)
            )

    def finish(self, k):
        place = self.place
        total = self.grads[k][place.z, place.slot()].astype(jnp.float32)
        for step in range(1, self.steps):
            self.wires.landed(self.third[k, step], self.from_z[k].at[step - 1])
            total = total + self.from_z[k][step - 1].astype(jnp.float32)
        return total


def times(a, b):
    return lax.dot_general(a, b, (((1,), (0,)), ((), ())), preferred_element_type=jnp.float32)


def times_turned(a, b):
    return lax.dot_general(a, b, (((1,), (1,)), ((), ())), preferred_element_type=jnp.float32)


def turned_times(a, b):
    return lax.dot_general(a, b, (((0,), (0,)), ((), ())), preferred_element_type=jnp.float32)


def aligned(index, size):
    return pl.ds(pl.multiple_of(index * size, size), size)


def head_masks(lanes, head_dim):
    lane = lax.broadcasted_iota(jnp.int32, (1, lanes), 1)
    return [
        jnp.where((lane >= h * head_dim) & (lane < (h + 1) * head_dim), 1.0, 0.0).astype(jnp.bfloat16)
        for h in range(lanes // head_dim)
    ]


def gelu_and_slope(u):
    near = 1.0 / (1.0 + (0.3275911 * math.sqrt(0.5)) * jnp.abs(u))
    bell = jnp.exp(-0.5 * (u * u))
    series = near * (
        0.127414796
        + near * (-0.142248368 + near * (0.7107068705 + near * (-0.7265760135 + near * 0.5307027145)))
    )
    tail = series * bell
    below = jnp.where(u < 0.0, tail, 1.0 - tail)
    return u * below, below + u * (bell * (1.0 / math.sqrt(2.0 * math.pi)))


def assemble(source, first, blocks, target):
    per_z, size = source.shape[1] // 2, 24

    def one(i, carry):
        z, pair = lax.div(i, per_z), lax.rem(i, per_z)
        left = source[z, 2 * pair].astype(jnp.float32)
        right = source[z, 2 * pair + 1].astype(jnp.float32)
        for b in range(blocks):
            rows = slice(first + b * size, first + (b + 1) * size)
            both = jnp.concatenate([left[rows], right[rows]], axis=0)
            target[b, aligned(i, 2 * size), :] = both.astype(target.dtype)
        return carry

    lax.fori_loop(0, source.shape[0] * per_z, one, 0)


def sum_slabs(source, first):
    def one(i, total):
        per_z = source.shape[1]
        slab = source[lax.div(i, per_z), lax.rem(i, per_z)].astype(jnp.float32)
        return total + slab[first : first + 8]

    count = source.shape[0] * source.shape[1]
    return lax.fori_loop(0, count, one, jnp.zeros((8, source.shape[-1]), jnp.float32))


def normalize(row_data):
    center = row_data - jnp.mean(row_data, axis=-1, keepdims=True)
    spread = jnp.mean(center * center, axis=-1, keepdims=True)
    scale = lax.rsqrt(spread + EPS)
    return center * scale, scale


def weights_forward(queries, keys_all, live):
    scores = jnp.where(live, times_turned(queries, keys_all), -1e30)
    exponent = jnp.exp(scores - jnp.max(scores, axis=-1, keepdims=True))
    return (exponent * (1.0 / jnp.sum(exponent, axis=-1, keepdims=True))).astype(jnp.bfloat16)


def as_column(row):
    size = row.shape[1]
    down = lax.broadcasted_iota(jnp.int32, (size, size), 0)
    across = lax.broadcasted_iota(jnp.int32, (size, size), 1)
    return jnp.sum(jnp.where(down == across, row, 0.0), axis=1, keepdims=True)


def put_at(row, start, width):
    size = row.shape[1]
    down = lax.broadcasted_iota(jnp.int32, (size, width), 0)
    across = lax.broadcasted_iota(jnp.int32, (size, width), 1)
    return jnp.sum(jnp.where(across == down + start, as_column(row), 0.0), axis=0, keepdims=True)


def forward_kernel(
    short_len, long_len, w_qkv, w_out, w_up, w_down, qv_bias, out_bias, gains, shifts, up_bias,
    short_pool, long_pool, short_tok, long_tok,
    out_down, out_wq, out_wu, out_rows, out_qkv, out_short_probs, out_long_probs, out_mixed,
    out_first, out_hat, out_scale, out_low, out_acted, out_slope, vectors, share,
    whole0, whole1, whole2, wq, wu, rows_in, qkv, short_probs, long_probs, mixed,
    first, hat, scale, low, acted, slope, far_pool,
    send, recv, here, leave,
):
    place = Place()
    x, other = place.x, 1 - place.x
    short_rows, half = short_tok.shape[0], long_tok.shape[1]
    total_rows, width = rows_in.shape
    long_rows = 2 * half
    count, cap = short_pool.shape
    mine = pl.ds(pl.multiple_of(short_rows + x * half, half), half)
    theirs = pl.ds(pl.multiple_of(short_rows + other * half, half), half)
    local = []

    def move(src, dst):
        copy = pltpu.make_async_copy(src, dst, here.at[len(local)])
        copy.start()
        local.append(copy)
        return copy

    move(w_down, out_down.at[place.z, place.slot()])
    loads = [
        move(short_tok, rows_in.at[pl.ds(0, short_rows)]),
        move(long_tok.at[x], rows_in.at[mine]),
    ]
    place.greet_start()

    device = place.dp * 2 + x
    size = w_out.shape[0]

    def blocks(matrix):
        data = matrix[...].astype(jnp.float32)
        return [data[:, i * width : (i + 1) * width] for i in range(data.shape[1] // width)]

    pairs = [
        put_at(member[i : i + 1, :].astype(jnp.float32), device * size, width)
        for member in (qv_bias, out_bias, gains, shifts)
        for i in range(2)
    ]
    ups = put_at(up_bias[...].astype(jnp.float32), lax.rem(device, 8) * (4 * size), width)
    ups = jnp.where(lax.broadcasted_iota(jnp.int32, (8, 1), 0) == lax.div(device, 8), ups, 0.0)
    z, slot = place.z, place.slot()
    whole0[z, slot] = jnp.concatenate(blocks(w_qkv) + pairs, axis=0).astype(jnp.bfloat16)
    whole1[z, slot] = jnp.concatenate(blocks(w_out) + [ups], axis=0).astype(jnp.bfloat16)
    whole2[z, slot] = jnp.concatenate(blocks(w_up), axis=0).astype(jnp.bfloat16)

    place.greet_wait()
    wires = Wires(send, recv)
    net = Gather(wires, place, (whole0, whole1, whole2, out_down), w_down)
    net.start(0)
    net.start(1)
    net.start_plane(2)
    net.start(2)
    net.start_plane(1)
    net.start_plane(0)
    pooled = wires.put(long_pool, far_pool, place.at_x())
    net.relay_z(0)
    net.relay_plane(0)
    tok = wires.put(long_tok.at[other], rows_in.at[mine], place.at_x())
    net.relay_z(1)
    net.relay_corner(0)
    for copy in loads:
        copy.wait()
    net.finish(0)
    assemble(whole0, 0, 3, wq)
    vectors[0:8, :] = sum_slabs(whole0, 72)

    head_dim = width // HEADS
    score_scale = 1.0 / math.sqrt(head_dim)

    def project(i, carry):
        rows = aligned(i, 256)
        data = rows_in[rows, :]
        queries = times(data, wq[0]) + vectors[0:1, :]
        qkv[0, rows, :] = (queries.astype(jnp.bfloat16).astype(jnp.float32) * score_scale).astype(jnp.bfloat16)
        qkv[1, rows, :] = times(data, wq[1]).astype(jnp.bfloat16)
        qkv[2, rows, :] = (times(data, wq[2]) + vectors[1:2, :]).astype(jnp.bfloat16)
        return carry

    lax.fori_loop(0, short_rows // 256, project, 0)

    masks = head_masks(2 * head_dim, head_dim)
    keep_first = lax.broadcasted_iota(jnp.int32, (1, 2 * head_dim), 1) < head_dim
    place_in_block = lax.broadcasted_iota(jnp.int32, (1, cap), 1)
    short_live = [place_in_block < short_len[i] for i in range(count)]
    passage_len = long_len[x]
    long_live = lax.broadcasted_iota(jnp.int32, (1, long_rows), 1) < passage_len
    pairs = width // (2 * head_dim)

    def attend_short(pair, carry):
        lanes = aligned(pair, 2 * head_dim)
        blocks_of = [pl.ds(i * cap, cap) for i in range(count)]
        queries, keys_all, values = [[qkv[b, rows, lanes] for rows in blocks_of] for b in range(3)]
        units = [(i, h) for i in range(count) for h in range(2)]
        scores = [times_turned(queries[i] * masks[h], keys_all[i]) for i, h in units]
        scores = [jnp.where(short_live[i], part, -1e30) for (i, h), part in zip(units, scores)]
        tops = [jnp.max(part, axis=-1, keepdims=True) for part in scores]
        exponents = [jnp.exp(part - top) for part, top in zip(scores, tops)]
        totals = [jnp.sum(part, axis=-1, keepdims=True) for part in exponents]
        probs = [(part * (1.0 / total)).astype(jnp.bfloat16) for part, total in zip(exponents, totals)]
        parts = [times(part, values[i]) for (i, h), part in zip(units, probs)]
        for (i, h), part in zip(units, probs):
            short_probs[i, 2 * pair + h] = part
        for i in range(count):
            mixed[blocks_of[i], lanes] = jnp.where(keep_first, parts[2 * i], parts[2 * i + 1]).astype(jnp.bfloat16)
        return carry

    lax.fori_loop(0, pairs // 2, attend_short, 0)
    net.relay_z(2)
    lax.fori_loop(pairs // 2, pairs - 1, attend_short, 0)
    net.start(3)
    net.relay_plane(1)
    lax.fori_loop(pairs - 1, pairs, attend_short, 0)
    net.start_plane(3)
    move(short_probs, out_short_probs)
    wires.landed(tok, rows_in.at[theirs])
    lax.fori_loop(short_rows // 256, total_rows // 256, project, 0)
    move(qkv, out_qkv)
    move(rows_in, out_rows)

    wires.landed(pooled, far_pool)
    chosen = []
    for block in range(total_rows // cap):
        if block < count:
            mask, start = short_pool[block : block + 1, :], 0
            limit = short_len[block]
        else:
            step = block - count
            in_half, start = step % (half // cap) * cap, step * cap
            at = slice(in_half, in_half + cap)
            own = jnp.where(x == 0, long_pool[0:1, at], long_pool[1:2, at])
            far = jnp.where(x == 0, far_pool[0:1, at], far_pool[1:2, at])
            mask = jnp.where(x == step // (half // cap), own, far)
            limit = passage_len - start
        keep = (place_in_block < limit) & ((mask > 0) | (place_in_block + start == 0))
        chosen.append(jnp.where(keep, 1.0, 0.0))
    for block in range(count):
        share[block : block + 1, :] = chosen[block] / jnp.sum(chosen[block], axis=-1, keepdims=True)
    long_total = sum(jnp.sum(row, axis=-1, keepdims=True) for row in chosen[count:])
    for block in range(count, total_rows // cap):
        share[block : block + 1, :] = chosen[block] / long_total

    def attend_long(pair, carry):
        lanes = aligned(pair, 2 * head_dim)
        rows = pl.ds(short_rows, long_rows)
        keys_all, values = qkv[1, rows, lanes], qkv[2, rows, lanes]
        for block in range(long_rows // 256):
            inner = pl.ds(block * 256, 256)
            rows = pl.ds(short_rows + block * 256, 256)
            queries = qkv[0, rows, lanes]
            parts = []
            for h in range(2):
                probs = weights_forward(queries * masks[h], keys_all, long_live)
                long_probs[2 * pair + h, inner, :] = probs
                parts.append(times(probs, values))
            mixed[rows, lanes] = jnp.where(keep_first, parts[0], parts[1]).astype(jnp.bfloat16)
        return carry

    lax.fori_loop(0, pairs - 2, attend_long, 0)
    net.relay_plane(2)
    net.relay_corner(1)
    lax.fori_loop(pairs - 2, pairs - 1, attend_long, 0)
    net.relay_z(3)
    lax.fori_loop(pairs - 1, pairs, attend_long, 0)
    move(long_probs, out_long_probs)
    move(mixed, out_mixed)
    net.finish(1)
    assemble(whole1, 0, 1, wq.at[pl.ds(3, 1)])
    vectors[8:16, :] = sum_slabs(whole1, 24)
    move(wq, out_wq)

    def attach(i, carry):
        rows = aligned(i, 256)
        first_in = rows_in[rows, :].astype(jnp.float32) + (times(mixed[rows, :], wq[3]) + vectors[2:3, :])
        normal, factor = normalize(first_in)
        out = normal * vectors[4:5, :] + vectors[6:7, :]
        first[rows, :] = out
        low[rows, :] = out.astype(jnp.bfloat16)
        hat[rows, :] = normal.astype(jnp.bfloat16)
        scale[rows, :] = jnp.broadcast_to(factor, (256, scale.shape[1]))
        return carry

    lax.fori_loop(0, total_rows // 256, attach, 0)
    move(first, out_first)
    move(low, out_low)
    move(hat, out_hat)
    move(scale, out_scale)
    net.relay_corner(2)
    net.finish(2)
    assemble(whole2, 0, 4, wu)
    move(wu, out_wu)

    def leaving(i):
        j, rows = lax.div(i, 4), aligned(lax.rem(i, 4), 256)
        return (
            pltpu.make_async_copy(acted.at[j, rows], out_acted.at[j, rows], leave.at[0, i]),
            pltpu.make_async_copy(slope.at[j, rows], out_slope.at[j, rows], leave.at[1, i]),
        )

    def expand(i, carry):
        j, rows = lax.div(i, 4), aligned(lax.rem(i, 4), 256)
        inner = times(low[rows, :], wu[j]) + vectors[pl.ds(8 + j, 1), :]
        value, grad = gelu_and_slope(inner)
        acted[j, rows, :] = value.astype(jnp.bfloat16)
        slope[j, rows, :] = grad.astype(jnp.bfloat16)
        for copy in leaving(i):
            copy.start()
        return carry

    def left(i, carry):
        for copy in leaving(i):
            copy.wait()
        return carry

    lax.fori_loop(0, 7, expand, 0)
    net.relay_plane(3)
    lax.fori_loop(7, 14, expand, 0)
    net.relay_corner(3)
    lax.fori_loop(14, 16, expand, 0)
    net.finish(3)
    wires.close()
    lax.fori_loop(0, 16, left, 0)
    for copy in [local[0]] + local[3:]:
        copy.wait()


def forward(lengths, parameters, pools, short_tok, long_tok, groups):
    short_rows, width = short_tok.shape
    half = long_tok.shape[1]
    long_rows = 2 * half
    rows = short_rows + long_rows
    count, cap = pools[0].shape
    inner = 4 * width
    copies = 4 * ((groups - 1) + 4 * groups + 4 * groups) + 2
    low = jnp.bfloat16
    shape = jax.ShapeDtypeStruct
    outs = (
        shape((groups, 8, SIZES[3], width), low),
        shape((4, width, width), low),
        shape((4, width, width), low),
        shape((rows, width), low),
        shape((3, rows, width), low),
        shape((count, HEADS, cap, cap), low),
        shape((HEADS, long_rows, long_rows), low),
        shape((rows, width), low),
        shape((rows, width), jnp.float32),
        shape((rows, width), low),
        shape((rows, 128), jnp.float32),
        shape((rows, width), low),
        shape((inner // width, rows, width), low),
        shape((inner // width, rows, width), low),
        shape((16, width), jnp.float32),
        shape((rows // cap, cap), jnp.float32),
    )
    anywhere, near = pl.BlockSpec(memory_space=pl.ANY), pl.BlockSpec(memory_space=pltpu.VMEM)
    scalars = pl.BlockSpec(memory_space=pltpu.SMEM)
    kept = [pltpu.VMEM(out.shape, out.dtype) for out in outs[1:14]]
    return pl.pallas_call(
        forward_kernel,
        name="forward",
        out_shape=outs,
        in_specs=[scalars] * 2 + [near] * 11 + [anywhere] * 2,
        out_specs=[anywhere] * 14 + [near] * 2,
        scratch_shapes=[pltpu.VMEM((groups, 8, SIZES[k], width), low) for k in range(3)]
        + kept
        + [
            pltpu.VMEM(pools[1].shape, pools[1].dtype),
            pltpu.SemaphoreType.DMA((copies,)),
            pltpu.SemaphoreType.DMA((copies,)),
            pltpu.SemaphoreType.DMA((24,)),
            pltpu.SemaphoreType.DMA((2, 16)),
        ],
        compiler_params=pltpu.CompilerParams(
            collective_id=0, has_side_effects=True, vmem_limit_bytes=60 * 1024 * 1024
        ),
    )(*lengths, *parameters, *pools, short_tok, long_tok)


def backward_kernel(
    short_len, long_len, vectors, share, short_pool_cot, long_pool_cot, short_cot, long_cot,
    in_down, in_wq, in_wu, in_rows, in_qkv, in_short_probs, in_long_probs, in_mixed,
    in_first, in_hat, in_scale, in_low, in_acted, in_slope,
    short_out, long_out, short_grad, long_grad, short_pooled, long_pooled,
    grad_qkv, grad_out, grad_up, grad_down, grad_vectors, grad_up_vector,
    wide, pair, w_up, w_far, hat, sums, branch, low, scale, halves, probs_short,
    vector_sums, pool_cots, pooled_rows, pooled_own, pooled_far,
    *more,
):
    place = Place()
    x, other = place.x, 1 - place.x
    *chunks, send, recv, here, blocks, fetch = more
    parts = len(SUMS)
    grads, *received = [chunks[i * parts : (i + 1) * parts] for i in range(7)]
    total_rows, width = sums.shape
    short_rows = short_out.shape[0]
    count, cap = probs_short.shape[1], probs_short.shape[-1]
    long_rows = total_rows - short_rows
    half = long_rows // 2
    head_dim = width // HEADS
    steps = total_rows // 256
    low_type = jnp.bfloat16
    local = []

    def move(src, dst):
        copy = pltpu.make_async_copy(src, dst, here.at[len(local)])
        copy.start()
        local.append(copy)
        return copy

    mine = pl.ds(pl.multiple_of(short_rows + x * half, half), half)
    theirs = pl.ds(pl.multiple_of(short_rows + other * half, half), half)
    place.greet_start()
    load_down = [move(in_down.at[j], w_far.at[j]) for j in range(4)]
    load_down += [
        move(short_cot, branch.at[pl.ds(0, short_rows)]),
        move(long_cot.at[x], branch.at[mine]),
    ]
    passage_len = long_len[x]

    def block_at(step):
        return jnp.where(step < 2, step, 2 + lax.rem(step + x, 2))

    def block_copies(i):
        rows = aligned(i, 256)
        return (
            pltpu.make_async_copy(in_acted.at[:, rows], wide.at[:, rows], blocks.at[0, i]),
            pltpu.make_async_copy(in_first.at[rows], sums.at[rows], blocks.at[1, i]),
        )

    for copy in block_copies(0):
        copy.start()
    vector_sums[...] = jnp.zeros_like(vector_sums)
    pool_cots[0:count, :] = short_pool_cot[...]
    pool_cots[count : 2 * count, :] = jnp.broadcast_to(long_pool_cot[pl.ds(x, 1), :], (count, width))
    place.greet_wait()
    wires = Wires(send, recv)
    swap_cot = wires.put(long_cot.at[other], branch.at[mine], place.at_x())
    net = Scatter(wires, place, grads, *received)
    for copy in load_down:
        copy.wait()
    tall = lax.broadcasted_iota(jnp.int32, (256, 1), 0)
    diagonal = lax.broadcasted_iota(jnp.int32, (cap, cap), 0) == lax.broadcasted_iota(jnp.int32, (cap, cap), 1)

    def add_vector(row, rows):
        vector_sums[row : row + 1, :] += jnp.sum(rows, axis=0, keepdims=True)

    def second(step, carry):
        i = block_at(step)
        rows = aligned(i, 256)

        @pl.when(step == steps - 1)
        def _():
            wires.landed(swap_cot, branch.at[theirs])

        @pl.when(step < steps - 1)
        def _():
            for copy in block_copies(block_at(step + 1)):
                copy.start()

        for copy in block_copies(i):
            copy.wait()
        product = times(wide[0, rows, :], w_far[0])
        for j in range(1, 4):
            product += times(wide[j, rows, :], w_far[j])
        normal, factor = normalize(sums[rows, :] + (product + vectors[3:4, :]))
        lens = [
            jnp.where(2 * i + part < count, short_len[lax.rem(2 * i + part, count)], passage_len - (2 * i + part - count) * cap)
            for part in range(2)
        ]
        live = tall < jnp.where(tall < cap, lens[0], lens[1] + cap)
        final = jnp.where(live, normal * vectors[5:6, :] + vectors[7:8, :], 0.0)
        low[rows, :] = final.astype(low_type)
        spread = []
        for part in range(2):
            share_row = share[pl.ds(2 * i + part, 1), :]
            column = jnp.sum(jnp.where(diagonal, share_row, 0.0), axis=1, keepdims=True)
            piece = final[part * cap : (part + 1) * cap]
            pooled_rows[pl.ds(2 * i + part, 1), :] = jnp.sum(piece * column, axis=0, keepdims=True)
            spread.append(column * pool_cots[pl.ds(2 * i + part, 1), :])
        grad_final = jnp.where(live, branch[rows, :].astype(jnp.float32), 0.0) + jnp.concatenate(spread, axis=0)
        add_vector(5, grad_final * normal)
        add_vector(7, grad_final)
        scaled = grad_final * vectors[5:6, :]
        mean_one = jnp.mean(scaled, axis=-1, keepdims=True)
        mean_two = jnp.mean(scaled * normal, axis=-1, keepdims=True)
        grad_second = factor * (scaled - mean_one - normal * mean_two)
        sums[rows, :] = grad_second
        grad_branch = grad_second.astype(low_type)
        branch[rows, :] = grad_branch
        add_vector(3, grad_branch.astype(jnp.float32))
        return carry

    lax.fori_loop(0, steps, second, 0)
    short_pooled[...] = pooled_rows[0:count, :]
    own_pooled = jnp.sum(pooled_rows[count : 2 * count, :], axis=0, keepdims=True)
    pooled_own[...] = jnp.broadcast_to(own_pooled, pooled_own.shape)
    long_pooled[pl.ds(x, 1), :] = own_pooled
    out_copies = [
        move(low.at[pl.ds(0, short_rows)], short_out),
        move(low.at[mine], long_out.at[x]),
    ]
    load_slope = [move(in_slope.at[0], pair.at[0]), move(in_slope.at[1], pair.at[1])]
    load_up = move(in_wu, w_up)
    load_hat, load_scale = move(in_hat, hat), move(in_scale, scale)

    swap_out = wires.put(low.at[theirs], long_out.at[x], place.at_x())
    swap_pooled = wires.put(pooled_own, pooled_far, place.at_x())

    def down_step(i, carry):
        j, part = lax.div(i, 2), lax.rem(i, 2)
        product = turned_times(wide[j, :, aligned(part, width // 2)], branch[...])
        grads[5][j, aligned(part, 4)] = product.reshape(4, SUMS[5], width).astype(low_type)
        return carry

    lax.fori_loop(0, 8, down_step, 0, unroll=2)
    net.send_core(5)

    def inner_block(j):
        def inner(i, carry):
            rows = aligned(i, 256)
            product = times_turned(branch[rows, :], w_far[j]) * pair[j % 2, rows, :].astype(jnp.float32)
            grad_inner = product.astype(low_type)
            wide[j, rows, :] = grad_inner
            add_vector(8 + j, grad_inner.astype(jnp.float32))
            return carry

        lax.fori_loop(0, steps, inner, 0, unroll=2)

    load_slope[0].wait()
    inner_block(0)
    load_slope.append(move(in_slope.at[2], pair.at[0]))
    load_slope[1].wait()
    inner_block(1)
    load_slope.append(move(in_slope.at[3], pair.at[1]))
    for copy in out_copies:
        copy.wait()
    wires.has_left(swap_out)
    load_low = move(in_low, low)
    load_slope[2].wait()
    inner_block(2)
    net.after_core(5)
    load_mixed = move(in_mixed, pair.at[0])
    load_slope[3].wait()
    inner_block(3)
    load_wq = move(in_wq, w_far)

    def up_step(i, carry):
        r, both = lax.div(i, 2), lax.rem(i, 2)
        data = low[:, aligned(r, width // 2)]
        halves[0] = turned_times(data, wide[2 * both])
        halves[1] = turned_times(data, wide[2 * both + 1])

        def one(k, carry):
            rows = pl.ds(pl.multiple_of(k * 24, 8), 24)
            data = jnp.concatenate([halves[0, rows, :], halves[1, rows, :]], axis=0)
            grads[4][2 * r + lax.div(k, 8), lax.rem(k, 8), aligned(both, 48), :] = data.astype(low_type)
            return carry

        return lax.fori_loop(0, 16, one, carry)

    load_low.wait()
    lax.fori_loop(0, 4, up_step, 0)
    net.send_core(4)

    load_up.wait()
    load_hat.wait()
    load_scale.wait()

    def first_back(i, carry):
        rows = aligned(i, 256)
        grad_first = sums[rows, :]
        for j in range(4):
            grad_first += times_turned(wide[j, rows, :], w_up[j])
        normal = hat[rows, :].astype(jnp.float32)
        add_vector(4, grad_first * normal)
        add_vector(6, grad_first)
        scaled = grad_first * vectors[4:5, :]
        mean_one = jnp.mean(scaled, axis=-1, keepdims=True)
        mean_two = jnp.mean(scaled * normal, axis=-1, keepdims=True)
        grad_in = scale[rows, 0:1] * (scaled - mean_one - normal * mean_two)
        sums[rows, :] = grad_in
        grad_attn = grad_in.astype(low_type)
        branch[rows, :] = grad_attn
        add_vector(2, grad_attn.astype(jnp.float32))
        return carry

    lax.fori_loop(0, steps // 2, first_back, 0)
    net.after_first(5)
    net.after_core(4)
    lax.fori_loop(steps // 2, steps, first_back, 0)
    load_qkv = move(in_qkv, wide.at[pl.ds(0, 3)])
    load_rows = move(in_rows, wide.at[3])
    net.after_second(5)

    load_mixed.wait()
    load_wq.wait()
    def out_step(r, carry):
        halves[0] = turned_times(pair[0, :, aligned(r, width // 2)], branch[...])

        def one(k, carry):
            rows = pl.ds(pl.multiple_of(k * 24, 8), 24)
            data = jnp.concatenate([halves[0, rows, :], vector_sums[8:16, :]], axis=0)
            grads[3][2 * r + lax.div(k, 8), lax.rem(k, 8)] = data.astype(low_type)
            return carry

        return lax.fori_loop(0, 16, one, carry)

    lax.fori_loop(0, 2, out_step, 0)

    def mixed_back(i, carry):
        rows = aligned(i, 256)
        pair[1, rows, :] = times_turned(branch[rows, :], w_far[3]).astype(low_type)
        return carry

    lax.fori_loop(0, steps, mixed_back, 0)
    net.send_core(3)

    def probs_copies(p, slot):
        lanes = pl.ds(2 * p, 2)
        return (
            pltpu.make_async_copy(in_short_probs.at[:, lanes], probs_short.at[slot], fetch.at[0, slot]),
            pltpu.make_async_copy(
                in_long_probs.at[lanes],
                w_up.at[pl.ds(2 * slot, 2), pl.ds(0, long_rows), pl.ds(0, long_rows)],
                fetch.at[1, slot],
            ),
        )

    for copy in probs_copies(0, 0):
        copy.start()
    load_qkv.wait()
    score_scale = 1.0 / math.sqrt(head_dim)
    masks = head_masks(2 * head_dim, head_dim)
    pairs = width // (2 * head_dim)

    def attend_back(lanes, units):
        heads = [(u, h) for u in range(len(units)) for h in range(2)]
        queries = [wide[0, rows, lanes] for rows, _, _, _ in units]
        grads_mixed = [pair[1, rows, lanes] for rows, _, _, _ in units]
        overlaps = [
            grad.astype(jnp.float32) * pair[0, rows, lanes].astype(jnp.float32)
            for grad, (rows, _, _, _) in zip(grads_mixed, units)
        ]
        centers = [
            jnp.sum(overlaps[u] * masks[h].astype(jnp.float32), axis=-1, keepdims=True) for u, h in heads
        ]
        grads_head = [grads_mixed[u] * masks[h] for u, h in heads]
        probs = [units[u][1](h) for u, h in heads]
        grads_probs = [times_turned(grad, units[u][3]) for grad, (u, h) in zip(grads_head, heads)]
        scores = [
            (part.astype(jnp.float32) * (grad - center)).astype(low_type)
            for part, grad, center in zip(probs, grads_probs, centers)
        ]
        grads_q = [times(part, units[u][2] * masks[h]) for part, (u, h) in zip(scores, heads)]
        grads_k = [turned_times(queries[u] * masks[h], part) for part, (u, h) in zip(scores, heads)]
        grads_v = [turned_times(grad, part) for part, grad in zip(probs, grads_head)]
        for u, (rows, _, _, _) in enumerate(units):
            total = grads_q[2 * u] + grads_q[2 * u + 1]
            wide[0, rows, lanes] = (total * score_scale).astype(low_type)
        return [
            [grads[2 * u] + grads[2 * u + 1] for u in range(len(units))] for grads in (grads_k, grads_v)
        ]

    def attention_back(p, carry):
        slot = lax.rem(p, 2)
        for copy in probs_copies(p, slot):
            copy.wait()

        @pl.when(p + 1 < pairs)
        def _():
            for copy in probs_copies(p + 1, 1 - slot):
                copy.start()

        lanes = aligned(p, 2 * head_dim)
        blocks_of = [pl.ds(i * cap, cap) for i in range(count)]
        units = [
            (rows, lambda h, i=i: probs_short[slot, i, h], wide[1, rows, lanes], wide[2, rows, lanes])
            for i, rows in enumerate(blocks_of)
        ]
        grads_k, grads_v = attend_back(lanes, units)
        for rows, grad_k, grad_v in zip(blocks_of, grads_k, grads_v):
            wide[1, rows, lanes] = grad_k.T.astype(low_type)
            wide[2, rows, lanes] = grad_v.T.astype(low_type)
        rows = pl.ds(short_rows, long_rows)
        keys_all, values = wide[1, rows, lanes], wide[2, rows, lanes]
        total_k, total_v = None, None
        for block in range(long_rows // 256):
            inner = pl.ds(block * 256, 256)
            unit = (
                pl.ds(short_rows + block * 256, 256),
                lambda h, inner=inner: w_up[2 * slot + h, inner, 0:long_rows],
                keys_all,
                values,
            )
            (grad_k,), (grad_v,) = attend_back(lanes, [unit])
            total_k = grad_k if total_k is None else total_k + grad_k
            total_v = grad_v if total_v is None else total_v + grad_v
        wide[1, rows, lanes] = total_k.T.astype(low_type)
        wide[2, rows, lanes] = total_v.T.astype(low_type)
        return carry

    third = width // 3

    def qkv_step(group):
        lanes = pl.ds(group * third, third)

        def bias(i, carry):
            rows = aligned(i, 256)
            for row, b in ((0, 0), (1, 2)):
                piece = wide[b, rows, lanes].astype(jnp.float32)
                vector_sums[row : row + 1, lanes] += jnp.sum(piece, axis=0, keepdims=True)
            return carry

        lax.fori_loop(0, steps, bias, 0)

        def step(r, carry):
            data = wide[3, :, aligned(r, width // 2)]
            for b in range(3):
                halves[0, :, b * third : (b + 1) * third] = turned_times(data, wide[b, :, lanes])

            def one(k, carry):
                rows = pl.ds(pl.multiple_of(k * 24, 8), 24)
                pieces = [halves[0, rows, b * third : (b + 1) * third] for b in range(3)]
                data = jnp.concatenate(pieces + [vector_sums[0:8, lanes]], axis=0)
                grads[group][2 * r + lax.div(k, 8), lax.rem(k, 8)] = data.astype(low_type)
                return carry

            return lax.fori_loop(0, 16, one, carry)

        lax.fori_loop(0, 2, step, 0)

    lax.fori_loop(0, pairs // 3, attention_back, 0)
    load_rows.wait()
    qkv_step(0)
    net.after_first(4)
    net.after_core(3)
    net.send_core(0)
    lax.fori_loop(pairs // 3, 2 * pairs // 3, attention_back, 0)
    qkv_step(1)
    net.after_second(4)
    net.send_core(1)
    net.after_core(0)
    net.after_first(3)
    net.after_core(1)
    lax.fori_loop(2 * pairs // 3, pairs, attention_back, 0)
    qkv_step(2)
    net.send_core(2)
    net.after_first(0)
    net.after_second(3)

    def tokens_back(rows):
        grad_in = sums[rows, :]
        for b in range(3):
            grad_in += times_turned(wide[b, rows, :], w_far[b])
        return grad_in

    far_low, far_in = low.at[pl.ds(0, half)], low.at[pl.ds(half, half)]
    far_low[...] = tokens_back(theirs).astype(low_type)
    net.after_first(1)

    def tokens_step(i, carry):
        rows = pl.ds(pl.multiple_of(jnp.where(i < 2, i * 256, short_rows + x * half), 256), 256)
        sums[rows, :] = tokens_back(rows)
        return carry

    lax.fori_loop(0, 1, tokens_step, 0)
    net.after_core(2)
    lax.fori_loop(1, 2, tokens_step, 0)
    net.after_second(0)
    net.after_second(1)
    net.after_first(2)
    swap_grad = wires.put(far_low, far_in, place.at_x())
    net.after_second(2)
    lax.fori_loop(2, 3, tokens_step, 0)
    move(sums.at[pl.ds(0, short_rows)], short_grad)
    move(sums.at[mine], long_grad.at[x])
    grad_down[...] = net.finish(5)
    total = net.finish(4)
    for j in range(4):
        grad_up[:, j * width : (j + 1) * width] = total[24 * j : 24 * j + 24]
    total = net.finish(3)
    grad_out[...] = total[0:24]
    grad_up_vector[...] = total[24:32]
    wires.landed(swap_pooled, pooled_far)
    long_pooled[pl.ds(other, 1), :] = pooled_far[0:1, :]
    wires.landed(swap_grad, far_in)
    sums[theirs, :] = far_in[...].astype(jnp.float32)
    move(sums.at[theirs], long_grad.at[other])
    wires.landed(swap_out, long_out.at[other])
    for group in range(3):
        total = net.finish(group)
        for b in range(3):
            columns = slice(b * width + group * third, b * width + (group + 1) * third)
            grad_qkv[:, columns] = total[24 * b : 24 * b + 24]
        grad_vectors[:, group * third : (group + 1) * third] = total[72:80]
    wires.close()
    for copy in local[-3:]:
        copy.wait()


def backward(lengths, vectors, share, pool_cots, cots, arrays, groups):
    width = vectors.shape[1]
    rows = arrays[3].shape[0]
    count, _, cap, _ = arrays[5].shape
    short_rows = count * cap
    half = (rows - short_rows) // 2
    low, wide_type = jnp.bfloat16, jnp.float32
    shape = jax.ShapeDtypeStruct
    rows24 = 24
    outs = (
        shape((short_rows, width), low),
        shape((2, half, width), low),
        shape((short_rows, width), wide_type),
        shape((2, half, width), wide_type),
        shape((count, width), wide_type),
        shape((2, width), wide_type),
        shape((rows24, 3 * width), wide_type),
        shape((rows24, width), wide_type),
        shape((rows24, 4 * width), wide_type),
        shape((4 * rows24, width), wide_type),
        shape((8, width), wide_type),
        shape((8, width), wide_type),
    )
    anywhere, near = pl.BlockSpec(memory_space=pl.ANY), pl.BlockSpec(memory_space=pltpu.VMEM)
    copies = len(SUMS) * (4 + 6 + (groups - 1)) + 4

    widths = (width // 3,) * 3 + (width,) * 3

    def chunks(parts, sizes):
        return [pltpu.VMEM(parts + (size, columns), low) for size, columns in zip(sizes, widths)]

    rest = tuple(size - some for size, some in zip(SUMS, SUMS_X))
    scratch = [
        pltpu.VMEM((4, rows, width), low),
        pltpu.VMEM((2, rows, width), low),
        pltpu.VMEM((4, width, width), low),
        pltpu.VMEM((4, width, width), low),
        pltpu.VMEM((rows, width), low),
        pltpu.VMEM((rows, width), wide_type),
        pltpu.VMEM((rows, width), low),
        pltpu.VMEM((rows, width), low),
        pltpu.VMEM((rows, 128), wide_type),
        pltpu.VMEM((2, width // 2, width), wide_type),
        pltpu.VMEM((2, count, 2, cap, cap), low),
        pltpu.VMEM((16, width), wide_type),
        pltpu.VMEM((2 * count, width), wide_type),
        pltpu.VMEM((2 * count, width), wide_type),
        pltpu.VMEM((8, width), wide_type),
        pltpu.VMEM((8, width), wide_type),
        *chunks((groups, 8), SUMS),
        *chunks((4, groups), SUMS),
        *chunks((2, groups), SUMS_X),
        *chunks((2, groups), rest),
        *chunks((groups,), rest),
        *chunks((groups,), SUMS_X),
        *chunks((groups - 1,), SUMS),
        pltpu.SemaphoreType.DMA((copies,)),
        pltpu.SemaphoreType.DMA((copies,)),
        pltpu.SemaphoreType.DMA((24,)),
        pltpu.SemaphoreType.DMA((2, rows // 256)),
        pltpu.SemaphoreType.DMA((2, 2)),
    ]
    return pl.pallas_call(
        backward_kernel,
        name="backward",
        out_shape=outs,
        in_specs=[pl.BlockSpec(memory_space=pltpu.SMEM)] * 2 + [near] * 4 + [anywhere] * 16,
        out_specs=[anywhere] * 4 + [near] * 8,
        scratch_shapes=scratch,
        compiler_params=pltpu.CompilerParams(
            collective_id=1, has_side_effects=True, vmem_limit_bytes=63 * 1024 * 1024
        ),
    )(*lengths, vectors, share, *pool_cots, *cots, *arrays)


def results_kernel(
    in_0, in_1, in_2, in_3, in_4, in_5, in_6, in_7, in_8, in_9, grad_vectors, grad_ups,
    out_0, out_1, out_2, out_3, out_4, out_5, out_6, out_7, out_8, out_9, pair_0, pair_1, ups, pair_2, pair_3,
    *more,
):
    *held, come, leave = more
    sources = (in_0, in_1, in_2, in_3, in_4, in_5, in_6, in_7, in_8, in_9)
    places = (out_0, out_1, out_4, out_5, out_2, out_3, out_6, out_7, out_8, out_9)
    ins = [pltpu.make_async_copy(sources[i], held[i], come.at[i]) for i in range(10)]
    outs = [pltpu.make_async_copy(held[i], places[i], leave.at[i]) for i in range(10)]
    for copy in ins:
        copy.start()
    device = lax.axis_index("dp") * 2 + lax.axis_index("seq")
    size, width = in_7.shape
    rows = pltpu.roll(grad_vectors[...], lax.rem(width - device * size, width), 1)
    for i, ref in enumerate((pair_0, pair_1, pair_2, pair_3)):
        ref[...] = rows[2 * i : 2 * i + 2, 0:size]
    start = lax.rem(device, 8) * (4 * size)
    row = grad_ups[pl.ds(lax.div(device, 8), 1), :]
    row = pltpu.roll(jnp.broadcast_to(row, (8, width)), lax.rem(width - start, width), 1)
    ups[...] = row[0:1, 0 : 4 * size]
    for i in range(10):
        ins[i].wait()
        outs[i].start()
    for copy in outs:
        copy.wait()


def results(arrays):
    size = arrays[7].shape[0]
    order = (0, 1, 4, 5, 2, 3, 6, 7, 8, 9)
    shape = jax.ShapeDtypeStruct
    pair = shape((2, size), jnp.float32)
    outs = tuple(shape(arrays[i].shape, arrays[i].dtype) for i in order)
    anywhere, near = pl.BlockSpec(memory_space=pl.ANY), pl.BlockSpec(memory_space=pltpu.VMEM)
    return pl.pallas_call(
        results_kernel,
        name="results",
        out_shape=outs + (pair, pair, shape((1, 4 * size), jnp.float32), pair, pair),
        in_specs=[anywhere] * 10 + [near] * 2,
        out_specs=[anywhere] * 10 + [near] * 5,
        scratch_shapes=[pltpu.VMEM(array.shape, array.dtype) for array in arrays[:10]]
        + [pltpu.SemaphoreType.DMA((10,)), pltpu.SemaphoreType.DMA((10,))],
        compiler_params=pltpu.CompilerParams(vmem_limit_bytes=56 * 1024 * 1024),
    )(*arrays)


def layer_norm(row_data, gain_vec, shift_vec):
    center = row_data - jnp.mean(row_data, axis=-1, keepdims=True)
    spread = jnp.mean(center * center, axis=-1, keepdims=True)
    return center * lax.rsqrt(spread + EPS) * gain_vec + shift_vec


def exact_gelu(inner_act):
    return jax.nn.gelu(inner_act, approximate=False)


def outer_sum(left_rows, right_rows):
    return lax.dot_general(
        left_rows, right_rows, (((0,), (0,)), ((), ())), preferred_element_type=jnp.float32
    )


def times_transposed(left_rows, matrix):
    return lax.dot_general(
        left_rows, matrix, (((1,), (1,)), ((), ())), preferred_element_type=jnp.float32
    )


def masked_scores(queries, keys_all, key_live, score_scale):
    scores = (
        jnp.einsum("bqhe,bkhe->bhqk", queries, keys_all, preferred_element_type=jnp.float32)
        * score_scale
    )
    return jnp.where(key_live[:, None, None, :], scores, -1e30)


def attend_forward(pieces, score_scale):
    queries, keys_all, values, key_live = pieces
    scores = masked_scores(queries, keys_all, key_live, score_scale)
    highest = jnp.max(scores, axis=-1, keepdims=True)
    exponent = jnp.exp(scores - highest)
    totals = jnp.sum(exponent, axis=-1, keepdims=True)
    soft_probs = (exponent / totals).astype(jnp.bfloat16)
    mixed_heads = jnp.einsum(
        "bhqk,bkhe->bqhe", soft_probs, values, preferred_element_type=jnp.float32
    )
    return (mixed_heads.astype(jnp.bfloat16), (highest + jnp.log(totals))[..., 0])


def attend_backward(pieces, score_scale):
    queries, keys_all, values, key_live, grad_mixed, log_total = pieces
    scores = masked_scores(queries, keys_all, key_live, score_scale)
    soft_probs = jnp.exp(scores - log_total[..., None])
    grad_probs = jnp.einsum(
        "bqhe,bkhe->bhqk", grad_mixed, values, preferred_element_type=jnp.float32
    )
    grad_values = jnp.einsum(
        "bhqk,bqhe->bkhe",
        soft_probs.astype(jnp.bfloat16),
        grad_mixed,
        preferred_element_type=jnp.float32,
    )
    center = jnp.sum(soft_probs * grad_probs, axis=-1, keepdims=True)
    grad_scores = (soft_probs * (grad_probs - center)).astype(jnp.bfloat16)
    grad_queries = (
        jnp.einsum("bhqk,bkhe->bqhe", grad_scores, keys_all, preferred_element_type=jnp.float32)
        * score_scale
    )
    grad_keys = (
        jnp.einsum("bhqk,bqhe->bkhe", grad_scores, queries, preferred_element_type=jnp.float32)
        * score_scale
    )
    return (grad_queries, grad_keys, grad_values)


def by_blocks(function, per_block, arrays):
    blocks = arrays[0].shape[0] // per_block
    stacked = tuple((member.reshape((blocks, per_block) + member.shape[1:]) for member in arrays))
    results = lax.map(function, stacked)
    return jax.tree.map(
        lambda member: member.reshape((blocks * per_block,) + member.shape[2:]), results
    )


def general_shards(
    short_tokens,
    long_tokens,
    short_len,
    long_len,
    short_pool,
    long_pool,
    short_cot,
    long_cot,
    short_pool_cot,
    long_pool_cot,
    w_qkv,
    w_out,
    w_up,
    w_down,
    qv_bias,
    out_bias,
    up_bias,
    norm_gain,
    norm_shift,
):
    gathered = (
        lax.all_gather(w_qkv, ("dp", "seq"), axis=0, tiled=True),
        lax.all_gather(w_out, ("dp", "seq"), axis=0, tiled=True),
        lax.all_gather(w_up, ("dp", "seq"), axis=0, tiled=True),
        lax.all_gather(w_down, ("dp", "seq"), axis=0, tiled=True),
        lax.all_gather(qv_bias, ("dp", "seq"), axis=0, tiled=True),
        lax.all_gather(out_bias, ("dp", "seq"), axis=0, tiled=True),
        lax.all_gather(up_bias, ("dp", "seq"), axis=0, tiled=True),
        lax.all_gather(norm_gain, ("dp", "seq"), axis=0, tiled=True),
        lax.all_gather(norm_shift, ("dp", "seq"), axis=0, tiled=True),
    )
    qkv_matrix, out_matrix, up_matrix, down_matrix, qv_vec, out_vec, up_vec, gains, shifts = (
        gathered
    )
    gains = gains.astype(jnp.float32)
    shifts = shifts.astype(jnp.float32)
    short_count, short_cap, model_width = short_tokens.shape
    long_count, long_half = (long_tokens.shape[0], long_tokens.shape[1])
    head_count = HEADS
    head_dim = model_width // head_count
    score_scale = 1.0 / math.sqrt(head_dim)
    short_rows = short_count * short_cap
    long_rows = long_count * long_half
    short_place = jnp.arange(short_cap, dtype=jnp.int32)
    short_live = short_place[None, :] < short_len[:, None]
    long_place = lax.axis_index("seq") * long_half + jnp.arange(long_half, dtype=jnp.int32)
    long_live = long_place[None, :] < long_len[:, None]
    short_weight = (short_live & ((short_pool > 0) | (short_place[None, :] == 0))).astype(
        jnp.float32
    )
    long_weight = (long_live & ((long_pool > 0) | (long_place[None, :] == 0))).astype(jnp.float32)
    row_live = jnp.concatenate([short_live.reshape(-1), long_live.reshape(-1)]).astype(jnp.float32)
    inputs = jnp.concatenate(
        [
            short_tokens.reshape(short_rows, model_width),
            long_tokens.reshape(long_rows, model_width),
        ],
        axis=0,
    )
    joined = jnp.dot(inputs, qkv_matrix, preferred_element_type=jnp.float32)
    queries = (joined[:, :model_width] + qv_vec[:, 0]).astype(jnp.bfloat16)
    keys_all = joined[:, model_width : 2 * model_width].astype(jnp.bfloat16)
    values = (joined[:, 2 * model_width :] + qv_vec[:, 1]).astype(jnp.bfloat16)
    short_shape = (short_count, short_cap, head_count, head_dim)
    long_shape = (long_count, long_half, head_count, head_dim)
    short_q = queries[:short_rows].reshape(short_shape)
    short_k = keys_all[:short_rows].reshape(short_shape)
    short_v = values[:short_rows].reshape(short_shape)
    long_q = queries[short_rows:].reshape(long_shape)
    long_k = keys_all[short_rows:].reshape(long_count, long_half, model_width)
    long_v = values[short_rows:].reshape(long_count, long_half, model_width)
    short_block = math.gcd(short_count, max(1, 512 // short_cap))
    long_block = math.gcd(long_count, max(1, 512 // long_half))

    def forward_blocks(pieces):
        return attend_forward(pieces, score_scale)

    def backward_blocks(pieces):
        return attend_backward(pieces, score_scale)

    short_mixed, short_logsum = by_blocks(
        forward_blocks, short_block, (short_q, short_k, short_v, short_live)
    )
    gathered_k, gathered_v = (
        lax.all_gather(long_k, "seq", axis=1, tiled=True),
        lax.all_gather(long_v, "seq", axis=1, tiled=True),
    )
    full_len = gathered_k.shape[1]
    full_shape = (long_count, full_len, head_count, head_dim)
    long_key_live = jnp.arange(full_len, dtype=jnp.int32)[None, :] < long_len[:, None]
    long_mixed, long_logsum = by_blocks(
        forward_blocks,
        long_block,
        (long_q, gathered_k.reshape(full_shape), gathered_v.reshape(full_shape), long_key_live),
    )
    mixed_heads = jnp.concatenate(
        [short_mixed.reshape(short_rows, model_width), long_mixed.reshape(long_rows, model_width)],
        axis=0,
    )
    attn_out = jnp.dot(mixed_heads, out_matrix, preferred_element_type=jnp.float32) + out_vec[:, 0]
    first_in = inputs.astype(jnp.float32) + attn_out
    first_norm = layer_norm(first_in, gains[:, 0], shifts[:, 0])
    first_low = first_norm.astype(jnp.bfloat16)
    inner_act = jnp.dot(first_low, up_matrix, preferred_element_type=jnp.float32) + up_vec
    activated = exact_gelu(inner_act).astype(jnp.bfloat16)
    branch = jnp.dot(activated, down_matrix, preferred_element_type=jnp.float32) + out_vec[:, 1]
    second_in = first_norm + branch
    final_norm = layer_norm(second_in, gains[:, 1], shifts[:, 1]) * row_live[:, None]
    short_final = final_norm[:short_rows].reshape(short_count, short_cap, model_width)
    long_final = final_norm[short_rows:].reshape(long_count, long_half, model_width)
    short_total = jnp.sum(short_weight, axis=1)
    short_pooled = jnp.sum(short_final * short_weight[..., None], axis=1) / short_total[:, None]
    long_partial = jnp.sum(long_final * long_weight[..., None], axis=1)
    long_sum, long_total = lax.psum((long_partial, jnp.sum(long_weight, axis=1)), "seq")
    long_pooled = long_sum / long_total[:, None]
    grad_short = (
        short_cot.astype(jnp.float32) * short_live[..., None]
        + short_weight[..., None] * short_pool_cot[:, None, :] / short_total[:, None, None]
    )
    grad_long = (
        long_cot.astype(jnp.float32) * long_live[..., None]
        + long_weight[..., None] * long_pool_cot[:, None, :] / long_total[:, None, None]
    )
    grad_top = jnp.concatenate(
        [grad_short.reshape(short_rows, model_width), grad_long.reshape(long_rows, model_width)],
        axis=0,
    )
    _, second_back = jax.vjp(layer_norm, second_in, gains[:, 1], shifts[:, 1])
    grad_second, grad_gain_two, grad_shift_two = second_back(grad_top)
    grad_branch = grad_second.astype(jnp.bfloat16)
    grad_down = outer_sum(activated, grad_branch)
    grad_bias_two = jnp.sum(grad_branch.astype(jnp.float32), axis=0)
    grad_acted = times_transposed(grad_branch, down_matrix)
    _, gelu_back = jax.vjp(exact_gelu, inner_act)
    grad_inner = gelu_back(grad_acted)[0].astype(jnp.bfloat16)
    grad_up = outer_sum(first_low, grad_inner)
    grad_up_bias = jnp.sum(grad_inner.astype(jnp.float32), axis=0)
    grad_first = grad_second + times_transposed(grad_inner, up_matrix)
    _, first_back = jax.vjp(layer_norm, first_in, gains[:, 0], shifts[:, 0])
    grad_first_in, grad_gain_one, grad_shift_one = first_back(grad_first)
    grad_attn = grad_first_in.astype(jnp.bfloat16)
    grad_out = outer_sum(mixed_heads, grad_attn)
    grad_bias_one = jnp.sum(grad_attn.astype(jnp.float32), axis=0)
    grad_mixed = times_transposed(grad_attn, out_matrix).astype(jnp.bfloat16)
    short_dq, short_dk, short_dv = by_blocks(
        backward_blocks,
        short_block,
        (
            short_q,
            short_k,
            short_v,
            short_live,
            grad_mixed[:short_rows].reshape(short_shape),
            short_logsum,
        ),
    )
    again_k, again_v = (gathered_k, gathered_v)
    long_dq, long_dk, long_dv = by_blocks(
        backward_blocks,
        long_block,
        (
            long_q,
            again_k.reshape(full_shape),
            again_v.reshape(full_shape),
            long_key_live,
            grad_mixed[short_rows:].reshape(long_shape),
            long_logsum,
        ),
    )
    own_dk, own_dv = (
        lax.psum_scatter(
            long_dk.reshape(long_count, full_len, model_width).astype(jnp.bfloat16),
            "seq",
            scatter_dimension=1,
            tiled=True,
        ).astype(jnp.float32),
        lax.psum_scatter(
            long_dv.reshape(long_count, full_len, model_width).astype(jnp.bfloat16),
            "seq",
            scatter_dimension=1,
            tiled=True,
        ).astype(jnp.float32),
    )
    grad_queries = jnp.concatenate(
        [short_dq.reshape(short_rows, model_width), long_dq.reshape(long_rows, model_width)], axis=0
    ).astype(jnp.bfloat16)
    grad_keys = jnp.concatenate(
        [short_dk.reshape(short_rows, model_width), own_dk.reshape(long_rows, model_width)], axis=0
    ).astype(jnp.bfloat16)
    grad_values = jnp.concatenate(
        [short_dv.reshape(short_rows, model_width), own_dv.reshape(long_rows, model_width)], axis=0
    ).astype(jnp.bfloat16)
    grad_joined = jnp.concatenate([grad_queries, grad_keys, grad_values], axis=1)
    grad_qkv = outer_sum(inputs, grad_joined)
    grad_qv = jnp.stack(
        [
            jnp.sum(grad_queries.astype(jnp.float32), axis=0),
            jnp.sum(grad_values.astype(jnp.float32), axis=0),
        ],
        axis=1,
    )
    grad_inputs = grad_first_in + times_transposed(grad_joined, qkv_matrix)
    grad_out_vec = jnp.stack([grad_bias_one, grad_bias_two], axis=1)
    grad_gains = jnp.stack([grad_gain_one, grad_gain_two], axis=1)
    grad_shifts = jnp.stack([grad_shift_one, grad_shift_two], axis=1)
    shard_grads = (
        lax.psum_scatter(grad_qkv, ("dp", "seq"), scatter_dimension=0, tiled=True),
        lax.psum_scatter(grad_out, ("dp", "seq"), scatter_dimension=0, tiled=True),
        lax.psum_scatter(grad_up, ("dp", "seq"), scatter_dimension=0, tiled=True),
        lax.psum_scatter(grad_down, ("dp", "seq"), scatter_dimension=0, tiled=True),
        lax.psum_scatter(grad_qv, ("dp", "seq"), scatter_dimension=0, tiled=True),
        lax.psum_scatter(grad_out_vec, ("dp", "seq"), scatter_dimension=0, tiled=True),
        lax.psum_scatter(grad_up_bias, ("dp", "seq"), scatter_dimension=0, tiled=True),
        lax.psum_scatter(grad_gains, ("dp", "seq"), scatter_dimension=0, tiled=True),
        lax.psum_scatter(grad_shifts, ("dp", "seq"), scatter_dimension=0, tiled=True),
    )
    short_out = short_final.astype(jnp.bfloat16)
    long_out = long_final.astype(jnp.bfloat16)
    short_grad_in = grad_inputs[:short_rows].reshape(short_count, short_cap, model_width)
    long_grad_in = grad_inputs[short_rows:].reshape(long_count, long_half, model_width)
    return (
        short_out,
        long_out,
        short_pooled,
        long_pooled,
        short_grad_in,
        long_grad_in,
        shard_grads[0],
        shard_grads[1],
        shard_grads[2],
        shard_grads[3],
        shard_grads[4],
        shard_grads[5],
        shard_grads[6],
        shard_grads[7],
        shard_grads[8],
    )


def fast_shards(
    short_tokens, long_tokens, short_len, long_len, short_pool, long_pool, short_cot, long_cot,
    short_pool_cot, long_pool_cot, w_qkv, w_out, w_up, w_down, qv_bias, out_bias, up_bias,
    norm_gain, norm_shift,
):
    groups = lax.axis_size("dp") // 4
    width = w_out.shape[1]
    count, cap, _ = short_tokens.shape
    short_rows = count * cap
    lengths = (short_len, long_len)
    parameters = (
        w_qkv, w_out, w_up, w_down, qv_bias.T, out_bias.T, norm_gain.T, norm_shift.T, up_bias[None, :],
    )
    (down, *kept, vectors, share) = forward(
        lengths,
        parameters,
        (short_pool, long_pool),
        short_tokens.reshape(short_rows, width),
        long_tokens,
        groups,
    )
    arrays = backward(
        lengths,
        vectors,
        share,
        (short_pool_cot, long_pool_cot),
        (short_cot.reshape(short_rows, width), long_cot),
        (down.reshape(4, width, width), *kept),
        groups,
    )
    (
        short_out, long_out, short_pooled, long_pooled, short_grad, long_grad,
        grad_qkv, grad_out, grad_up, grad_down, qv, out, ups, gain, shift,
    ) = results(arrays)
    return (
        short_out.reshape(short_tokens.shape), long_out, short_pooled, long_pooled,
        short_grad.reshape(short_tokens.shape), long_grad, grad_qkv, grad_out, grad_up, grad_down,
        qv.T, out.T, ups[0], gain.T, shift.T,
    )


def solution(mesh):
    short_spec, long_spec, spread = P(("dp", "seq"), None, None), P("dp", "seq", None), P(("dp", "seq"), None)
    vector, parameters = P(("dp", "seq")), [P(("dp", "seq"), None)] * 6
    in_specs = (
        short_spec, long_spec, vector, P("dp"), spread, P("dp", "seq"), short_spec, long_spec,
        spread, P("dp", None), *parameters, vector, spread, spread,
    )
    out_specs = (
        short_spec, long_spec, spread, P("dp", None), short_spec, long_spec, *parameters, vector,
        spread, spread,
    )
    dp, seq = mesh.shape["dp"], mesh.shape["seq"]

    def run(*arrays):
        width = arrays[11].shape[1]
        passages = arrays[1].shape[0] // dp
        regular = dp == 16 and seq == 2 and passages == 2 and width == 24 * dp * seq
        body = fast_shards if regular else general_shards
        return jax.shard_map(body, mesh=mesh, in_specs=in_specs, out_specs=out_specs, check_vma=False)(*arrays)

    return run
```

```python
import functools
import math

import jax
import jax.numpy as jnp
from jax import lax
from jax.experimental import pallas as pl
from jax.experimental.pallas import tpu as pltpu
from jax.sharding import PartitionSpec as P

HEADS = 12
EPS = 1e-12
MESH = pl.DeviceIdType.MESH

SIZES = (80, 32, 96, 96)
GATHER_X = (48, 16, 48, 48)
SUMS = (80, 80, 80, 32, 96, 96)
SUMS_X = (32, 48, 32, 16, 48, 48)


FLIPS = ((0, 0), (0, 1), (1, 0), (1, 1))


class Place:
    def __init__(self):
        dp = lax.axis_index("dp")
        self.x = lax.axis_index("seq")
        self.groups = lax.axis_size("dp") // 4
        self.z = lax.div(dp, 4)
        self.y = lax.rem(lax.div(dp, 2), 2)
        self.c = lax.rem(dp, 2)
        self.dp = dp

    def z_of(self, step):
        if step == 1:
            return self.z + 1 - 2 * lax.rem(self.z, 2)
        return lax.rem(self.z + 2, 4) if step == 2 else 3 - self.z

    def at_z(self, step):
        return (self.z_of(step) * 4 + self.y * 2 + self.c, self.x)

    def at_x(self):
        return (self.dp, 1 - self.x)

    def at_y(self):
        return (self.z * 4 + (1 - self.y) * 2 + self.c, self.x)

    def at_core(self):
        return (self.z * 4 + self.y * 2 + 1 - self.c, self.x)

    def slot(self, flip_y=0, flip_c=0, flip_x=0):
        y = 1 - self.y if flip_y else self.y
        c = 1 - self.c if flip_c else self.c
        x = 1 - self.x if flip_x else self.x
        return y * 4 + c * 2 + x

    def z_back(self, step):
        return self.z if step == 0 else self.z_of(step)

    def partners(self):
        return [self.at_z(step) for step in range(1, self.groups)] + [
            self.at_x(),
            self.at_y(),
            self.at_core(),
        ]

    def greet_start(self):
        for partner in self.partners():
            pl.semaphore_signal(
                pltpu.get_barrier_semaphore(), inc=1, device_id=partner, device_id_type=MESH
            )

    def greet_wait(self):
        pl.semaphore_wait(pltpu.get_barrier_semaphore(), len(self.partners()))


class Wires:
    def __init__(self, send, recv):
        self.send, self.recv, self.sent, self.left = send, recv, [], set()

    def put(self, src, dst, to):
        number = len(self.sent)
        copy = pltpu.make_async_remote_copy(
            src_ref=src,
            dst_ref=dst,
            send_sem=self.send.at[number],
            recv_sem=self.recv.at[number],
            device_id=to,
            device_id_type=MESH,
        )
        copy.start()
        self.sent.append(copy)
        return (number, to)

    def landed(self, ticket, ref):
        number, to = ticket
        pltpu.make_async_remote_copy(
            src_ref=ref,
            dst_ref=ref,
            send_sem=self.send.at[number],
            recv_sem=self.recv.at[number],
            device_id=to,
            device_id_type=MESH,
        ).wait_recv()

    def has_left(self, ticket):
        self.sent[ticket[0]].wait_send()
        self.left.add(ticket[0])

    def close(self):
        for number, copy in enumerate(self.sent):
            if number not in self.left:
                copy.wait_send()


class Gather:
    def __init__(self, wires, place, wholes, last):
        self.wires, self.place, self.wholes, self.last = wires, place, wholes, last
        self.steps = place.groups
        self.along_z, self.along_x, self.along_y = {}, {}, {}
        self.by_x, self.by_y, self.core = {}, {}, {}

    def halves(self, k):
        some = GATHER_X[k]
        return pl.ds(0, some), pl.ds(some, SIZES[k] - some)

    def start(self, k):
        place, wires = self.place, self.wires
        dst = self.wholes[k].at[place.z, place.slot()]
        src = self.last if k == 3 else dst
        for step in range(1, self.steps):
            self.along_z[k, step] = wires.put(src, dst, place.at_z(step))

    def start_plane(self, k):
        place, wires = self.place, self.wires
        dst = self.wholes[k].at[place.z, place.slot()]
        src = self.last if k == 3 else dst
        self.along_x[k, 0] = wires.put(src, dst, place.at_x())
        self.along_y[k, 0] = wires.put(src, dst, place.at_y())
        self.core[k, 0, 0] = wires.put(src, dst, place.at_core())

    def relay_z(self, k):
        place, wires = self.place, self.wires
        for step in range(1, self.steps):
            ref = self.wholes[k].at[place.z_back(step), place.slot()]
            wires.landed(self.along_z[k, step], ref)
            self.along_x[k, step] = wires.put(ref, ref, place.at_x())
            self.along_y[k, step] = wires.put(ref, ref, place.at_y())
            self.core[k, 0, step] = wires.put(ref, ref, place.at_core())

    def relay_plane(self, k):
        upper, lower = self.halves(k)
        place, wires, whole = self.place, self.wires, self.wholes[k]
        for step in range(self.steps):
            z = place.z_back(step)
            slot = place.slot(flip_x=1)
            ref = whole.at[z, slot]
            wires.landed(self.along_x[k, step], ref)
            half = whole.at[z, slot, upper]
            self.by_y[k, step] = wires.put(half, half, place.at_y())
            self.core[k, 1, step] = wires.put(ref, ref, place.at_core())
            slot = place.slot(flip_y=1)
            ref = whole.at[z, slot]
            wires.landed(self.along_y[k, step], ref)
            half = whole.at[z, slot, lower]
            self.by_x[k, step] = wires.put(half, half, place.at_x())
            self.core[k, 2, step] = wires.put(ref, ref, place.at_core())

    def relay_corner(self, k):
        upper, lower = self.halves(k)
        place, wires, whole = self.place, self.wires, self.wholes[k]
        slot = place.slot(flip_x=1, flip_y=1)
        for step in range(self.steps):
            z = place.z_back(step)
            wires.landed(self.by_y[k, step], whole.at[z, slot, upper])
            wires.landed(self.by_x[k, step], whole.at[z, slot, lower])
            ref = whole.at[z, slot]
            self.core[k, 3, step] = wires.put(ref, ref, place.at_core())

    def finish(self, k):
        place = self.place
        for part, (flip_y, flip_x) in enumerate(FLIPS):
            slot = place.slot(flip_y=flip_y, flip_c=1, flip_x=flip_x)
            for step in range(self.steps):
                ref = self.wholes[k].at[place.z_back(step), slot]
                self.wires.landed(self.core[k, part, step], ref)


class Scatter:
    def __init__(self, wires, place, grads, from_core, from_x, from_y, last_x, last_y, from_z):
        self.wires, self.place, self.grads = wires, place, grads
        self.from_core, self.from_x, self.from_y = from_core, from_x, from_y
        self.last_x, self.last_y, self.from_z = last_x, last_y, from_z
        self.steps = place.groups
        self.core, self.first, self.second, self.third = {}, {}, {}, {}

    def halves(self, k):
        some = SUMS_X[k]
        return pl.ds(0, some), pl.ds(some, SUMS[k] - some)

    def own(self, k, part, rows):
        flip_y, flip_x = FLIPS[part]
        return self.grads[k].at[:, self.place.slot(flip_y=flip_y, flip_x=flip_x), rows]

    def send_core(self, k):
        place = self.place
        for part in (3, 1, 2, 0):
            flip_y, flip_x = FLIPS[part]
            slot = place.slot(flip_y=flip_y, flip_c=1, flip_x=flip_x)
            self.core[k, part] = self.wires.put(
                self.grads[k].at[:, slot], self.from_core[k].at[part], place.at_core()
            )

    def add(self, into, other):
        def one(z, carry):
            total = into[z].astype(jnp.float32) + other[z].astype(jnp.float32)
            into[z] = total.astype(into.dtype)
            return carry

        lax.fori_loop(0, self.steps, one, 0)

    def after_core(self, k):
        upper, lower = self.halves(k)
        whole = pl.ds(0, SUMS[k])
        wires, place = self.wires, self.place
        for part in (3, 1, 2, 0):
            wires.landed(self.core[k, part], self.from_core[k].at[part])
            self.add(self.own(k, part, whole), self.from_core[k].at[part])
            if part == 3:
                self.first[k, "x", 1] = wires.put(
                    self.own(k, 3, upper), self.from_x[k].at[1], place.at_x()
                )
                self.first[k, "y", 1] = wires.put(
                    self.own(k, 3, lower), self.from_y[k].at[1], place.at_y()
                )
            elif part == 1:
                self.first[k, "x", 0] = wires.put(
                    self.own(k, 1, upper), self.from_x[k].at[0], place.at_x()
                )
            elif part == 2:
                self.first[k, "y", 0] = wires.put(
                    self.own(k, 2, lower), self.from_y[k].at[0], place.at_y()
                )

    def after_first(self, k):
        upper, lower = self.halves(k)
        wires, place = self.wires, self.place
        wires.landed(self.first[k, "x", 1], self.from_x[k].at[1])
        self.add(self.own(k, 2, upper), self.from_x[k].at[1])
        self.second[k, "y"] = wires.put(self.own(k, 2, upper), self.last_y[k], place.at_y())
        wires.landed(self.first[k, "y", 1], self.from_y[k].at[1])
        self.add(self.own(k, 1, lower), self.from_y[k].at[1])
        self.second[k, "x"] = wires.put(self.own(k, 1, lower), self.last_x[k], place.at_x())
        wires.landed(self.first[k, "x", 0], self.from_x[k].at[0])
        self.add(self.own(k, 0, upper), self.from_x[k].at[0])
        wires.landed(self.first[k, "y", 0], self.from_y[k].at[0])
        self.add(self.own(k, 0, lower), self.from_y[k].at[0])

    def after_second(self, k):
        upper, lower = self.halves(k)
        wires, place = self.wires, self.place
        wires.landed(self.second[k, "y"], self.last_y[k])
        self.add(self.own(k, 0, upper), self.last_y[k])
        wires.landed(self.second[k, "x"], self.last_x[k])
        self.add(self.own(k, 0, lower), self.last_x[k])
        for step in range(1, self.steps):
            z = place.z_of(step)
            self.third[k, step] = wires.put(
                self.grads[k].at[z, place.slot()], self.from_z[k].at[step - 1], place.at_z(step)
            )

    def finish(self, k):
        place = self.place
        total = self.grads[k][place.z, place.slot()].astype(jnp.float32)
        for step in range(1, self.steps):
            self.wires.landed(self.third[k, step], self.from_z[k].at[step - 1])
            total = total + self.from_z[k][step - 1].astype(jnp.float32)
        return total


def times(a, b):
    return lax.dot_general(a, b, (((1,), (0,)), ((), ())), preferred_element_type=jnp.float32)


def times_turned(a, b):
    return lax.dot_general(a, b, (((1,), (1,)), ((), ())), preferred_element_type=jnp.float32)


def turned_times(a, b):
    return lax.dot_general(a, b, (((0,), (0,)), ((), ())), preferred_element_type=jnp.float32)


def aligned(index, size):
    return pl.ds(pl.multiple_of(index * size, size), size)


def head_masks(lanes, head_dim):
    lane = lax.broadcasted_iota(jnp.int32, (1, lanes), 1)
    return [
        jnp.where((lane >= h * head_dim) & (lane < (h + 1) * head_dim), 1.0, 0.0).astype(jnp.bfloat16)
        for h in range(lanes // head_dim)
    ]


def gelu_and_slope(u):
    near = 1.0 / (1.0 + (0.3275911 * math.sqrt(0.5)) * jnp.abs(u))
    bell = jnp.exp(-0.5 * (u * u))
    series = near * (
        0.127414796
        + near * (-0.142248368 + near * (0.7107068705 + near * (-0.7265760135 + near * 0.5307027145)))
    )
    tail = series * bell
    below = jnp.where(u < 0.0, tail, 1.0 - tail)
    return u * below, below + u * (bell * (1.0 / math.sqrt(2.0 * math.pi)))


def assemble(source, first, blocks, target):
    per_z, size = source.shape[1] // 2, 24

    def one(i, carry):
        z, pair = lax.div(i, per_z), lax.rem(i, per_z)
        left = source[z, 2 * pair].astype(jnp.float32)
        right = source[z, 2 * pair + 1].astype(jnp.float32)
        for b in range(blocks):
            rows = slice(first + b * size, first + (b + 1) * size)
            both = jnp.concatenate([left[rows], right[rows]], axis=0)
            target[b, aligned(i, 2 * size), :] = both.astype(target.dtype)
        return carry

    lax.fori_loop(0, source.shape[0] * per_z, one, 0)


def sum_slabs(source, first):
    def one(i, total):
        per_z = source.shape[1]
        slab = source[lax.div(i, per_z), lax.rem(i, per_z)].astype(jnp.float32)
        return total + slab[first : first + 8]

    count = source.shape[0] * source.shape[1]
    return lax.fori_loop(0, count, one, jnp.zeros((8, source.shape[-1]), jnp.float32))


def normalize(row_data):
    center = row_data - jnp.mean(row_data, axis=-1, keepdims=True)
    spread = jnp.mean(center * center, axis=-1, keepdims=True)
    scale = lax.rsqrt(spread + EPS)
    return center * scale, scale


def weights_forward(queries, keys_all, live):
    scores = jnp.where(live, times_turned(queries, keys_all), -1e30)
    exponent = jnp.exp(scores - jnp.max(scores, axis=-1, keepdims=True))
    return (exponent * (1.0 / jnp.sum(exponent, axis=-1, keepdims=True))).astype(jnp.bfloat16)


def as_column(row):
    size = row.shape[1]
    down = lax.broadcasted_iota(jnp.int32, (size, size), 0)
    across = lax.broadcasted_iota(jnp.int32, (size, size), 1)
    return jnp.sum(jnp.where(down == across, row, 0.0), axis=1, keepdims=True)


def put_at(row, start, width):
    size = row.shape[1]
    down = lax.broadcasted_iota(jnp.int32, (size, width), 0)
    across = lax.broadcasted_iota(jnp.int32, (size, width), 1)
    return jnp.sum(jnp.where(across == down + start, as_column(row), 0.0), axis=0, keepdims=True)


def forward_kernel(
    short_len, long_len, w_qkv, w_out, w_up, w_down, qv_bias, out_bias, gains, shifts, up_bias,
    short_pool, long_pool, short_tok, long_tok,
    out_down, out_wq, out_wu, out_rows, out_qkv, out_short_probs, out_long_probs, out_mixed,
    out_first, out_hat, out_scale, out_low, out_acted, out_slope, vectors, share,
    whole0, whole1, whole2, wq, wu, rows_in, qkv, short_probs, long_probs, mixed,
    first, hat, scale, low, acted, slope, far_pool,
    send, recv, here, leave,
):
    place = Place()
    x, other = place.x, 1 - place.x
    short_rows, half = short_tok.shape[0], long_tok.shape[1]
    total_rows, width = rows_in.shape
    long_rows = 2 * half
    count, cap = short_pool.shape
    mine = pl.ds(pl.multiple_of(short_rows + x * half, half), half)
    theirs = pl.ds(pl.multiple_of(short_rows + other * half, half), half)
    local = []

    def move(src, dst):
        copy = pltpu.make_async_copy(src, dst, here.at[len(local)])
        copy.start()
        local.append(copy)
        return copy

    move(w_down, out_down.at[place.z, place.slot()])
    loads = [
        move(short_tok, rows_in.at[pl.ds(0, short_rows)]),
        move(long_tok.at[x], rows_in.at[mine]),
    ]
    place.greet_start()

    device = place.dp * 2 + x
    size = w_out.shape[0]

    def blocks(matrix):
        data = matrix[...].astype(jnp.float32)
        return [data[:, i * width : (i + 1) * width] for i in range(data.shape[1] // width)]

    pairs = [
        put_at(member[i : i + 1, :].astype(jnp.float32), device * size, width)
        for member in (qv_bias, out_bias, gains, shifts)
        for i in range(2)
    ]
    ups = put_at(up_bias[...].astype(jnp.float32), lax.rem(device, 8) * (4 * size), width)
    ups = jnp.where(lax.broadcasted_iota(jnp.int32, (8, 1), 0) == lax.div(device, 8), ups, 0.0)
    z, slot = place.z, place.slot()
    whole0[z, slot] = jnp.concatenate(blocks(w_qkv) + pairs, axis=0).astype(jnp.bfloat16)
    whole1[z, slot] = jnp.concatenate(blocks(w_out) + [ups], axis=0).astype(jnp.bfloat16)
    whole2[z, slot] = jnp.concatenate(blocks(w_up), axis=0).astype(jnp.bfloat16)

    place.greet_wait()
    wires = Wires(send, recv)
    net = Gather(wires, place, (whole0, whole1, whole2, out_down), w_down)
    net.start(0)
    net.start(1)
    net.start_plane(2)
    net.start(2)
    net.start_plane(1)
    net.start_plane(0)
    pooled = wires.put(long_pool, far_pool, place.at_x())
    net.relay_z(0)
    net.relay_plane(0)
    tok = wires.put(long_tok.at[other], rows_in.at[mine], place.at_x())
    net.relay_z(1)
    net.relay_corner(0)
    for copy in loads:
        copy.wait()
    net.finish(0)
    assemble(whole0, 0, 3, wq)
    vectors[0:8, :] = sum_slabs(whole0, 72)

    head_dim = width // HEADS
    score_scale = 1.0 / math.sqrt(head_dim)

    def project(i, carry):
        rows = aligned(i, 256)
        data = rows_in[rows, :]
        queries = times(data, wq[0]) + vectors[0:1, :]
        qkv[0, rows, :] = (queries.astype(jnp.bfloat16).astype(jnp.float32) * score_scale).astype(jnp.bfloat16)
        qkv[1, rows, :] = times(data, wq[1]).astype(jnp.bfloat16)
        qkv[2, rows, :] = (times(data, wq[2]) + vectors[1:2, :]).astype(jnp.bfloat16)
        return carry

    lax.fori_loop(0, short_rows // 256, project, 0)

    masks = head_masks(2 * head_dim, head_dim)
    keep_first = lax.broadcasted_iota(jnp.int32, (1, 2 * head_dim), 1) < head_dim
    place_in_block = lax.broadcasted_iota(jnp.int32, (1, cap), 1)
    short_live = [place_in_block < short_len[i] for i in range(count)]
    passage_len = long_len[x]
    long_live = lax.broadcasted_iota(jnp.int32, (1, long_rows), 1) < passage_len
    pairs = width // (2 * head_dim)

    def attend_short(pair, carry):
        lanes = aligned(pair, 2 * head_dim)
        blocks_of = [pl.ds(i * cap, cap) for i in range(count)]
        queries, keys_all, values = [[qkv[b, rows, lanes] for rows in blocks_of] for b in range(3)]
        units = [(i, h) for i in range(count) for h in range(2)]
        scores = [times_turned(queries[i] * masks[h], keys_all[i]) for i, h in units]
        scores = [jnp.where(short_live[i], part, -1e30) for (i, h), part in zip(units, scores)]
        tops = [jnp.max(part, axis=-1, keepdims=True) for part in scores]
        exponents = [jnp.exp(part - top) for part, top in zip(scores, tops)]
        totals = [jnp.sum(part, axis=-1, keepdims=True) for part in exponents]
        probs = [(part * (1.0 / total)).astype(jnp.bfloat16) for part, total in zip(exponents, totals)]
        parts = [times(part, values[i]) for (i, h), part in zip(units, probs)]
        for (i, h), part in zip(units, probs):
            short_probs[i, 2 * pair + h] = part
        for i in range(count):
            mixed[blocks_of[i], lanes] = jnp.where(keep_first, parts[2 * i], parts[2 * i + 1]).astype(jnp.bfloat16)
        return carry

    lax.fori_loop(0, pairs // 2, attend_short, 0)
    net.relay_z(2)
    lax.fori_loop(pairs // 2, pairs - 1, attend_short, 0)
    net.start(3)
    net.relay_plane(1)
    lax.fori_loop(pairs - 1, pairs, attend_short, 0)
    net.start_plane(3)
    move(short_probs, out_short_probs)
    wires.landed(tok, rows_in.at[theirs])
    lax.fori_loop(short_rows // 256, total_rows // 256, project, 0)
    move(qkv, out_qkv)
    move(rows_in, out_rows)

    wires.landed(pooled, far_pool)
    chosen = []
    for block in range(total_rows // cap):
        if block < count:
            mask, start = short_pool[block : block + 1, :], 0
            limit = short_len[block]
        else:
            step = block - count
            in_half, start = step % (half // cap) * cap, step * cap
            at = slice(in_half, in_half + cap)
            own = jnp.where(x == 0, long_pool[0:1, at], long_pool[1:2, at])
            far = jnp.where(x == 0, far_pool[0:1, at], far_pool[1:2, at])
            mask = jnp.where(x == step // (half // cap), own, far)
            limit = passage_len - start
        keep = (place_in_block < limit) & ((mask > 0) | (place_in_block + start == 0))
        chosen.append(jnp.where(keep, 1.0, 0.0))
    for block in range(count):
        share[block : block + 1, :] = chosen[block] / jnp.sum(chosen[block], axis=-1, keepdims=True)
    long_total = sum(jnp.sum(row, axis=-1, keepdims=True) for row in chosen[count:])
    for block in range(count, total_rows // cap):
        share[block : block + 1, :] = chosen[block] / long_total

    def attend_long(pair, carry):
        lanes = aligned(pair, 2 * head_dim)
        rows = pl.ds(short_rows, long_rows)
        keys_all, values = qkv[1, rows, lanes], qkv[2, rows, lanes]
        for block in range(long_rows // 256):
            inner = pl.ds(block * 256, 256)
            rows = pl.ds(short_rows + block * 256, 256)
            queries = qkv[0, rows, lanes]
            parts = []
            for h in range(2):
                probs = weights_forward(queries * masks[h], keys_all, long_live)
                long_probs[2 * pair + h, inner, :] = probs
                parts.append(times(probs, values))
            mixed[rows, lanes] = jnp.where(keep_first, parts[0], parts[1]).astype(jnp.bfloat16)
        return carry

    lax.fori_loop(0, pairs - 2, attend_long, 0)
    net.relay_plane(2)
    net.relay_corner(1)
    lax.fori_loop(pairs - 2, pairs - 1, attend_long, 0)
    net.relay_z(3)
    lax.fori_loop(pairs - 1, pairs, attend_long, 0)
    move(long_probs, out_long_probs)
    move(mixed, out_mixed)
    net.finish(1)
    assemble(whole1, 0, 1, wq.at[pl.ds(3, 1)])
    vectors[8:16, :] = sum_slabs(whole1, 24)
    move(wq, out_wq)

    def attach(i, carry):
        rows = aligned(i, 256)
        first_in = rows_in[rows, :].astype(jnp.float32) + (times(mixed[rows, :], wq[3]) + vectors[2:3, :])
        normal, factor = normalize(first_in)
        out = normal * vectors[4:5, :] + vectors[6:7, :]
        first[rows, :] = out
        low[rows, :] = out.astype(jnp.bfloat16)
        hat[rows, :] = normal.astype(jnp.bfloat16)
        scale[rows, :] = jnp.broadcast_to(factor, (256, scale.shape[1]))
        return carry

    lax.fori_loop(0, total_rows // 256, attach, 0)
    move(first, out_first)
    move(low, out_low)
    move(hat, out_hat)
    move(scale, out_scale)
    net.relay_corner(2)
    net.finish(2)
    assemble(whole2, 0, 4, wu)
    move(wu, out_wu)

    def leaving(i):
        j, rows = lax.div(i, 4), aligned(lax.rem(i, 4), 256)
        return (
            pltpu.make_async_copy(acted.at[j, rows], out_acted.at[j, rows], leave.at[0, i]),
            pltpu.make_async_copy(slope.at[j, rows], out_slope.at[j, rows], leave.at[1, i]),
        )

    def expand(i, carry):
        j, rows = lax.div(i, 4), aligned(lax.rem(i, 4), 256)
        inner = times(low[rows, :], wu[j]) + vectors[pl.ds(8 + j, 1), :]
        value, grad = gelu_and_slope(inner)
        acted[j, rows, :] = value.astype(jnp.bfloat16)
        slope[j, rows, :] = grad.astype(jnp.bfloat16)
        for copy in leaving(i):
            copy.start()
        return carry

    def left(i, carry):
        for copy in leaving(i):
            copy.wait()
        return carry

    lax.fori_loop(0, 7, expand, 0)
    net.relay_plane(3)
    lax.fori_loop(7, 14, expand, 0)
    net.relay_corner(3)
    lax.fori_loop(14, 16, expand, 0)
    net.finish(3)
    wires.close()
    lax.fori_loop(0, 16, left, 0)
    for copy in [local[0]] + local[3:]:
        copy.wait()


def forward(lengths, parameters, pools, short_tok, long_tok, groups):
    short_rows, width = short_tok.shape
    half = long_tok.shape[1]
    long_rows = 2 * half
    rows = short_rows + long_rows
    count, cap = pools[0].shape
    inner = 4 * width
    copies = 4 * ((groups - 1) + 4 * groups + 4 * groups) + 2
    low = jnp.bfloat16
    shape = jax.ShapeDtypeStruct
    outs = (
        shape((groups, 8, SIZES[3], width), low),
        shape((4, width, width), low),
        shape((4, width, width), low),
        shape((rows, width), low),
        shape((3, rows, width), low),
        shape((count, HEADS, cap, cap), low),
        shape((HEADS, long_rows, long_rows), low),
        shape((rows, width), low),
        shape((rows, width), jnp.float32),
        shape((rows, width), low),
        shape((rows, 128), jnp.float32),
        shape((rows, width), low),
        shape((inner // width, rows, width), low),
        shape((inner // width, rows, width), low),
        shape((16, width), jnp.float32),
        shape((rows // cap, cap), jnp.float32),
    )
    anywhere, near = pl.BlockSpec(memory_space=pl.ANY), pl.BlockSpec(memory_space=pltpu.VMEM)
    scalars = pl.BlockSpec(memory_space=pltpu.SMEM)
    kept = [pltpu.VMEM(out.shape, out.dtype) for out in outs[1:14]]
    return pl.pallas_call(
        forward_kernel,
        name="forward",
        out_shape=outs,
        in_specs=[scalars] * 2 + [near] * 11 + [anywhere] * 2,
        out_specs=[anywhere] * 14 + [near] * 2,
        scratch_shapes=[pltpu.VMEM((groups, 8, SIZES[k], width), low) for k in range(3)]
        + kept
        + [
            pltpu.VMEM(pools[1].shape, pools[1].dtype),
            pltpu.SemaphoreType.DMA((copies,)),
            pltpu.SemaphoreType.DMA((copies,)),
            pltpu.SemaphoreType.DMA((24,)),
            pltpu.SemaphoreType.DMA((2, 16)),
        ],
        compiler_params=pltpu.CompilerParams(
            collective_id=0, has_side_effects=True, vmem_limit_bytes=60 * 1024 * 1024
        ),
    )(*lengths, *parameters, *pools, short_tok, long_tok)


def backward_kernel(
    short_len, long_len, vectors, share, short_pool_cot, long_pool_cot, short_cot, long_cot,
    in_down, in_wq, in_wu, in_rows, in_qkv, in_short_probs, in_long_probs, in_mixed,
    in_first, in_hat, in_scale, in_low, in_acted, in_slope,
    short_out, long_out, short_grad, long_grad, short_pooled, long_pooled,
    grad_qkv, grad_out, grad_up, grad_down, grad_vectors, grad_up_vector,
    wide, pair, w_up, w_far, hat, sums, branch, low, scale, halves, probs_short,
    vector_sums, pool_cots, pooled_rows, pooled_own, pooled_far,
    *more,
):
    place = Place()
    x, other = place.x, 1 - place.x
    *chunks, send, recv, here, blocks, fetch = more
    parts = len(SUMS)
    grads, *received = [chunks[i * parts : (i + 1) * parts] for i in range(7)]
    total_rows, width = sums.shape
    short_rows = short_out.shape[0]
    count, cap = probs_short.shape[1], probs_short.shape[-1]
    long_rows = total_rows - short_rows
    half = long_rows // 2
    head_dim = width // HEADS
    steps = total_rows // 256
    low_type = jnp.bfloat16
    local = []

    def move(src, dst):
        copy = pltpu.make_async_copy(src, dst, here.at[len(local)])
        copy.start()
        local.append(copy)
        return copy

    mine = pl.ds(pl.multiple_of(short_rows + x * half, half), half)
    theirs = pl.ds(pl.multiple_of(short_rows + other * half, half), half)
    place.greet_start()
    load_down = [move(in_down.at[j], w_far.at[j]) for j in range(4)]
    load_down += [
        move(short_cot, branch.at[pl.ds(0, short_rows)]),
        move(long_cot.at[x], branch.at[mine]),
    ]
    passage_len = long_len[x]

    def block_at(step):
        return jnp.where(step < 2, step, 2 + lax.rem(step + x, 2))

    def block_copies(i):
        rows = aligned(i, 256)
        return (
            pltpu.make_async_copy(in_acted.at[:, rows], wide.at[:, rows], blocks.at[0, i]),
            pltpu.make_async_copy(in_first.at[rows], sums.at[rows], blocks.at[1, i]),
        )

    for copy in block_copies(0):
        copy.start()
    vector_sums[...] = jnp.zeros_like(vector_sums)
    pool_cots[0:count, :] = short_pool_cot[...]
    pool_cots[count : 2 * count, :] = jnp.broadcast_to(long_pool_cot[pl.ds(x, 1), :], (count, width))
    place.greet_wait()
    wires = Wires(send, recv)
    swap_cot = wires.put(long_cot.at[other], branch.at[mine], place.at_x())
    net = Scatter(wires, place, grads, *received)
    for copy in load_down:
        copy.wait()
    tall = lax.broadcasted_iota(jnp.int32, (256, 1), 0)
    diagonal = lax.broadcasted_iota(jnp.int32, (cap, cap), 0) == lax.broadcasted_iota(jnp.int32, (cap, cap), 1)

    def add_vector(row, rows):
        vector_sums[row : row + 1, :] += jnp.sum(rows, axis=0, keepdims=True)

    def second(step, carry):
        i = block_at(step)
        rows = aligned(i, 256)

        @pl.when(step == steps - 1)
        def _():
            wires.landed(swap_cot, branch.at[theirs])

        @pl.when(step < steps - 1)
        def _():
            for copy in block_copies(block_at(step + 1)):
                copy.start()

        for copy in block_copies(i):
            copy.wait()
        product = times(wide[0, rows, :], w_far[0])
        for j in range(1, 4):
            product += times(wide[j, rows, :], w_far[j])
        normal, factor = normalize(sums[rows, :] + (product + vectors[3:4, :]))
        lens = [
            jnp.where(2 * i + part < count, short_len[lax.rem(2 * i + part, count)], passage_len - (2 * i + part - count) * cap)
            for part in range(2)
        ]
        live = tall < jnp.where(tall < cap, lens[0], lens[1] + cap)
        final = jnp.where(live, normal * vectors[5:6, :] + vectors[7:8, :], 0.0)
        low[rows, :] = final.astype(low_type)
        spread = []
        for part in range(2):
            share_row = share[pl.ds(2 * i + part, 1), :]
            column = jnp.sum(jnp.where(diagonal, share_row, 0.0), axis=1, keepdims=True)
            piece = final[part * cap : (part + 1) * cap]
            pooled_rows[pl.ds(2 * i + part, 1), :] = jnp.sum(piece * column, axis=0, keepdims=True)
            spread.append(column * pool_cots[pl.ds(2 * i + part, 1), :])
        grad_final = jnp.where(live, branch[rows, :].astype(jnp.float32), 0.0) + jnp.concatenate(spread, axis=0)
        add_vector(5, grad_final * normal)
        add_vector(7, grad_final)
        scaled = grad_final * vectors[5:6, :]
        mean_one = jnp.mean(scaled, axis=-1, keepdims=True)
        mean_two = jnp.mean(scaled * normal, axis=-1, keepdims=True)
        grad_second = factor * (scaled - mean_one - normal * mean_two)
        sums[rows, :] = grad_second
        grad_branch = grad_second.astype(low_type)
        branch[rows, :] = grad_branch
        add_vector(3, grad_branch.astype(jnp.float32))
        return carry

    lax.fori_loop(0, steps, second, 0)
    short_pooled[...] = pooled_rows[0:count, :]
    own_pooled = jnp.sum(pooled_rows[count : 2 * count, :], axis=0, keepdims=True)
    pooled_own[...] = jnp.broadcast_to(own_pooled, pooled_own.shape)
    long_pooled[pl.ds(x, 1), :] = own_pooled
    out_copies = [
        move(low.at[pl.ds(0, short_rows)], short_out),
        move(low.at[mine], long_out.at[x]),
    ]
    load_slope = [move(in_slope.at[0], pair.at[0]), move(in_slope.at[1], pair.at[1])]
    load_up = move(in_wu, w_up)
    load_hat, load_scale = move(in_hat, hat), move(in_scale, scale)

    swap_out = wires.put(low.at[theirs], long_out.at[x], place.at_x())
    swap_pooled = wires.put(pooled_own, pooled_far, place.at_x())

    def down_step(i, carry):
        j, part = lax.div(i, 2), lax.rem(i, 2)
        product = turned_times(wide[j, :, aligned(part, width // 2)], branch[...])
        grads[5][j, aligned(part, 4)] = product.reshape(4, SUMS[5], width).astype(low_type)
        return carry

    lax.fori_loop(0, 8, down_step, 0, unroll=2)
    net.send_core(5)

    def inner_block(j):
        def inner(i, carry):
            rows = aligned(i, 256)
            product = times_turned(branch[rows, :], w_far[j]) * pair[j % 2, rows, :].astype(jnp.float32)
            grad_inner = product.astype(low_type)
            wide[j, rows, :] = grad_inner
            add_vector(8 + j, grad_inner.astype(jnp.float32))
            return carry

        lax.fori_loop(0, steps, inner, 0, unroll=2)

    load_slope[0].wait()
    inner_block(0)
    load_slope.append(move(in_slope.at[2], pair.at[0]))
    load_slope[1].wait()
    inner_block(1)
    load_slope.append(move(in_slope.at[3], pair.at[1]))
    for copy in out_copies:
        copy.wait()
    wires.has_left(swap_out)
    load_low = move(in_low, low)
    load_slope[2].wait()
    inner_block(2)
    net.after_core(5)
    load_mixed = move(in_mixed, pair.at[0])
    load_slope[3].wait()
    inner_block(3)
    load_wq = move(in_wq, w_far)

    def up_step(i, carry):
        r, both = lax.div(i, 2), lax.rem(i, 2)
        data = low[:, aligned(r, width // 2)]
        halves[0] = turned_times(data, wide[2 * both])
        halves[1] = turned_times(data, wide[2 * both + 1])

        def one(k, carry):
            rows = pl.ds(pl.multiple_of(k * 24, 8), 24)
            data = jnp.concatenate([halves[0, rows, :], halves[1, rows, :]], axis=0)
            grads[4][2 * r + lax.div(k, 8), lax.rem(k, 8), aligned(both, 48), :] = data.astype(low_type)
            return carry

        return lax.fori_loop(0, 16, one, carry)

    load_low.wait()
    lax.fori_loop(0, 4, up_step, 0)
    net.send_core(4)

    load_up.wait()
    load_hat.wait()
    load_scale.wait()

    def first_back(i, carry):
        rows = aligned(i, 256)
        grad_first = sums[rows, :]
        for j in range(4):
            grad_first += times_turned(wide[j, rows, :], w_up[j])
        normal = hat[rows, :].astype(jnp.float32)
        add_vector(4, grad_first * normal)
        add_vector(6, grad_first)
        scaled = grad_first * vectors[4:5, :]
        mean_one = jnp.mean(scaled, axis=-1, keepdims=True)
        mean_two = jnp.mean(scaled * normal, axis=-1, keepdims=True)
        grad_in = scale[rows, 0:1] * (scaled - mean_one - normal * mean_two)
        sums[rows, :] = grad_in
        grad_attn = grad_in.astype(low_type)
        branch[rows, :] = grad_attn
        add_vector(2, grad_attn.astype(jnp.float32))
        return carry

    lax.fori_loop(0, steps // 2, first_back, 0)
    net.after_first(5)
    net.after_core(4)
    lax.fori_loop(steps // 2, steps, first_back, 0)
    load_qkv = move(in_qkv, wide.at[pl.ds(0, 3)])
    load_rows = move(in_rows, wide.at[3])
    net.after_second(5)

    load_mixed.wait()
    load_wq.wait()
    def out_step(r, carry):
        halves[0] = turned_times(pair[0, :, aligned(r, width // 2)], branch[...])

        def one(k, carry):
            rows = pl.ds(pl.multiple_of(k * 24, 8), 24)
            data = jnp.concatenate([halves[0, rows, :], vector_sums[8:16, :]], axis=0)
            grads[3][2 * r + lax.div(k, 8), lax.rem(k, 8)] = data.astype(low_type)
            return carry

        return lax.fori_loop(0, 16, one, carry)

    lax.fori_loop(0, 2, out_step, 0)

    def mixed_back(i, carry):
        rows = aligned(i, 256)
        pair[1, rows, :] = times_turned(branch[rows, :], w_far[3]).astype(low_type)
        return carry

    lax.fori_loop(0, steps, mixed_back, 0)
    net.send_core(3)

    def probs_copies(p, slot):
        lanes = pl.ds(2 * p, 2)
        return (
            pltpu.make_async_copy(in_short_probs.at[:, lanes], probs_short.at[slot], fetch.at[0, slot]),
            pltpu.make_async_copy(
                in_long_probs.at[lanes],
                w_up.at[pl.ds(2 * slot, 2), pl.ds(0, long_rows), pl.ds(0, long_rows)],
                fetch.at[1, slot],
            ),
        )

    for copy in probs_copies(0, 0):
        copy.start()
    load_qkv.wait()
    score_scale = 1.0 / math.sqrt(head_dim)
    masks = head_masks(2 * head_dim, head_dim)
    pairs = width // (2 * head_dim)

    def attend_back(lanes, units):
        heads = [(u, h) for u in range(len(units)) for h in range(2)]
        queries = [wide[0, rows, lanes] for rows, _, _, _ in units]
        grads_mixed = [pair[1, rows, lanes] for rows, _, _, _ in units]
        overlaps = [
            grad.astype(jnp.float32) * pair[0, rows, lanes].astype(jnp.float32)
            for grad, (rows, _, _, _) in zip(grads_mixed, units)
        ]
        centers = [
            jnp.sum(overlaps[u] * masks[h].astype(jnp.float32), axis=-1, keepdims=True) for u, h in heads
        ]
        grads_head = [grads_mixed[u] * masks[h] for u, h in heads]
        probs = [units[u][1](h) for u, h in heads]
        grads_probs = [times_turned(grad, units[u][3]) for grad, (u, h) in zip(grads_head, heads)]
        scores = [
            (part.astype(jnp.float32) * (grad - center)).astype(low_type)
            for part, grad, center in zip(probs, grads_probs, centers)
        ]
        grads_q = [times(part, units[u][2] * masks[h]) for part, (u, h) in zip(scores, heads)]
        grads_k = [turned_times(queries[u] * masks[h], part) for part, (u, h) in zip(scores, heads)]
        grads_v = [turned_times(grad, part) for part, grad in zip(probs, grads_head)]
        for u, (rows, _, _, _) in enumerate(units):
            total = grads_q[2 * u] + grads_q[2 * u + 1]
            wide[0, rows, lanes] = (total * score_scale).astype(low_type)
        return [
            [grads[2 * u] + grads[2 * u + 1] for u in range(len(units))] for grads in (grads_k, grads_v)
        ]

    def attention_back(p, carry):
        slot = lax.rem(p, 2)
        for copy in probs_copies(p, slot):
            copy.wait()

        @pl.when(p + 1 < pairs)
        def _():
            for copy in probs_copies(p + 1, 1 - slot):
                copy.start()

        lanes = aligned(p, 2 * head_dim)
        blocks_of = [pl.ds(i * cap, cap) for i in range(count)]
        units = [
            (rows, lambda h, i=i: probs_short[slot, i, h], wide[1, rows, lanes], wide[2, rows, lanes])
            for i, rows in enumerate(blocks_of)
        ]
        grads_k, grads_v = attend_back(lanes, units)
        for rows, grad_k, grad_v in zip(blocks_of, grads_k, grads_v):
            wide[1, rows, lanes] = grad_k.T.astype(low_type)
            wide[2, rows, lanes] = grad_v.T.astype(low_type)
        rows = pl.ds(short_rows, long_rows)
        keys_all, values = wide[1, rows, lanes], wide[2, rows, lanes]
        total_k, total_v = None, None
        for block in range(long_rows // 256):
            inner = pl.ds(block * 256, 256)
            unit = (
                pl.ds(short_rows + block * 256, 256),
                lambda h, inner=inner: w_up[2 * slot + h, inner, 0:long_rows],
                keys_all,
                values,
            )
            (grad_k,), (grad_v,) = attend_back(lanes, [unit])
            total_k = grad_k if total_k is None else total_k + grad_k
            total_v = grad_v if total_v is None else total_v + grad_v
        wide[1, rows, lanes] = total_k.T.astype(low_type)
        wide[2, rows, lanes] = total_v.T.astype(low_type)
        return carry

    third = width // 3

    def qkv_step(group):
        lanes = pl.ds(group * third, third)

        def bias(i, carry):
            rows = aligned(i, 256)
            for row, b in ((0, 0), (1, 2)):
                piece = wide[b, rows, lanes].astype(jnp.float32)
                vector_sums[row : row + 1, lanes] += jnp.sum(piece, axis=0, keepdims=True)
            return carry

        lax.fori_loop(0, steps, bias, 0)

        def step(r, carry):
            data = wide[3, :, aligned(r, width // 2)]
            for b in range(3):
                halves[0, :, b * third : (b + 1) * third] = turned_times(data, wide[b, :, lanes])

            def one(k, carry):
                rows = pl.ds(pl.multiple_of(k * 24, 8), 24)
                pieces = [halves[0, rows, b * third : (b + 1) * third] for b in range(3)]
                data = jnp.concatenate(pieces + [vector_sums[0:8, lanes]], axis=0)
                grads[group][2 * r + lax.div(k, 8), lax.rem(k, 8)] = data.astype(low_type)
                return carry

            return lax.fori_loop(0, 16, one, carry)

        lax.fori_loop(0, 2, step, 0)

    lax.fori_loop(0, pairs // 3, attention_back, 0)
    load_rows.wait()
    qkv_step(0)
    net.after_first(4)
    net.after_core(3)
    net.send_core(0)
    lax.fori_loop(pairs // 3, 2 * pairs // 3, attention_back, 0)
    qkv_step(1)
    net.after_second(4)
    net.send_core(1)
    net.after_core(0)
    net.after_first(3)
    net.after_core(1)
    lax.fori_loop(2 * pairs // 3, pairs, attention_back, 0)
    qkv_step(2)
    net.send_core(2)
    net.after_first(0)
    net.after_second(3)

    def tokens_back(rows):
        grad_in = sums[rows, :]
        for b in range(3):
            grad_in += times_turned(wide[b, rows, :], w_far[b])
        return grad_in

    far_low, far_in = low.at[pl.ds(0, half)], low.at[pl.ds(half, half)]
    far_low[...] = tokens_back(theirs).astype(low_type)
    net.after_first(1)

    def tokens_step(i, carry):
        rows = pl.ds(pl.multiple_of(jnp.where(i < 2, i * 256, short_rows + x * half), 256), 256)
        sums[rows, :] = tokens_back(rows)
        return carry

    net.after_core(2)
    lax.fori_loop(0, 2, tokens_step, 0)
    net.after_second(0)
    net.after_second(1)
    net.after_first(2)
    swap_grad = wires.put(far_low, far_in, place.at_x())
    net.after_second(2)
    lax.fori_loop(2, 3, tokens_step, 0)
    move(sums.at[pl.ds(0, short_rows)], short_grad)
    move(sums.at[mine], long_grad.at[x])
    grad_down[...] = net.finish(5)
    total = net.finish(4)
    for j in range(4):
        grad_up[:, j * width : (j + 1) * width] = total[24 * j : 24 * j + 24]
    total = net.finish(3)
    grad_out[...] = total[0:24]
    grad_up_vector[...] = total[24:32]
    wires.landed(swap_pooled, pooled_far)
    long_pooled[pl.ds(other, 1), :] = pooled_far[0:1, :]
    wires.landed(swap_grad, far_in)
    sums[theirs, :] = far_in[...].astype(jnp.float32)
    move(sums.at[theirs], long_grad.at[other])
    wires.landed(swap_out, long_out.at[other])
    for group in range(3):
        total = net.finish(group)
        for b in range(3):
            columns = slice(b * width + group * third, b * width + (group + 1) * third)
            grad_qkv[:, columns] = total[24 * b : 24 * b + 24]
        grad_vectors[:, group * third : (group + 1) * third] = total[72:80]
    wires.close()
    for copy in local[-3:]:
        copy.wait()


def backward(lengths, vectors, share, pool_cots, cots, arrays, groups):
    width = vectors.shape[1]
    rows = arrays[3].shape[0]
    count, _, cap, _ = arrays[5].shape
    short_rows = count * cap
    half = (rows - short_rows) // 2
    low, wide_type = jnp.bfloat16, jnp.float32
    shape = jax.ShapeDtypeStruct
    rows24 = 24
    outs = (
        shape((short_rows, width), low),
        shape((2, half, width), low),
        shape((short_rows, width), wide_type),
        shape((2, half, width), wide_type),
        shape((count, width), wide_type),
        shape((2, width), wide_type),
        shape((rows24, 3 * width), wide_type),
        shape((rows24, width), wide_type),
        shape((rows24, 4 * width), wide_type),
        shape((4 * rows24, width), wide_type),
        shape((8, width), wide_type),
        shape((8, width), wide_type),
    )
    anywhere, near = pl.BlockSpec(memory_space=pl.ANY), pl.BlockSpec(memory_space=pltpu.VMEM)
    copies = len(SUMS) * (4 + 6 + (groups - 1)) + 4

    widths = (width // 3,) * 3 + (width,) * 3

    def chunks(parts, sizes):
        return [pltpu.VMEM(parts + (size, columns), low) for size, columns in zip(sizes, widths)]

    rest = tuple(size - some for size, some in zip(SUMS, SUMS_X))
    scratch = [
        pltpu.VMEM((4, rows, width), low),
        pltpu.VMEM((2, rows, width), low),
        pltpu.VMEM((4, width, width), low),
        pltpu.VMEM((4, width, width), low),
        pltpu.VMEM((rows, width), low),
        pltpu.VMEM((rows, width), wide_type),
        pltpu.VMEM((rows, width), low),
        pltpu.VMEM((rows, width), low),
        pltpu.VMEM((rows, 128), wide_type),
        pltpu.VMEM((2, width // 2, width), wide_type),
        pltpu.VMEM((2, count, 2, cap, cap), low),
        pltpu.VMEM((16, width), wide_type),
        pltpu.VMEM((2 * count, width), wide_type),
        pltpu.VMEM((2 * count, width), wide_type),
        pltpu.VMEM((8, width), wide_type),
        pltpu.VMEM((8, width), wide_type),
        *chunks((groups, 8), SUMS),
        *chunks((4, groups), SUMS),
        *chunks((2, groups), SUMS_X),
        *chunks((2, groups), rest),
        *chunks((groups,), rest),
        *chunks((groups,), SUMS_X),
        *chunks((groups - 1,), SUMS),
        pltpu.SemaphoreType.DMA((copies,)),
        pltpu.SemaphoreType.DMA((copies,)),
        pltpu.SemaphoreType.DMA((24,)),
        pltpu.SemaphoreType.DMA((2, rows // 256)),
        pltpu.SemaphoreType.DMA((2, 2)),
    ]
    return pl.pallas_call(
        backward_kernel,
        name="backward",
        out_shape=outs,
        in_specs=[pl.BlockSpec(memory_space=pltpu.SMEM)] * 2 + [near] * 4 + [anywhere] * 16,
        out_specs=[anywhere] * 4 + [near] * 8,
        scratch_shapes=scratch,
        compiler_params=pltpu.CompilerParams(
            collective_id=1, has_side_effects=True, vmem_limit_bytes=63 * 1024 * 1024
        ),
    )(*lengths, vectors, share, *pool_cots, *cots, *arrays)


def results_kernel(
    in_0, in_1, in_2, in_3, in_4, in_5, in_6, in_7, in_8, in_9, grad_vectors, grad_ups,
    out_0, out_1, out_2, out_3, out_4, out_5, out_6, out_7, out_8, out_9, pair_0, pair_1, ups, pair_2, pair_3,
    *more,
):
    *held, come, leave = more
    sources = (in_0, in_1, in_2, in_3, in_4, in_5, in_6, in_7, in_8, in_9)
    places = (out_0, out_1, out_4, out_5, out_2, out_3, out_6, out_7, out_8, out_9)
    ins = [pltpu.make_async_copy(sources[i], held[i], come.at[i]) for i in range(10)]
    outs = [pltpu.make_async_copy(held[i], places[i], leave.at[i]) for i in range(10)]
    for copy in ins:
        copy.start()
    device = lax.axis_index("dp") * 2 + lax.axis_index("seq")
    size, width = in_7.shape
    rows = pltpu.roll(grad_vectors[...], lax.rem(width - device * size, width), 1)
    for i, ref in enumerate((pair_0, pair_1, pair_2, pair_3)):
        ref[...] = rows[2 * i : 2 * i + 2, 0:size]
    start = lax.rem(device, 8) * (4 * size)
    row = grad_ups[pl.ds(lax.div(device, 8), 1), :]
    row = pltpu.roll(jnp.broadcast_to(row, (8, width)), lax.rem(width - start, width), 1)
    ups[...] = row[0:1, 0 : 4 * size]
    for i in range(10):
        ins[i].wait()
        outs[i].start()
    for copy in outs:
        copy.wait()


def results(arrays):
    size = arrays[7].shape[0]
    order = (0, 1, 4, 5, 2, 3, 6, 7, 8, 9)
    shape = jax.ShapeDtypeStruct
    pair = shape((2, size), jnp.float32)
    outs = tuple(shape(arrays[i].shape, arrays[i].dtype) for i in order)
    anywhere, near = pl.BlockSpec(memory_space=pl.ANY), pl.BlockSpec(memory_space=pltpu.VMEM)
    return pl.pallas_call(
        results_kernel,
        name="results",
        out_shape=outs + (pair, pair, shape((1, 4 * size), jnp.float32), pair, pair),
        in_specs=[anywhere] * 10 + [near] * 2,
        out_specs=[anywhere] * 10 + [near] * 5,
        scratch_shapes=[pltpu.VMEM(array.shape, array.dtype) for array in arrays[:10]]
        + [pltpu.SemaphoreType.DMA((10,)), pltpu.SemaphoreType.DMA((10,))],
        compiler_params=pltpu.CompilerParams(vmem_limit_bytes=56 * 1024 * 1024),
    )(*arrays)


def layer_norm(row_data, gain_vec, shift_vec):
    center = row_data - jnp.mean(row_data, axis=-1, keepdims=True)
    spread = jnp.mean(center * center, axis=-1, keepdims=True)
    return center * lax.rsqrt(spread + EPS) * gain_vec + shift_vec


def exact_gelu(inner_act):
    return jax.nn.gelu(inner_act, approximate=False)


def outer_sum(left_rows, right_rows):
    return lax.dot_general(
        left_rows, right_rows, (((0,), (0,)), ((), ())), preferred_element_type=jnp.float32
    )


def times_transposed(left_rows, matrix):
    return lax.dot_general(
        left_rows, matrix, (((1,), (1,)), ((), ())), preferred_element_type=jnp.float32
    )


def masked_scores(queries, keys_all, key_live, score_scale):
    scores = (
        jnp.einsum("bqhe,bkhe->bhqk", queries, keys_all, preferred_element_type=jnp.float32)
        * score_scale
    )
    return jnp.where(key_live[:, None, None, :], scores, -1e30)


def attend_forward(pieces, score_scale):
    queries, keys_all, values, key_live = pieces
    scores = masked_scores(queries, keys_all, key_live, score_scale)
    highest = jnp.max(scores, axis=-1, keepdims=True)
    exponent = jnp.exp(scores - highest)
    totals = jnp.sum(exponent, axis=-1, keepdims=True)
    soft_probs = (exponent / totals).astype(jnp.bfloat16)
    mixed_heads = jnp.einsum(
        "bhqk,bkhe->bqhe", soft_probs, values, preferred_element_type=jnp.float32
    )
    return (mixed_heads.astype(jnp.bfloat16), (highest + jnp.log(totals))[..., 0])


def attend_backward(pieces, score_scale):
    queries, keys_all, values, key_live, grad_mixed, log_total = pieces
    scores = masked_scores(queries, keys_all, key_live, score_scale)
    soft_probs = jnp.exp(scores - log_total[..., None])
    grad_probs = jnp.einsum(
        "bqhe,bkhe->bhqk", grad_mixed, values, preferred_element_type=jnp.float32
    )
    grad_values = jnp.einsum(
        "bhqk,bqhe->bkhe",
        soft_probs.astype(jnp.bfloat16),
        grad_mixed,
        preferred_element_type=jnp.float32,
    )
    center = jnp.sum(soft_probs * grad_probs, axis=-1, keepdims=True)
    grad_scores = (soft_probs * (grad_probs - center)).astype(jnp.bfloat16)
    grad_queries = (
        jnp.einsum("bhqk,bkhe->bqhe", grad_scores, keys_all, preferred_element_type=jnp.float32)
        * score_scale
    )
    grad_keys = (
        jnp.einsum("bhqk,bqhe->bkhe", grad_scores, queries, preferred_element_type=jnp.float32)
        * score_scale
    )
    return (grad_queries, grad_keys, grad_values)


def by_blocks(function, per_block, arrays):
    blocks = arrays[0].shape[0] // per_block
    stacked = tuple((member.reshape((blocks, per_block) + member.shape[1:]) for member in arrays))
    results = lax.map(function, stacked)
    return jax.tree.map(
        lambda member: member.reshape((blocks * per_block,) + member.shape[2:]), results
    )


def general_shards(
    short_tokens,
    long_tokens,
    short_len,
    long_len,
    short_pool,
    long_pool,
    short_cot,
    long_cot,
    short_pool_cot,
    long_pool_cot,
    w_qkv,
    w_out,
    w_up,
    w_down,
    qv_bias,
    out_bias,
    up_bias,
    norm_gain,
    norm_shift,
):
    gathered = (
        lax.all_gather(w_qkv, ("dp", "seq"), axis=0, tiled=True),
        lax.all_gather(w_out, ("dp", "seq"), axis=0, tiled=True),
        lax.all_gather(w_up, ("dp", "seq"), axis=0, tiled=True),
        lax.all_gather(w_down, ("dp", "seq"), axis=0, tiled=True),
        lax.all_gather(qv_bias, ("dp", "seq"), axis=0, tiled=True),
        lax.all_gather(out_bias, ("dp", "seq"), axis=0, tiled=True),
        lax.all_gather(up_bias, ("dp", "seq"), axis=0, tiled=True),
        lax.all_gather(norm_gain, ("dp", "seq"), axis=0, tiled=True),
        lax.all_gather(norm_shift, ("dp", "seq"), axis=0, tiled=True),
    )
    qkv_matrix, out_matrix, up_matrix, down_matrix, qv_vec, out_vec, up_vec, gains, shifts = (
        gathered
    )
    gains = gains.astype(jnp.float32)
    shifts = shifts.astype(jnp.float32)
    short_count, short_cap, model_width = short_tokens.shape
    long_count, long_half = (long_tokens.shape[0], long_tokens.shape[1])
    head_count = HEADS
    head_dim = model_width // head_count
    score_scale = 1.0 / math.sqrt(head_dim)
    short_rows = short_count * short_cap
    long_rows = long_count * long_half
    short_place = jnp.arange(short_cap, dtype=jnp.int32)
    short_live = short_place[None, :] < short_len[:, None]
    long_place = lax.axis_index("seq") * long_half + jnp.arange(long_half, dtype=jnp.int32)
    long_live = long_place[None, :] < long_len[:, None]
    short_weight = (short_live & ((short_pool > 0) | (short_place[None, :] == 0))).astype(
        jnp.float32
    )
    long_weight = (long_live & ((long_pool > 0) | (long_place[None, :] == 0))).astype(jnp.float32)
    row_live = jnp.concatenate([short_live.reshape(-1), long_live.reshape(-1)]).astype(jnp.float32)
    inputs = jnp.concatenate(
        [
            short_tokens.reshape(short_rows, model_width),
            long_tokens.reshape(long_rows, model_width),
        ],
        axis=0,
    )
    joined = jnp.dot(inputs, qkv_matrix, preferred_element_type=jnp.float32)
    queries = (joined[:, :model_width] + qv_vec[:, 0]).astype(jnp.bfloat16)
    keys_all = joined[:, model_width : 2 * model_width].astype(jnp.bfloat16)
    values = (joined[:, 2 * model_width :] + qv_vec[:, 1]).astype(jnp.bfloat16)
    short_shape = (short_count, short_cap, head_count, head_dim)
    long_shape = (long_count, long_half, head_count, head_dim)
    short_q = queries[:short_rows].reshape(short_shape)
    short_k = keys_all[:short_rows].reshape(short_shape)
    short_v = values[:short_rows].reshape(short_shape)
    long_q = queries[short_rows:].reshape(long_shape)
    long_k = keys_all[short_rows:].reshape(long_count, long_half, model_width)
    long_v = values[short_rows:].reshape(long_count, long_half, model_width)
    short_block = math.gcd(short_count, max(1, 512 // short_cap))
    long_block = math.gcd(long_count, max(1, 512 // long_half))

    def forward_blocks(pieces):
        return attend_forward(pieces, score_scale)

    def backward_blocks(pieces):
        return attend_backward(pieces, score_scale)

    short_mixed, short_logsum = by_blocks(
        forward_blocks, short_block, (short_q, short_k, short_v, short_live)
    )
    gathered_k, gathered_v = (
        lax.all_gather(long_k, "seq", axis=1, tiled=True),
        lax.all_gather(long_v, "seq", axis=1, tiled=True),
    )
    full_len = gathered_k.shape[1]
    full_shape = (long_count, full_len, head_count, head_dim)
    long_key_live = jnp.arange(full_len, dtype=jnp.int32)[None, :] < long_len[:, None]
    long_mixed, long_logsum = by_blocks(
        forward_blocks,
        long_block,
        (long_q, gathered_k.reshape(full_shape), gathered_v.reshape(full_shape), long_key_live),
    )
    mixed_heads = jnp.concatenate(
        [short_mixed.reshape(short_rows, model_width), long_mixed.reshape(long_rows, model_width)],
        axis=0,
    )
    attn_out = jnp.dot(mixed_heads, out_matrix, preferred_element_type=jnp.float32) + out_vec[:, 0]
    first_in = inputs.astype(jnp.float32) + attn_out
    first_norm = layer_norm(first_in, gains[:, 0], shifts[:, 0])
    first_low = first_norm.astype(jnp.bfloat16)
    inner_act = jnp.dot(first_low, up_matrix, preferred_element_type=jnp.float32) + up_vec
    activated = exact_gelu(inner_act).astype(jnp.bfloat16)
    branch = jnp.dot(activated, down_matrix, preferred_element_type=jnp.float32) + out_vec[:, 1]
    second_in = first_norm + branch
    final_norm = layer_norm(second_in, gains[:, 1], shifts[:, 1]) * row_live[:, None]
    short_final = final_norm[:short_rows].reshape(short_count, short_cap, model_width)
    long_final = final_norm[short_rows:].reshape(long_count, long_half, model_width)
    short_total = jnp.sum(short_weight, axis=1)
    short_pooled = jnp.sum(short_final * short_weight[..., None], axis=1) / short_total[:, None]
    long_partial = jnp.sum(long_final * long_weight[..., None], axis=1)
    long_sum, long_total = lax.psum((long_partial, jnp.sum(long_weight, axis=1)), "seq")
    long_pooled = long_sum / long_total[:, None]
    grad_short = (
        short_cot.astype(jnp.float32) * short_live[..., None]
        + short_weight[..., None] * short_pool_cot[:, None, :] / short_total[:, None, None]
    )
    grad_long = (
        long_cot.astype(jnp.float32) * long_live[..., None]
        + long_weight[..., None] * long_pool_cot[:, None, :] / long_total[:, None, None]
    )
    grad_top = jnp.concatenate(
        [grad_short.reshape(short_rows, model_width), grad_long.reshape(long_rows, model_width)],
        axis=0,
    )
    _, second_back = jax.vjp(layer_norm, second_in, gains[:, 1], shifts[:, 1])
    grad_second, grad_gain_two, grad_shift_two = second_back(grad_top)
    grad_branch = grad_second.astype(jnp.bfloat16)
    grad_down = outer_sum(activated, grad_branch)
    grad_bias_two = jnp.sum(grad_branch.astype(jnp.float32), axis=0)
    grad_acted = times_transposed(grad_branch, down_matrix)
    _, gelu_back = jax.vjp(exact_gelu, inner_act)
    grad_inner = gelu_back(grad_acted)[0].astype(jnp.bfloat16)
    grad_up = outer_sum(first_low, grad_inner)
    grad_up_bias = jnp.sum(grad_inner.astype(jnp.float32), axis=0)
    grad_first = grad_second + times_transposed(grad_inner, up_matrix)
    _, first_back = jax.vjp(layer_norm, first_in, gains[:, 0], shifts[:, 0])
    grad_first_in, grad_gain_one, grad_shift_one = first_back(grad_first)
    grad_attn = grad_first_in.astype(jnp.bfloat16)
    grad_out = outer_sum(mixed_heads, grad_attn)
    grad_bias_one = jnp.sum(grad_attn.astype(jnp.float32), axis=0)
    grad_mixed = times_transposed(grad_attn, out_matrix).astype(jnp.bfloat16)
    short_dq, short_dk, short_dv = by_blocks(
        backward_blocks,
        short_block,
        (
            short_q,
            short_k,
            short_v,
            short_live,
            grad_mixed[:short_rows].reshape(short_shape),
            short_logsum,
        ),
    )
    again_k, again_v = (gathered_k, gathered_v)
    long_dq, long_dk, long_dv = by_blocks(
        backward_blocks,
        long_block,
        (
            long_q,
            again_k.reshape(full_shape),
            again_v.reshape(full_shape),
            long_key_live,
            grad_mixed[short_rows:].reshape(long_shape),
            long_logsum,
        ),
    )
    own_dk, own_dv = (
        lax.psum_scatter(
            long_dk.reshape(long_count, full_len, model_width).astype(jnp.bfloat16),
            "seq",
            scatter_dimension=1,
            tiled=True,
        ).astype(jnp.float32),
        lax.psum_scatter(
            long_dv.reshape(long_count, full_len, model_width).astype(jnp.bfloat16),
            "seq",
            scatter_dimension=1,
            tiled=True,
        ).astype(jnp.float32),
    )
    grad_queries = jnp.concatenate(
        [short_dq.reshape(short_rows, model_width), long_dq.reshape(long_rows, model_width)], axis=0
    ).astype(jnp.bfloat16)
    grad_keys = jnp.concatenate(
        [short_dk.reshape(short_rows, model_width), own_dk.reshape(long_rows, model_width)], axis=0
    ).astype(jnp.bfloat16)
    grad_values = jnp.concatenate(
        [short_dv.reshape(short_rows, model_width), own_dv.reshape(long_rows, model_width)], axis=0
    ).astype(jnp.bfloat16)
    grad_joined = jnp.concatenate([grad_queries, grad_keys, grad_values], axis=1)
    grad_qkv = outer_sum(inputs, grad_joined)
    grad_qv = jnp.stack(
        [
            jnp.sum(grad_queries.astype(jnp.float32), axis=0),
            jnp.sum(grad_values.astype(jnp.float32), axis=0),
        ],
        axis=1,
    )
    grad_inputs = grad_first_in + times_transposed(grad_joined, qkv_matrix)
    grad_out_vec = jnp.stack([grad_bias_one, grad_bias_two], axis=1)
    grad_gains = jnp.stack([grad_gain_one, grad_gain_two], axis=1)
    grad_shifts = jnp.stack([grad_shift_one, grad_shift_two], axis=1)
    shard_grads = (
        lax.psum_scatter(grad_qkv, ("dp", "seq"), scatter_dimension=0, tiled=True),
        lax.psum_scatter(grad_out, ("dp", "seq"), scatter_dimension=0, tiled=True),
        lax.psum_scatter(grad_up, ("dp", "seq"), scatter_dimension=0, tiled=True),
        lax.psum_scatter(grad_down, ("dp", "seq"), scatter_dimension=0, tiled=True),
        lax.psum_scatter(grad_qv, ("dp", "seq"), scatter_dimension=0, tiled=True),
        lax.psum_scatter(grad_out_vec, ("dp", "seq"), scatter_dimension=0, tiled=True),
        lax.psum_scatter(grad_up_bias, ("dp", "seq"), scatter_dimension=0, tiled=True),
        lax.psum_scatter(grad_gains, ("dp", "seq"), scatter_dimension=0, tiled=True),
        lax.psum_scatter(grad_shifts, ("dp", "seq"), scatter_dimension=0, tiled=True),
    )
    short_out = short_final.astype(jnp.bfloat16)
    long_out = long_final.astype(jnp.bfloat16)
    short_grad_in = grad_inputs[:short_rows].reshape(short_count, short_cap, model_width)
    long_grad_in = grad_inputs[short_rows:].reshape(long_count, long_half, model_width)
    return (
        short_out,
        long_out,
        short_pooled,
        long_pooled,
        short_grad_in,
        long_grad_in,
        shard_grads[0],
        shard_grads[1],
        shard_grads[2],
        shard_grads[3],
        shard_grads[4],
        shard_grads[5],
        shard_grads[6],
        shard_grads[7],
        shard_grads[8],
    )


def fast_shards(
    short_tokens, long_tokens, short_len, long_len, short_pool, long_pool, short_cot, long_cot,
    short_pool_cot, long_pool_cot, w_qkv, w_out, w_up, w_down, qv_bias, out_bias, up_bias,
    norm_gain, norm_shift,
):
    groups = lax.axis_size("dp") // 4
    width = w_out.shape[1]
    count, cap, _ = short_tokens.shape
    short_rows = count * cap
    lengths = (short_len, long_len)
    parameters = (
        w_qkv, w_out, w_up, w_down, qv_bias.T, out_bias.T, norm_gain.T, norm_shift.T, up_bias[None, :],
    )
    (down, *kept, vectors, share) = forward(
        lengths,
        parameters,
        (short_pool, long_pool),
        short_tokens.reshape(short_rows, width),
        long_tokens,
        groups,
    )
    arrays = backward(
        lengths,
        vectors,
        share,
        (short_pool_cot, long_pool_cot),
        (short_cot.reshape(short_rows, width), long_cot),
        (down.reshape(4, width, width), *kept),
        groups,
    )
    (
        short_out, long_out, short_pooled, long_pooled, short_grad, long_grad,
        grad_qkv, grad_out, grad_up, grad_down, qv, out, ups, gain, shift,
    ) = results(arrays)
    return (
        short_out.reshape(short_tokens.shape), long_out, short_pooled, long_pooled,
        short_grad.reshape(short_tokens.shape), long_grad, grad_qkv, grad_out, grad_up, grad_down,
        qv.T, out.T, ups[0], gain.T, shift.T,
    )


def solution(mesh):
    short_spec, long_spec, spread = P(("dp", "seq"), None, None), P("dp", "seq", None), P(("dp", "seq"), None)
    vector, parameters = P(("dp", "seq")), [P(("dp", "seq"), None)] * 6
    in_specs = (
        short_spec, long_spec, vector, P("dp"), spread, P("dp", "seq"), short_spec, long_spec,
        spread, P("dp", None), *parameters, vector, spread, spread,
    )
    out_specs = (
        short_spec, long_spec, spread, P("dp", None), short_spec, long_spec, *parameters, vector,
        spread, spread,
    )
    dp, seq = mesh.shape["dp"], mesh.shape["seq"]

    def run(*arrays):
        width = arrays[11].shape[1]
        passages = arrays[1].shape[0] // dp
        regular = dp == 16 and seq == 2 and passages == 2 and width == 24 * dp * seq
        body = fast_shards if regular else general_shards
        return jax.shard_map(body, mesh=mesh, in_specs=in_specs, out_specs=out_specs, check_vma=False)(*arrays)

    return run
```

```python
import functools
import math

import jax
import jax.numpy as jnp
from jax import lax
from jax.experimental import pallas as pl
from jax.experimental.pallas import tpu as pltpu
from jax.sharding import PartitionSpec as P

HEADS = 12
EPS = 1e-12
MESH = pl.DeviceIdType.MESH

SIZES = (80, 32, 96, 96)
GATHER_X = (48, 16, 48, 48)
SUMS = (80, 80, 80, 32, 96, 96)
SUMS_X = (48, 48, 32, 16, 48, 48)


FLIPS = ((0, 0), (0, 1), (1, 0), (1, 1))


class Place:
    def __init__(self):
        dp = lax.axis_index("dp")
        self.x = lax.axis_index("seq")
        self.groups = lax.axis_size("dp") // 4
        self.z = lax.div(dp, 4)
        self.y = lax.rem(lax.div(dp, 2), 2)
        self.c = lax.rem(dp, 2)
        self.dp = dp

    def z_of(self, step):
        if step == 1:
            return self.z + 1 - 2 * lax.rem(self.z, 2)
        return lax.rem(self.z + 2, 4) if step == 2 else 3 - self.z

    def at_z(self, step):
        return (self.z_of(step) * 4 + self.y * 2 + self.c, self.x)

    def at_x(self):
        return (self.dp, 1 - self.x)

    def at_y(self):
        return (self.z * 4 + (1 - self.y) * 2 + self.c, self.x)

    def at_core(self):
        return (self.z * 4 + self.y * 2 + 1 - self.c, self.x)

    def slot(self, flip_y=0, flip_c=0, flip_x=0):
        y = 1 - self.y if flip_y else self.y
        c = 1 - self.c if flip_c else self.c
        x = 1 - self.x if flip_x else self.x
        return y * 4 + c * 2 + x

    def z_back(self, step):
        return self.z if step == 0 else self.z_of(step)

    def partners(self):
        return [self.at_z(step) for step in range(1, self.groups)] + [
            self.at_x(),
            self.at_y(),
            self.at_core(),
        ]

    def greet_start(self):
        for partner in self.partners():
            pl.semaphore_signal(
                pltpu.get_barrier_semaphore(), inc=1, device_id=partner, device_id_type=MESH
            )

    def greet_wait(self):
        pl.semaphore_wait(pltpu.get_barrier_semaphore(), len(self.partners()))


class Wires:
    def __init__(self, send, recv):
        self.send, self.recv, self.sent, self.left = send, recv, [], set()

    def put(self, src, dst, to):
        number = len(self.sent)
        copy = pltpu.make_async_remote_copy(
            src_ref=src,
            dst_ref=dst,
            send_sem=self.send.at[number],
            recv_sem=self.recv.at[number],
            device_id=to,
            device_id_type=MESH,
        )
        copy.start()
        self.sent.append(copy)
        return (number, to)

    def landed(self, ticket, ref):
        number, to = ticket
        pltpu.make_async_remote_copy(
            src_ref=ref,
            dst_ref=ref,
            send_sem=self.send.at[number],
            recv_sem=self.recv.at[number],
            device_id=to,
            device_id_type=MESH,
        ).wait_recv()

    def has_left(self, ticket):
        self.sent[ticket[0]].wait_send()
        self.left.add(ticket[0])

    def close(self):
        for number, copy in enumerate(self.sent):
            if number not in self.left:
                copy.wait_send()


class Gather:
    def __init__(self, wires, place, wholes, last):
        self.wires, self.place, self.wholes, self.last = wires, place, wholes, last
        self.steps = place.groups
        self.along_z, self.along_x, self.along_y = {}, {}, {}
        self.by_x, self.by_y, self.core = {}, {}, {}

    def halves(self, k):
        some = GATHER_X[k]
        return pl.ds(0, some), pl.ds(some, SIZES[k] - some)

    def start(self, k):
        place, wires = self.place, self.wires
        dst = self.wholes[k].at[place.z, place.slot()]
        src = self.last if k == 3 else dst
        for step in range(1, self.steps):
            self.along_z[k, step] = wires.put(src, dst, place.at_z(step))

    def start_plane(self, k):
        place, wires = self.place, self.wires
        dst = self.wholes[k].at[place.z, place.slot()]
        src = self.last if k == 3 else dst
        self.along_x[k, 0] = wires.put(src, dst, place.at_x())
        self.along_y[k, 0] = wires.put(src, dst, place.at_y())
        self.core[k, 0, 0] = wires.put(src, dst, place.at_core())

    def relay_z(self, k):
        place, wires = self.place, self.wires
        for step in range(1, self.steps):
            ref = self.wholes[k].at[place.z_back(step), place.slot()]
            wires.landed(self.along_z[k, step], ref)
            self.along_x[k, step] = wires.put(ref, ref, place.at_x())
            self.along_y[k, step] = wires.put(ref, ref, place.at_y())
            self.core[k, 0, step] = wires.put(ref, ref, place.at_core())

    def relay_plane(self, k):
        upper, lower = self.halves(k)
        place, wires, whole = self.place, self.wires, self.wholes[k]
        for step in range(self.steps):
            z = place.z_back(step)
            slot = place.slot(flip_x=1)
            ref = whole.at[z, slot]
            wires.landed(self.along_x[k, step], ref)
            half = whole.at[z, slot, upper]
            self.by_y[k, step] = wires.put(half, half, place.at_y())
            self.core[k, 1, step] = wires.put(ref, ref, place.at_core())
            slot = place.slot(flip_y=1)
            ref = whole.at[z, slot]
            wires.landed(self.along_y[k, step], ref)
            half = whole.at[z, slot, lower]
            self.by_x[k, step] = wires.put(half, half, place.at_x())
            self.core[k, 2, step] = wires.put(ref, ref, place.at_core())

    def relay_corner(self, k):
        upper, lower = self.halves(k)
        place, wires, whole = self.place, self.wires, self.wholes[k]
        slot = place.slot(flip_x=1, flip_y=1)
        for step in range(self.steps):
            z = place.z_back(step)
            wires.landed(self.by_y[k, step], whole.at[z, slot, upper])
            wires.landed(self.by_x[k, step], whole.at[z, slot, lower])
            ref = whole.at[z, slot]
            self.core[k, 3, step] = wires.put(ref, ref, place.at_core())

    def finish(self, k):
        place = self.place
        for part, (flip_y, flip_x) in enumerate(FLIPS):
            slot = place.slot(flip_y=flip_y, flip_c=1, flip_x=flip_x)
            for step in range(self.steps):
                ref = self.wholes[k].at[place.z_back(step), slot]
                self.wires.landed(self.core[k, part, step], ref)


class Scatter:
    def __init__(self, wires, place, grads, from_core, from_x, from_y, last_x, last_y, from_z):
        self.wires, self.place, self.grads = wires, place, grads
        self.from_core, self.from_x, self.from_y = from_core, from_x, from_y
        self.last_x, self.last_y, self.from_z = last_x, last_y, from_z
        self.steps = place.groups
        self.core, self.first, self.second, self.third = {}, {}, {}, {}

    def halves(self, k):
        some = SUMS_X[k]
        return pl.ds(0, some), pl.ds(some, SUMS[k] - some)

    def own(self, k, part, rows):
        flip_y, flip_x = FLIPS[part]
        return self.grads[k].at[:, self.place.slot(flip_y=flip_y, flip_x=flip_x), rows]

    def send_core(self, k):
        place = self.place
        for part in (3, 1, 2, 0):
            flip_y, flip_x = FLIPS[part]
            slot = place.slot(flip_y=flip_y, flip_c=1, flip_x=flip_x)
            self.core[k, part] = self.wires.put(
                self.grads[k].at[:, slot], self.from_core[k].at[part], place.at_core()
            )

    def add(self, into, other):
        def one(z, carry):
            total = into[z].astype(jnp.float32) + other[z].astype(jnp.float32)
            into[z] = total.astype(into.dtype)
            return carry

        lax.fori_loop(0, self.steps, one, 0)

    def after_core(self, k):
        upper, lower = self.halves(k)
        whole = pl.ds(0, SUMS[k])
        wires, place = self.wires, self.place
        for part in (3, 1, 2, 0):
            wires.landed(self.core[k, part], self.from_core[k].at[part])
            self.add(self.own(k, part, whole), self.from_core[k].at[part])
            if part == 3:
                self.first[k, "x", 1] = wires.put(
                    self.own(k, 3, upper), self.from_x[k].at[1], place.at_x()
                )
                self.first[k, "y", 1] = wires.put(
                    self.own(k, 3, lower), self.from_y[k].at[1], place.at_y()
                )
            elif part == 1:
                self.first[k, "x", 0] = wires.put(
                    self.own(k, 1, upper), self.from_x[k].at[0], place.at_x()
                )
            elif part == 2:
                self.first[k, "y", 0] = wires.put(
                    self.own(k, 2, lower), self.from_y[k].at[0], place.at_y()
                )

    def after_first(self, k):
        upper, lower = self.halves(k)
        wires, place = self.wires, self.place
        wires.landed(self.first[k, "x", 1], self.from_x[k].at[1])
        self.add(self.own(k, 2, upper), self.from_x[k].at[1])
        self.second[k, "y"] = wires.put(self.own(k, 2, upper), self.last_y[k], place.at_y())
        wires.landed(self.first[k, "y", 1], self.from_y[k].at[1])
        self.add(self.own(k, 1, lower), self.from_y[k].at[1])
        self.second[k, "x"] = wires.put(self.own(k, 1, lower), self.last_x[k], place.at_x())
        wires.landed(self.first[k, "x", 0], self.from_x[k].at[0])
        self.add(self.own(k, 0, upper), self.from_x[k].at[0])
        wires.landed(self.first[k, "y", 0], self.from_y[k].at[0])
        self.add(self.own(k, 0, lower), self.from_y[k].at[0])

    def after_second(self, k):
        upper, lower = self.halves(k)
        wires, place = self.wires, self.place
        wires.landed(self.second[k, "y"], self.last_y[k])
        self.add(self.own(k, 0, upper), self.last_y[k])
        wires.landed(self.second[k, "x"], self.last_x[k])
        self.add(self.own(k, 0, lower), self.last_x[k])
        for step in range(1, self.steps):
            z = place.z_of(step)
            self.third[k, step] = wires.put(
                self.grads[k].at[z, place.slot()], self.from_z[k].at[step - 1], place.at_z(step)
            )

    def finish(self, k):
        place = self.place
        total = self.grads[k][place.z, place.slot()].astype(jnp.float32)
        for step in range(1, self.steps):
            self.wires.landed(self.third[k, step], self.from_z[k].at[step - 1])
            total = total + self.from_z[k][step - 1].astype(jnp.float32)
        return total


def times(a, b):
    return lax.dot_general(a, b, (((1,), (0,)), ((), ())), preferred_element_type=jnp.float32)


def times_turned(a, b):
    return lax.dot_general(a, b, (((1,), (1,)), ((), ())), preferred_element_type=jnp.float32)


def turned_times(a, b):
    return lax.dot_general(a, b, (((0,), (0,)), ((), ())), preferred_element_type=jnp.float32)


def aligned(index, size):
    return pl.ds(pl.multiple_of(index * size, size), size)


def head_masks(lanes, head_dim):
    lane = lax.broadcasted_iota(jnp.int32, (1, lanes), 1)
    return [
        jnp.where((lane >= h * head_dim) & (lane < (h + 1) * head_dim), 1.0, 0.0).astype(jnp.bfloat16)
        for h in range(lanes // head_dim)
    ]


def gelu_and_slope(u):
    near = 1.0 / (1.0 + (0.3275911 * math.sqrt(0.5)) * jnp.abs(u))
    bell = jnp.exp(-0.5 * (u * u))
    series = near * (
        0.127414796
        + near * (-0.142248368 + near * (0.7107068705 + near * (-0.7265760135 + near * 0.5307027145)))
    )
    tail = series * bell
    below = jnp.where(u < 0.0, tail, 1.0 - tail)
    return u * below, below + u * (bell * (1.0 / math.sqrt(2.0 * math.pi)))


def assemble(source, first, blocks, target):
    per_z, size = source.shape[1] // 2, 24

    def one(i, carry):
        z, pair = lax.div(i, per_z), lax.rem(i, per_z)
        left = source[z, 2 * pair].astype(jnp.float32)
        right = source[z, 2 * pair + 1].astype(jnp.float32)
        for b in range(blocks):
            rows = slice(first + b * size, first + (b + 1) * size)
            both = jnp.concatenate([left[rows], right[rows]], axis=0)
            target[b, aligned(i, 2 * size), :] = both.astype(target.dtype)
        return carry

    lax.fori_loop(0, source.shape[0] * per_z, one, 0)


def sum_slabs(source, first):
    def one(i, total):
        per_z = source.shape[1]
        slab = source[lax.div(i, per_z), lax.rem(i, per_z)].astype(jnp.float32)
        return total + slab[first : first + 8]

    count = source.shape[0] * source.shape[1]
    return lax.fori_loop(0, count, one, jnp.zeros((8, source.shape[-1]), jnp.float32))


def normalize(row_data):
    center = row_data - jnp.mean(row_data, axis=-1, keepdims=True)
    spread = jnp.mean(center * center, axis=-1, keepdims=True)
    scale = lax.rsqrt(spread + EPS)
    return center * scale, scale


def weights_forward(queries, keys_all, live):
    scores = jnp.where(live, times_turned(queries, keys_all), -1e30)
    exponent = jnp.exp(scores - jnp.max(scores, axis=-1, keepdims=True))
    return (exponent * (1.0 / jnp.sum(exponent, axis=-1, keepdims=True))).astype(jnp.bfloat16)


def as_column(row):
    size = row.shape[1]
    down = lax.broadcasted_iota(jnp.int32, (size, size), 0)
    across = lax.broadcasted_iota(jnp.int32, (size, size), 1)
    return jnp.sum(jnp.where(down == across, row, 0.0), axis=1, keepdims=True)


def put_at(row, start, width):
    size = row.shape[1]
    down = lax.broadcasted_iota(jnp.int32, (size, width), 0)
    across = lax.broadcasted_iota(jnp.int32, (size, width), 1)
    return jnp.sum(jnp.where(across == down + start, as_column(row), 0.0), axis=0, keepdims=True)


def forward_kernel(
    short_len, long_len, w_qkv, w_out, w_up, w_down, qv_bias, out_bias, gains, shifts, up_bias,
    short_pool, long_pool, short_tok, long_tok,
    out_down, out_wq, out_wu, out_rows, out_qkv, out_short_probs, out_long_probs, out_mixed,
    out_first, out_hat, out_scale, out_low, out_acted, out_slope, vectors, share,
    whole0, whole1, whole2, wq, wu, rows_in, qkv, short_probs, long_probs, mixed,
    first, hat, scale, low, acted, slope, far_pool,
    send, recv, here, leave,
):
    place = Place()
    x, other = place.x, 1 - place.x
    short_rows, half = short_tok.shape[0], long_tok.shape[1]
    total_rows, width = rows_in.shape
    long_rows = 2 * half
    count, cap = short_pool.shape
    mine = pl.ds(pl.multiple_of(short_rows + x * half, half), half)
    theirs = pl.ds(pl.multiple_of(short_rows + other * half, half), half)
    local = []

    def move(src, dst):
        copy = pltpu.make_async_copy(src, dst, here.at[len(local)])
        copy.start()
        local.append(copy)
        return copy

    move(w_down, out_down.at[place.z, place.slot()])
    loads = [
        move(short_tok, rows_in.at[pl.ds(0, short_rows)]),
        move(long_tok.at[x], rows_in.at[mine]),
    ]
    place.greet_start()

    device = place.dp * 2 + x
    size = w_out.shape[0]

    def blocks(matrix):
        data = matrix[...].astype(jnp.float32)
        return [data[:, i * width : (i + 1) * width] for i in range(data.shape[1] // width)]

    pairs = [
        put_at(member[i : i + 1, :].astype(jnp.float32), device * size, width)
        for member in (qv_bias, out_bias, gains, shifts)
        for i in range(2)
    ]
    ups = put_at(up_bias[...].astype(jnp.float32), lax.rem(device, 8) * (4 * size), width)
    ups = jnp.where(lax.broadcasted_iota(jnp.int32, (8, 1), 0) == lax.div(device, 8), ups, 0.0)
    z, slot = place.z, place.slot()
    whole0[z, slot] = jnp.concatenate(blocks(w_qkv) + pairs, axis=0).astype(jnp.bfloat16)
    whole1[z, slot] = jnp.concatenate(blocks(w_out) + [ups], axis=0).astype(jnp.bfloat16)
    whole2[z, slot] = jnp.concatenate(blocks(w_up), axis=0).astype(jnp.bfloat16)

    place.greet_wait()
    wires = Wires(send, recv)
    net = Gather(wires, place, (whole0, whole1, whole2, out_down), w_down)
    net.start(0)
    net.start(1)
    net.start_plane(2)
    net.start(2)
    net.start_plane(1)
    net.start_plane(0)
    pooled = wires.put(long_pool, far_pool, place.at_x())
    net.relay_z(0)
    net.relay_plane(0)
    tok = wires.put(long_tok.at[other], rows_in.at[mine], place.at_x())
    net.relay_z(1)
    net.relay_corner(0)
    for copy in loads:
        copy.wait()
    net.finish(0)
    assemble(whole0, 0, 3, wq)
    vectors[0:8, :] = sum_slabs(whole0, 72)

    head_dim = width // HEADS
    score_scale = 1.0 / math.sqrt(head_dim)

    def project(i, carry):
        rows = aligned(i, 256)
        data = rows_in[rows, :]
        queries = times(data, wq[0]) + vectors[0:1, :]
        qkv[0, rows, :] = (queries.astype(jnp.bfloat16).astype(jnp.float32) * score_scale).astype(jnp.bfloat16)
        qkv[1, rows, :] = times(data, wq[1]).astype(jnp.bfloat16)
        qkv[2, rows, :] = (times(data, wq[2]) + vectors[1:2, :]).astype(jnp.bfloat16)
        return carry

    lax.fori_loop(0, short_rows // 256, project, 0)

    masks = head_masks(2 * head_dim, head_dim)
    keep_first = lax.broadcasted_iota(jnp.int32, (1, 2 * head_dim), 1) < head_dim
    place_in_block = lax.broadcasted_iota(jnp.int32, (1, cap), 1)
    short_live = [place_in_block < short_len[i] for i in range(count)]
    passage_len = long_len[x]
    long_live = lax.broadcasted_iota(jnp.int32, (1, long_rows), 1) < passage_len
    pairs = width // (2 * head_dim)

    def attend_short(pair, carry):
        lanes = aligned(pair, 2 * head_dim)
        blocks_of = [pl.ds(i * cap, cap) for i in range(count)]
        queries, keys_all, values = [[qkv[b, rows, lanes] for rows in blocks_of] for b in range(3)]
        units = [(i, h) for i in range(count) for h in range(2)]
        scores = [times_turned(queries[i] * masks[h], keys_all[i]) for i, h in units]
        scores = [jnp.where(short_live[i], part, -1e30) for (i, h), part in zip(units, scores)]
        tops = [jnp.max(part, axis=-1, keepdims=True) for part in scores]
        exponents = [jnp.exp(part - top) for part, top in zip(scores, tops)]
        totals = [jnp.sum(part, axis=-1, keepdims=True) for part in exponents]
        probs = [(part * (1.0 / total)).astype(jnp.bfloat16) for part, total in zip(exponents, totals)]
        parts = [times(part, values[i]) for (i, h), part in zip(units, probs)]
        for (i, h), part in zip(units, probs):
            short_probs[i, 2 * pair + h] = part
        for i in range(count):
            mixed[blocks_of[i], lanes] = jnp.where(keep_first, parts[2 * i], parts[2 * i + 1]).astype(jnp.bfloat16)
        return carry

    lax.fori_loop(0, pairs // 2, attend_short, 0)
    net.relay_z(2)
    lax.fori_loop(pairs // 2, pairs - 1, attend_short, 0)
    net.start(3)
    net.relay_plane(1)
    lax.fori_loop(pairs - 1, pairs, attend_short, 0)
    net.start_plane(3)
    move(short_probs, out_short_probs)
    wires.landed(tok, rows_in.at[theirs])
    lax.fori_loop(short_rows // 256, total_rows // 256, project, 0)
    move(qkv, out_qkv)
    move(rows_in, out_rows)

    wires.landed(pooled, far_pool)
    chosen = []
    for block in range(total_rows // cap):
        if block < count:
            mask, start = short_pool[block : block + 1, :], 0
            limit = short_len[block]
        else:
            step = block - count
            in_half, start = step % (half // cap) * cap, step * cap
            at = slice(in_half, in_half + cap)
            own = jnp.where(x == 0, long_pool[0:1, at], long_pool[1:2, at])
            far = jnp.where(x == 0, far_pool[0:1, at], far_pool[1:2, at])
            mask = jnp.where(x == step // (half // cap), own, far)
            limit = passage_len - start
        keep = (place_in_block < limit) & ((mask > 0) | (place_in_block + start == 0))
        chosen.append(jnp.where(keep, 1.0, 0.0))
    for block in range(count):
        share[block : block + 1, :] = chosen[block] / jnp.sum(chosen[block], axis=-1, keepdims=True)
    long_total = sum(jnp.sum(row, axis=-1, keepdims=True) for row in chosen[count:])
    for block in range(count, total_rows // cap):
        share[block : block + 1, :] = chosen[block] / long_total

    def attend_long(pair, carry):
        lanes = aligned(pair, 2 * head_dim)
        rows = pl.ds(short_rows, long_rows)
        keys_all, values = qkv[1, rows, lanes], qkv[2, rows, lanes]
        for block in range(long_rows // 256):
            inner = pl.ds(block * 256, 256)
            rows = pl.ds(short_rows + block * 256, 256)
            queries = qkv[0, rows, lanes]
            parts = []
            for h in range(2):
                probs = weights_forward(queries * masks[h], keys_all, long_live)
                long_probs[2 * pair + h, inner, :] = probs
                parts.append(times(probs, values))
            mixed[rows, lanes] = jnp.where(keep_first, parts[0], parts[1]).astype(jnp.bfloat16)
        return carry

    lax.fori_loop(0, pairs - 2, attend_long, 0)
    net.relay_plane(2)
    net.relay_corner(1)
    lax.fori_loop(pairs - 2, pairs - 1, attend_long, 0)
    net.relay_z(3)
    lax.fori_loop(pairs - 1, pairs, attend_long, 0)
    move(long_probs, out_long_probs)
    move(mixed, out_mixed)
    net.finish(1)
    assemble(whole1, 0, 1, wq.at[pl.ds(3, 1)])
    vectors[8:16, :] = sum_slabs(whole1, 24)
    move(wq, out_wq)

    def attach(i, carry):
        rows = aligned(i, 256)
        first_in = rows_in[rows, :].astype(jnp.float32) + (times(mixed[rows, :], wq[3]) + vectors[2:3, :])
        normal, factor = normalize(first_in)
        out = normal * vectors[4:5, :] + vectors[6:7, :]
        first[rows, :] = out
        low[rows, :] = out.astype(jnp.bfloat16)
        hat[rows, :] = normal.astype(jnp.bfloat16)
        scale[rows, :] = jnp.broadcast_to(factor, (256, scale.shape[1]))
        return carry

    lax.fori_loop(0, total_rows // 256, attach, 0)
    move(first, out_first)
    move(low, out_low)
    move(hat, out_hat)
    move(scale, out_scale)
    net.relay_corner(2)
    net.finish(2)
    assemble(whole2, 0, 4, wu)
    move(wu, out_wu)

    def leaving(i):
        j, rows = lax.div(i, 4), aligned(lax.rem(i, 4), 256)
        return (
            pltpu.make_async_copy(acted.at[j, rows], out_acted.at[j, rows], leave.at[0, i]),
            pltpu.make_async_copy(slope.at[j, rows], out_slope.at[j, rows], leave.at[1, i]),
        )

    def expand(i, carry):
        j, rows = lax.div(i, 4), aligned(lax.rem(i, 4), 256)
        inner = times(low[rows, :], wu[j]) + vectors[pl.ds(8 + j, 1), :]
        value, grad = gelu_and_slope(inner)
        acted[j, rows, :] = value.astype(jnp.bfloat16)
        slope[j, rows, :] = grad.astype(jnp.bfloat16)
        for copy in leaving(i):
            copy.start()
        return carry

    def left(i, carry):
        for copy in leaving(i):
            copy.wait()
        return carry

    lax.fori_loop(0, 7, expand, 0)
    net.relay_plane(3)
    lax.fori_loop(7, 14, expand, 0)
    net.relay_corner(3)
    lax.fori_loop(14, 16, expand, 0)
    net.finish(3)
    wires.close()
    lax.fori_loop(0, 16, left, 0)
    for copy in [local[0]] + local[3:]:
        copy.wait()


def forward(lengths, parameters, pools, short_tok, long_tok, groups):
    short_rows, width = short_tok.shape
    half = long_tok.shape[1]
    long_rows = 2 * half
    rows = short_rows + long_rows
    count, cap = pools[0].shape
    inner = 4 * width
    copies = 4 * ((groups - 1) + 4 * groups + 4 * groups) + 2
    low = jnp.bfloat16
    shape = jax.ShapeDtypeStruct
    outs = (
        shape((groups, 8, SIZES[3], width), low),
        shape((4, width, width), low),
        shape((4, width, width), low),
        shape((rows, width), low),
        shape((3, rows, width), low),
        shape((count, HEADS, cap, cap), low),
        shape((HEADS, long_rows, long_rows), low),
        shape((rows, width), low),
        shape((rows, width), jnp.float32),
        shape((rows, width), low),
        shape((rows, 128), jnp.float32),
        shape((rows, width), low),
        shape((inner // width, rows, width), low),
        shape((inner // width, rows, width), low),
        shape((16, width), jnp.float32),
        shape((rows // cap, cap), jnp.float32),
    )
    anywhere, near = pl.BlockSpec(memory_space=pl.ANY), pl.BlockSpec(memory_space=pltpu.VMEM)
    scalars = pl.BlockSpec(memory_space=pltpu.SMEM)
    kept = [pltpu.VMEM(out.shape, out.dtype) for out in outs[1:14]]
    return pl.pallas_call(
        forward_kernel,
        name="forward",
        out_shape=outs,
        in_specs=[scalars] * 2 + [near] * 11 + [anywhere] * 2,
        out_specs=[anywhere] * 14 + [near] * 2,
        scratch_shapes=[pltpu.VMEM((groups, 8, SIZES[k], width), low) for k in range(3)]
        + kept
        + [
            pltpu.VMEM(pools[1].shape, pools[1].dtype),
            pltpu.SemaphoreType.DMA((copies,)),
            pltpu.SemaphoreType.DMA((copies,)),
            pltpu.SemaphoreType.DMA((24,)),
            pltpu.SemaphoreType.DMA((2, 16)),
        ],
        compiler_params=pltpu.CompilerParams(
            collective_id=0, has_side_effects=True, vmem_limit_bytes=60 * 1024 * 1024
        ),
    )(*lengths, *parameters, *pools, short_tok, long_tok)


def backward_kernel(
    short_len, long_len, vectors, share, short_pool_cot, long_pool_cot, short_cot, long_cot,
    in_down, in_wq, in_wu, in_rows, in_qkv, in_short_probs, in_long_probs, in_mixed,
    in_first, in_hat, in_scale, in_low, in_acted, in_slope,
    short_out, long_out, short_grad, long_grad, short_pooled, long_pooled,
    grad_qkv, grad_out, grad_up, grad_down, grad_vectors, grad_up_vector,
    wide, pair, w_up, w_far, hat, sums, branch, low, scale, halves, probs_short,
    vector_sums, pool_cots, pooled_rows, pooled_own, pooled_far,
    *more,
):
    place = Place()
    x, other = place.x, 1 - place.x
    *chunks, send, recv, here, blocks, fetch = more
    parts = len(SUMS)
    grads, *received = [chunks[i * parts : (i + 1) * parts] for i in range(7)]
    total_rows, width = sums.shape
    short_rows = short_out.shape[0]
    count, cap = probs_short.shape[1], probs_short.shape[-1]
    long_rows = total_rows - short_rows
    half = long_rows // 2
    head_dim = width // HEADS
    steps = total_rows // 256
    low_type = jnp.bfloat16
    local = []

    def move(src, dst):
        copy = pltpu.make_async_copy(src, dst, here.at[len(local)])
        copy.start()
        local.append(copy)
        return copy

    mine = pl.ds(pl.multiple_of(short_rows + x * half, half), half)
    theirs = pl.ds(pl.multiple_of(short_rows + other * half, half), half)
    place.greet_start()
    load_down = [move(in_down.at[j], w_far.at[j]) for j in range(4)]
    load_down += [
        move(short_cot, branch.at[pl.ds(0, short_rows)]),
        move(long_cot.at[x], branch.at[mine]),
    ]
    passage_len = long_len[x]

    def block_at(step):
        return jnp.where(step < 2, step, 2 + lax.rem(step + x, 2))

    def block_copies(i):
        rows = aligned(i, 256)
        return (
            pltpu.make_async_copy(in_acted.at[:, rows], wide.at[:, rows], blocks.at[0, i]),
            pltpu.make_async_copy(in_first.at[rows], sums.at[rows], blocks.at[1, i]),
        )

    for copy in block_copies(0):
        copy.start()
    vector_sums[...] = jnp.zeros_like(vector_sums)
    pool_cots[0:count, :] = short_pool_cot[...]
    pool_cots[count : 2 * count, :] = jnp.broadcast_to(long_pool_cot[pl.ds(x, 1), :], (count, width))
    place.greet_wait()
    wires = Wires(send, recv)
    swap_cot = wires.put(long_cot.at[other], branch.at[mine], place.at_x())
    net = Scatter(wires, place, grads, *received)
    for copy in load_down:
        copy.wait()
    tall = lax.broadcasted_iota(jnp.int32, (256, 1), 0)
    diagonal = lax.broadcasted_iota(jnp.int32, (cap, cap), 0) == lax.broadcasted_iota(jnp.int32, (cap, cap), 1)

    def add_vector(row, rows):
        vector_sums[row : row + 1, :] += jnp.sum(rows, axis=0, keepdims=True)

    def second(step, carry):
        i = block_at(step)
        rows = aligned(i, 256)

        @pl.when(step == steps - 1)
        def _():
            wires.landed(swap_cot, branch.at[theirs])

        @pl.when(step < steps - 1)
        def _():
            for copy in block_copies(block_at(step + 1)):
                copy.start()

        for copy in block_copies(i):
            copy.wait()
        product = times(wide[0, rows, :], w_far[0])
        for j in range(1, 4):
            product += times(wide[j, rows, :], w_far[j])
        normal, factor = normalize(sums[rows, :] + (product + vectors[3:4, :]))
        lens = [
            jnp.where(2 * i + part < count, short_len[lax.rem(2 * i + part, count)], passage_len - (2 * i + part - count) * cap)
            for part in range(2)
        ]
        live = tall < jnp.where(tall < cap, lens[0], lens[1] + cap)
        final = jnp.where(live, normal * vectors[5:6, :] + vectors[7:8, :], 0.0)
        low[rows, :] = final.astype(low_type)
        spread = []
        for part in range(2):
            share_row = share[pl.ds(2 * i + part, 1), :]
            column = jnp.sum(jnp.where(diagonal, share_row, 0.0), axis=1, keepdims=True)
            piece = final[part * cap : (part + 1) * cap]
            pooled_rows[pl.ds(2 * i + part, 1), :] = jnp.sum(piece * column, axis=0, keepdims=True)
            spread.append(column * pool_cots[pl.ds(2 * i + part, 1), :])
        grad_final = jnp.where(live, branch[rows, :].astype(jnp.float32), 0.0) + jnp.concatenate(spread, axis=0)
        add_vector(5, grad_final * normal)
        add_vector(7, grad_final)
        scaled = grad_final * vectors[5:6, :]
        mean_one = jnp.mean(scaled, axis=-1, keepdims=True)
        mean_two = jnp.mean(scaled * normal, axis=-1, keepdims=True)
        grad_second = factor * (scaled - mean_one - normal * mean_two)
        sums[rows, :] = grad_second
        grad_branch = grad_second.astype(low_type)
        branch[rows, :] = grad_branch
        add_vector(3, grad_branch.astype(jnp.float32))
        return carry

    lax.fori_loop(0, steps, second, 0)
    short_pooled[...] = pooled_rows[0:count, :]
    own_pooled = jnp.sum(pooled_rows[count : 2 * count, :], axis=0, keepdims=True)
    pooled_own[...] = jnp.broadcast_to(own_pooled, pooled_own.shape)
    long_pooled[pl.ds(x, 1), :] = own_pooled
    out_copies = [
        move(low.at[pl.ds(0, short_rows)], short_out),
        move(low.at[mine], long_out.at[x]),
    ]
    load_slope = [move(in_slope.at[0], pair.at[0]), move(in_slope.at[1], pair.at[1])]
    load_up = move(in_wu, w_up)
    load_hat, load_scale = move(in_hat, hat), move(in_scale, scale)

    swap_out = wires.put(low.at[theirs], long_out.at[x], place.at_x())
    swap_pooled = wires.put(pooled_own, pooled_far, place.at_x())

    def down_step(i, carry):
        j, part = lax.div(i, 2), lax.rem(i, 2)
        product = turned_times(wide[j, :, aligned(part, width // 2)], branch[...])
        grads[5][j, aligned(part, 4)] = product.reshape(4, SUMS[5], width).astype(low_type)
        return carry

    lax.fori_loop(0, 8, down_step, 0, unroll=2)
    net.send_core(5)

    def inner_block(j):
        def inner(i, carry):
            rows = aligned(i, 256)
            product = times_turned(branch[rows, :], w_far[j]) * pair[j % 2, rows, :].astype(jnp.float32)
            grad_inner = product.astype(low_type)
            wide[j, rows, :] = grad_inner
            add_vector(8 + j, grad_inner.astype(jnp.float32))
            return carry

        lax.fori_loop(0, steps, inner, 0, unroll=2)

    load_slope[0].wait()
    inner_block(0)
    load_slope.append(move(in_slope.at[2], pair.at[0]))
    load_slope[1].wait()
    inner_block(1)
    load_slope.append(move(in_slope.at[3], pair.at[1]))
    for copy in out_copies:
        copy.wait()
    wires.has_left(swap_out)
    load_low = move(in_low, low)
    net.after_core(5)
    load_slope[2].wait()
    inner_block(2)
    load_mixed = move(in_mixed, pair.at[0])
    load_slope[3].wait()
    inner_block(3)
    load_wq = move(in_wq, w_far)

    def up_step(i, carry):
        r, both = lax.div(i, 2), lax.rem(i, 2)
        data = low[:, aligned(r, width // 2)]
        halves[0] = turned_times(data, wide[2 * both])
        halves[1] = turned_times(data, wide[2 * both + 1])

        def one(k, carry):
            rows = pl.ds(pl.multiple_of(k * 24, 8), 24)
            data = jnp.concatenate([halves[0, rows, :], halves[1, rows, :]], axis=0)
            grads[4][2 * r + lax.div(k, 8), lax.rem(k, 8), aligned(both, 48), :] = data.astype(low_type)
            return carry

        return lax.fori_loop(0, 16, one, carry)

    load_low.wait()
    lax.fori_loop(0, 4, up_step, 0)
    net.send_core(4)
    net.after_first(5)

    load_up.wait()
    load_hat.wait()
    load_scale.wait()

    def first_back(i, carry):
        rows = aligned(i, 256)
        grad_first = sums[rows, :]
        for j in range(4):
            grad_first += times_turned(wide[j, rows, :], w_up[j])
        normal = hat[rows, :].astype(jnp.float32)
        add_vector(4, grad_first * normal)
        add_vector(6, grad_first)
        scaled = grad_first * vectors[4:5, :]
        mean_one = jnp.mean(scaled, axis=-1, keepdims=True)
        mean_two = jnp.mean(scaled * normal, axis=-1, keepdims=True)
        grad_in = scale[rows, 0:1] * (scaled - mean_one - normal * mean_two)
        sums[rows, :] = grad_in
        grad_attn = grad_in.astype(low_type)
        branch[rows, :] = grad_attn
        add_vector(2, grad_attn.astype(jnp.float32))
        return carry

    lax.fori_loop(0, steps // 2, first_back, 0)
    net.after_core(4)
    lax.fori_loop(steps // 2, steps, first_back, 0)
    load_qkv = move(in_qkv, wide.at[pl.ds(0, 3)])
    load_rows = move(in_rows, wide.at[3])
    net.after_second(5)

    load_mixed.wait()
    load_wq.wait()
    def out_step(r, carry):
        halves[0] = turned_times(pair[0, :, aligned(r, width // 2)], branch[...])

        def one(k, carry):
            rows = pl.ds(pl.multiple_of(k * 24, 8), 24)
            data = jnp.concatenate([halves[0, rows, :], vector_sums[8:16, :]], axis=0)
            grads[3][2 * r + lax.div(k, 8), lax.rem(k, 8)] = data.astype(low_type)
            return carry

        return lax.fori_loop(0, 16, one, carry)

    lax.fori_loop(0, 2, out_step, 0)

    def mixed_back(i, carry):
        rows = aligned(i, 256)
        pair[1, rows, :] = times_turned(branch[rows, :], w_far[3]).astype(low_type)
        return carry

    lax.fori_loop(0, steps, mixed_back, 0)
    net.send_core(3)

    def probs_copies(p, slot):
        lanes = pl.ds(2 * p, 2)
        return (
            pltpu.make_async_copy(in_short_probs.at[:, lanes], probs_short.at[slot], fetch.at[0, slot]),
            pltpu.make_async_copy(
                in_long_probs.at[lanes],
                w_up.at[pl.ds(2 * slot, 2), pl.ds(0, long_rows), pl.ds(0, long_rows)],
                fetch.at[1, slot],
            ),
        )

    for copy in probs_copies(0, 0):
        copy.start()
    load_qkv.wait()
    score_scale = 1.0 / math.sqrt(head_dim)
    masks = head_masks(2 * head_dim, head_dim)
    pairs = width // (2 * head_dim)

    def attend_back(lanes, units):
        heads = [(u, h) for u in range(len(units)) for h in range(2)]
        queries = [wide[0, rows, lanes] for rows, _, _, _ in units]
        grads_mixed = [pair[1, rows, lanes] for rows, _, _, _ in units]
        overlaps = [
            grad.astype(jnp.float32) * pair[0, rows, lanes].astype(jnp.float32)
            for grad, (rows, _, _, _) in zip(grads_mixed, units)
        ]
        centers = [
            jnp.sum(overlaps[u] * masks[h].astype(jnp.float32), axis=-1, keepdims=True) for u, h in heads
        ]
        grads_head = [grads_mixed[u] * masks[h] for u, h in heads]
        probs = [units[u][1](h) for u, h in heads]
        grads_probs = [times_turned(grad, units[u][3]) for grad, (u, h) in zip(grads_head, heads)]
        scores = [
            (part.astype(jnp.float32) * (grad - center)).astype(low_type)
            for part, grad, center in zip(probs, grads_probs, centers)
        ]
        grads_q = [times(part, units[u][2] * masks[h]) for part, (u, h) in zip(scores, heads)]
        grads_k = [turned_times(queries[u] * masks[h], part) for part, (u, h) in zip(scores, heads)]
        grads_v = [turned_times(grad, part) for part, grad in zip(probs, grads_head)]
        for u, (rows, _, _, _) in enumerate(units):
            total = grads_q[2 * u] + grads_q[2 * u + 1]
            wide[0, rows, lanes] = (total * score_scale).astype(low_type)
        return [
            [grads[2 * u] + grads[2 * u + 1] for u in range(len(units))] for grads in (grads_k, grads_v)
        ]

    def attention_back(p, carry):
        slot = lax.rem(p, 2)
        for copy in probs_copies(p, slot):
            copy.wait()

        @pl.when(p + 1 < pairs)
        def _():
            for copy in probs_copies(p + 1, 1 - slot):
                copy.start()

        lanes = aligned(p, 2 * head_dim)
        blocks_of = [pl.ds(i * cap, cap) for i in range(count)]
        units = [
            (rows, lambda h, i=i: probs_short[slot, i, h], wide[1, rows, lanes], wide[2, rows, lanes])
            for i, rows in enumerate(blocks_of)
        ]
        grads_k, grads_v = attend_back(lanes, units)
        for rows, grad_k, grad_v in zip(blocks_of, grads_k, grads_v):
            wide[1, rows, lanes] = grad_k.T.astype(low_type)
            wide[2, rows, lanes] = grad_v.T.astype(low_type)
        rows = pl.ds(short_rows, long_rows)
        keys_all, values = wide[1, rows, lanes], wide[2, rows, lanes]
        total_k, total_v = None, None
        for block in range(long_rows // 256):
            inner = pl.ds(block * 256, 256)
            unit = (
                pl.ds(short_rows + block * 256, 256),
                lambda h, inner=inner: w_up[2 * slot + h, inner, 0:long_rows],
                keys_all,
                values,
            )
            (grad_k,), (grad_v,) = attend_back(lanes, [unit])
            total_k = grad_k if total_k is None else total_k + grad_k
            total_v = grad_v if total_v is None else total_v + grad_v
        wide[1, rows, lanes] = total_k.T.astype(low_type)
        wide[2, rows, lanes] = total_v.T.astype(low_type)
        return carry

    third = width // 3

    def qkv_step(group):
        lanes = pl.ds(group * third, third)

        def bias(i, carry):
            rows = aligned(i, 256)
            for row, b in ((0, 0), (1, 2)):
                piece = wide[b, rows, lanes].astype(jnp.float32)
                vector_sums[row : row + 1, lanes] += jnp.sum(piece, axis=0, keepdims=True)
            return carry

        lax.fori_loop(0, steps, bias, 0)

        def step(r, carry):
            data = wide[3, :, aligned(r, width // 2)]
            for b in range(3):
                halves[0, :, b * third : (b + 1) * third] = turned_times(data, wide[b, :, lanes])

            def one(k, carry):
                rows = pl.ds(pl.multiple_of(k * 24, 8), 24)
                pieces = [halves[0, rows, b * third : (b + 1) * third] for b in range(3)]
                data = jnp.concatenate(pieces + [vector_sums[0:8, lanes]], axis=0)
                grads[group][2 * r + lax.div(k, 8), lax.rem(k, 8)] = data.astype(low_type)
                return carry

            return lax.fori_loop(0, 16, one, carry)

        lax.fori_loop(0, 2, step, 0)

    lax.fori_loop(0, pairs // 3, attention_back, 0)
    net.after_first(4)
    load_rows.wait()
    qkv_step(0)
    net.after_core(3)
    net.send_core(0)
    lax.fori_loop(pairs // 3, 2 * pairs // 3, attention_back, 0)
    net.after_second(4)
    net.after_core(0)
    qkv_step(1)
    net.send_core(1)
    net.after_first(3)
    lax.fori_loop(2 * pairs // 3, pairs, attention_back, 0)
    net.after_core(1)
    net.after_first(0)
    qkv_step(2)
    net.send_core(2)
    net.after_second(3)

    def tokens_back(rows):
        grad_in = sums[rows, :]
        for b in range(3):
            grad_in += times_turned(wide[b, rows, :], w_far[b])
        return grad_in

    far_low, far_in = low.at[pl.ds(0, half)], low.at[pl.ds(half, half)]
    far_low[...] = tokens_back(theirs).astype(low_type)

    def tokens_step(i, carry):
        rows = pl.ds(pl.multiple_of(jnp.where(i < 2, i * 256, short_rows + x * half), 256), 256)
        sums[rows, :] = tokens_back(rows)
        return carry

    lax.fori_loop(0, 1, tokens_step, 0)
    net.after_core(2)
    net.after_first(1)
    net.after_second(0)
    net.after_first(2)
    swap_grad = wires.put(far_low, far_in, place.at_x())
    net.after_second(1)
    net.after_second(2)
    lax.fori_loop(1, 3, tokens_step, 0)
    move(sums.at[pl.ds(0, short_rows)], short_grad)
    move(sums.at[mine], long_grad.at[x])
    grad_down[...] = net.finish(5)
    total = net.finish(4)
    for j in range(4):
        grad_up[:, j * width : (j + 1) * width] = total[24 * j : 24 * j + 24]
    total = net.finish(3)
    grad_out[...] = total[0:24]
    grad_up_vector[...] = total[24:32]
    wires.landed(swap_pooled, pooled_far)
    long_pooled[pl.ds(other, 1), :] = pooled_far[0:1, :]
    wires.landed(swap_grad, far_in)
    sums[theirs, :] = far_in[...].astype(jnp.float32)
    move(sums.at[theirs], long_grad.at[other])
    wires.landed(swap_out, long_out.at[other])
    for group in range(3):
        total = net.finish(group)
        for b in range(3):
            columns = slice(b * width + group * third, b * width + (group + 1) * third)
            grad_qkv[:, columns] = total[24 * b : 24 * b + 24]
        grad_vectors[:, group * third : (group + 1) * third] = total[72:80]
    wires.close()
    for copy in local[-3:]:
        copy.wait()


def backward(lengths, vectors, share, pool_cots, cots, arrays, groups):
    width = vectors.shape[1]
    rows = arrays[3].shape[0]
    count, _, cap, _ = arrays[5].shape
    short_rows = count * cap
    half = (rows - short_rows) // 2
    low, wide_type = jnp.bfloat16, jnp.float32
    shape = jax.ShapeDtypeStruct
    rows24 = 24
    outs = (
        shape((short_rows, width), low),
        shape((2, half, width), low),
        shape((short_rows, width), wide_type),
        shape((2, half, width), wide_type),
        shape((count, width), wide_type),
        shape((2, width), wide_type),
        shape((rows24, 3 * width), wide_type),
        shape((rows24, width), wide_type),
        shape((rows24, 4 * width), wide_type),
        shape((4 * rows24, width), wide_type),
        shape((8, width), wide_type),
        shape((8, width), wide_type),
    )
    anywhere, near = pl.BlockSpec(memory_space=pl.ANY), pl.BlockSpec(memory_space=pltpu.VMEM)
    copies = len(SUMS) * (4 + 6 + (groups - 1)) + 4

    widths = (width // 3,) * 3 + (width,) * 3

    def chunks(parts, sizes):
        return [pltpu.VMEM(parts + (size, columns), low) for size, columns in zip(sizes, widths)]

    rest = tuple(size - some for size, some in zip(SUMS, SUMS_X))
    scratch = [
        pltpu.VMEM((4, rows, width), low),
        pltpu.VMEM((2, rows, width), low),
        pltpu.VMEM((4, width, width), low),
        pltpu.VMEM((4, width, width), low),
        pltpu.VMEM((rows, width), low),
        pltpu.VMEM((rows, width), wide_type),
        pltpu.VMEM((rows, width), low),
        pltpu.VMEM((rows, width), low),
        pltpu.VMEM((rows, 128), wide_type),
        pltpu.VMEM((2, width // 2, width), wide_type),
        pltpu.VMEM((2, count, 2, cap, cap), low),
        pltpu.VMEM((16, width), wide_type),
        pltpu.VMEM((2 * count, width), wide_type),
        pltpu.VMEM((2 * count, width), wide_type),
        pltpu.VMEM((8, width), wide_type),
        pltpu.VMEM((8, width), wide_type),
        *chunks((groups, 8), SUMS),
        *chunks((4, groups), SUMS),
        *chunks((2, groups), SUMS_X),
        *chunks((2, groups), rest),
        *chunks((groups,), rest),
        *chunks((groups,), SUMS_X),
        *chunks((groups - 1,), SUMS),
        pltpu.SemaphoreType.DMA((copies,)),
        pltpu.SemaphoreType.DMA((copies,)),
        pltpu.SemaphoreType.DMA((24,)),
        pltpu.SemaphoreType.DMA((2, rows // 256)),
        pltpu.SemaphoreType.DMA((2, 2)),
    ]
    return pl.pallas_call(
        backward_kernel,
        name="backward",
        out_shape=outs,
        in_specs=[pl.BlockSpec(memory_space=pltpu.SMEM)] * 2 + [near] * 4 + [anywhere] * 16,
        out_specs=[anywhere] * 4 + [near] * 8,
        scratch_shapes=scratch,
        compiler_params=pltpu.CompilerParams(
            collective_id=1, has_side_effects=True, vmem_limit_bytes=63 * 1024 * 1024
        ),
    )(*lengths, vectors, share, *pool_cots, *cots, *arrays)


def results_kernel(
    in_0, in_1, in_2, in_3, in_4, in_5, in_6, in_7, in_8, in_9, grad_vectors, grad_ups,
    out_0, out_1, out_2, out_3, out_4, out_5, out_6, out_7, out_8, out_9, pair_0, pair_1, ups, pair_2, pair_3,
    *more,
):
    *held, come, leave = more
    sources = (in_0, in_1, in_2, in_3, in_4, in_5, in_6, in_7, in_8, in_9)
    places = (out_0, out_1, out_4, out_5, out_2, out_3, out_6, out_7, out_8, out_9)
    ins = [pltpu.make_async_copy(sources[i], held[i], come.at[i]) for i in range(10)]
    outs = [pltpu.make_async_copy(held[i], places[i], leave.at[i]) for i in range(10)]
    for copy in ins:
        copy.start()
    device = lax.axis_index("dp") * 2 + lax.axis_index("seq")
    size, width = in_7.shape
    rows = pltpu.roll(grad_vectors[...], lax.rem(width - device * size, width), 1)
    for i, ref in enumerate((pair_0, pair_1, pair_2, pair_3)):
        ref[...] = rows[2 * i : 2 * i + 2, 0:size]
    start = lax.rem(device, 8) * (4 * size)
    row = grad_ups[pl.ds(lax.div(device, 8), 1), :]
    row = pltpu.roll(jnp.broadcast_to(row, (8, width)), lax.rem(width - start, width), 1)
    ups[...] = row[0:1, 0 : 4 * size]
    for i in range(10):
        ins[i].wait()
        outs[i].start()
    for copy in outs:
        copy.wait()


def results(arrays):
    size = arrays[7].shape[0]
    order = (0, 1, 4, 5, 2, 3, 6, 7, 8, 9)
    shape = jax.ShapeDtypeStruct
    pair = shape((2, size), jnp.float32)
    outs = tuple(shape(arrays[i].shape, arrays[i].dtype) for i in order)
    anywhere, near = pl.BlockSpec(memory_space=pl.ANY), pl.BlockSpec(memory_space=pltpu.VMEM)
    return pl.pallas_call(
        results_kernel,
        name="results",
        out_shape=outs + (pair, pair, shape((1, 4 * size), jnp.float32), pair, pair),
        in_specs=[anywhere] * 10 + [near] * 2,
        out_specs=[anywhere] * 10 + [near] * 5,
        scratch_shapes=[pltpu.VMEM(array.shape, array.dtype) for array in arrays[:10]]
        + [pltpu.SemaphoreType.DMA((10,)), pltpu.SemaphoreType.DMA((10,))],
        compiler_params=pltpu.CompilerParams(vmem_limit_bytes=56 * 1024 * 1024),
    )(*arrays)


def layer_norm(row_data, gain_vec, shift_vec):
    center = row_data - jnp.mean(row_data, axis=-1, keepdims=True)
    spread = jnp.mean(center * center, axis=-1, keepdims=True)
    return center * lax.rsqrt(spread + EPS) * gain_vec + shift_vec


def exact_gelu(inner_act):
    return jax.nn.gelu(inner_act, approximate=False)


def outer_sum(left_rows, right_rows):
    return lax.dot_general(
        left_rows, right_rows, (((0,), (0,)), ((), ())), preferred_element_type=jnp.float32
    )


def times_transposed(left_rows, matrix):
    return lax.dot_general(
        left_rows, matrix, (((1,), (1,)), ((), ())), preferred_element_type=jnp.float32
    )


def masked_scores(queries, keys_all, key_live, score_scale):
    scores = (
        jnp.einsum("bqhe,bkhe->bhqk", queries, keys_all, preferred_element_type=jnp.float32)
        * score_scale
    )
    return jnp.where(key_live[:, None, None, :], scores, -1e30)


def attend_forward(pieces, score_scale):
    queries, keys_all, values, key_live = pieces
    scores = masked_scores(queries, keys_all, key_live, score_scale)
    highest = jnp.max(scores, axis=-1, keepdims=True)
    exponent = jnp.exp(scores - highest)
    totals = jnp.sum(exponent, axis=-1, keepdims=True)
    soft_probs = (exponent / totals).astype(jnp.bfloat16)
    mixed_heads = jnp.einsum(
        "bhqk,bkhe->bqhe", soft_probs, values, preferred_element_type=jnp.float32
    )
    return (mixed_heads.astype(jnp.bfloat16), (highest + jnp.log(totals))[..., 0])


def attend_backward(pieces, score_scale):
    queries, keys_all, values, key_live, grad_mixed, log_total = pieces
    scores = masked_scores(queries, keys_all, key_live, score_scale)
    soft_probs = jnp.exp(scores - log_total[..., None])
    grad_probs = jnp.einsum(
        "bqhe,bkhe->bhqk", grad_mixed, values, preferred_element_type=jnp.float32
    )
    grad_values = jnp.einsum(
        "bhqk,bqhe->bkhe",
        soft_probs.astype(jnp.bfloat16),
        grad_mixed,
        preferred_element_type=jnp.float32,
    )
    center = jnp.sum(soft_probs * grad_probs, axis=-1, keepdims=True)
    grad_scores = (soft_probs * (grad_probs - center)).astype(jnp.bfloat16)
    grad_queries = (
        jnp.einsum("bhqk,bkhe->bqhe", grad_scores, keys_all, preferred_element_type=jnp.float32)
        * score_scale
    )
    grad_keys = (
        jnp.einsum("bhqk,bqhe->bkhe", grad_scores, queries, preferred_element_type=jnp.float32)
        * score_scale
    )
    return (grad_queries, grad_keys, grad_values)


def by_blocks(function, per_block, arrays):
    blocks = arrays[0].shape[0] // per_block
    stacked = tuple((member.reshape((blocks, per_block) + member.shape[1:]) for member in arrays))
    results = lax.map(function, stacked)
    return jax.tree.map(
        lambda member: member.reshape((blocks * per_block,) + member.shape[2:]), results
    )


def general_shards(
    short_tokens,
    long_tokens,
    short_len,
    long_len,
    short_pool,
    long_pool,
    short_cot,
    long_cot,
    short_pool_cot,
    long_pool_cot,
    w_qkv,
    w_out,
    w_up,
    w_down,
    qv_bias,
    out_bias,
    up_bias,
    norm_gain,
    norm_shift,
):
    gathered = (
        lax.all_gather(w_qkv, ("dp", "seq"), axis=0, tiled=True),
        lax.all_gather(w_out, ("dp", "seq"), axis=0, tiled=True),
        lax.all_gather(w_up, ("dp", "seq"), axis=0, tiled=True),
        lax.all_gather(w_down, ("dp", "seq"), axis=0, tiled=True),
        lax.all_gather(qv_bias, ("dp", "seq"), axis=0, tiled=True),
        lax.all_gather(out_bias, ("dp", "seq"), axis=0, tiled=True),
        lax.all_gather(up_bias, ("dp", "seq"), axis=0, tiled=True),
        lax.all_gather(norm_gain, ("dp", "seq"), axis=0, tiled=True),
        lax.all_gather(norm_shift, ("dp", "seq"), axis=0, tiled=True),
    )
    qkv_matrix, out_matrix, up_matrix, down_matrix, qv_vec, out_vec, up_vec, gains, shifts = (
        gathered
    )
    gains = gains.astype(jnp.float32)
    shifts = shifts.astype(jnp.float32)
    short_count, short_cap, model_width = short_tokens.shape
    long_count, long_half = (long_tokens.shape[0], long_tokens.shape[1])
    head_count = HEADS
    head_dim = model_width // head_count
    score_scale = 1.0 / math.sqrt(head_dim)
    short_rows = short_count * short_cap
    long_rows = long_count * long_half
    short_place = jnp.arange(short_cap, dtype=jnp.int32)
    short_live = short_place[None, :] < short_len[:, None]
    long_place = lax.axis_index("seq") * long_half + jnp.arange(long_half, dtype=jnp.int32)
    long_live = long_place[None, :] < long_len[:, None]
    short_weight = (short_live & ((short_pool > 0) | (short_place[None, :] == 0))).astype(
        jnp.float32
    )
    long_weight = (long_live & ((long_pool > 0) | (long_place[None, :] == 0))).astype(jnp.float32)
    row_live = jnp.concatenate([short_live.reshape(-1), long_live.reshape(-1)]).astype(jnp.float32)
    inputs = jnp.concatenate(
        [
            short_tokens.reshape(short_rows, model_width),
            long_tokens.reshape(long_rows, model_width),
        ],
        axis=0,
    )
    joined = jnp.dot(inputs, qkv_matrix, preferred_element_type=jnp.float32)
    queries = (joined[:, :model_width] + qv_vec[:, 0]).astype(jnp.bfloat16)
    keys_all = joined[:, model_width : 2 * model_width].astype(jnp.bfloat16)
    values = (joined[:, 2 * model_width :] + qv_vec[:, 1]).astype(jnp.bfloat16)
    short_shape = (short_count, short_cap, head_count, head_dim)
    long_shape = (long_count, long_half, head_count, head_dim)
    short_q = queries[:short_rows].reshape(short_shape)
    short_k = keys_all[:short_rows].reshape(short_shape)
    short_v = values[:short_rows].reshape(short_shape)
    long_q = queries[short_rows:].reshape(long_shape)
    long_k = keys_all[short_rows:].reshape(long_count, long_half, model_width)
    long_v = values[short_rows:].reshape(long_count, long_half, model_width)
    short_block = math.gcd(short_count, max(1, 512 // short_cap))
    long_block = math.gcd(long_count, max(1, 512 // long_half))

    def forward_blocks(pieces):
        return attend_forward(pieces, score_scale)

    def backward_blocks(pieces):
        return attend_backward(pieces, score_scale)

    short_mixed, short_logsum = by_blocks(
        forward_blocks, short_block, (short_q, short_k, short_v, short_live)
    )
    gathered_k, gathered_v = (
        lax.all_gather(long_k, "seq", axis=1, tiled=True),
        lax.all_gather(long_v, "seq", axis=1, tiled=True),
    )
    full_len = gathered_k.shape[1]
    full_shape = (long_count, full_len, head_count, head_dim)
    long_key_live = jnp.arange(full_len, dtype=jnp.int32)[None, :] < long_len[:, None]
    long_mixed, long_logsum = by_blocks(
        forward_blocks,
        long_block,
        (long_q, gathered_k.reshape(full_shape), gathered_v.reshape(full_shape), long_key_live),
    )
    mixed_heads = jnp.concatenate(
        [short_mixed.reshape(short_rows, model_width), long_mixed.reshape(long_rows, model_width)],
        axis=0,
    )
    attn_out = jnp.dot(mixed_heads, out_matrix, preferred_element_type=jnp.float32) + out_vec[:, 0]
    first_in = inputs.astype(jnp.float32) + attn_out
    first_norm = layer_norm(first_in, gains[:, 0], shifts[:, 0])
    first_low = first_norm.astype(jnp.bfloat16)
    inner_act = jnp.dot(first_low, up_matrix, preferred_element_type=jnp.float32) + up_vec
    activated = exact_gelu(inner_act).astype(jnp.bfloat16)
    branch = jnp.dot(activated, down_matrix, preferred_element_type=jnp.float32) + out_vec[:, 1]
    second_in = first_norm + branch
    final_norm = layer_norm(second_in, gains[:, 1], shifts[:, 1]) * row_live[:, None]
    short_final = final_norm[:short_rows].reshape(short_count, short_cap, model_width)
    long_final = final_norm[short_rows:].reshape(long_count, long_half, model_width)
    short_total = jnp.sum(short_weight, axis=1)
    short_pooled = jnp.sum(short_final * short_weight[..., None], axis=1) / short_total[:, None]
    long_partial = jnp.sum(long_final * long_weight[..., None], axis=1)
    long_sum, long_total = lax.psum((long_partial, jnp.sum(long_weight, axis=1)), "seq")
    long_pooled = long_sum / long_total[:, None]
    grad_short = (
        short_cot.astype(jnp.float32) * short_live[..., None]
        + short_weight[..., None] * short_pool_cot[:, None, :] / short_total[:, None, None]
    )
    grad_long = (
        long_cot.astype(jnp.float32) * long_live[..., None]
        + long_weight[..., None] * long_pool_cot[:, None, :] / long_total[:, None, None]
    )
    grad_top = jnp.concatenate(
        [grad_short.reshape(short_rows, model_width), grad_long.reshape(long_rows, model_width)],
        axis=0,
    )
    _, second_back = jax.vjp(layer_norm, second_in, gains[:, 1], shifts[:, 1])
    grad_second, grad_gain_two, grad_shift_two = second_back(grad_top)
    grad_branch = grad_second.astype(jnp.bfloat16)
    grad_down = outer_sum(activated, grad_branch)
    grad_bias_two = jnp.sum(grad_branch.astype(jnp.float32), axis=0)
    grad_acted = times_transposed(grad_branch, down_matrix)
    _, gelu_back = jax.vjp(exact_gelu, inner_act)
    grad_inner = gelu_back(grad_acted)[0].astype(jnp.bfloat16)
    grad_up = outer_sum(first_low, grad_inner)
    grad_up_bias = jnp.sum(grad_inner.astype(jnp.float32), axis=0)
    grad_first = grad_second + times_transposed(grad_inner, up_matrix)
    _, first_back = jax.vjp(layer_norm, first_in, gains[:, 0], shifts[:, 0])
    grad_first_in, grad_gain_one, grad_shift_one = first_back(grad_first)
    grad_attn = grad_first_in.astype(jnp.bfloat16)
    grad_out = outer_sum(mixed_heads, grad_attn)
    grad_bias_one = jnp.sum(grad_attn.astype(jnp.float32), axis=0)
    grad_mixed = times_transposed(grad_attn, out_matrix).astype(jnp.bfloat16)
    short_dq, short_dk, short_dv = by_blocks(
        backward_blocks,
        short_block,
        (
            short_q,
            short_k,
            short_v,
            short_live,
            grad_mixed[:short_rows].reshape(short_shape),
            short_logsum,
        ),
    )
    again_k, again_v = (gathered_k, gathered_v)
    long_dq, long_dk, long_dv = by_blocks(
        backward_blocks,
        long_block,
        (
            long_q,
            again_k.reshape(full_shape),
            again_v.reshape(full_shape),
            long_key_live,
            grad_mixed[short_rows:].reshape(long_shape),
            long_logsum,
        ),
    )
    own_dk, own_dv = (
        lax.psum_scatter(
            long_dk.reshape(long_count, full_len, model_width).astype(jnp.bfloat16),
            "seq",
            scatter_dimension=1,
            tiled=True,
        ).astype(jnp.float32),
        lax.psum_scatter(
            long_dv.reshape(long_count, full_len, model_width).astype(jnp.bfloat16),
            "seq",
            scatter_dimension=1,
            tiled=True,
        ).astype(jnp.float32),
    )
    grad_queries = jnp.concatenate(
        [short_dq.reshape(short_rows, model_width), long_dq.reshape(long_rows, model_width)], axis=0
    ).astype(jnp.bfloat16)
    grad_keys = jnp.concatenate(
        [short_dk.reshape(short_rows, model_width), own_dk.reshape(long_rows, model_width)], axis=0
    ).astype(jnp.bfloat16)
    grad_values = jnp.concatenate(
        [short_dv.reshape(short_rows, model_width), own_dv.reshape(long_rows, model_width)], axis=0
    ).astype(jnp.bfloat16)
    grad_joined = jnp.concatenate([grad_queries, grad_keys, grad_values], axis=1)
    grad_qkv = outer_sum(inputs, grad_joined)
    grad_qv = jnp.stack(
        [
            jnp.sum(grad_queries.astype(jnp.float32), axis=0),
            jnp.sum(grad_values.astype(jnp.float32), axis=0),
        ],
        axis=1,
    )
    grad_inputs = grad_first_in + times_transposed(grad_joined, qkv_matrix)
    grad_out_vec = jnp.stack([grad_bias_one, grad_bias_two], axis=1)
    grad_gains = jnp.stack([grad_gain_one, grad_gain_two], axis=1)
    grad_shifts = jnp.stack([grad_shift_one, grad_shift_two], axis=1)
    shard_grads = (
        lax.psum_scatter(grad_qkv, ("dp", "seq"), scatter_dimension=0, tiled=True),
        lax.psum_scatter(grad_out, ("dp", "seq"), scatter_dimension=0, tiled=True),
        lax.psum_scatter(grad_up, ("dp", "seq"), scatter_dimension=0, tiled=True),
        lax.psum_scatter(grad_down, ("dp", "seq"), scatter_dimension=0, tiled=True),
        lax.psum_scatter(grad_qv, ("dp", "seq"), scatter_dimension=0, tiled=True),
        lax.psum_scatter(grad_out_vec, ("dp", "seq"), scatter_dimension=0, tiled=True),
        lax.psum_scatter(grad_up_bias, ("dp", "seq"), scatter_dimension=0, tiled=True),
        lax.psum_scatter(grad_gains, ("dp", "seq"), scatter_dimension=0, tiled=True),
        lax.psum_scatter(grad_shifts, ("dp", "seq"), scatter_dimension=0, tiled=True),
    )
    short_out = short_final.astype(jnp.bfloat16)
    long_out = long_final.astype(jnp.bfloat16)
    short_grad_in = grad_inputs[:short_rows].reshape(short_count, short_cap, model_width)
    long_grad_in = grad_inputs[short_rows:].reshape(long_count, long_half, model_width)
    return (
        short_out,
        long_out,
        short_pooled,
        long_pooled,
        short_grad_in,
        long_grad_in,
        shard_grads[0],
        shard_grads[1],
        shard_grads[2],
        shard_grads[3],
        shard_grads[4],
        shard_grads[5],
        shard_grads[6],
        shard_grads[7],
        shard_grads[8],
    )


def fast_shards(
    short_tokens, long_tokens, short_len, long_len, short_pool, long_pool, short_cot, long_cot,
    short_pool_cot, long_pool_cot, w_qkv, w_out, w_up, w_down, qv_bias, out_bias, up_bias,
    norm_gain, norm_shift,
):
    groups = lax.axis_size("dp") // 4
    width = w_out.shape[1]
    count, cap, _ = short_tokens.shape
    short_rows = count * cap
    lengths = (short_len, long_len)
    parameters = (
        w_qkv, w_out, w_up, w_down, qv_bias.T, out_bias.T, norm_gain.T, norm_shift.T, up_bias[None, :],
    )
    (down, *kept, vectors, share) = forward(
        lengths,
        parameters,
        (short_pool, long_pool),
        short_tokens.reshape(short_rows, width),
        long_tokens,
        groups,
    )
    arrays = backward(
        lengths,
        vectors,
        share,
        (short_pool_cot, long_pool_cot),
        (short_cot.reshape(short_rows, width), long_cot),
        (down.reshape(4, width, width), *kept),
        groups,
    )
    (
        short_out, long_out, short_pooled, long_pooled, short_grad, long_grad,
        grad_qkv, grad_out, grad_up, grad_down, qv, out, ups, gain, shift,
    ) = results(arrays)
    return (
        short_out.reshape(short_tokens.shape), long_out, short_pooled, long_pooled,
        short_grad.reshape(short_tokens.shape), long_grad, grad_qkv, grad_out, grad_up, grad_down,
        qv.T, out.T, ups[0], gain.T, shift.T,
    )


def solution(mesh):
    short_spec, long_spec, spread = P(("dp", "seq"), None, None), P("dp", "seq", None), P(("dp", "seq"), None)
    vector, parameters = P(("dp", "seq")), [P(("dp", "seq"), None)] * 6
    in_specs = (
        short_spec, long_spec, vector, P("dp"), spread, P("dp", "seq"), short_spec, long_spec,
        spread, P("dp", None), *parameters, vector, spread, spread,
    )
    out_specs = (
        short_spec, long_spec, spread, P("dp", None), short_spec, long_spec, *parameters, vector,
        spread, spread,
    )
    dp, seq = mesh.shape["dp"], mesh.shape["seq"]

    def run(*arrays):
        width = arrays[11].shape[1]
        passages = arrays[1].shape[0] // dp
        regular = dp == 16 and seq == 2 and passages == 2 and width == 24 * dp * seq
        body = fast_shards if regular else general_shards
        return jax.shard_map(body, mesh=mesh, in_specs=in_specs, out_specs=out_specs, check_vma=False)(*arrays)

    return run
```

```python
import functools
import math

import jax
import jax.numpy as jnp
from jax import lax
from jax.experimental import pallas as pl
from jax.experimental.pallas import tpu as pltpu
from jax.sharding import PartitionSpec as P

HEADS = 12
EPS = 1e-12
MESH = pl.DeviceIdType.MESH

SIZES = (80, 32, 96, 96)
GATHER_X = (48, 16, 48, 48)
SUMS = (80, 80, 80, 32, 96, 96)
SUMS_X = (48, 48, 32, 16, 48, 48)


FLIPS = ((0, 0), (0, 1), (1, 0), (1, 1))


class Place:
    def __init__(self):
        dp = lax.axis_index("dp")
        self.x = lax.axis_index("seq")
        self.groups = lax.axis_size("dp") // 4
        self.z = lax.div(dp, 4)
        self.y = lax.rem(lax.div(dp, 2), 2)
        self.c = lax.rem(dp, 2)
        self.dp = dp

    def z_of(self, step):
        if step == 1:
            return self.z + 1 - 2 * lax.rem(self.z, 2)
        return lax.rem(self.z + 2, 4) if step == 2 else 3 - self.z

    def at_z(self, step):
        return (self.z_of(step) * 4 + self.y * 2 + self.c, self.x)

    def at_x(self):
        return (self.dp, 1 - self.x)

    def at_y(self):
        return (self.z * 4 + (1 - self.y) * 2 + self.c, self.x)

    def at_core(self):
        return (self.z * 4 + self.y * 2 + 1 - self.c, self.x)

    def slot(self, flip_y=0, flip_c=0, flip_x=0):
        y = 1 - self.y if flip_y else self.y
        c = 1 - self.c if flip_c else self.c
        x = 1 - self.x if flip_x else self.x
        return y * 4 + c * 2 + x

    def z_back(self, step):
        return self.z if step == 0 else self.z_of(step)

    def partners(self):
        return [self.at_z(step) for step in range(1, self.groups)] + [
            self.at_x(),
            self.at_y(),
            self.at_core(),
        ]

    def greet_start(self):
        for partner in self.partners():
            pl.semaphore_signal(
                pltpu.get_barrier_semaphore(), inc=1, device_id=partner, device_id_type=MESH
            )

    def greet_wait(self):
        pl.semaphore_wait(pltpu.get_barrier_semaphore(), len(self.partners()))


class Wires:
    def __init__(self, send, recv):
        self.send, self.recv, self.sent, self.left = send, recv, [], set()

    def put(self, src, dst, to):
        number = len(self.sent)
        copy = pltpu.make_async_remote_copy(
            src_ref=src,
            dst_ref=dst,
            send_sem=self.send.at[number],
            recv_sem=self.recv.at[number],
            device_id=to,
            device_id_type=MESH,
        )
        copy.start()
        self.sent.append(copy)
        return (number, to)

    def landed(self, ticket, ref):
        number, to = ticket
        pltpu.make_async_remote_copy(
            src_ref=ref,
            dst_ref=ref,
            send_sem=self.send.at[number],
            recv_sem=self.recv.at[number],
            device_id=to,
            device_id_type=MESH,
        ).wait_recv()

    def has_left(self, ticket):
        self.sent[ticket[0]].wait_send()
        self.left.add(ticket[0])

    def close(self):
        for number, copy in enumerate(self.sent):
            if number not in self.left:
                copy.wait_send()


class Gather:
    def __init__(self, wires, place, wholes, last):
        self.wires, self.place, self.wholes, self.last = wires, place, wholes, last
        self.steps = place.groups
        self.along_z, self.along_x, self.along_y = {}, {}, {}
        self.by_x, self.by_y, self.core = {}, {}, {}

    def halves(self, k):
        some = GATHER_X[k]
        return pl.ds(0, some), pl.ds(some, SIZES[k] - some)

    def start(self, k):
        place, wires = self.place, self.wires
        dst = self.wholes[k].at[place.z, place.slot()]
        src = self.last if k == 3 else dst
        for step in range(1, self.steps):
            self.along_z[k, step] = wires.put(src, dst, place.at_z(step))

    def start_plane(self, k):
        place, wires = self.place, self.wires
        dst = self.wholes[k].at[place.z, place.slot()]
        src = self.last if k == 3 else dst
        self.along_x[k, 0] = wires.put(src, dst, place.at_x())
        self.along_y[k, 0] = wires.put(src, dst, place.at_y())
        self.core[k, 0, 0] = wires.put(src, dst, place.at_core())

    def relay_z(self, k):
        place, wires = self.place, self.wires
        for step in range(1, self.steps):
            ref = self.wholes[k].at[place.z_back(step), place.slot()]
            wires.landed(self.along_z[k, step], ref)
            self.along_x[k, step] = wires.put(ref, ref, place.at_x())
            self.along_y[k, step] = wires.put(ref, ref, place.at_y())
            self.core[k, 0, step] = wires.put(ref, ref, place.at_core())

    def relay_plane(self, k):
        upper, lower = self.halves(k)
        place, wires, whole = self.place, self.wires, self.wholes[k]
        for step in range(self.steps):
            z = place.z_back(step)
            slot = place.slot(flip_x=1)
            ref = whole.at[z, slot]
            wires.landed(self.along_x[k, step], ref)
            half = whole.at[z, slot, upper]
            self.by_y[k, step] = wires.put(half, half, place.at_y())
            self.core[k, 1, step] = wires.put(ref, ref, place.at_core())
            slot = place.slot(flip_y=1)
            ref = whole.at[z, slot]
            wires.landed(self.along_y[k, step], ref)
            half = whole.at[z, slot, lower]
            self.by_x[k, step] = wires.put(half, half, place.at_x())
            self.core[k, 2, step] = wires.put(ref, ref, place.at_core())

    def relay_corner(self, k):
        upper, lower = self.halves(k)
        place, wires, whole = self.place, self.wires, self.wholes[k]
        slot = place.slot(flip_x=1, flip_y=1)
        for step in range(self.steps):
            z = place.z_back(step)
            wires.landed(self.by_y[k, step], whole.at[z, slot, upper])
            wires.landed(self.by_x[k, step], whole.at[z, slot, lower])
            ref = whole.at[z, slot]
            self.core[k, 3, step] = wires.put(ref, ref, place.at_core())

    def finish(self, k):
        place = self.place
        for part, (flip_y, flip_x) in enumerate(FLIPS):
            slot = place.slot(flip_y=flip_y, flip_c=1, flip_x=flip_x)
            for step in range(self.steps):
                ref = self.wholes[k].at[place.z_back(step), slot]
                self.wires.landed(self.core[k, part, step], ref)


class Scatter:
    def __init__(self, wires, place, grads, from_core, from_x, from_y, last_x, last_y, from_z):
        self.wires, self.place, self.grads = wires, place, grads
        self.from_core, self.from_x, self.from_y = from_core, from_x, from_y
        self.last_x, self.last_y, self.from_z = last_x, last_y, from_z
        self.steps = place.groups
        self.core, self.first, self.second, self.third = {}, {}, {}, {}

    def halves(self, k):
        some = SUMS_X[k]
        return pl.ds(0, some), pl.ds(some, SUMS[k] - some)

    def own(self, k, part, rows):
        flip_y, flip_x = FLIPS[part]
        return self.grads[k].at[:, self.place.slot(flip_y=flip_y, flip_x=flip_x), rows]

    def send_core(self, k):
        place = self.place
        for part in (3, 1, 2, 0):
            flip_y, flip_x = FLIPS[part]
            slot = place.slot(flip_y=flip_y, flip_c=1, flip_x=flip_x)
            self.core[k, part] = self.wires.put(
                self.grads[k].at[:, slot], self.from_core[k].at[part], place.at_core()
            )

    def add(self, into, other):
        def one(z, carry):
            total = into[z].astype(jnp.float32) + other[z].astype(jnp.float32)
            into[z] = total.astype(into.dtype)
            return carry

        lax.fori_loop(0, self.steps, one, 0)

    def after_core(self, k):
        upper, lower = self.halves(k)
        whole = pl.ds(0, SUMS[k])
        wires, place = self.wires, self.place
        for part in (3, 1, 2, 0):
            wires.landed(self.core[k, part], self.from_core[k].at[part])
            self.add(self.own(k, part, whole), self.from_core[k].at[part])
            if part == 3:
                self.first[k, "x", 1] = wires.put(
                    self.own(k, 3, upper), self.from_x[k].at[1], place.at_x()
                )
                self.first[k, "y", 1] = wires.put(
                    self.own(k, 3, lower), self.from_y[k].at[1], place.at_y()
                )
            elif part == 1:
                self.first[k, "x", 0] = wires.put(
                    self.own(k, 1, upper), self.from_x[k].at[0], place.at_x()
                )
            elif part == 2:
                self.first[k, "y", 0] = wires.put(
                    self.own(k, 2, lower), self.from_y[k].at[0], place.at_y()
                )

    def after_first(self, k):
        upper, lower = self.halves(k)
        wires, place = self.wires, self.place
        wires.landed(self.first[k, "x", 1], self.from_x[k].at[1])
        self.add(self.own(k, 2, upper), self.from_x[k].at[1])
        self.second[k, "y"] = wires.put(self.own(k, 2, upper), self.last_y[k], place.at_y())
        wires.landed(self.first[k, "y", 1], self.from_y[k].at[1])
        self.add(self.own(k, 1, lower), self.from_y[k].at[1])
        self.second[k, "x"] = wires.put(self.own(k, 1, lower), self.last_x[k], place.at_x())
        wires.landed(self.first[k, "x", 0], self.from_x[k].at[0])
        self.add(self.own(k, 0, upper), self.from_x[k].at[0])
        wires.landed(self.first[k, "y", 0], self.from_y[k].at[0])
        self.add(self.own(k, 0, lower), self.from_y[k].at[0])

    def after_second(self, k):
        upper, lower = self.halves(k)
        wires, place = self.wires, self.place
        wires.landed(self.second[k, "y"], self.last_y[k])
        self.add(self.own(k, 0, upper), self.last_y[k])
        wires.landed(self.second[k, "x"], self.last_x[k])
        self.add(self.own(k, 0, lower), self.last_x[k])
        for step in range(1, self.steps):
            z = place.z_of(step)
            self.third[k, step] = wires.put(
                self.grads[k].at[z, place.slot()], self.from_z[k].at[step - 1], place.at_z(step)
            )

    def finish(self, k):
        place = self.place
        total = self.grads[k][place.z, place.slot()].astype(jnp.float32)
        for step in range(1, self.steps):
            self.wires.landed(self.third[k, step], self.from_z[k].at[step - 1])
            total = total + self.from_z[k][step - 1].astype(jnp.float32)
        return total


def times(a, b):
    return lax.dot_general(a, b, (((1,), (0,)), ((), ())), preferred_element_type=jnp.float32)


def times_turned(a, b):
    return lax.dot_general(a, b, (((1,), (1,)), ((), ())), preferred_element_type=jnp.float32)


def turned_times(a, b):
    return lax.dot_general(a, b, (((0,), (0,)), ((), ())), preferred_element_type=jnp.float32)


def aligned(index, size):
    return pl.ds(pl.multiple_of(index * size, size), size)


def head_masks(lanes, head_dim):
    lane = lax.broadcasted_iota(jnp.int32, (1, lanes), 1)
    return [
        jnp.where((lane >= h * head_dim) & (lane < (h + 1) * head_dim), 1.0, 0.0).astype(jnp.bfloat16)
        for h in range(lanes // head_dim)
    ]


def gelu_and_slope(u):
    near = 1.0 / (1.0 + (0.3275911 * math.sqrt(0.5)) * jnp.abs(u))
    bell = jnp.exp(-0.5 * (u * u))
    series = near * (
        0.127414796
        + near * (-0.142248368 + near * (0.7107068705 + near * (-0.7265760135 + near * 0.5307027145)))
    )
    tail = series * bell
    below = jnp.where(u < 0.0, tail, 1.0 - tail)
    return u * below, below + u * (bell * (1.0 / math.sqrt(2.0 * math.pi)))


def assemble(source, first, blocks, target):
    per_z, size = source.shape[1] // 2, 24

    def one(i, carry):
        z, pair = lax.div(i, per_z), lax.rem(i, per_z)
        left = source[z, 2 * pair].astype(jnp.float32)
        right = source[z, 2 * pair + 1].astype(jnp.float32)
        for b in range(blocks):
            rows = slice(first + b * size, first + (b + 1) * size)
            both = jnp.concatenate([left[rows], right[rows]], axis=0)
            target[b, aligned(i, 2 * size), :] = both.astype(target.dtype)
        return carry

    lax.fori_loop(0, source.shape[0] * per_z, one, 0)


def sum_slabs(source, first):
    def one(i, total):
        per_z = source.shape[1]
        slab = source[lax.div(i, per_z), lax.rem(i, per_z)].astype(jnp.float32)
        return total + slab[first : first + 8]

    count = source.shape[0] * source.shape[1]
    return lax.fori_loop(0, count, one, jnp.zeros((8, source.shape[-1]), jnp.float32))


def normalize(row_data):
    center = row_data - jnp.mean(row_data, axis=-1, keepdims=True)
    spread = jnp.mean(center * center, axis=-1, keepdims=True)
    scale = lax.rsqrt(spread + EPS)
    return center * scale, scale


def weights_forward(queries, keys_all, live):
    scores = jnp.where(live, times_turned(queries, keys_all), -1e30)
    exponent = jnp.exp(scores - jnp.max(scores, axis=-1, keepdims=True))
    return (exponent * (1.0 / jnp.sum(exponent, axis=-1, keepdims=True))).astype(jnp.bfloat16)


def as_column(row):
    size = row.shape[1]
    down = lax.broadcasted_iota(jnp.int32, (size, size), 0)
    across = lax.broadcasted_iota(jnp.int32, (size, size), 1)
    return jnp.sum(jnp.where(down == across, row, 0.0), axis=1, keepdims=True)


def put_at(row, start, width):
    size = row.shape[1]
    down = lax.broadcasted_iota(jnp.int32, (size, width), 0)
    across = lax.broadcasted_iota(jnp.int32, (size, width), 1)
    return jnp.sum(jnp.where(across == down + start, as_column(row), 0.0), axis=0, keepdims=True)


def forward_kernel(
    short_len, long_len, w_qkv, w_out, w_up, w_down, qv_bias, out_bias, gains, shifts, up_bias,
    short_pool, long_pool, short_tok, long_tok,
    out_down, out_wq, out_wu, out_rows, out_qkv, out_short_probs, out_long_probs, out_mixed,
    out_first, out_hat, out_scale, out_low, out_acted, out_slope, vectors, share,
    whole0, whole1, whole2, wq, wu, rows_in, qkv, short_probs, long_probs, mixed,
    first, hat, scale, low, acted, slope, far_pool,
    send, recv, here, leave,
):
    place = Place()
    x, other = place.x, 1 - place.x
    short_rows, half = short_tok.shape[0], long_tok.shape[1]
    total_rows, width = rows_in.shape
    long_rows = 2 * half
    count, cap = short_pool.shape
    mine = pl.ds(pl.multiple_of(short_rows + x * half, half), half)
    theirs = pl.ds(pl.multiple_of(short_rows + other * half, half), half)
    local = []

    def move(src, dst):
        copy = pltpu.make_async_copy(src, dst, here.at[len(local)])
        copy.start()
        local.append(copy)
        return copy

    move(w_down, out_down.at[place.z, place.slot()])
    loads = [
        move(short_tok, rows_in.at[pl.ds(0, short_rows)]),
        move(long_tok.at[x], rows_in.at[mine]),
    ]
    place.greet_start()

    device = place.dp * 2 + x
    size = w_out.shape[0]

    def blocks(matrix):
        data = matrix[...].astype(jnp.float32)
        return [data[:, i * width : (i + 1) * width] for i in range(data.shape[1] // width)]

    pairs = [
        put_at(member[i : i + 1, :].astype(jnp.float32), device * size, width)
        for member in (qv_bias, out_bias, gains, shifts)
        for i in range(2)
    ]
    z, slot = place.z, place.slot()
    whole0[z, slot] = jnp.concatenate(blocks(w_qkv) + pairs, axis=0).astype(jnp.bfloat16)

    place.greet_wait()
    wires = Wires(send, recv)
    net = Gather(wires, place, (whole0, whole1, whole2, out_down), w_down)
    net.start(0)
    net.start_plane(0)
    ups = put_at(up_bias[...].astype(jnp.float32), lax.rem(device, 8) * (4 * size), width)
    ups = jnp.where(lax.broadcasted_iota(jnp.int32, (8, 1), 0) == lax.div(device, 8), ups, 0.0)
    whole1[z, slot] = jnp.concatenate(blocks(w_out) + [ups], axis=0).astype(jnp.bfloat16)
    net.start(1)
    net.start_plane(1)
    whole2[z, slot] = jnp.concatenate(blocks(w_up), axis=0).astype(jnp.bfloat16)
    net.start(2)
    net.start_plane(2)
    pooled = wires.put(long_pool, far_pool, place.at_x())
    net.relay_z(0)
    net.relay_plane(0)
    tok = wires.put(long_tok.at[other], rows_in.at[mine], place.at_x())
    net.relay_z(1)
    net.relay_corner(0)
    for copy in loads:
        copy.wait()
    net.finish(0)
    assemble(whole0, 0, 3, wq)
    vectors[0:8, :] = sum_slabs(whole0, 72)

    head_dim = width // HEADS
    score_scale = 1.0 / math.sqrt(head_dim)

    def project(i, carry):
        rows = aligned(i, 256)
        data = rows_in[rows, :]
        queries = times(data, wq[0]) + vectors[0:1, :]
        qkv[0, rows, :] = (queries.astype(jnp.bfloat16).astype(jnp.float32) * score_scale).astype(jnp.bfloat16)
        qkv[1, rows, :] = times(data, wq[1]).astype(jnp.bfloat16)
        qkv[2, rows, :] = (times(data, wq[2]) + vectors[1:2, :]).astype(jnp.bfloat16)
        return carry

    lax.fori_loop(0, short_rows // 256, project, 0)

    masks = head_masks(2 * head_dim, head_dim)
    keep_first = lax.broadcasted_iota(jnp.int32, (1, 2 * head_dim), 1) < head_dim
    place_in_block = lax.broadcasted_iota(jnp.int32, (1, cap), 1)
    short_live = [place_in_block < short_len[i] for i in range(count)]
    passage_len = long_len[x]
    long_live = lax.broadcasted_iota(jnp.int32, (1, long_rows), 1) < passage_len
    pairs = width // (2 * head_dim)

    def attend_short(pair, carry):
        lanes = aligned(pair, 2 * head_dim)
        blocks_of = [pl.ds(i * cap, cap) for i in range(count)]
        queries, keys_all, values = [[qkv[b, rows, lanes] for rows in blocks_of] for b in range(3)]
        units = [(i, h) for i in range(count) for h in range(2)]
        scores = [times_turned(queries[i] * masks[h], keys_all[i]) for i, h in units]
        scores = [jnp.where(short_live[i], part, -1e30) for (i, h), part in zip(units, scores)]
        tops = [jnp.max(part, axis=-1, keepdims=True) for part in scores]
        exponents = [jnp.exp(part - top) for part, top in zip(scores, tops)]
        totals = [jnp.sum(part, axis=-1, keepdims=True) for part in exponents]
        probs = [(part * (1.0 / total)).astype(jnp.bfloat16) for part, total in zip(exponents, totals)]
        parts = [times(part, values[i]) for (i, h), part in zip(units, probs)]
        for (i, h), part in zip(units, probs):
            short_probs[i, 2 * pair + h] = part
        for i in range(count):
            mixed[blocks_of[i], lanes] = jnp.where(keep_first, parts[2 * i], parts[2 * i + 1]).astype(jnp.bfloat16)
        return carry

    lax.fori_loop(0, pairs // 2, attend_short, 0)
    net.relay_z(2)
    lax.fori_loop(pairs // 2, pairs - 1, attend_short, 0)
    net.start(3)
    net.relay_plane(1)
    lax.fori_loop(pairs - 1, pairs, attend_short, 0)
    net.start_plane(3)
    move(short_probs, out_short_probs)
    wires.landed(tok, rows_in.at[theirs])
    lax.fori_loop(short_rows // 256, total_rows // 256, project, 0)
    move(qkv, out_qkv)
    move(rows_in, out_rows)

    wires.landed(pooled, far_pool)
    chosen = []
    for block in range(total_rows // cap):
        if block < count:
            mask, start = short_pool[block : block + 1, :], 0
            limit = short_len[block]
        else:
            step = block - count
            in_half, start = step % (half // cap) * cap, step * cap
            at = slice(in_half, in_half + cap)
            own = jnp.where(x == 0, long_pool[0:1, at], long_pool[1:2, at])
            far = jnp.where(x == 0, far_pool[0:1, at], far_pool[1:2, at])
            mask = jnp.where(x == step // (half // cap), own, far)
            limit = passage_len - start
        keep = (place_in_block < limit) & ((mask > 0) | (place_in_block + start == 0))
        chosen.append(jnp.where(keep, 1.0, 0.0))
    for block in range(count):
        share[block : block + 1, :] = chosen[block] / jnp.sum(chosen[block], axis=-1, keepdims=True)
    long_total = sum(jnp.sum(row, axis=-1, keepdims=True) for row in chosen[count:])
    for block in range(count, total_rows // cap):
        share[block : block + 1, :] = chosen[block] / long_total

    def attend_long(pair, carry):
        lanes = aligned(pair, 2 * head_dim)
        rows = pl.ds(short_rows, long_rows)
        keys_all, values = qkv[1, rows, lanes], qkv[2, rows, lanes]
        for block in range(long_rows // 256):
            inner = pl.ds(block * 256, 256)
            rows = pl.ds(short_rows + block * 256, 256)
            queries = qkv[0, rows, lanes]
            parts = []
            for h in range(2):
                probs = weights_forward(queries * masks[h], keys_all, long_live)
                long_probs[2 * pair + h, inner, :] = probs
                parts.append(times(probs, values))
            mixed[rows, lanes] = jnp.where(keep_first, parts[0], parts[1]).astype(jnp.bfloat16)
        return carry

    lax.fori_loop(0, pairs - 2, attend_long, 0)
    net.relay_plane(2)
    net.relay_corner(1)
    lax.fori_loop(pairs - 2, pairs - 1, attend_long, 0)
    net.relay_z(3)
    lax.fori_loop(pairs - 1, pairs, attend_long, 0)
    move(long_probs, out_long_probs)
    move(mixed, out_mixed)
    net.finish(1)
    assemble(whole1, 0, 1, wq.at[pl.ds(3, 1)])
    vectors[8:16, :] = sum_slabs(whole1, 24)
    move(wq, out_wq)

    def attach(i, carry):
        rows = aligned(i, 256)
        first_in = rows_in[rows, :].astype(jnp.float32) + (times(mixed[rows, :], wq[3]) + vectors[2:3, :])
        normal, factor = normalize(first_in)
        out = normal * vectors[4:5, :] + vectors[6:7, :]
        first[rows, :] = out
        low[rows, :] = out.astype(jnp.bfloat16)
        hat[rows, :] = normal.astype(jnp.bfloat16)
        scale[rows, :] = jnp.broadcast_to(factor, (256, scale.shape[1]))
        return carry

    lax.fori_loop(0, total_rows // 256, attach, 0)
    move(first, out_first)
    move(low, out_low)
    move(hat, out_hat)
    move(scale, out_scale)
    net.relay_corner(2)
    net.finish(2)
    assemble(whole2, 0, 4, wu)
    move(wu, out_wu)

    def leaving(i):
        j, rows = lax.div(i, 4), aligned(lax.rem(i, 4), 256)
        return (
            pltpu.make_async_copy(acted.at[j, rows], out_acted.at[j, rows], leave.at[0, i]),
            pltpu.make_async_copy(slope.at[j, rows], out_slope.at[j, rows], leave.at[1, i]),
        )

    def expand(i, carry):
        j, rows = lax.div(i, 4), aligned(lax.rem(i, 4), 256)
        inner = times(low[rows, :], wu[j]) + vectors[pl.ds(8 + j, 1), :]
        value, grad = gelu_and_slope(inner)
        acted[j, rows, :] = value.astype(jnp.bfloat16)
        slope[j, rows, :] = grad.astype(jnp.bfloat16)
        for copy in leaving(i):
            copy.start()
        return carry

    def left(i, carry):
        for copy in leaving(i):
            copy.wait()
        return carry

    lax.fori_loop(0, 7, expand, 0)
    net.relay_plane(3)
    lax.fori_loop(7, 14, expand, 0)
    net.relay_corner(3)
    lax.fori_loop(14, 16, expand, 0)
    net.finish(3)
    wires.close()
    lax.fori_loop(0, 16, left, 0)
    for copy in [local[0]] + local[3:]:
        copy.wait()


def forward(lengths, parameters, pools, short_tok, long_tok, groups):
    short_rows, width = short_tok.shape
    half = long_tok.shape[1]
    long_rows = 2 * half
    rows = short_rows + long_rows
    count, cap = pools[0].shape
    inner = 4 * width
    copies = 4 * ((groups - 1) + 4 * groups + 4 * groups) + 2
    low = jnp.bfloat16
    shape = jax.ShapeDtypeStruct
    outs = (
        shape((groups, 8, SIZES[3], width), low),
        shape((4, width, width), low),
        shape((4, width, width), low),
        shape((rows, width), low),
        shape((3, rows, width), low),
        shape((count, HEADS, cap, cap), low),
        shape((HEADS, long_rows, long_rows), low),
        shape((rows, width), low),
        shape((rows, width), jnp.float32),
        shape((rows, width), low),
        shape((rows, 128), jnp.float32),
        shape((rows, width), low),
        shape((inner // width, rows, width), low),
        shape((inner // width, rows, width), low),
        shape((16, width), jnp.float32),
        shape((rows // cap, cap), jnp.float32),
    )
    anywhere, near = pl.BlockSpec(memory_space=pl.ANY), pl.BlockSpec(memory_space=pltpu.VMEM)
    scalars = pl.BlockSpec(memory_space=pltpu.SMEM)
    kept = [pltpu.VMEM(out.shape, out.dtype) for out in outs[1:14]]
    return pl.pallas_call(
        forward_kernel,
        name="forward",
        out_shape=outs,
        in_specs=[scalars] * 2 + [near] * 11 + [anywhere] * 2,
        out_specs=[anywhere] * 14 + [near] * 2,
        scratch_shapes=[pltpu.VMEM((groups, 8, SIZES[k], width), low) for k in range(3)]
        + kept
        + [
            pltpu.VMEM(pools[1].shape, pools[1].dtype),
            pltpu.SemaphoreType.DMA((copies,)),
            pltpu.SemaphoreType.DMA((copies,)),
            pltpu.SemaphoreType.DMA((24,)),
            pltpu.SemaphoreType.DMA((2, 16)),
        ],
        compiler_params=pltpu.CompilerParams(
            collective_id=0, has_side_effects=True, vmem_limit_bytes=60 * 1024 * 1024
        ),
    )(*lengths, *parameters, *pools, short_tok, long_tok)


def backward_kernel(
    short_len, long_len, vectors, share, short_pool_cot, long_pool_cot, short_cot, long_cot,
    in_down, in_wq, in_wu, in_rows, in_qkv, in_short_probs, in_long_probs, in_mixed,
    in_first, in_hat, in_scale, in_low, in_acted, in_slope,
    short_out, long_out, short_grad, long_grad, short_pooled, long_pooled,
    grad_qkv, grad_out, grad_up, grad_down, grad_vectors, grad_up_vector,
    wide, pair, w_up, w_far, hat, sums, branch, low, scale, halves, probs_short,
    vector_sums, pool_cots, pooled_rows, pooled_own, pooled_far,
    *more,
):
    place = Place()
    x, other = place.x, 1 - place.x
    *chunks, send, recv, here, blocks, fetch = more
    parts = len(SUMS)
    grads, *received = [chunks[i * parts : (i + 1) * parts] for i in range(7)]
    total_rows, width = sums.shape
    short_rows = short_out.shape[0]
    count, cap = probs_short.shape[1], probs_short.shape[-1]
    long_rows = total_rows - short_rows
    half = long_rows // 2
    head_dim = width // HEADS
    steps = total_rows // 256
    low_type = jnp.bfloat16
    local = []

    def move(src, dst):
        copy = pltpu.make_async_copy(src, dst, here.at[len(local)])
        copy.start()
        local.append(copy)
        return copy

    mine = pl.ds(pl.multiple_of(short_rows + x * half, half), half)
    theirs = pl.ds(pl.multiple_of(short_rows + other * half, half), half)
    place.greet_start()
    load_down = [move(in_down.at[j], w_far.at[j]) for j in range(4)]
    load_down += [
        move(short_cot, branch.at[pl.ds(0, short_rows)]),
        move(long_cot.at[x], branch.at[mine]),
    ]
    passage_len = long_len[x]

    def block_at(step):
        return jnp.where(step < 2, step, 2 + lax.rem(step + x, 2))

    def block_copies(i):
        rows = aligned(i, 256)
        return (
            pltpu.make_async_copy(in_acted.at[:, rows], wide.at[:, rows], blocks.at[0, i]),
            pltpu.make_async_copy(in_first.at[rows], sums.at[rows], blocks.at[1, i]),
        )

    for copy in block_copies(0):
        copy.start()
    vector_sums[...] = jnp.zeros_like(vector_sums)
    pool_cots[0:count, :] = short_pool_cot[...]
    pool_cots[count : 2 * count, :] = jnp.broadcast_to(long_pool_cot[pl.ds(x, 1), :], (count, width))
    place.greet_wait()
    wires = Wires(send, recv)
    swap_cot = wires.put(long_cot.at[other], branch.at[mine], place.at_x())
    net = Scatter(wires, place, grads, *received)
    for copy in load_down:
        copy.wait()
    tall = lax.broadcasted_iota(jnp.int32, (256, 1), 0)
    diagonal = lax.broadcasted_iota(jnp.int32, (cap, cap), 0) == lax.broadcasted_iota(jnp.int32, (cap, cap), 1)

    def add_vector(row, rows):
        vector_sums[row : row + 1, :] += jnp.sum(rows, axis=0, keepdims=True)

    def second(step, carry):
        i = block_at(step)
        rows = aligned(i, 256)

        @pl.when(step == steps - 1)
        def _():
            wires.landed(swap_cot, branch.at[theirs])

        @pl.when(step < steps - 1)
        def _():
            for copy in block_copies(block_at(step + 1)):
                copy.start()

        for copy in block_copies(i):
            copy.wait()
        product = times(wide[0, rows, :], w_far[0])
        for j in range(1, 4):
            product += times(wide[j, rows, :], w_far[j])
        normal, factor = normalize(sums[rows, :] + (product + vectors[3:4, :]))
        lens = [
            jnp.where(2 * i + part < count, short_len[lax.rem(2 * i + part, count)], passage_len - (2 * i + part - count) * cap)
            for part in range(2)
        ]
        live = tall < jnp.where(tall < cap, lens[0], lens[1] + cap)
        final = jnp.where(live, normal * vectors[5:6, :] + vectors[7:8, :], 0.0)
        low[rows, :] = final.astype(low_type)
        spread = []
        for part in range(2):
            share_row = share[pl.ds(2 * i + part, 1), :]
            column = jnp.sum(jnp.where(diagonal, share_row, 0.0), axis=1, keepdims=True)
            piece = final[part * cap : (part + 1) * cap]
            pooled_rows[pl.ds(2 * i + part, 1), :] = jnp.sum(piece * column, axis=0, keepdims=True)
            spread.append(column * pool_cots[pl.ds(2 * i + part, 1), :])
        grad_final = jnp.where(live, branch[rows, :].astype(jnp.float32), 0.0) + jnp.concatenate(spread, axis=0)
        add_vector(5, grad_final * normal)
        add_vector(7, grad_final)
        scaled = grad_final * vectors[5:6, :]
        mean_one = jnp.mean(scaled, axis=-1, keepdims=True)
        mean_two = jnp.mean(scaled * normal, axis=-1, keepdims=True)
        grad_second = factor * (scaled - mean_one - normal * mean_two)
        sums[rows, :] = grad_second
        grad_branch = grad_second.astype(low_type)
        branch[rows, :] = grad_branch
        add_vector(3, grad_branch.astype(jnp.float32))
        return carry

    lax.fori_loop(0, steps, second, 0)
    short_pooled[...] = pooled_rows[0:count, :]
    own_pooled = jnp.sum(pooled_rows[count : 2 * count, :], axis=0, keepdims=True)
    pooled_own[...] = jnp.broadcast_to(own_pooled, pooled_own.shape)
    long_pooled[pl.ds(x, 1), :] = own_pooled
    out_copies = [
        move(low.at[pl.ds(0, short_rows)], short_out),
        move(low.at[mine], long_out.at[x]),
    ]
    load_slope = [move(in_slope.at[0], pair.at[0]), move(in_slope.at[1], pair.at[1])]
    load_up = move(in_wu, w_up)
    load_hat, load_scale = move(in_hat, hat), move(in_scale, scale)

    swap_out = wires.put(low.at[theirs], long_out.at[x], place.at_x())
    swap_pooled = wires.put(pooled_own, pooled_far, place.at_x())

    def down_step(i, carry):
        j, part = lax.div(i, 2), lax.rem(i, 2)
        product = turned_times(wide[j, :, aligned(part, width // 2)], branch[...])
        grads[5][j, aligned(part, 4)] = product.reshape(4, SUMS[5], width).astype(low_type)
        return carry

    lax.fori_loop(0, 8, down_step, 0, unroll=2)
    net.send_core(5)

    def inner_block(j):
        def inner(i, carry):
            rows = aligned(i, 256)
            product = times_turned(branch[rows, :], w_far[j]) * pair[j % 2, rows, :].astype(jnp.float32)
            grad_inner = product.astype(low_type)
            wide[j, rows, :] = grad_inner
            add_vector(8 + j, grad_inner.astype(jnp.float32))
            return carry

        lax.fori_loop(0, steps, inner, 0, unroll=2)

    load_slope[0].wait()
    inner_block(0)
    load_slope.append(move(in_slope.at[2], pair.at[0]))
    load_slope[1].wait()
    inner_block(1)
    load_slope.append(move(in_slope.at[3], pair.at[1]))
    for copy in out_copies:
        copy.wait()
    wires.has_left(swap_out)
    load_low = move(in_low, low)
    net.after_core(5)
    load_slope[2].wait()
    inner_block(2)
    load_mixed = move(in_mixed, pair.at[0])
    load_slope[3].wait()
    inner_block(3)
    load_wq = move(in_wq, w_far)

    def up_step(i, carry):
        r, both = lax.div(i, 2), lax.rem(i, 2)
        data = low[:, aligned(r, width // 2)]
        halves[0] = turned_times(data, wide[2 * both])
        halves[1] = turned_times(data, wide[2 * both + 1])

        def one(k, carry):
            rows = pl.ds(pl.multiple_of(k * 24, 8), 24)
            data = jnp.concatenate([halves[0, rows, :], halves[1, rows, :]], axis=0)
            grads[4][2 * r + lax.div(k, 8), lax.rem(k, 8), aligned(both, 48), :] = data.astype(low_type)
            return carry

        return lax.fori_loop(0, 16, one, carry)

    load_low.wait()
    lax.fori_loop(0, 4, up_step, 0)
    net.send_core(4)
    net.after_first(5)

    load_up.wait()
    load_hat.wait()
    load_scale.wait()

    def first_back(i, carry):
        rows = aligned(i, 256)
        grad_first = sums[rows, :]
        for j in range(4):
            grad_first += times_turned(wide[j, rows, :], w_up[j])
        normal = hat[rows, :].astype(jnp.float32)
        add_vector(4, grad_first * normal)
        add_vector(6, grad_first)
        scaled = grad_first * vectors[4:5, :]
        mean_one = jnp.mean(scaled, axis=-1, keepdims=True)
        mean_two = jnp.mean(scaled * normal, axis=-1, keepdims=True)
        grad_in = scale[rows, 0:1] * (scaled - mean_one - normal * mean_two)
        sums[rows, :] = grad_in
        grad_attn = grad_in.astype(low_type)
        branch[rows, :] = grad_attn
        add_vector(2, grad_attn.astype(jnp.float32))
        return carry

    lax.fori_loop(0, steps // 2, first_back, 0)
    net.after_core(4)
    lax.fori_loop(steps // 2, steps, first_back, 0)
    load_qkv = move(in_qkv, wide.at[pl.ds(0, 3)])
    load_rows = move(in_rows, wide.at[3])
    net.after_second(5)

    load_mixed.wait()
    load_wq.wait()
    def out_step(r, carry):
        halves[0] = turned_times(pair[0, :, aligned(r, width // 2)], branch[...])

        def one(k, carry):
            rows = pl.ds(pl.multiple_of(k * 24, 8), 24)
            data = jnp.concatenate([halves[0, rows, :], vector_sums[8:16, :]], axis=0)
            grads[3][2 * r + lax.div(k, 8), lax.rem(k, 8)] = data.astype(low_type)
            return carry

        return lax.fori_loop(0, 16, one, carry)

    lax.fori_loop(0, 2, out_step, 0)

    def mixed_back(i, carry):
        rows = aligned(i, 256)
        pair[1, rows, :] = times_turned(branch[rows, :], w_far[3]).astype(low_type)
        return carry

    lax.fori_loop(0, steps, mixed_back, 0)
    net.send_core(3)

    def probs_copies(p, slot):
        lanes = pl.ds(2 * p, 2)
        return (
            pltpu.make_async_copy(in_short_probs.at[:, lanes], probs_short.at[slot], fetch.at[0, slot]),
            pltpu.make_async_copy(
                in_long_probs.at[lanes],
                w_up.at[pl.ds(2 * slot, 2), pl.ds(0, long_rows), pl.ds(0, long_rows)],
                fetch.at[1, slot],
            ),
        )

    for copy in probs_copies(0, 0):
        copy.start()
    load_qkv.wait()
    score_scale = 1.0 / math.sqrt(head_dim)
    masks = head_masks(2 * head_dim, head_dim)
    pairs = width // (2 * head_dim)

    def attend_back(lanes, units):
        heads = [(u, h) for u in range(len(units)) for h in range(2)]
        queries = [wide[0, rows, lanes] for rows, _, _, _ in units]
        grads_mixed = [pair[1, rows, lanes] for rows, _, _, _ in units]
        overlaps = [
            grad.astype(jnp.float32) * pair[0, rows, lanes].astype(jnp.float32)
            for grad, (rows, _, _, _) in zip(grads_mixed, units)
        ]
        centers = [
            jnp.sum(overlaps[u] * masks[h].astype(jnp.float32), axis=-1, keepdims=True) for u, h in heads
        ]
        grads_head = [grads_mixed[u] * masks[h] for u, h in heads]
        probs = [units[u][1](h) for u, h in heads]
        grads_probs = [times_turned(grad, units[u][3]) for grad, (u, h) in zip(grads_head, heads)]
        scores = [
            (part.astype(jnp.float32) * (grad - center)).astype(low_type)
            for part, grad, center in zip(probs, grads_probs, centers)
        ]
        grads_q = [times(part, units[u][2] * masks[h]) for part, (u, h) in zip(scores, heads)]
        grads_k = [turned_times(queries[u] * masks[h], part) for part, (u, h) in zip(scores, heads)]
        grads_v = [turned_times(grad, part) for part, grad in zip(probs, grads_head)]
        for u, (rows, _, _, _) in enumerate(units):
            total = grads_q[2 * u] + grads_q[2 * u + 1]
            wide[0, rows, lanes] = (total * score_scale).astype(low_type)
        return [
            [grads[2 * u] + grads[2 * u + 1] for u in range(len(units))] for grads in (grads_k, grads_v)
        ]

    def attention_back(p, carry):
        slot = lax.rem(p, 2)
        for copy in probs_copies(p, slot):
            copy.wait()

        @pl.when(p + 1 < pairs)
        def _():
            for copy in probs_copies(p + 1, 1 - slot):
                copy.start()

        lanes = aligned(p, 2 * head_dim)
        blocks_of = [pl.ds(i * cap, cap) for i in range(count)]
        units = [
            (rows, lambda h, i=i: probs_short[slot, i, h], wide[1, rows, lanes], wide[2, rows, lanes])
            for i, rows in enumerate(blocks_of)
        ]
        grads_k, grads_v = attend_back(lanes, units)
        for rows, grad_k, grad_v in zip(blocks_of, grads_k, grads_v):
            wide[1, rows, lanes] = grad_k.T.astype(low_type)
            wide[2, rows, lanes] = grad_v.T.astype(low_type)
        rows = pl.ds(short_rows, long_rows)
        keys_all, values = wide[1, rows, lanes], wide[2, rows, lanes]
        total_k, total_v = None, None
        for block in range(long_rows // 256):
            inner = pl.ds(block * 256, 256)
            unit = (
                pl.ds(short_rows + block * 256, 256),
                lambda h, inner=inner: w_up[2 * slot + h, inner, 0:long_rows],
                keys_all,
                values,
            )
            (grad_k,), (grad_v,) = attend_back(lanes, [unit])
            total_k = grad_k if total_k is None else total_k + grad_k
            total_v = grad_v if total_v is None else total_v + grad_v
        wide[1, rows, lanes] = total_k.T.astype(low_type)
        wide[2, rows, lanes] = total_v.T.astype(low_type)
        return carry

    third = width // 3

    def qkv_step(group):
        lanes = pl.ds(group * third, third)

        def bias(i, carry):
            rows = aligned(i, 256)
            for row, b in ((0, 0), (1, 2)):
                piece = wide[b, rows, lanes].astype(jnp.float32)
                vector_sums[row : row + 1, lanes] += jnp.sum(piece, axis=0, keepdims=True)
            return carry

        lax.fori_loop(0, steps, bias, 0)

        def step(r, carry):
            data = wide[3, :, aligned(r, width // 2)]
            for b in range(3):
                halves[0, :, b * third : (b + 1) * third] = turned_times(data, wide[b, :, lanes])

            def one(k, carry):
                rows = pl.ds(pl.multiple_of(k * 24, 8), 24)
                pieces = [halves[0, rows, b * third : (b + 1) * third] for b in range(3)]
                data = jnp.concatenate(pieces + [vector_sums[0:8, lanes]], axis=0)
                grads[group][2 * r + lax.div(k, 8), lax.rem(k, 8)] = data.astype(low_type)
                return carry

            return lax.fori_loop(0, 16, one, carry)

        lax.fori_loop(0, 2, step, 0)

    lax.fori_loop(0, pairs // 3, attention_back, 0)
    net.after_first(4)
    load_rows.wait()
    qkv_step(0)
    net.after_core(3)
    net.send_core(0)
    lax.fori_loop(pairs // 3, 2 * pairs // 3, attention_back, 0)
    net.after_second(4)
    net.after_core(0)
    qkv_step(1)
    net.send_core(1)
    net.after_first(3)
    lax.fori_loop(2 * pairs // 3, pairs, attention_back, 0)
    net.after_core(1)
    net.after_first(0)
    qkv_step(2)
    net.send_core(2)
    net.after_second(3)

    def tokens_back(rows):
        grad_in = sums[rows, :]
        for b in range(3):
            grad_in += times_turned(wide[b, rows, :], w_far[b])
        return grad_in

    far_low, far_in = low.at[pl.ds(0, half)], low.at[pl.ds(half, half)]
    far_low[...] = tokens_back(theirs).astype(low_type)

    def tokens_step(i, carry):
        rows = pl.ds(pl.multiple_of(jnp.where(i < 2, i * 256, short_rows + x * half), 256), 256)
        sums[rows, :] = tokens_back(rows)
        return carry

    lax.fori_loop(0, 1, tokens_step, 0)
    net.after_core(2)
    net.after_first(1)
    net.after_second(0)
    net.after_first(2)
    swap_grad = wires.put(far_low, far_in, place.at_x())
    net.after_second(1)
    net.after_second(2)
    lax.fori_loop(1, 3, tokens_step, 0)
    move(sums.at[pl.ds(0, short_rows)], short_grad)
    move(sums.at[mine], long_grad.at[x])
    grad_down[...] = net.finish(5)
    total = net.finish(4)
    for j in range(4):
        grad_up[:, j * width : (j + 1) * width] = total[24 * j : 24 * j + 24]
    total = net.finish(3)
    grad_out[...] = total[0:24]
    grad_up_vector[...] = total[24:32]
    wires.landed(swap_pooled, pooled_far)
    long_pooled[pl.ds(other, 1), :] = pooled_far[0:1, :]
    wires.landed(swap_grad, far_in)
    sums[theirs, :] = far_in[...].astype(jnp.float32)
    move(sums.at[theirs], long_grad.at[other])
    wires.landed(swap_out, long_out.at[other])
    for group in range(3):
        total = net.finish(group)
        for b in range(3):
            columns = slice(b * width + group * third, b * width + (group + 1) * third)
            grad_qkv[:, columns] = total[24 * b : 24 * b + 24]
        grad_vectors[:, group * third : (group + 1) * third] = total[72:80]
    wires.close()
    for copy in local[-3:]:
        copy.wait()


def backward(lengths, vectors, share, pool_cots, cots, arrays, groups):
    width = vectors.shape[1]
    rows = arrays[3].shape[0]
    count, _, cap, _ = arrays[5].shape
    short_rows = count * cap
    half = (rows - short_rows) // 2
    low, wide_type = jnp.bfloat16, jnp.float32
    shape = jax.ShapeDtypeStruct
    rows24 = 24
    outs = (
        shape((short_rows, width), low),
        shape((2, half, width), low),
        shape((short_rows, width), wide_type),
        shape((2, half, width), wide_type),
        shape((count, width), wide_type),
        shape((2, width), wide_type),
        shape((rows24, 3 * width), wide_type),
        shape((rows24, width), wide_type),
        shape((rows24, 4 * width), wide_type),
        shape((4 * rows24, width), wide_type),
        shape((8, width), wide_type),
        shape((8, width), wide_type),
    )
    anywhere, near = pl.BlockSpec(memory_space=pl.ANY), pl.BlockSpec(memory_space=pltpu.VMEM)
    copies = len(SUMS) * (4 + 6 + (groups - 1)) + 4

    widths = (width // 3,) * 3 + (width,) * 3

    def chunks(parts, sizes):
        return [pltpu.VMEM(parts + (size, columns), low) for size, columns in zip(sizes, widths)]

    rest = tuple(size - some for size, some in zip(SUMS, SUMS_X))
    scratch = [
        pltpu.VMEM((4, rows, width), low),
        pltpu.VMEM((2, rows, width), low),
        pltpu.VMEM((4, width, width), low),
        pltpu.VMEM((4, width, width), low),
        pltpu.VMEM((rows, width), low),
        pltpu.VMEM((rows, width), wide_type),
        pltpu.VMEM((rows, width), low),
        pltpu.VMEM((rows, width), low),
        pltpu.VMEM((rows, 128), wide_type),
        pltpu.VMEM((2, width // 2, width), wide_type),
        pltpu.VMEM((2, count, 2, cap, cap), low),
        pltpu.VMEM((16, width), wide_type),
        pltpu.VMEM((2 * count, width), wide_type),
        pltpu.VMEM((2 * count, width), wide_type),
        pltpu.VMEM((8, width), wide_type),
        pltpu.VMEM((8, width), wide_type),
        *chunks((groups, 8), SUMS),
        *chunks((4, groups), SUMS),
        *chunks((2, groups), SUMS_X),
        *chunks((2, groups), rest),
        *chunks((groups,), rest),
        *chunks((groups,), SUMS_X),
        *chunks((groups - 1,), SUMS),
        pltpu.SemaphoreType.DMA((copies,)),
        pltpu.SemaphoreType.DMA((copies,)),
        pltpu.SemaphoreType.DMA((24,)),
        pltpu.SemaphoreType.DMA((2, rows // 256)),
        pltpu.SemaphoreType.DMA((2, 2)),
    ]
    return pl.pallas_call(
        backward_kernel,
        name="backward",
        out_shape=outs,
        in_specs=[pl.BlockSpec(memory_space=pltpu.SMEM)] * 2 + [near] * 4 + [anywhere] * 16,
        out_specs=[anywhere] * 4 + [near] * 8,
        scratch_shapes=scratch,
        compiler_params=pltpu.CompilerParams(
            collective_id=1, has_side_effects=True, vmem_limit_bytes=63 * 1024 * 1024
        ),
    )(*lengths, vectors, share, *pool_cots, *cots, *arrays)


def results_kernel(
    in_0, in_1, in_2, in_3, in_4, in_5, in_6, in_7, in_8, in_9, in_10, in_11,
    out_0, out_1, out_2, out_3, out_4, out_5, out_6, out_7, out_8, out_9, pair_0, pair_1, ups, pair_2, pair_3,
    *more,
):
    *held, come, leave = more
    grad_vectors, grad_ups = held[10:]
    sources = (in_0, in_1, in_2, in_3, in_4, in_5, in_6, in_7, in_8, in_9, in_10, in_11)
    places = (out_0, out_1, out_4, out_5, out_2, out_3, out_6, out_7, out_8, out_9)
    ins = [pltpu.make_async_copy(sources[i], held[i], come.at[i]) for i in range(12)]
    outs = [pltpu.make_async_copy(held[i], places[i], leave.at[i]) for i in range(10)]
    for copy in ins:
        copy.start()
    for i in range(10):
        ins[i].wait()
        outs[i].start()
    ins[10].wait()
    ins[11].wait()
    device = lax.axis_index("dp") * 2 + lax.axis_index("seq")
    size, width = in_7.shape
    rows = pltpu.roll(grad_vectors[...], lax.rem(width - device * size, width), 1)
    for i, ref in enumerate((pair_0, pair_1, pair_2, pair_3)):
        ref[...] = rows[2 * i : 2 * i + 2, 0:size]
    start = lax.rem(device, 8) * (4 * size)
    row = grad_ups[pl.ds(lax.div(device, 8), 1), :]
    row = pltpu.roll(jnp.broadcast_to(row, (8, width)), lax.rem(width - start, width), 1)
    ups[...] = row[0:1, 0 : 4 * size]
    for copy in outs:
        copy.wait()


def results(arrays):
    size = arrays[7].shape[0]
    order = (0, 1, 4, 5, 2, 3, 6, 7, 8, 9)
    shape = jax.ShapeDtypeStruct
    pair = shape((2, size), jnp.float32)
    outs = tuple(shape(arrays[i].shape, arrays[i].dtype) for i in order)
    anywhere, near = pl.BlockSpec(memory_space=pl.ANY), pl.BlockSpec(memory_space=pltpu.VMEM)
    return pl.pallas_call(
        results_kernel,
        name="results",
        out_shape=outs + (pair, pair, shape((1, 4 * size), jnp.float32), pair, pair),
        in_specs=[anywhere] * 12,
        out_specs=[anywhere] * 10 + [near] * 5,
        scratch_shapes=[pltpu.VMEM(array.shape, array.dtype) for array in arrays]
        + [pltpu.SemaphoreType.DMA((12,)), pltpu.SemaphoreType.DMA((10,))],
        compiler_params=pltpu.CompilerParams(vmem_limit_bytes=56 * 1024 * 1024),
    )(*arrays)


def layer_norm(row_data, gain_vec, shift_vec):
    center = row_data - jnp.mean(row_data, axis=-1, keepdims=True)
    spread = jnp.mean(center * center, axis=-1, keepdims=True)
    return center * lax.rsqrt(spread + EPS) * gain_vec + shift_vec


def exact_gelu(inner_act):
    return jax.nn.gelu(inner_act, approximate=False)


def outer_sum(left_rows, right_rows):
    return lax.dot_general(
        left_rows, right_rows, (((0,), (0,)), ((), ())), preferred_element_type=jnp.float32
    )


def times_transposed(left_rows, matrix):
    return lax.dot_general(
        left_rows, matrix, (((1,), (1,)), ((), ())), preferred_element_type=jnp.float32
    )


def masked_scores(queries, keys_all, key_live, score_scale):
    scores = (
        jnp.einsum("bqhe,bkhe->bhqk", queries, keys_all, preferred_element_type=jnp.float32)
        * score_scale
    )
    return jnp.where(key_live[:, None, None, :], scores, -1e30)


def attend_forward(pieces, score_scale):
    queries, keys_all, values, key_live = pieces
    scores = masked_scores(queries, keys_all, key_live, score_scale)
    highest = jnp.max(scores, axis=-1, keepdims=True)
    exponent = jnp.exp(scores - highest)
    totals = jnp.sum(exponent, axis=-1, keepdims=True)
    soft_probs = (exponent / totals).astype(jnp.bfloat16)
    mixed_heads = jnp.einsum(
        "bhqk,bkhe->bqhe", soft_probs, values, preferred_element_type=jnp.float32
    )
    return (mixed_heads.astype(jnp.bfloat16), (highest + jnp.log(totals))[..., 0])


def attend_backward(pieces, score_scale):
    queries, keys_all, values, key_live, grad_mixed, log_total = pieces
    scores = masked_scores(queries, keys_all, key_live, score_scale)
    soft_probs = jnp.exp(scores - log_total[..., None])
    grad_probs = jnp.einsum(
        "bqhe,bkhe->bhqk", grad_mixed, values, preferred_element_type=jnp.float32
    )
    grad_values = jnp.einsum(
        "bhqk,bqhe->bkhe",
        soft_probs.astype(jnp.bfloat16),
        grad_mixed,
        preferred_element_type=jnp.float32,
    )
    center = jnp.sum(soft_probs * grad_probs, axis=-1, keepdims=True)
    grad_scores = (soft_probs * (grad_probs - center)).astype(jnp.bfloat16)
    grad_queries = (
        jnp.einsum("bhqk,bkhe->bqhe", grad_scores, keys_all, preferred_element_type=jnp.float32)
        * score_scale
    )
    grad_keys = (
        jnp.einsum("bhqk,bqhe->bkhe", grad_scores, queries, preferred_element_type=jnp.float32)
        * score_scale
    )
    return (grad_queries, grad_keys, grad_values)


def by_blocks(function, per_block, arrays):
    blocks = arrays[0].shape[0] // per_block
    stacked = tuple((member.reshape((blocks, per_block) + member.shape[1:]) for member in arrays))
    results = lax.map(function, stacked)
    return jax.tree.map(
        lambda member: member.reshape((blocks * per_block,) + member.shape[2:]), results
    )


def general_shards(
    short_tokens,
    long_tokens,
    short_len,
    long_len,
    short_pool,
    long_pool,
    short_cot,
    long_cot,
    short_pool_cot,
    long_pool_cot,
    w_qkv,
    w_out,
    w_up,
    w_down,
    qv_bias,
    out_bias,
    up_bias,
    norm_gain,
    norm_shift,
):
    gathered = (
        lax.all_gather(w_qkv, ("dp", "seq"), axis=0, tiled=True),
        lax.all_gather(w_out, ("dp", "seq"), axis=0, tiled=True),
        lax.all_gather(w_up, ("dp", "seq"), axis=0, tiled=True),
        lax.all_gather(w_down, ("dp", "seq"), axis=0, tiled=True),
        lax.all_gather(qv_bias, ("dp", "seq"), axis=0, tiled=True),
        lax.all_gather(out_bias, ("dp", "seq"), axis=0, tiled=True),
        lax.all_gather(up_bias, ("dp", "seq"), axis=0, tiled=True),
        lax.all_gather(norm_gain, ("dp", "seq"), axis=0, tiled=True),
        lax.all_gather(norm_shift, ("dp", "seq"), axis=0, tiled=True),
    )
    qkv_matrix, out_matrix, up_matrix, down_matrix, qv_vec, out_vec, up_vec, gains, shifts = (
        gathered
    )
    gains = gains.astype(jnp.float32)
    shifts = shifts.astype(jnp.float32)
    short_count, short_cap, model_width = short_tokens.shape
    long_count, long_half = (long_tokens.shape[0], long_tokens.shape[1])
    head_count = HEADS
    head_dim = model_width // head_count
    score_scale = 1.0 / math.sqrt(head_dim)
    short_rows = short_count * short_cap
    long_rows = long_count * long_half
    short_place = jnp.arange(short_cap, dtype=jnp.int32)
    short_live = short_place[None, :] < short_len[:, None]
    long_place = lax.axis_index("seq") * long_half + jnp.arange(long_half, dtype=jnp.int32)
    long_live = long_place[None, :] < long_len[:, None]
    short_weight = (short_live & ((short_pool > 0) | (short_place[None, :] == 0))).astype(
        jnp.float32
    )
    long_weight = (long_live & ((long_pool > 0) | (long_place[None, :] == 0))).astype(jnp.float32)
    row_live = jnp.concatenate([short_live.reshape(-1), long_live.reshape(-1)]).astype(jnp.float32)
    inputs = jnp.concatenate(
        [
            short_tokens.reshape(short_rows, model_width),
            long_tokens.reshape(long_rows, model_width),
        ],
        axis=0,
    )
    joined = jnp.dot(inputs, qkv_matrix, preferred_element_type=jnp.float32)
    queries = (joined[:, :model_width] + qv_vec[:, 0]).astype(jnp.bfloat16)
    keys_all = joined[:, model_width : 2 * model_width].astype(jnp.bfloat16)
    values = (joined[:, 2 * model_width :] + qv_vec[:, 1]).astype(jnp.bfloat16)
    short_shape = (short_count, short_cap, head_count, head_dim)
    long_shape = (long_count, long_half, head_count, head_dim)
    short_q = queries[:short_rows].reshape(short_shape)
    short_k = keys_all[:short_rows].reshape(short_shape)
    short_v = values[:short_rows].reshape(short_shape)
    long_q = queries[short_rows:].reshape(long_shape)
    long_k = keys_all[short_rows:].reshape(long_count, long_half, model_width)
    long_v = values[short_rows:].reshape(long_count, long_half, model_width)
    short_block = math.gcd(short_count, max(1, 512 // short_cap))
    long_block = math.gcd(long_count, max(1, 512 // long_half))

    def forward_blocks(pieces):
        return attend_forward(pieces, score_scale)

    def backward_blocks(pieces):
        return attend_backward(pieces, score_scale)

    short_mixed, short_logsum = by_blocks(
        forward_blocks, short_block, (short_q, short_k, short_v, short_live)
    )
    gathered_k, gathered_v = (
        lax.all_gather(long_k, "seq", axis=1, tiled=True),
        lax.all_gather(long_v, "seq", axis=1, tiled=True),
    )
    full_len = gathered_k.shape[1]
    full_shape = (long_count, full_len, head_count, head_dim)
    long_key_live = jnp.arange(full_len, dtype=jnp.int32)[None, :] < long_len[:, None]
    long_mixed, long_logsum = by_blocks(
        forward_blocks,
        long_block,
        (long_q, gathered_k.reshape(full_shape), gathered_v.reshape(full_shape), long_key_live),
    )
    mixed_heads = jnp.concatenate(
        [short_mixed.reshape(short_rows, model_width), long_mixed.reshape(long_rows, model_width)],
        axis=0,
    )
    attn_out = jnp.dot(mixed_heads, out_matrix, preferred_element_type=jnp.float32) + out_vec[:, 0]
    first_in = inputs.astype(jnp.float32) + attn_out
    first_norm = layer_norm(first_in, gains[:, 0], shifts[:, 0])
    first_low = first_norm.astype(jnp.bfloat16)
    inner_act = jnp.dot(first_low, up_matrix, preferred_element_type=jnp.float32) + up_vec
    activated = exact_gelu(inner_act).astype(jnp.bfloat16)
    branch = jnp.dot(activated, down_matrix, preferred_element_type=jnp.float32) + out_vec[:, 1]
    second_in = first_norm + branch
    final_norm = layer_norm(second_in, gains[:, 1], shifts[:, 1]) * row_live[:, None]
    short_final = final_norm[:short_rows].reshape(short_count, short_cap, model_width)
    long_final = final_norm[short_rows:].reshape(long_count, long_half, model_width)
    short_total = jnp.sum(short_weight, axis=1)
    short_pooled = jnp.sum(short_final * short_weight[..., None], axis=1) / short_total[:, None]
    long_partial = jnp.sum(long_final * long_weight[..., None], axis=1)
    long_sum, long_total = lax.psum((long_partial, jnp.sum(long_weight, axis=1)), "seq")
    long_pooled = long_sum / long_total[:, None]
    grad_short = (
        short_cot.astype(jnp.float32) * short_live[..., None]
        + short_weight[..., None] * short_pool_cot[:, None, :] / short_total[:, None, None]
    )
    grad_long = (
        long_cot.astype(jnp.float32) * long_live[..., None]
        + long_weight[..., None] * long_pool_cot[:, None, :] / long_total[:, None, None]
    )
    grad_top = jnp.concatenate(
        [grad_short.reshape(short_rows, model_width), grad_long.reshape(long_rows, model_width)],
        axis=0,
    )
    _, second_back = jax.vjp(layer_norm, second_in, gains[:, 1], shifts[:, 1])
    grad_second, grad_gain_two, grad_shift_two = second_back(grad_top)
    grad_branch = grad_second.astype(jnp.bfloat16)
    grad_down = outer_sum(activated, grad_branch)
    grad_bias_two = jnp.sum(grad_branch.astype(jnp.float32), axis=0)
    grad_acted = times_transposed(grad_branch, down_matrix)
    _, gelu_back = jax.vjp(exact_gelu, inner_act)
    grad_inner = gelu_back(grad_acted)[0].astype(jnp.bfloat16)
    grad_up = outer_sum(first_low, grad_inner)
    grad_up_bias = jnp.sum(grad_inner.astype(jnp.float32), axis=0)
    grad_first = grad_second + times_transposed(grad_inner, up_matrix)
    _, first_back = jax.vjp(layer_norm, first_in, gains[:, 0], shifts[:, 0])
    grad_first_in, grad_gain_one, grad_shift_one = first_back(grad_first)
    grad_attn = grad_first_in.astype(jnp.bfloat16)
    grad_out = outer_sum(mixed_heads, grad_attn)
    grad_bias_one = jnp.sum(grad_attn.astype(jnp.float32), axis=0)
    grad_mixed = times_transposed(grad_attn, out_matrix).astype(jnp.bfloat16)
    short_dq, short_dk, short_dv = by_blocks(
        backward_blocks,
        short_block,
        (
            short_q,
            short_k,
            short_v,
            short_live,
            grad_mixed[:short_rows].reshape(short_shape),
            short_logsum,
        ),
    )
    again_k, again_v = (gathered_k, gathered_v)
    long_dq, long_dk, long_dv = by_blocks(
        backward_blocks,
        long_block,
        (
            long_q,
            again_k.reshape(full_shape),
            again_v.reshape(full_shape),
            long_key_live,
            grad_mixed[short_rows:].reshape(long_shape),
            long_logsum,
        ),
    )
    own_dk, own_dv = (
        lax.psum_scatter(
            long_dk.reshape(long_count, full_len, model_width).astype(jnp.bfloat16),
            "seq",
            scatter_dimension=1,
            tiled=True,
        ).astype(jnp.float32),
        lax.psum_scatter(
            long_dv.reshape(long_count, full_len, model_width).astype(jnp.bfloat16),
            "seq",
            scatter_dimension=1,
            tiled=True,
        ).astype(jnp.float32),
    )
    grad_queries = jnp.concatenate(
        [short_dq.reshape(short_rows, model_width), long_dq.reshape(long_rows, model_width)], axis=0
    ).astype(jnp.bfloat16)
    grad_keys = jnp.concatenate(
        [short_dk.reshape(short_rows, model_width), own_dk.reshape(long_rows, model_width)], axis=0
    ).astype(jnp.bfloat16)
    grad_values = jnp.concatenate(
        [short_dv.reshape(short_rows, model_width), own_dv.reshape(long_rows, model_width)], axis=0
    ).astype(jnp.bfloat16)
    grad_joined = jnp.concatenate([grad_queries, grad_keys, grad_values], axis=1)
    grad_qkv = outer_sum(inputs, grad_joined)
    grad_qv = jnp.stack(
        [
            jnp.sum(grad_queries.astype(jnp.float32), axis=0),
            jnp.sum(grad_values.astype(jnp.float32), axis=0),
        ],
        axis=1,
    )
    grad_inputs = grad_first_in + times_transposed(grad_joined, qkv_matrix)
    grad_out_vec = jnp.stack([grad_bias_one, grad_bias_two], axis=1)
    grad_gains = jnp.stack([grad_gain_one, grad_gain_two], axis=1)
    grad_shifts = jnp.stack([grad_shift_one, grad_shift_two], axis=1)
    shard_grads = (
        lax.psum_scatter(grad_qkv, ("dp", "seq"), scatter_dimension=0, tiled=True),
        lax.psum_scatter(grad_out, ("dp", "seq"), scatter_dimension=0, tiled=True),
        lax.psum_scatter(grad_up, ("dp", "seq"), scatter_dimension=0, tiled=True),
        lax.psum_scatter(grad_down, ("dp", "seq"), scatter_dimension=0, tiled=True),
        lax.psum_scatter(grad_qv, ("dp", "seq"), scatter_dimension=0, tiled=True),
        lax.psum_scatter(grad_out_vec, ("dp", "seq"), scatter_dimension=0, tiled=True),
        lax.psum_scatter(grad_up_bias, ("dp", "seq"), scatter_dimension=0, tiled=True),
        lax.psum_scatter(grad_gains, ("dp", "seq"), scatter_dimension=0, tiled=True),
        lax.psum_scatter(grad_shifts, ("dp", "seq"), scatter_dimension=0, tiled=True),
    )
    short_out = short_final.astype(jnp.bfloat16)
    long_out = long_final.astype(jnp.bfloat16)
    short_grad_in = grad_inputs[:short_rows].reshape(short_count, short_cap, model_width)
    long_grad_in = grad_inputs[short_rows:].reshape(long_count, long_half, model_width)
    return (
        short_out,
        long_out,
        short_pooled,
        long_pooled,
        short_grad_in,
        long_grad_in,
        shard_grads[0],
        shard_grads[1],
        shard_grads[2],
        shard_grads[3],
        shard_grads[4],
        shard_grads[5],
        shard_grads[6],
        shard_grads[7],
        shard_grads[8],
    )


def fast_shards(
    short_tokens, long_tokens, short_len, long_len, short_pool, long_pool, short_cot, long_cot,
    short_pool_cot, long_pool_cot, w_qkv, w_out, w_up, w_down, qv_bias, out_bias, up_bias,
    norm_gain, norm_shift,
):
    groups = lax.axis_size("dp") // 4
    width = w_out.shape[1]
    count, cap, _ = short_tokens.shape
    short_rows = count * cap
    lengths = (short_len, long_len)
    parameters = (
        w_qkv, w_out, w_up, w_down, qv_bias.T, out_bias.T, norm_gain.T, norm_shift.T, up_bias[None, :],
    )
    (down, *kept, vectors, share) = forward(
        lengths,
        parameters,
        (short_pool, long_pool),
        short_tokens.reshape(short_rows, width),
        long_tokens,
        groups,
    )
    arrays = backward(
        lengths,
        vectors,
        share,
        (short_pool_cot, long_pool_cot),
        (short_cot.reshape(short_rows, width), long_cot),
        (down.reshape(4, width, width), *kept),
        groups,
    )
    (
        short_out, long_out, short_pooled, long_pooled, short_grad, long_grad,
        grad_qkv, grad_out, grad_up, grad_down, qv, out, ups, gain, shift,
    ) = results(arrays)
    return (
        short_out.reshape(short_tokens.shape), long_out, short_pooled, long_pooled,
        short_grad.reshape(short_tokens.shape), long_grad, grad_qkv, grad_out, grad_up, grad_down,
        qv.T, out.T, ups[0], gain.T, shift.T,
    )


def solution(mesh):
    short_spec, long_spec, spread = P(("dp", "seq"), None, None), P("dp", "seq", None), P(("dp", "seq"), None)
    vector, parameters = P(("dp", "seq")), [P(("dp", "seq"), None)] * 6
    in_specs = (
        short_spec, long_spec, vector, P("dp"), spread, P("dp", "seq"), short_spec, long_spec,
        spread, P("dp", None), *parameters, vector, spread, spread,
    )
    out_specs = (
        short_spec, long_spec, spread, P("dp", None), short_spec, long_spec, *parameters, vector,
        spread, spread,
    )
    dp, seq = mesh.shape["dp"], mesh.shape["seq"]

    def run(*arrays):
        width = arrays[11].shape[1]
        passages = arrays[1].shape[0] // dp
        regular = dp == 16 and seq == 2 and passages == 2 and width == 24 * dp * seq
        body = fast_shards if regular else general_shards
        return jax.shard_map(body, mesh=mesh, in_specs=in_specs, out_specs=out_specs, check_vma=False)(*arrays)

    return run
```
